128 devices in a mesh: dp: 32 (over z, y_hi, x), tp: 4 (over y_lo, core).
Axes of the slice: x: 4, y: 4 (y_hi: 2, y_lo: 2; y = y_hi * 2 + y_lo), z: 4, core: 2. Of those that a mesh axis runs over, the one named last changes fastest.
Arguments:
- tokens: bfloat16 [8192, 2048], P(('dp', 'tp')), may hold values from -6 to 6
- cotangent: bfloat16 [8192, 2048], P(('dp', 'tp')), may hold values from -6 to 6
- seg_ids: int32 [8192], P('dp'), may hold values from 0 to 17, as said below
- parents: int32 [18], replicated, may hold values from 0 to 9, as said below
- tau: float32 [1], replicated, may hold values from 6 to 12
- w_query: bfloat16 [2048, 2048], P('dp', 'tp')
- w_up: bfloat16 [2048, 8192], P('dp', 'tp'), may hold values from -0.125 to 0.125
- w_out: bfloat16 [2048, 2048], P('dp', 'tp'), may hold values from -0.5 to 0.5
- w_down: bfloat16 [2048, 8192], P('dp', 'tp'), may hold values from -0.125 to 0.125
- query_bias: bfloat16 [128, 16], P('dp', 'tp'), may hold values from -3 to 3
- up_bias: bfloat16 [128, 64], P('dp', 'tp'), may hold values from -3 to 3
- w_keyval: bfloat16 [2048, 256], P(('dp', 'tp')), may hold values from -0.125 to 0.125
- value_bias: bfloat16 [128], P(('dp', 'tp')), may hold values from -3 to 3
- norm1_gain: bfloat16 [2048], P(('dp', 'tp')), may hold values from 0.5 to 1.5
- norm1_bias: bfloat16 [2048], P(('dp', 'tp')), may hold values from -2 to 2
- norm2_gain: bfloat16 [2048], P(('dp', 'tp')), may hold values from 0.5 to 1.5
- norm2_bias: bfloat16 [2048], P(('dp', 'tp')), may hold values from -2 to 2
- out_bias: bfloat16 [2048], P(('dp', 'tp')), may hold values from -2 to 2
- down_bias: bfloat16 [2048], P(('dp', 'tp')), may hold values from -2 to 2
Outputs:
- output: bfloat16 [8192, 2048], P(('dp', 'tp'))
- grad_input: float32 [8192, 2048], P(('dp', 'tp'))
- grad_w_query: float32 [2048, 2048], P('dp', 'tp')
- grad_w_up: float32 [2048, 8192], P('dp', 'tp')
- grad_w_out: float32 [2048, 2048], P('dp', 'tp')
- grad_w_down: float32 [2048, 8192], P('dp', 'tp')
- grad_query_bias: float32 [128, 16], P('dp', 'tp')
- grad_up_bias: float32 [128, 64], P('dp', 'tp')
- grad_w_keyval: float32 [2048, 256], P(('dp', 'tp'))
- grad_value_bias: float32 [128], P(('dp', 'tp'))
- grad_norm1_gain: float32 [2048], P(('dp', 'tp'))
- grad_norm1_bias: float32 [2048], P(('dp', 'tp'))
- grad_norm2_gain: float32 [2048], P(('dp', 'tp'))
- grad_norm2_bias: float32 [2048], P(('dp', 'tp'))
- grad_out_bias: float32 [2048], P(('dp', 'tp'))
- grad_down_bias: float32 [2048], P(('dp', 'tp'))
- clipped_query: bfloat16 [2048, 2048], P('dp', 'tp')
- clipped_query_bias: bfloat16 [128, 16], P('dp', 'tp')
The draws below stay inside these ranges and needn't reach their ends.
Inputs may be any that keep to these rules, and one draw needn't show every extreme that they name: `seg_ids`: each of 2 trees has a trunk segment of 2048 tokens, 4 branch segments and 4 leaf segments of 256 tokens each. Tokens 8 * t * 256 to 8 * (t + 1) * 256 - 1 form trunk t (segment t); after all trunks, aligned blocks of 256 tokens hold the branches (segments 2 to 9) and leaves (the segments after), each leaf after its branch. `parents`: A trunk is its own parent; a branch's parent is a trunk, 4 branches to a trunk; leaf 2 + 2 * 4 + b has branch 2 + b as parent.
All inputs are finite; a program needn't handle non-finite values.
Results may differ from the reference program's by a relative error of at most 0.03.
Values may be sent and summed in bfloat16 or wider, within the bound.
A program may use at most 192 MiB of HBM per device.

```python
from functools import partial
import jax
import jax.numpy as jnp
from jax import lax

D = 2048
HEADS = 16
HD = 128
FF = 8192
TREES = 2
BRANCHES = 4
TOKENS = 8192
UNIT = 256
SEGS = 18


def tree_layout(key):
    pairs = TREES * BRANCHES
    slot_key, owner_key = jax.random.split(key)
    slot_of = jax.random.permutation(slot_key, 2 * pairs).astype(jnp.int32)
    first = jnp.minimum(slot_of[:pairs], slot_of[pairs:])
    second = jnp.maximum(slot_of[:pairs], slot_of[pairs:])
    owner = jax.random.permutation(owner_key, pairs).astype(jnp.int32) // BRANCHES
    final_pair = jnp.argmax((second == 2 * pairs - 1).astype(jnp.int32))
    owner = (owner - owner[final_pair]) % TREES
    index = jnp.arange(pairs, dtype=jnp.int32)
    slot_seg = jnp.zeros((2 * pairs,), jnp.int32).at[first].set(TREES + index).at[second].set(TREES + pairs + index)
    trunk_seg = jnp.repeat(jnp.arange(TREES, dtype=jnp.int32), 8)
    block_seg = jnp.concatenate([trunk_seg, slot_seg])
    seg_ids = jnp.repeat(block_seg, UNIT, total_repeat_length=TOKENS)
    parents = jnp.concatenate([jnp.arange(TREES, dtype=jnp.int32), owner, TREES + index])
    return (seg_ids, parents)


def draw_seg_ids(key, part):
    return tree_layout(key)[0]


def draw_parents(key, part):
    return tree_layout(key)[1]


def draw_w_query(key, part):
    key = jax.random.fold_in(key, 11)
    scale_key, entry_key = jax.random.split(key)
    head_scale = jnp.exp(jax.random.uniform(scale_key, (HEADS,), jnp.float32, 0.0, 1.0986))
    entries = jnp.clip(jax.random.normal(entry_key, (D, HEADS, HD), jnp.float32), -4.0, 4.0)
    return (entries * head_scale[None, :, None] * D ** (-0.5)).reshape(D, D).astype(jnp.bfloat16)


def block_levels(own_key, extent, shards, low, high):
    loudness = 1.0
    for position, shards_of in shards:
        draws = jax.random.uniform(jax.random.fold_in(jax.random.fold_in(own_key, 6), position), (shards_of,), jnp.float32, low / len(shards), high / len(shards))
        loudness = loudness * jnp.repeat(jnp.exp(draws), extent[position] // shards_of).reshape((-1,) + (1,) * (len(extent) - 1 - position))
    return loudness


def scatter_about(rng, dims, width, reach, shards=(), held_as=jnp.bfloat16):
    level = block_levels(rng, dims, shards, -0.22, 0.18) if shards else 1.0
    values = jax.random.normal(rng, dims, jnp.float32) * width * level
    return jnp.minimum(jnp.maximum(values, -reach), reach).astype(held_as)


def setup_inputs(seed: int = 0) -> dict:
    key_list = jax.random.split(jax.random.key(seed), 20)
    tokens = scatter_about(key_list[0], (TOKENS, D), 1.0, 6.0, ((0, 128),))
    cotangent = scatter_about(key_list[1], (TOKENS, D), 1.0, 6.0, ((0, 128),))
    seg_ids = draw_seg_ids(jax.random.fold_in(key_list[19], 71), 0)
    parents = draw_parents(jax.random.fold_in(key_list[19], 71), 0)
    tau = jnp.clip(jax.random.uniform(key_list[4], (1,), jnp.float32, 6.0, 12.0), 6.0, 12.0)
    w_query = draw_w_query(jax.random.fold_in(key_list[19], 71), 0)
    w_up = scatter_about(key_list[6], (D, FF), D ** -0.5, 0.125, ((0, 32), (1, 4)))
    w_out = scatter_about(key_list[7], (D, D), (D // 16) ** -0.5, 0.5, ((0, 32), (1, 4)))
    w_down = scatter_about(key_list[8], (D, FF), (FF // 4) ** -0.5, 0.125, ((0, 32), (1, 4)))
    query_bias = scatter_about(key_list[9], (HD, HEADS), 0.5, 3.0, ((0, 32), (1, 4)))
    up_bias = scatter_about(key_list[10], (128, FF // 128), 0.5, 3.0, ((0, 32), (1, 4)))
    w_keyval = scatter_about(key_list[11], (D, 2 * HD), D ** -0.5, 0.125, ((0, 128),))
    value_bias = scatter_about(key_list[12], (HD,), 0.5, 3.0, ((0, 128),))
    norm1_gain = jnp.clip(1.0 + 0.1 * jax.random.normal(key_list[13], (D,), jnp.float32), 0.5, 1.5).astype(jnp.bfloat16)
    norm1_bias = scatter_about(key_list[14], (D,), 0.3, 2.0, ((0, 128),))
    norm2_gain = jnp.clip(1.0 + 0.1 * jax.random.normal(key_list[15], (D,), jnp.float32), 0.5, 1.5).astype(jnp.bfloat16)
    norm2_bias = scatter_about(key_list[16], (D,), 0.3, 2.0, ((0, 128),))
    out_bias = scatter_about(key_list[17], (D,), 0.3, 2.0, ((0, 128),))
    down_bias = scatter_about(key_list[18], (D,), 0.3, 2.0, ((0, 128),))
    return dict(tokens=tokens, cotangent=cotangent, seg_ids=seg_ids, parents=parents, tau=tau, w_query=w_query, w_up=w_up, w_out=w_out, w_down=w_down, query_bias=query_bias, up_bias=up_bias, w_keyval=w_keyval, value_bias=value_bias, norm1_gain=norm1_gain, norm1_bias=norm1_bias, norm2_gain=norm2_gain, norm2_bias=norm2_bias, out_bias=out_bias, down_bias=down_bias)


@jax.custom_vjp
def low(v):
    return lax.optimization_barrier(v.astype(jnp.bfloat16)).astype(jnp.float32)

@jax.custom_vjp
def low_back(v):
    return v

def low_keep(v):
    return (low(v), None)

def low_pass(kept, grad):
    return (grad,)

def back_keep(v):
    return (v, None)

def back_low(kept, grad):
    return (low(grad),)
low.defvjp(low_keep, low_pass)
low_back.defvjp(back_keep, back_low)
EPS = 1e-05

def matmul(left, right):
    return jnp.dot(left, right, precision=lax.Precision.HIGHEST)

def layer_norm(values, gain, shift):
    centred = values - lax.optimization_barrier(jnp.mean(values, axis=-1, keepdims=True))
    inverse = lax.rsqrt(lax.optimization_barrier(jnp.mean(centred * centred, axis=-1, keepdims=True)) + EPS)
    return centred * inverse * gain + shift

def attention(queries, keyvals, seg_ids, ancestry):
    keys = keyvals[:, :HD]
    values = keyvals[:, HD:]
    block = min(512, TOKENS)
    count = TOKENS // block
    query_blocks = queries.reshape(count, block, HEADS, HD)
    seg_blocks = seg_ids.reshape(count, block)
    pos_blocks = jnp.arange(TOKENS, dtype=jnp.int32).reshape(count, block)
    key_pos = jnp.arange(TOKENS, dtype=jnp.int32)
    scale = HD ** (-0.5)

    def one_block(pieces):
        query_blk, seg_blk, pos_blk = pieces
        scores = low_back(jnp.einsum('qhd,kd->hqk', query_blk, keys, precision=lax.Precision.HIGHEST) * scale)
        allowed = ancestry[seg_blk][:, seg_ids] & (key_pos[None, :] <= pos_blk[:, None])
        masked = jnp.where(allowed[None], scores, -jnp.inf)
        top = lax.optimization_barrier(jnp.max(masked, axis=2, keepdims=True))
        weights = jnp.exp(masked - top)
        probs = weights / lax.optimization_barrier(jnp.sum(weights, axis=2, keepdims=True))
        heads = jnp.einsum('hqk,kd->qhd', low(probs), values, precision=lax.Precision.HIGHEST)
        return (low(low_back(heads)), lax.optimization_barrier(jnp.max(top[:, :, 0], axis=1)))
    outs, tops = lax.map(jax.checkpoint(one_block), (query_blocks, seg_blocks, pos_blocks))
    return (outs.reshape(TOKENS, HEADS * HD), lax.optimization_barrier(jnp.max(tops, axis=0)))

def layer(seg_ids, ancestry, resid, w_query, w_up, w_out, w_down, query_bias, up_bias, w_keyval, value_bias, norm1_gain, norm1_bias, norm2_gain, norm2_bias, out_bias, down_bias):
    h_one = low(layer_norm(resid, norm1_gain, norm1_bias))
    queries = low(low_back(matmul(h_one, w_query) + query_bias.T.reshape(-1)))
    shift = jnp.concatenate([jnp.zeros((HD,), jnp.float32), value_bias])
    keyvals = low(low_back(matmul(h_one, w_keyval) + shift))
    heads, top = attention(queries, keyvals, seg_ids, ancestry)
    middle = resid + low_back(matmul(heads, w_out.T) + out_bias)
    h_two = low(layer_norm(middle, norm2_gain, norm2_bias))
    hidden_pre = low_back(matmul(h_two, w_up) + up_bias.T.reshape(-1))
    hidden = low(jax.nn.gelu(hidden_pre, approximate=True))
    result = middle + (matmul(hidden, w_down.T) + down_bias)
    return (result, top)

def reference(tokens, cotangent, seg_ids, parents, tau, w_query, w_up, w_out, w_down, query_bias, up_bias, w_keyval, value_bias, norm1_gain, norm1_bias, norm2_gain, norm2_bias, out_bias, down_bias):
    labels = jnp.arange(SEGS, dtype=jnp.int32)
    grand = parents[parents]
    ancestry = (labels[None, :] == labels[:, None]) | (labels[None, :] == parents[:, None]) | (labels[None, :] == grand[:, None])
    params = [p.astype(jnp.float32) for p in (w_query, w_up, w_out, w_down, query_bias, up_bias, w_keyval, value_bias, norm1_gain, norm1_bias, norm2_gain, norm2_bias, out_bias, down_bias)]
    result, back, top = jax.vjp(partial(layer, seg_ids, ancestry), tokens.astype(jnp.float32), *params, has_aux=True)
    grads = back(cotangent.astype(jnp.float32))
    limit = tau[0]
    factor = limit / jnp.maximum(top, limit)
    clipped_query = (params[0] * jnp.repeat(factor, HD)[None, :]).astype(jnp.bfloat16)
    clipped_bias = (params[4] * factor[None, :]).astype(jnp.bfloat16)
    return (result.astype(jnp.bfloat16), grads[0], grads[1], grads[2], grads[3], grads[4], grads[5], grads[6], grads[7], grads[8], grads[9], grads[10], grads[11], grads[12], grads[13], grads[14], clipped_query, clipped_bias)
```

```python
import itertools

import jax
import jax.numpy as jnp
from jax import lax
from jax.experimental import pallas as pl
from jax.experimental.pallas import tpu as pltpu
from jax.sharding import Mesh, PartitionSpec as P

EPS = 1e-05
AXES = ("z", "yh", "x", "yl", "c")
F32 = jnp.float32
BF16 = jnp.bfloat16
VMEM = pltpu.VMEM
NEG = -1e30


class Net:
    def __init__(self, send_sems, recv_sems):
        self.z, self.yh, self.x, self.yl, self.c = (lax.axis_index(a) for a in AXES)
        self.y = self.yh * 2 + self.yl
        self.yu, self.yo, self.yd = (lax.rem(self.y + s, 4) for s in (1, 2, 3))
        self.xu, self.xo, self.xd = (lax.rem(self.x + s, 4) for s in (1, 2, 3))
        self.zu, self.zo, self.zd = (lax.rem(self.z + s, 4) for s in (1, 2, 3))
        up, down = lax.rem(self.yh + self.yl, 2), lax.rem(self.yh + 1 - self.yl, 2)
        self.dev = {
            "yu": {"yh": up, "yl": 1 - self.yl},
            "yd": {"yh": down, "yl": 1 - self.yl},
            "yo": {"yh": 1 - self.yh},
            "c": {"c": 1 - self.c},
            "xu": {"x": self.xu},
            "xd": {"x": self.xd},
            "xo": {"x": self.xo},
            "zu": {"z": self.zu},
            "zd": {"z": self.zd},
            "zo": {"z": self.zo},
        }
        self.send_sems, self.recv_sems = send_sems, recv_sems
        self.count = 0
        self.sent = []

    def barrier(self, names):
        sem = pltpu.get_barrier_semaphore()
        for name in names:
            pl.semaphore_signal(
                sem, inc=1, device_id=self.dev[name], device_id_type=pl.DeviceIdType.MESH
            )
        pl.semaphore_wait(sem, len(names))

    def slot(self):
        self.count += 1
        return self.count - 1

    def copy(self, src, dst, k, name):
        return pltpu.make_async_remote_copy(
            src_ref=src,
            dst_ref=dst,
            send_sem=self.send_sems.at[k],
            recv_sem=self.recv_sems.at[k],
            device_id=self.dev[name],
            device_id_type=pl.DeviceIdType.MESH,
        )

    def send(self, src, dst, k, name):
        one = self.copy(src, dst, k, name)
        one.start()
        self.sent.append(one)

    def got(self, ref, k):
        self.copy(ref, ref, k, "c").wait_recv()

    def finish(self):
        for one in self.sent:
            one.wait_send()


def run_all(*steps):
    live = list(steps)
    while live:
        rest = []
        for one in live:
            try:
                next(one)
                rest.append(one)
            except StopIteration:
                pass
        live = rest


def group_gather(net, src, out):
    y, c, yu, yd, yo = net.y, net.c, net.yu, net.yd, net.yo
    k = [net.slot() for _ in range(9)]
    half = src.shape[0] // 2
    lo, hi = pl.ds(0, half), pl.ds(half, half)
    mine = out.at[y, c]
    net.send(src, mine, k[0], "yu")
    net.send(src, mine, k[1], "yd")
    net.send(src, mine, k[2], "c")
    yield
    net.got(out.at[yd, c], k[0])
    net.send(out.at[yd, c, lo], out.at[yd, c, lo], k[3], "yu")
    net.send(out.at[yd, c], out.at[yd, c], k[4], "c")
    net.got(out.at[yu, c], k[1])
    net.send(out.at[yu, c, hi], out.at[yu, c, hi], k[5], "yd")
    net.send(out.at[yu, c], out.at[yu, c], k[6], "c")
    yield
    net.got(out.at[yo, c, lo], k[3])
    net.send(out.at[yo, c, lo], out.at[yo, c, lo], k[7], "c")
    net.got(out.at[yo, c, hi], k[5])
    net.send(out.at[yo, c, hi], out.at[yo, c, hi], k[8], "c")
    yield
    net.got(out.at[y, 1 - c], k[2])
    net.got(out.at[yd, 1 - c], k[4])
    net.got(out.at[yu, 1 - c], k[6])
    net.got(out.at[yo, 1 - c, lo], k[7])
    net.got(out.at[yo, 1 - c, hi], k[8])


def group_scatter(net, part, from_core, held, from_half, from_full, total):
    y, c, yu, yd, yo = net.y, net.c, net.yu, net.yd, net.yo
    k = [net.slot() for _ in range(8)]
    n = part.shape[2]
    half = n // 2
    lo, hi = pl.ds(0, half), pl.ds(half, half)
    for i, d in enumerate((yo, yu, yd, y)):
        net.send(part.at[d, 1 - c], from_core.at[d], k[i], "c")

    def core_sum(i, d):
        net.got(from_core.at[d], k[i])
        held[d] = (part[d, c].astype(F32) + from_core[d].astype(F32)).astype(BF16)

    yield
    core_sum(0, yo)
    net.send(held.at[yo, lo], from_half.at[0], k[4], "yu")
    net.send(held.at[yo, hi], from_half.at[1], k[5], "yd")
    core_sum(1, yu)
    core_sum(2, yd)
    yield
    net.got(from_half.at[0], k[4])
    held[yu, lo] = (held[yu, lo].astype(F32) + from_half[0].astype(F32)).astype(BF16)
    net.send(held.at[yu], from_full.at[0], k[6], "yu")
    net.got(from_half.at[1], k[5])
    held[yd, hi] = (held[yd, hi].astype(F32) + from_half[1].astype(F32)).astype(BF16)
    net.send(held.at[yd], from_full.at[1], k[7], "yd")
    core_sum(3, y)
    yield
    net.got(from_full.at[0], k[6])
    net.got(from_full.at[1], k[7])
    total(held[y].astype(F32) + from_full[0].astype(F32) + from_full[1].astype(F32))


def scatter_scratch(n, w):
    return [VMEM((4, n, w), BF16), VMEM((4, n, w), BF16), VMEM((2, n // 2, w), BF16), VMEM((2, n, w), BF16)]


BOTH = slice(None)


def plane_gather(net, o):
    z, x, xu, xd, xo, zu, zd, zo = net.z, net.x, net.xu, net.xd, net.xo, net.zu, net.zd, net.zo
    k = [net.slot() for _ in range(16)]
    every = slice(None)

    def send(view, i, name):
        net.send(view, view, k[i], name)

    def got(view, i):
        net.got(view, k[i])

    send(o(z, BOTH, x, 0), 0, "xu")
    send(o(z, BOTH, x, 0), 1, "xd")
    send(o(z, BOTH, x, 1), 2, "zu")
    send(o(z, BOTH, x, 1), 3, "zd")
    yield
    got(o(z, BOTH, xd, 0), 0)
    send(o(z, 0, xd, 0), 4, "xu")
    got(o(zd, BOTH, x, 1), 2)
    send(o(zd, 0, x, 1), 6, "zu")
    got(o(z, BOTH, xu, 0), 1)
    send(o(z, 1, xu, 0), 5, "xd")
    got(o(zu, BOTH, x, 1), 3)
    send(o(zu, 1, x, 1), 7, "zd")
    yield
    got(o(z, 0, xo, 0), 4)
    got(o(z, 1, xo, 0), 5)
    send(o(z, BOTH, every, 0), 8, "zu")
    send(o(z, BOTH, every, 0), 9, "zd")
    got(o(zo, 0, x, 1), 6)
    got(o(zo, 1, x, 1), 7)
    send(o(every, BOTH, x, 1), 10, "xu")
    send(o(every, BOTH, x, 1), 11, "xd")
    yield
    got(o(zd, BOTH, every, 0), 8)
    send(o(zd, 0, every, 0), 12, "zu")
    got(o(every, BOTH, xd, 1), 10)
    send(o(every, 0, xd, 1), 14, "xu")
    got(o(zu, BOTH, every, 0), 9)
    send(o(zu, 1, every, 0), 13, "zd")
    got(o(every, BOTH, xu, 1), 11)
    send(o(every, 1, xu, 1), 15, "xd")
    yield
    got(o(zo, 0, every, 0), 12)
    got(o(zo, 1, every, 0), 13)
    got(o(every, 0, xo, 1), 14)
    got(o(every, 1, xo, 1), 15)


def add_into(dst, *others):
    for index in itertools.product(*[range(n) for n in dst.shape[:-2]]):
        at = index + (slice(None), slice(None))
        total = dst[at].astype(F32)
        for other in others:
            total = total + other[at].astype(F32)
        dst[at] = total.astype(dst.dtype)


def plane_scatter(net, g, tmp):
    z, x, xu, xd, xo, zu, zd, zo = net.z, net.x, net.xu, net.xd, net.xo, net.zu, net.zd, net.zo
    t1, t2, u1, u2, t3, t4, u3, u4 = tmp
    k = [net.slot() for _ in range(16)]
    every = slice(None)

    def send(src, dst, i, name):
        net.send(src, dst, k[i], name)

    def got(ref, i):
        net.got(ref, k[i])

    send(g(zo, 0, every, 0), t1.at[0], 0, "zu")
    send(g(zo, 1, every, 0), t1.at[1], 1, "zd")
    send(g(every, 0, xo, 1), t2.at[0], 2, "xu")
    send(g(every, 1, xo, 1), t2.at[1], 3, "xd")
    yield
    got(t1.at[0], 0)
    add_into(g(zu, 0, every, 0), t1.at[0])
    send(g(zu, BOTH, every, 0), u1.at[0], 4, "zu")
    got(t2.at[0], 2)
    add_into(g(every, 0, xu, 1), t2.at[0])
    send(g(every, BOTH, xu, 1), u2.at[0], 6, "xu")
    got(t1.at[1], 1)
    add_into(g(zd, 1, every, 0), t1.at[1])
    send(g(zd, BOTH, every, 0), u1.at[1], 5, "zd")
    got(t2.at[1], 3)
    add_into(g(every, 1, xd, 1), t2.at[1])
    send(g(every, BOTH, xd, 1), u2.at[1], 7, "xd")
    yield
    got(u1.at[0], 4)
    got(u1.at[1], 5)
    add_into(g(z, BOTH, every, 0), u1.at[0], u1.at[1])
    send(g(z, 0, xo, 0), t3.at[0], 8, "xu")
    send(g(z, 1, xo, 0), t3.at[1], 9, "xd")
    got(u2.at[0], 6)
    got(u2.at[1], 7)
    add_into(g(every, BOTH, x, 1), u2.at[0], u2.at[1])
    send(g(zo, 0, x, 1), t4.at[0], 10, "zu")
    send(g(zo, 1, x, 1), t4.at[1], 11, "zd")
    yield
    got(t3.at[0], 8)
    add_into(g(z, 0, xu, 0), t3.at[0])
    send(g(z, BOTH, xu, 0), u3.at[0], 12, "xu")
    got(t4.at[0], 10)
    add_into(g(zu, 0, x, 1), t4.at[0])
    send(g(zu, BOTH, x, 1), u4.at[0], 14, "zu")
    got(t3.at[1], 9)
    add_into(g(z, 1, xd, 0), t3.at[1])
    send(g(z, BOTH, xd, 0), u3.at[1], 13, "xd")
    got(t4.at[1], 11)
    add_into(g(zd, 1, x, 1), t4.at[1])
    send(g(zd, BOTH, x, 1), u4.at[1], 15, "zd")
    yield
    got(u3.at[0], 12)
    got(u3.at[1], 13)
    add_into(g(z, BOTH, x, 0), u3.at[0], u3.at[1])
    got(u4.at[0], 14)
    got(u4.at[1], 15)
    add_into(g(z, BOTH, x, 1), u4.at[0], u4.at[1])


def plane_scratch(n, w):
    return [
        VMEM((2, 4, n, w), BF16),
        VMEM((2, 4, n, w), BF16),
        VMEM((2, 2, 4, n, w), BF16),
        VMEM((2, 4, 2, n, w), BF16),
        VMEM((2, n, w), BF16),
        VMEM((2, n, w), BF16),
        VMEM((2, 2, n, w), BF16),
        VMEM((2, 2, n, w), BF16),
    ]


def column_view(ref):
    w = ref.shape[-1] // 2

    def view(zz, half, xx, part):
        return ref.at[zz, half, xx, :, pl.ds(part * w, w)]

    return view


def sems(n):
    return [pltpu.SemaphoreType.DMA((n,)), pltpu.SemaphoreType.DMA((n,))]


def params(cid, limit=56 << 20):
    return pltpu.CompilerParams(collective_id=cid, has_side_effects=True, vmem_limit_bytes=limit)


ANY = pl.BlockSpec(memory_space=pl.ANY)
INV = pl.BlockSpec(memory_space=pltpu.VMEM)
INS = pl.BlockSpec(memory_space=pltpu.SMEM)
PLANE = ("xu", "xd", "zu", "zd")
RING = ("yu", "yd", "c")


def opening(tokens, cotangent, small, wq_own, wq_oth, wo_own, wo_oth):
    def kernel(tok, cot, small, qa, qb, oa, ob, tok_out, cot_out, small_out, q_out, o_out, local, ss, rs):
        net = Net(ss, rs)
        z, yh, x, yl, c = net.z, net.yh, net.x, net.yl, net.c
        locals_ = [
            pltpu.make_async_copy(src, dst, local.at[i])
            for i, (src, dst) in enumerate(
                (
                    (qa, q_out.at[z, yh, x]),
                    (oa, o_out.at[z, yh, x]),
                    (tok, tok_out.at[net.y, c]),
                    (cot, cot_out.at[net.y, c]),
                    (small, small_out.at[z, net.y * 2 + c, x]),
                )
            )
        ]
        for one in locals_:
            one.start()
        net.barrier(PLANE + RING + ("yo",))

        def weight(own, oth, out, i):
            k = net.slot()
            net.send(oth, out.at[z, yh, x], k, "yo")
            yield
            locals_[i].wait()
            net.got(out.at[z, 1 - yh, x], k)
            yield from plane_gather(net, column_view(out))

        def small_all():
            k = [net.slot() for _ in range(7)]
            y = net.y

            def at(yy, cc):
                return small_out.at[z, yy * 2 + cc, x]

            net.send(small, at(y, c), k[0], "yu")
            net.send(small, at(y, c), k[1], "yd")
            net.send(small, at(y, c), k[2], "yo")
            net.send(small, at(y, c), k[3], "c")
            yield
            for i, d in enumerate((net.yd, net.yu, net.yo)):
                net.got(at(d, c), k[i])
                net.send(at(d, c), at(d, c), k[4 + i], "c")
            yield
            for i, d in enumerate((y, net.yd, net.yu, net.yo)):
                net.got(at(d, 1 - c), k[3 + i])
            locals_[4].wait()

            def view(zz, half, xx, part):
                which = pl.ds(0, 8) if half == BOTH else pl.ds(4 * half, 4)
                cols = pl.ds(0, 256) if part == 0 else pl.ds(256, 128)
                return small_out.at[zz, which, xx, :, cols]

            yield from plane_gather(net, view)

        run_all(
            small_all(),
            weight(qa, qb, q_out, 0),
            weight(oa, ob, o_out, 1),
            group_gather(net, tok, tok_out),
            group_gather(net, cot, cot_out),
        )
        locals_[2].wait()
        locals_[3].wait()
        net.finish()

    n, d = tokens.shape
    weight = jax.ShapeDtypeStruct((4, 2, 4, n, wq_own.shape[1]), BF16)
    rows = jax.ShapeDtypeStruct((4, 2, n, d), BF16)
    return pl.pallas_call(
        kernel,
        out_shape=(rows, rows, jax.ShapeDtypeStruct((4, 8, 4) + small.shape, BF16), weight, weight),
        in_specs=[ANY] * 7,
        out_specs=(ANY,) * 5,
        scratch_shapes=[pltpu.SemaphoreType.DMA((5,))] + sems(17 * 2 + 7 + 16 + 18),
        compiler_params=params(1),
        name="opening",
    )(tokens, cotangent, small, wq_own, wq_oth, wo_own, wo_oth)


def gather_ff(up_own, up_oth, dn_own, dn_oth):
    def kernel(ua, ub, da, db, u_out, d_out, local, ss, rs):
        net = Net(ss, rs)
        z, yh, x = net.z, net.yh, net.x
        mine = [
            pltpu.make_async_copy(ua, u_out.at[z, yh, x], local.at[0]),
            pltpu.make_async_copy(da, d_out.at[z, yh, x], local.at[1]),
        ]
        for one in mine:
            one.start()
        net.barrier(PLANE + ("yo",))

        def weight(oth, out, one):
            k = net.slot()
            net.send(oth, out.at[z, yh, x], k, "yo")
            yield
            one.wait()
            net.got(out.at[z, 1 - yh, x], k)
            yield from plane_gather(net, column_view(out))

        run_all(weight(ub, u_out, mine[0]), weight(db, d_out, mine[1]))
        net.finish()

    shape = jax.ShapeDtypeStruct((4, 2, 4) + up_own.shape, BF16)
    return pl.pallas_call(
        kernel,
        out_shape=(shape, shape),
        in_specs=[ANY] * 4,
        out_specs=(ANY, ANY),
        scratch_shapes=[pltpu.SemaphoreType.DMA((2,))] + sems(34),
        compiler_params=params(2),
        name="gather_ff",
    )(up_own, up_oth, dn_own, dn_oth)


def gather_kv(kv):
    def kernel(kv, out, local, ss, rs):
        net = Net(ss, rs)
        z, x, c = net.z, net.x, net.c
        me = pltpu.make_async_copy(kv.at[c], out.at[z, c, x], local)
        me.start()
        net.barrier(PLANE + ("c",))
        me.wait()

        def view(zz, half, xx, part):
            rows = pl.ds(0, 256) if half == BOTH else pl.ds(128 * half, 128)
            return out.at[zz, c, xx, rows, pl.ds(part * 128, 128)]

        run_all(plane_gather(net, view))
        k = net.slot()
        net.send(out.at[:, c], out.at[:, c], k, "c")
        net.got(out.at[:, 1 - c], k)
        net.finish()

    return pl.pallas_call(
        kernel,
        out_shape=jax.ShapeDtypeStruct((4, 2, 4, 256, 256), BF16),
        in_specs=[ANY],
        out_specs=ANY,
        scratch_shapes=[pltpu.SemaphoreType.DMA] + sems(17),
        compiler_params=params(3),
        name="gather_kv",
    )(kv)


def block_place(segs, parents, block):
    seg = segs[block]
    parent = parents[seg]
    trunk = parents[parent]
    parent_block = jnp.int32(16)
    for b in range(16, 32):
        parent_block = jnp.where(segs[b] == parent, b, parent_block)
    return trunk, parent_block, seg >= 10, seg >= 2


def attend(q, kv, segs, parents):
    def kernel(segs, parents, q, kv, o, log_sum, tops, scores):
        z, x = lax.axis_index("z"), lax.axis_index("x")
        lane = lax.broadcasted_iota(jnp.int32, (256, 512), 1) & 255
        row = lax.broadcasted_iota(jnp.int32, (256, 512), 0)
        best = []
        for b in range(2):
            block = z * 8 + b * 4 + x
            trunk, parent_block, leaf, branch = block_place(segs, parents, block)
            both = jnp.concatenate([q[b, :, :128], q[b, :, 128:]], axis=0)

            def score(key_block):
                return (
                    lax.dot_general(
                        kv[key_block, :, :128], both, (((1,), (1,)), ((), ())), preferred_element_type=F32
                    )
                    * 128**-0.5
                )

            def trunk_score(i, top):
                s = score(trunk * 8 + i)
                gap = (block - trunk * 8 - i) * 256
                s = jnp.where(row - lane <= gap, s, NEG)
                scores[i] = s
                return jnp.maximum(top, jnp.max(s, axis=0, keepdims=True))

            top = lax.fori_loop(0, 8, trunk_score, jnp.full((1, 512), NEG, F32))
            s = jnp.where(leaf, score(parent_block), NEG)
            scores[8] = s
            top = jnp.maximum(top, jnp.max(s, axis=0, keepdims=True))
            s = jnp.where((row <= lane) & branch, score(block), NEG)
            scores[9] = s
            top = jnp.maximum(top, jnp.max(s, axis=0, keepdims=True))

            def weigh(i, carry):
                acc, total = carry
                w = jnp.exp(scores[i] - top)
                key_block = jnp.where(i < 8, trunk * 8 + i, jnp.where(i == 8, parent_block, block))
                acc = acc + lax.dot_general(
                    kv[key_block, :, 128:], w.astype(BF16), (((0,), (0,)), ((), ())), preferred_element_type=F32
                )
                return acc, total + jnp.sum(w, axis=0, keepdims=True)

            acc, total = lax.fori_loop(0, 10, weigh, (jnp.zeros((128, 512), F32), jnp.zeros((1, 512), F32)))
            heads = (acc / total).T.astype(BF16)
            o[b, :, :128] = heads[:256]
            o[b, :, 128:] = heads[256:]
            log_sum[b] = jnp.broadcast_to(top + jnp.log(total), (8, 512))
            best.append(top)
        top = jnp.maximum(best[0], best[1])
        for h in range(2):
            tops[h] = jnp.full((8, 128), jnp.max(top[:, h * 256 : (h + 1) * 256]), F32)

    return pl.pallas_call(
        kernel,
        out_shape=(
            jax.ShapeDtypeStruct((2, 256, 256), BF16),
            jax.ShapeDtypeStruct((2, 8, 512), F32),
            jax.ShapeDtypeStruct((2, 8, 128), F32),
        ),
        in_specs=[INS, INS, INV, INV],
        out_specs=(INV, INV, INV),
        scratch_shapes=[VMEM((10, 256, 512), F32)],
        compiler_params=pltpu.CompilerParams(vmem_limit_bytes=56 << 20),
        name="attend",
    )(segs, parents, q, kv)


def attend_back(q, kv, o, go, log_sum, segs, parents):
    def kernel(segs, parents, q, kv, o, go, log_sum, dq, dkv):
        z, x = lax.axis_index("z"), lax.axis_index("x")
        lane = lax.broadcasted_iota(jnp.int32, (256, 512), 1) & 255
        row = lax.broadcasted_iota(jnp.int32, (256, 512), 0)
        for b in range(2):
            block = z * 8 + b * 4 + x
            trunk, parent_block, leaf, branch = block_place(segs, parents, block)

            def stacked(ref):
                return jnp.concatenate([ref[b, :, :128], ref[b, :, 128:]], axis=0)

            both, grad = stacked(q), stacked(go)
            logs = log_sum[b, 0:1]
            inner = jnp.sum((grad.astype(F32) * stacked(o).astype(F32)).T, axis=0, keepdims=True)

            def one(i, key_block, mask, acc):
                key, value = kv[key_block, :, :128], kv[key_block, :, 128:]
                nt = (((1,), (1,)), ((), ()))
                s = lax.dot_general(key, both, nt, preferred_element_type=F32) * 128**-0.5
                p = jnp.where(mask, jnp.exp(jnp.minimum(s - logs, 1.0)), 0.0)
                dp = lax.dot_general(value, grad, nt, preferred_element_type=F32)
                ds = (p * (dp - inner)).astype(BF16)
                dk = jnp.dot(ds, both, preferred_element_type=F32) * 128**-0.5
                dv = jnp.dot(p.astype(BF16), grad, preferred_element_type=F32)
                dkv[b, i, :, :128] = dk.astype(BF16)
                dkv[b, i, :, 128:] = dv.astype(BF16)
                return acc + lax.dot_general(key, ds, (((0,), (0,)), ((), ())), preferred_element_type=F32)

            def trunk_one(i, acc):
                gap = (block - trunk * 8 - i) * 256
                return one(i, trunk * 8 + i, row - lane <= gap, acc)

            acc = lax.fori_loop(0, 8, trunk_one, jnp.zeros((128, 512), F32))
            acc = one(8, parent_block, jnp.broadcast_to(leaf, (256, 512)), acc)
            acc = one(9, block, (row <= lane) & branch, acc)
            grad_q = (acc * 128**-0.5).T.astype(BF16)
            dq[b, :, :128] = grad_q[:256]
            dq[b, :, 128:] = grad_q[256:]

    return pl.pallas_call(
        kernel,
        out_shape=(
            jax.ShapeDtypeStruct((2, 256, 256), BF16),
            jax.ShapeDtypeStruct((2, 10, 256, 256), BF16),
        ),
        in_specs=[INS, INS, INV, INV, INV, INV, INV],
        out_specs=(INV, INV),
        compiler_params=pltpu.CompilerParams(vmem_limit_bytes=56 << 20),
        name="attend_back",
    )(segs, parents, q, kv, o, go, log_sum)


def normed(values):
    centred = values - jnp.mean(values, axis=-1, keepdims=True)
    inverse = lax.rsqrt(jnp.mean(centred * centred, axis=-1, keepdims=True) + EPS)
    return centred * inverse, inverse


def norm_back(grad, norm, inverse, gain):
    scaled = grad * gain
    return inverse * (
        scaled
        - jnp.mean(scaled, axis=-1, keepdims=True)
        - norm * jnp.mean(scaled * norm, axis=-1, keepdims=True)
    )


def middle(part, tokens, out_bias, gain, shift, tops):
    def kernel(part, tokens, bias, gain, shift, tops, x1, h2, best, own, mine, got, local, *rest):
        *scratch, ss, rs = rest
        net = Net(ss, rs)
        net.barrier(PLANE + RING + ("yo",))

        def rows():
            def total(summed):
                value = tokens[...].astype(F32) + (summed + bias[...])
                x1[...] = value
                own[...] = (normed(value)[0] * gain[...] + shift[...]).astype(BF16)

            yield from group_scatter(net, part, *scratch, total)
            me = pltpu.make_async_copy(own, h2.at[net.y, net.c], local)
            me.start()
            yield from group_gather(net, own, h2)
            me.wait()

        def largest():
            mine[0] = tops[...]
            yield from heads_max(net, mine, got, best)

        run_all(rows(), largest())
        net.finish()

    n, d = tokens.shape
    return pl.pallas_call(
        kernel,
        out_shape=(
            jax.ShapeDtypeStruct((n, d), F32),
            jax.ShapeDtypeStruct((4, 2, n, d), BF16),
            jax.ShapeDtypeStruct((2, 16, 128), F32),
        ),
        in_specs=[INV] * 6,
        out_specs=(INV, ANY, INV),
        scratch_shapes=[
            VMEM((n, d), BF16),
            VMEM((5, 16, 128), F32),
            VMEM((7, 16, 128), F32),
            pltpu.SemaphoreType.DMA,
        ]
        + scatter_scratch(n, d)
        + sems(9 + 8 + 7),
        compiler_params=params(4),
        name="middle",
    )(part, tokens, out_bias, gain, shift, tops)


def heads_max(net, mine, got, best):
    for i, (up, down) in enumerate((("xu", "xd"), ("zu", "zd"))):
        k = [net.slot() for _ in range(3)]
        a, b, d = got.at[3 * i], got.at[3 * i + 1], got.at[3 * i + 2]
        net.send(mine.at[2 * i], a, k[0], up)
        net.send(mine.at[2 * i], b, k[1], down)
        yield
        net.got(a, k[0])
        net.got(b, k[1])
        mine[2 * i + 1] = jnp.maximum(mine[2 * i], jnp.maximum(a[...], b[...]))
        net.send(mine.at[2 * i + 1], d, k[2], up)
        yield
        net.got(d, k[2])
        mine[2 * i + 2] = jnp.maximum(mine[2 * i + 1], d[...])
    k = net.slot()
    net.send(mine.at[4], got.at[6], k, "yo")
    yield
    net.got(got.at[6], k)
    best[net.yh] = mine[4]
    best[1 - net.yh] = got[6]


def turn(mlp, back, x1, cotangent, gain, down_bias):
    def kernel(mlp, back, x1, cot, gain, bias, output, dx1, dz, sums, own, local, *rest):
        first, second, (ss, rs) = rest[:4], rest[4:8], rest[8:]
        net = Net(ss, rs)
        net.barrier(RING)

        def gradient():
            def total(summed):
                norm, inverse = normed(x1[...])
                grad = cot[...].astype(F32) + norm_back(summed, norm, inverse, gain[...])
                dx1[...] = grad
                rounded = grad.astype(BF16)
                own[...] = rounded
                parts = [
                    jnp.sum(v, axis=0, keepdims=True)
                    for v in (summed * norm, summed, rounded.astype(F32), cot[...].astype(F32))
                ]
                zero = jnp.zeros((2, parts[0].shape[1]), F32)
                sums[...] = jnp.concatenate([zero] + parts + [zero], axis=0)

            yield from group_scatter(net, back, *first, total)
            me = pltpu.make_async_copy(own, dz.at[net.y, net.c], local)
            me.start()
            yield from group_gather(net, own, dz)
            me.wait()

        def forward():
            def total(summed):
                output[...] = (x1[...] + (summed + bias[...])).astype(BF16)

            yield
            yield from group_scatter(net, mlp, *second, total)

        run_all(gradient(), forward())
        net.finish()

    n, d = cotangent.shape
    return pl.pallas_call(
        kernel,
        out_shape=(
            jax.ShapeDtypeStruct((n, d), BF16),
            jax.ShapeDtypeStruct((n, d), F32),
            jax.ShapeDtypeStruct((4, 2, n, d), BF16),
            jax.ShapeDtypeStruct((8, d), F32),
        ),
        in_specs=[INV] * 6,
        out_specs=(INV, INV, ANY, INV),
        scratch_shapes=[VMEM((n, d), BF16), pltpu.SemaphoreType.DMA]
        + scatter_scratch(n, d)
        + scatter_scratch(n, d)
        + sems(9 + 8 + 8),
        compiler_params=params(5),
        name="turn",
    )(mlp, back, x1, cotangent, gain, down_bias)


def weight_scatter(net, g, tmp, swap, out):
    z, yh, x = net.z, net.yh, net.x
    w = g.shape[-1]
    k = net.slot()
    yield from plane_scatter(net, column_view(g), tmp)
    net.send(g.at[z, 1 - yh, x], swap, k, "yo")
    out[:, pl.ds(pl.multiple_of(yh * w, 128), w)] = g[z, yh, x].astype(F32)
    yield
    net.got(swap, k)
    out[:, pl.ds(pl.multiple_of((1 - yh) * w, 128), w)] = swap[...].astype(F32)


def scatter_weights(grads, cid):
    count = len(grads)

    def kernel(*refs):
        g, outs = refs[:count], refs[count : 2 * count]
        scratch, (ss, rs) = refs[2 * count : -2], refs[-2:]
        net = Net(ss, rs)
        net.barrier(PLANE + ("yo",))
        run_all(
            *[
                weight_scatter(net, g[i], scratch[9 * i : 9 * i + 8], scratch[9 * i + 8], outs[i])
                for i in range(count)
            ]
        )
        net.finish()

    scratch = []
    for one in grads:
        n, w = one.shape[-2:]
        scratch += plane_scratch(n, w // 2) + [VMEM((n, w), BF16)]
    return pl.pallas_call(
        kernel,
        out_shape=tuple(jax.ShapeDtypeStruct((g.shape[-2], 2 * g.shape[-1]), F32) for g in grads),
        in_specs=[INV] * count,
        out_specs=(INV,) * count,
        scratch_shapes=scratch + sems(17 * count),
        compiler_params=params(cid),
        name="scatter_weights",
    )(*grads)


def scatter_kv(slots, segs, parents):
    def kernel(segs, parents, slots, out, full, from_core, held, ring, *rest):
        tmp, (ss, rs) = rest[:8], rest[8:]
        net = Net(ss, rs)
        z, x, c, y = net.z, net.x, net.c, net.y
        net.barrier(PLANE + RING + ("yo",))
        for b in range(2):
            block = z * 8 + b * 4 + x
            trunk, parent_block, leaf, branch = block_place(segs, parents, block)

            def place(kb, carry):
                slot = jnp.where(kb < 16, kb & 7, jnp.where(kb == block, 9, 8))
                valid = jnp.where(
                    kb < 16,
                    (kb >> 3) == trunk,
                    ((kb == block) & branch) | ((kb == parent_block) & leaf),
                )
                value = jnp.where(valid, slots[b, slot], jnp.zeros((256, 256), BF16))
                at = (kb >> 3, (kb >> 2) & 1, kb & 3)
                if b == 0:
                    full[at] = value
                else:
                    full[at] = full[at] + value
                return carry

            lax.fori_loop(0, 32, place, 0)
        k = [net.slot() for _ in range(8)]
        net.send(full.at[:, 1 - c], from_core, k[0], "c")
        net.got(from_core, k[0])
        for zz in range(4):
            for xx in range(4):
                held[zz, xx] = (full[zz, c, xx].astype(F32) + from_core[zz, xx].astype(F32)).astype(BF16)

        def view(zz, half, xx, part):
            rows = pl.ds(0, 256) if half == BOTH else pl.ds(128 * half, 128)
            return held.at[zz, xx, rows, pl.ds(part * 128, 128)]

        run_all(plane_scatter(net, view, tmp))
        mine = held.at[z, x]

        def rows(yy):
            return pl.ds(pl.multiple_of(yy * 64, 64), 64)

        for i, (name, d) in enumerate((("yu", net.yu), ("yd", net.yd), ("yo", net.yo))):
            net.send(mine.at[rows(d)], ring.at[i], k[1 + i], name)
        for i in range(3):
            net.got(ring.at[i], k[1 + i])
        own = held[z, x, rows(y)].astype(F32)
        for i in range(3):
            own = own + ring[i].astype(F32)
        out[c, rows(y)] = own.astype(BF16)
        view = out.at[c, rows(y)]
        for i, name in enumerate(("yu", "yd", "yo")):
            net.send(view, view, k[4 + i], name)
        for i, d in enumerate((net.yd, net.yu, net.yo)):
            net.got(out.at[c, rows(d)], k[4 + i])
        net.send(out.at[c], out.at[c], k[7], "c")
        net.got(out.at[1 - c], k[7])
        net.finish()

    return pl.pallas_call(
        kernel,
        out_shape=jax.ShapeDtypeStruct((2, 256, 256), BF16),
        in_specs=[INS, INS, INV],
        out_specs=INV,
        scratch_shapes=[
            VMEM((4, 2, 4, 256, 256), BF16),
            VMEM((4, 4, 256, 256), BF16),
            VMEM((4, 4, 256, 256), BF16),
            VMEM((3, 64, 256), BF16),
            VMEM((2, 4, 128, 128), BF16),
            VMEM((2, 4, 128, 128), BF16),
            VMEM((2, 4, 256, 128), BF16),
            VMEM((2, 4, 256, 128), BF16),
            VMEM((2, 128, 128), BF16),
            VMEM((2, 128, 128), BF16),
            VMEM((2, 256, 128), BF16),
            VMEM((2, 256, 128), BF16),
        ]
        + sems(16 + 8),
        compiler_params=params(6),
        name="scatter_kv",
    )(segs, parents, slots)


def closing(back, tokens, dx1, from_kv, gain, sums, grad_q, small):
    def kernel(back, tokens, dx1, from_kv, gain, sums, gq, small, grad_input, out_q, vec, small_out,
               vecs, vec_z, vec_x, lone, small_z, small_x, small_y, swap, *rest):
        first, tmp, (ss, rs) = rest[:4], rest[4:12], rest[12:]
        net = Net(ss, rs)
        z, yh, x, y, c = net.z, net.yh, net.x, net.y, net.c
        net.barrier(PLANE + RING + ("yo", "xo", "zo"))

        def rows():
            def total(summed):
                grad = summed + from_kv[...]
                norm, inverse = normed(tokens[...].astype(F32))
                grad_input[...] = dx1[...] + norm_back(grad, norm, inverse, gain[...])
                one = jnp.sum(grad * norm, axis=0, keepdims=True)
                two = jnp.sum(grad, axis=0, keepdims=True)
                vecs[y, c] = jnp.concatenate([one, two, sums[2:8]], axis=0)

            yield from group_scatter(net, back, *first, total)
            k = [net.slot() for _ in range(13)]
            at = vecs.at[y, c]
            for i, name in enumerate(("yu", "yd", "yo", "c")):
                net.send(at, at, k[i], name)
            yield
            for i, d in enumerate((net.yd, net.yu, net.yo)):
                net.got(vecs.at[d, c], k[i])
                net.send(vecs.at[d, c], vecs.at[d, c], k[4 + i], "c")
            yield
            for i, d in enumerate((y, net.yd, net.yu, net.yo)):
                net.got(vecs.at[d, 1 - c], k[3 + i])
            acc = vecs[0, 0]
            for i in range(1, 8):
                acc = acc + vecs[i // 2, i % 2]
            for i in range(4):
                vec_z[i] = acc[:, i * 512 : (i + 1) * 512]
            for i, (name, d) in enumerate((("zu", net.zu), ("zd", net.zd), ("zo", net.zo))):
                net.send(vec_z.at[d], vec_z.at[4 + i], k[7 + i], name)
            yield
            for i in range(3):
                net.got(vec_z.at[4 + i], k[7 + i])
            acc = vec_z[z] + vec_z[4] + vec_z[5] + vec_z[6]
            vec_x[0] = jnp.where(yh == 0, acc[:, :256], acc[:, 256:])
            for i, name in enumerate(("xu", "xd", "xo")):
                net.send(vec_x.at[0], vec_x.at[1 + i], k[10 + i], name)
            yield
            for i in range(3):
                net.got(vec_x.at[1 + i], k[10 + i])
            vec[...] = vec_x[0] + vec_x[1] + vec_x[2] + vec_x[3]

        def small_sums():
            k = [net.slot() for _ in range(7)]
            for i, (name, d) in enumerate((("zu", net.zu), ("zd", net.zd), ("zo", net.zo))):
                net.send(small.at[d], small_z.at[i], k[i], name)
            yield
            for i in range(3):
                net.got(small_z.at[i], k[i])
            for xx in range(4):
                small_x[xx] = small[z, xx] + small_z[0, xx] + small_z[1, xx] + small_z[2, xx]
            for i, (name, d) in enumerate((("xu", net.xu), ("xd", net.xd), ("xo", net.xo))):
                net.send(small_x.at[d], small_x.at[4 + i], k[3 + i], name)
            yield
            for i in range(3):
                net.got(small_x.at[4 + i], k[3 + i])
            lone[...] = small_x[x] + small_x[4] + small_x[5] + small_x[6]
            net.send(lone, small_y, k[6], "yo")
            yield
            net.got(small_y, k[6])
            small_out[0] = lone[...]
            small_out[1] = small_y[...]

        run_all(rows(), weight_scatter(net, gq, tmp, swap, out_q), small_sums())
        net.finish()

    n, d = tokens.shape
    w = grad_q.shape[-1]
    tile = small.shape[-2:]
    return pl.pallas_call(
        kernel,
        out_shape=(
            jax.ShapeDtypeStruct((n, d), F32),
            jax.ShapeDtypeStruct((n, 2 * w), F32),
            jax.ShapeDtypeStruct((8, 256), F32),
            jax.ShapeDtypeStruct((2,) + tile, F32),
        ),
        in_specs=[INV] * 8,
        out_specs=(INV,) * 4,
        scratch_shapes=[
            VMEM((4, 2, 8, d), F32),
            VMEM((7, 8, 512), F32),
            VMEM((4, 8, 256), F32),
            VMEM(tile, F32),
            VMEM((3, 4) + tile, F32),
            VMEM((7,) + tile, F32),
            VMEM(tile, F32),
            VMEM((n, w), BF16),
        ]
        + scatter_scratch(n, d)
        + plane_scratch(n, w // 2)
        + sems(8 + 13 + 7 + 17),
        compiler_params=params(7),
        name="closing",
    )(back, tokens, dx1, from_kv, gain, sums, grad_q, small)


def local(
    tokens,
    cotangent,
    seg_ids,
    parents,
    tau,
    w_query,
    w_up,
    w_out,
    w_down,
    query_bias,
    up_bias,
    w_keyval,
    value_bias,
    norm1_gain,
    norm1_bias,
    norm2_gain,
    norm2_bias,
    out_bias,
    down_bias,
):
    z, yh, x, yl, c = (lax.axis_index(a) for a in AXES)
    tp = yl * 2 + c
    d = tokens.shape[1]

    def dot(left, right, dims):
        return lax.dot_general(left, right, ((dims[:1], dims[1:]), ((), ())), preferred_element_type=F32)

    def halves(weight):
        w = weight.shape[1] // 2
        return (
            lax.dynamic_slice_in_dim(weight, yh * w, w, 1),
            lax.dynamic_slice_in_dim(weight, (1 - yh) * w, w, 1),
        )

    def lanes(values):
        flat = values.reshape(1, -1).astype(BF16)
        return jnp.pad(flat, ((0, 0), (0, 128 - flat.shape[1])))

    pieces = [norm1_gain, norm1_bias, norm2_gain, norm2_bias, out_bias, down_bias, value_bias, up_bias, query_bias]
    pieces = [lanes(v) for v in pieces] + [lanes(seg_ids[:1])]
    small = jnp.concatenate(pieces + [jnp.zeros((16 - len(pieces), 128), BF16)], axis=0)
    small = jnp.concatenate([w_keyval, small], axis=1)
    tok_all, cot_all, small_all, wq, wo = opening(
        tokens, cotangent, small, *halves(w_query), *halves(w_out)
    )
    tok_all = tok_all.reshape(512, d)
    cot_all = cot_all.reshape(512, d)
    wq = wq.reshape(d, -1)
    wo = wo.reshape(d, -1)
    small_all = small_all.reshape(4, 2, 4, 4, 16, 384).transpose(0, 1, 3, 2, 4, 5)
    w_kv = small_all[..., :256].reshape(d, 256)
    tail = small_all[..., 256:]
    vectors = tail[..., :6, :16].transpose(4, 0, 1, 2, 3, 5).reshape(6, d).astype(F32)
    gain1, shift1, gain2, shift2, bias_out, bias_down = (vectors[i : i + 1] for i in range(6))
    value_full = tail[..., 6, 0].reshape(128).astype(F32)
    mine = lax.dynamic_index_in_dim(tail, tp, axis=3, keepdims=False)
    ub = lax.dynamic_slice_in_dim(mine[..., 7, :64].reshape(128, 16), yh * 8, 8, 1)
    ub = ub.T.reshape(1, 1024).astype(F32)
    qb = lax.dynamic_slice_in_dim(mine[..., 8, :16].reshape(128, 4), yh * 2, 2, 1)
    qb = qb.T.reshape(1, 256).astype(F32)
    segs = tail[..., 0, 9, 0].reshape(32).astype(jnp.int32)

    h1 = (normed(tok_all.astype(F32))[0] * gain1 + shift1).astype(BF16)
    q = (dot(h1, wq, (1, 0)) + qb).astype(BF16)
    kv = (dot(h1, w_kv, (1, 0)) + jnp.concatenate([jnp.zeros((128,), F32), value_full])).astype(BF16)
    kv_all = gather_kv(kv.reshape(2, 256, 256)).reshape(32, 256, 256)
    q_blocks = q.reshape(2, 256, 256)
    o, log_sum, tops = attend(q_blocks, kv_all, segs, parents)
    o_rows = o.reshape(512, 256)
    attn = dot(o_rows, wo, (1, 1)).astype(BF16).reshape(4, 2, 64, d)
    x1, h2, best = middle(attn, tokens, bias_out, gain2, shift2, tops.reshape(16, 128))
    h2 = h2.reshape(512, d)
    wu, wd = gather_ff(*halves(w_up), *halves(w_down))
    wu = wu.reshape(d, -1)
    wd = wd.reshape(d, -1)

    limit = tau[0]
    head_max = best.reshape(4, 8, 128)[:, 0, 0]
    factor = limit / jnp.maximum(head_max, limit)
    clipped_query = (w_query.astype(F32) * jnp.repeat(factor, 128)[None, :]).astype(BF16)
    clipped_bias = (query_bias.astype(F32) * factor[None, :]).astype(BF16)

    def gate(values):
        return jax.nn.gelu(values, approximate=True)

    u = dot(h2, wu, (1, 0)) + ub
    a, gate_back = jax.vjp(gate, u)
    a = a.astype(BF16)
    mlp = dot(a, wd, (1, 1)).astype(BF16).reshape(4, 2, 64, d)
    du = gate_back(dot(cot_all, wd, (1, 0)))[0].astype(BF16)
    grad_ub = jnp.sum(du.astype(F32), axis=0)
    grad_down = dot(cot_all, a, (0, 0)).astype(BF16)
    grad_up = dot(h2, du, (0, 0)).astype(BF16)
    back2 = dot(du, wu, (1, 1)).astype(BF16).reshape(4, 2, 64, d)
    output, dx1, dz, sums = turn(mlp, back2, x1, cotangent, gain2, bias_down)
    dz = dz.reshape(512, d)
    go = dot(dz, wo, (1, 0)).astype(BF16).reshape(2, 256, 256)
    grad_out = dot(dz, o_rows, (0, 0)).astype(BF16)
    up_sum, down_sum, out_sum = scatter_weights(
        [v.reshape(4, 2, 4, 64, -1) for v in (grad_up, grad_down, grad_out)], 8
    )
    dq, slots = attend_back(q_blocks, kv_all, o, go, log_sum, segs, parents)
    dq = dq.reshape(512, 256)
    dkv = scatter_kv(slots, segs, parents).reshape(512, 256)
    back1 = dot(dq, wq, (1, 1)).astype(BF16).reshape(4, 2, 64, d)
    grad_q = dot(h1, dq, (0, 0)).astype(BF16).reshape(4, 2, 4, 64, 256)
    grad_kv = dot(h1, dkv, (0, 0)).reshape(4, 2, 4, 4, 16, 256)
    grad_kv = lax.dynamic_index_in_dim(lax.dynamic_index_in_dim(grad_kv, yh, 1, False), tp, 2, False)
    dkv_own = lax.dynamic_slice_in_dim(dkv, yh * 256 + tp * 64, 64, 0)
    from_kv = dot(dkv_own, w_kv, (1, 1))
    gqb = jnp.sum(dq.astype(F32), axis=0).reshape(2, 128).T.reshape(4, 2, 4, 8)
    gub = grad_ub.reshape(8, 128).T.reshape(4, 2, 4, 32)
    gvb = jnp.sum(dkv[:, 128:].astype(F32), axis=0).reshape(4, 2, 4, 4)
    gvb = lax.dynamic_index_in_dim(lax.dynamic_index_in_dim(gvb, yh, 1, False), tp, 2, False)
    bias_rows = jnp.concatenate([gqb, gub], axis=3).transpose(0, 2, 1, 3)
    bias_rows = jnp.pad(bias_rows, ((0, 0), (0, 0), (0, 1), (0, 256 - 40)))
    bias_rows = bias_rows.at[:, :, 2, 0].set(gvb)
    bias_rows = jnp.pad(bias_rows, ((0, 0), (0, 0), (0, 5), (0, 0)))
    small_grads = jnp.concatenate([grad_kv, bias_rows], axis=2)
    grad_input, query_sum, vec, small_sum = closing(
        back1, tokens, dx1, from_kv, gain1, sums, grad_q, small_grads
    )
    keyval_sum = small_sum[0, :16]
    valueb_sum = small_sum[0, 18, :1]
    own_bias = lax.dynamic_index_in_dim(small_sum[0, 16:18, :40], yh, 0, False)
    oth_bias = lax.dynamic_index_in_dim(small_sum[1, 16:18, :40], yh, 0, False)
    first = jnp.where(yh == 0, own_bias, oth_bias)
    second = jnp.where(yh == 0, oth_bias, own_bias)
    qbias_sum = jnp.concatenate([first[:8].reshape(4, 2), second[:8].reshape(4, 2)], axis=1)
    ubias_sum = jnp.concatenate([first[8:].reshape(4, 8), second[8:].reshape(4, 8)], axis=1)
    vec = lax.dynamic_slice(vec, (jnp.int32(0), x * 64 + tp * 16), (6, 16))
    return (
        output,
        grad_input,
        query_sum,
        up_sum,
        out_sum,
        down_sum,
        qbias_sum,
        ubias_sum,
        keyval_sum,
        valueb_sum,
        vec[0],
        vec[1],
        vec[2],
        vec[3],
        vec[4],
        vec[5],
        clipped_query,
        clipped_bias,
    )


def solution(mesh):
    fine = Mesh(mesh.devices.reshape(4, 2, 4, 2, 2), AXES)
    dp, tp = ("z", "yh", "x"), ("yl", "c")
    rows, flat, weight = P(AXES, None), P(AXES), P(dp, tp)
    in_specs = (rows, rows, P(dp), P(), P()) + (weight,) * 6 + (rows,) + (flat,) * 7
    out_specs = (rows, rows) + (weight,) * 6 + (rows,) + (flat,) * 7 + (weight, weight)
    return jax.shard_map(local, mesh=fine, in_specs=in_specs, out_specs=out_specs, check_vma=False)
```

```python
import itertools

import jax
import jax.numpy as jnp
from jax import lax
from jax.experimental import pallas as pl
from jax.experimental.pallas import tpu as pltpu
from jax.sharding import Mesh, PartitionSpec as P

EPS = 1e-05
AXES = ("z", "yh", "x", "yl", "c")
F32 = jnp.float32
BF16 = jnp.bfloat16
VMEM = pltpu.VMEM
NEG = -1e30


class Net:
    def __init__(self, send_sems, recv_sems):
        self.z, self.yh, self.x, self.yl, self.c = (lax.axis_index(a) for a in AXES)
        self.y = self.yh * 2 + self.yl
        self.yu, self.yo, self.yd = (lax.rem(self.y + s, 4) for s in (1, 2, 3))
        self.xu, self.xo, self.xd = (lax.rem(self.x + s, 4) for s in (1, 2, 3))
        self.zu, self.zo, self.zd = (lax.rem(self.z + s, 4) for s in (1, 2, 3))
        up, down = lax.rem(self.yh + self.yl, 2), lax.rem(self.yh + 1 - self.yl, 2)
        self.dev = {
            "yu": {"yh": up, "yl": 1 - self.yl},
            "yd": {"yh": down, "yl": 1 - self.yl},
            "yo": {"yh": 1 - self.yh},
            "c": {"c": 1 - self.c},
            "xu": {"x": self.xu},
            "xd": {"x": self.xd},
            "xo": {"x": self.xo},
            "zu": {"z": self.zu},
            "zd": {"z": self.zd},
            "zo": {"z": self.zo},
        }
        self.send_sems, self.recv_sems = send_sems, recv_sems
        self.count = 0
        self.sent = []

    def barrier(self, names):
        sem = pltpu.get_barrier_semaphore()
        for name in names:
            pl.semaphore_signal(
                sem, inc=1, device_id=self.dev[name], device_id_type=pl.DeviceIdType.MESH
            )
        pl.semaphore_wait(sem, len(names))

    def slot(self):
        self.count += 1
        return self.count - 1

    def copy(self, src, dst, k, name):
        return pltpu.make_async_remote_copy(
            src_ref=src,
            dst_ref=dst,
            send_sem=self.send_sems.at[k],
            recv_sem=self.recv_sems.at[k],
            device_id=self.dev[name],
            device_id_type=pl.DeviceIdType.MESH,
        )

    def send(self, src, dst, k, name):
        one = self.copy(src, dst, k, name)
        one.start()
        self.sent.append(one)

    def got(self, ref, k):
        self.copy(ref, ref, k, "c").wait_recv()

    def finish(self):
        for one in self.sent:
            one.wait_send()


def run_all(*steps):
    live = list(steps)
    while live:
        rest = []
        for one in live:
            try:
                next(one)
                rest.append(one)
            except StopIteration:
                pass
        live = rest


def group_gather(net, src, out):
    y, c, yu, yd, yo = net.y, net.c, net.yu, net.yd, net.yo
    k = [net.slot() for _ in range(9)]
    half = src.shape[0] // 2
    lo, hi = pl.ds(0, half), pl.ds(half, half)
    mine = out.at[y, c]
    net.send(src, mine, k[0], "yu")
    net.send(src, mine, k[1], "yd")
    net.send(src, mine, k[2], "c")
    yield
    net.got(out.at[yd, c], k[0])
    net.send(out.at[yd, c, lo], out.at[yd, c, lo], k[3], "yu")
    net.send(out.at[yd, c], out.at[yd, c], k[4], "c")
    net.got(out.at[yu, c], k[1])
    net.send(out.at[yu, c, hi], out.at[yu, c, hi], k[5], "yd")
    net.send(out.at[yu, c], out.at[yu, c], k[6], "c")
    yield
    net.got(out.at[yo, c, lo], k[3])
    net.send(out.at[yo, c, lo], out.at[yo, c, lo], k[7], "c")
    net.got(out.at[yo, c, hi], k[5])
    net.send(out.at[yo, c, hi], out.at[yo, c, hi], k[8], "c")
    yield
    net.got(out.at[y, 1 - c], k[2])
    net.got(out.at[yd, 1 - c], k[4])
    net.got(out.at[yu, 1 - c], k[6])
    net.got(out.at[yo, 1 - c, lo], k[7])
    net.got(out.at[yo, 1 - c, hi], k[8])


def group_scatter(net, part, from_core, held, from_half, from_full, total, make=None):
    y, c, yu, yd, yo = net.y, net.c, net.yu, net.yd, net.yo
    k = [net.slot() for _ in range(8)]
    n = part.shape[2]
    half = n // 2
    lo, hi = pl.ds(0, half), pl.ds(half, half)
    for i, d in enumerate((yo, yu, yd, y)):
        if make is not None:
            make(i, d)
        net.send(part.at[d, 1 - c], from_core.at[d], k[i], "c")

    def core_sum(i, d):
        net.got(from_core.at[d], k[i])
        held[d] = (part[d, c].astype(F32) + from_core[d].astype(F32)).astype(BF16)

    yield
    core_sum(0, yo)
    net.send(held.at[yo, lo], from_half.at[0], k[4], "yu")
    net.send(held.at[yo, hi], from_half.at[1], k[5], "yd")
    core_sum(1, yu)
    core_sum(2, yd)
    yield
    net.got(from_half.at[0], k[4])
    held[yu, lo] = (held[yu, lo].astype(F32) + from_half[0].astype(F32)).astype(BF16)
    net.send(held.at[yu], from_full.at[0], k[6], "yu")
    net.got(from_half.at[1], k[5])
    held[yd, hi] = (held[yd, hi].astype(F32) + from_half[1].astype(F32)).astype(BF16)
    net.send(held.at[yd], from_full.at[1], k[7], "yd")
    core_sum(3, y)
    yield
    net.got(from_full.at[0], k[6])
    net.got(from_full.at[1], k[7])
    total(held[y].astype(F32) + from_full[0].astype(F32) + from_full[1].astype(F32))


def scatter_scratch(n, w):
    return [VMEM((4, n, w), BF16), VMEM((4, n, w), BF16), VMEM((2, n // 2, w), BF16), VMEM((2, n, w), BF16)]


BOTH = slice(None)


def plane_gather(net, o):
    z, x, xu, xd, xo, zu, zd, zo = net.z, net.x, net.xu, net.xd, net.xo, net.zu, net.zd, net.zo
    k = [net.slot() for _ in range(16)]
    every = slice(None)

    def send(view, i, name):
        net.send(view, view, k[i], name)

    def got(view, i):
        net.got(view, k[i])

    send(o(z, BOTH, x, 0), 0, "xu")
    send(o(z, BOTH, x, 0), 1, "xd")
    send(o(z, BOTH, x, 1), 2, "zu")
    send(o(z, BOTH, x, 1), 3, "zd")
    yield
    got(o(z, BOTH, xd, 0), 0)
    send(o(z, 0, xd, 0), 4, "xu")
    got(o(zd, BOTH, x, 1), 2)
    send(o(zd, 0, x, 1), 6, "zu")
    got(o(z, BOTH, xu, 0), 1)
    send(o(z, 1, xu, 0), 5, "xd")
    got(o(zu, BOTH, x, 1), 3)
    send(o(zu, 1, x, 1), 7, "zd")
    yield
    got(o(z, 0, xo, 0), 4)
    got(o(z, 1, xo, 0), 5)
    send(o(z, BOTH, every, 0), 8, "zu")
    send(o(z, BOTH, every, 0), 9, "zd")
    got(o(zo, 0, x, 1), 6)
    got(o(zo, 1, x, 1), 7)
    send(o(every, BOTH, x, 1), 10, "xu")
    send(o(every, BOTH, x, 1), 11, "xd")
    yield
    got(o(zd, BOTH, every, 0), 8)
    send(o(zd, 0, every, 0), 12, "zu")
    got(o(every, BOTH, xd, 1), 10)
    send(o(every, 0, xd, 1), 14, "xu")
    got(o(zu, BOTH, every, 0), 9)
    send(o(zu, 1, every, 0), 13, "zd")
    got(o(every, BOTH, xu, 1), 11)
    send(o(every, 1, xu, 1), 15, "xd")
    yield
    got(o(zo, 0, every, 0), 12)
    got(o(zo, 1, every, 0), 13)
    got(o(every, 0, xo, 1), 14)
    got(o(every, 1, xo, 1), 15)


def add_into(dst, *others):
    for index in itertools.product(*[range(n) for n in dst.shape[:-2]]):
        at = index + (slice(None), slice(None))
        total = dst[at].astype(F32)
        for other in others:
            total = total + other[at].astype(F32)
        dst[at] = total.astype(dst.dtype)


def plane_scatter(net, g, tmp):
    z, x, xu, xd, xo, zu, zd, zo = net.z, net.x, net.xu, net.xd, net.xo, net.zu, net.zd, net.zo
    t1, t2, u1, u2, t3, t4, u3, u4 = tmp
    k = [net.slot() for _ in range(16)]
    every = slice(None)

    def send(src, dst, i, name):
        net.send(src, dst, k[i], name)

    def got(ref, i):
        net.got(ref, k[i])

    send(g(zo, 0, every, 0), t1.at[0], 0, "zu")
    send(g(zo, 1, every, 0), t1.at[1], 1, "zd")
    send(g(every, 0, xo, 1), t2.at[0], 2, "xu")
    send(g(every, 1, xo, 1), t2.at[1], 3, "xd")
    yield
    got(t1.at[0], 0)
    add_into(g(zu, 0, every, 0), t1.at[0])
    send(g(zu, BOTH, every, 0), u1.at[0], 4, "zu")
    got(t2.at[0], 2)
    add_into(g(every, 0, xu, 1), t2.at[0])
    send(g(every, BOTH, xu, 1), u2.at[0], 6, "xu")
    got(t1.at[1], 1)
    add_into(g(zd, 1, every, 0), t1.at[1])
    send(g(zd, BOTH, every, 0), u1.at[1], 5, "zd")
    got(t2.at[1], 3)
    add_into(g(every, 1, xd, 1), t2.at[1])
    send(g(every, BOTH, xd, 1), u2.at[1], 7, "xd")
    yield
    got(u1.at[0], 4)
    got(u1.at[1], 5)
    add_into(g(z, BOTH, every, 0), u1.at[0], u1.at[1])
    send(g(z, 0, xo, 0), t3.at[0], 8, "xu")
    send(g(z, 1, xo, 0), t3.at[1], 9, "xd")
    got(u2.at[0], 6)
    got(u2.at[1], 7)
    add_into(g(every, BOTH, x, 1), u2.at[0], u2.at[1])
    send(g(zo, 0, x, 1), t4.at[0], 10, "zu")
    send(g(zo, 1, x, 1), t4.at[1], 11, "zd")
    yield
    got(t3.at[0], 8)
    add_into(g(z, 0, xu, 0), t3.at[0])
    send(g(z, BOTH, xu, 0), u3.at[0], 12, "xu")
    got(t4.at[0], 10)
    add_into(g(zu, 0, x, 1), t4.at[0])
    send(g(zu, BOTH, x, 1), u4.at[0], 14, "zu")
    got(t3.at[1], 9)
    add_into(g(z, 1, xd, 0), t3.at[1])
    send(g(z, BOTH, xd, 0), u3.at[1], 13, "xd")
    got(t4.at[1], 11)
    add_into(g(zd, 1, x, 1), t4.at[1])
    send(g(zd, BOTH, x, 1), u4.at[1], 15, "zd")
    yield
    got(u3.at[0], 12)
    got(u3.at[1], 13)
    add_into(g(z, BOTH, x, 0), u3.at[0], u3.at[1])
    got(u4.at[0], 14)
    got(u4.at[1], 15)
    add_into(g(z, BOTH, x, 1), u4.at[0], u4.at[1])


def plane_scratch(n, w):
    return [
        VMEM((2, 4, n, w), BF16),
        VMEM((2, 4, n, w), BF16),
        VMEM((2, 2, 4, n, w), BF16),
        VMEM((2, 4, 2, n, w), BF16),
        VMEM((2, n, w), BF16),
        VMEM((2, n, w), BF16),
        VMEM((2, 2, n, w), BF16),
        VMEM((2, 2, n, w), BF16),
    ]


def column_view(ref):
    w = ref.shape[-1] // 2

    def view(zz, half, xx, part):
        return ref.at[zz, half, xx, :, pl.ds(part * w, w)]

    return view


def sems(n):
    return [pltpu.SemaphoreType.DMA((n,)), pltpu.SemaphoreType.DMA((n,))]


def params(cid, limit=56 << 20):
    return pltpu.CompilerParams(collective_id=cid, has_side_effects=True, vmem_limit_bytes=limit)


ANY = pl.BlockSpec(memory_space=pl.ANY)
INV = pl.BlockSpec(memory_space=pltpu.VMEM)
INS = pl.BlockSpec(memory_space=pltpu.SMEM)
PLANE = ("xu", "xd", "zu", "zd")
RING = ("yu", "yd", "c")


class Ticks:
    def __init__(self, *steps):
        self.steps = list(steps)

    def tick(self, count=1):
        for _ in range(count):
            for one in self.steps:
                next(one, None)


def weight_gather(net, weight, out, local):
    z, yh, x = net.z, net.yh, net.x
    n, w = weight.shape[0], weight.shape[1] // 2
    k = net.slot()

    def half(which):
        return weight.at[:, pl.ds(pl.multiple_of(which * w, 128), w)]

    mine = pltpu.make_async_copy(half(yh), out.at[z, yh, x, pl.ds(0, n)], local)
    mine.start()
    net.send(half(1 - yh), out.at[z, yh, x, pl.ds(0, n)], k, "yo")
    yield
    mine.wait()
    net.got(out.at[z, 1 - yh, x, pl.ds(0, n)], k)
    yield from plane_gather(net, column_view(out))


def splat(row, lane, at):
    return jnp.sum(jnp.where(lane == at, row, 0.0), axis=1, keepdims=True)


def place_of(segs, parents, block):
    lane = lax.broadcasted_iota(jnp.int32, (1, 128), 1)
    seg = splat(segs, lane, block)
    lanes = lane.astype(F32)
    parent = splat(parents, lanes, seg)
    trunk = splat(parents, lanes, parent)
    leaf = (seg >= 10.0).astype(F32)
    branch = (seg >= 2.0).astype(F32)
    above = [(splat(segs, lane, b) == parent).astype(F32) * leaf for b in range(16, 32)]
    return trunk, leaf, branch, above


def wide(value):
    return jnp.broadcast_to(value, (1, 128)).astype(BF16)


def trunk_block(kv, which, i, trunk):
    one = wide(trunk)
    return kv[which, 0, i // 4, i % 4] * (1 - one) + kv[which, 1, i // 4, i % 4] * one


def parent_block(kv, which, above):
    total = kv[which, 2, 0, 0] * wide(above[0])
    for j in range(1, 16):
        total = total + kv[which, 2 + j // 8, j // 4 % 2, j % 4] * wide(above[j])
    return total


NT = (((1,), (1,)), ((), ()))
TN = (((0,), (0,)), ((), ()))
SCALE = 128**-0.5


def attend(b, z, x, q, kv, segs, parents, scores, o, log_sum):
    lane = (lax.broadcasted_iota(jnp.int32, (256, 512), 1) & 255).astype(F32)
    row = lax.broadcasted_iota(jnp.int32, (256, 512), 0).astype(F32)
    block = z * 8 + b * 4 + x
    trunk, leaf, branch, above = place_of(segs, parents, block)
    rows = pl.ds(b * 256, 256)
    both = jnp.concatenate([q[rows, :128], q[rows, 128:]], axis=0)
    start = block.astype(F32) - 8.0 * trunk

    def score(key):
        return lax.dot_general(key, both, NT, preferred_element_type=F32) * SCALE

    def trunk_score(i, top):
        gap = (start - i.astype(F32)) * 256.0
        s = jnp.where(row - lane <= gap, score(trunk_block(kv, 0, i, trunk)), NEG)
        scores[i] = s
        return jnp.maximum(top, jnp.max(s, axis=0, keepdims=True))

    top = lax.fori_loop(0, 8, trunk_score, jnp.full((1, 512), NEG, F32))
    s = score(parent_block(kv, 0, above)) + (leaf - 1.0) * 1e30
    scores[8] = s
    top = jnp.maximum(top, jnp.max(s, axis=0, keepdims=True))
    s = jnp.where(row <= lane, score(kv[0, z, b, x]), NEG) + (branch - 1.0) * 1e30
    scores[9] = s
    top = jnp.maximum(top, jnp.max(s, axis=0, keepdims=True))

    def weigh(i, value, carry):
        acc, total = carry
        w = jnp.exp(scores[i] - top)
        acc = acc + lax.dot_general(value, w.astype(BF16), TN, preferred_element_type=F32)
        return acc, total + jnp.sum(w, axis=0, keepdims=True)

    carry = (jnp.zeros((128, 512), F32), jnp.zeros((1, 512), F32))
    carry = lax.fori_loop(0, 8, lambda i, c: weigh(i, trunk_block(kv, 1, i, trunk), c), carry)
    carry = weigh(8, parent_block(kv, 1, above), carry)
    acc, total = weigh(9, kv[1, z, b, x], carry)
    heads = (acc / total).T.astype(BF16)
    o[rows, :128] = heads[:256]
    o[rows, 128:] = heads[256:]
    log_sum[b] = jnp.broadcast_to(top + jnp.log(total), (8, 512))
    return top


def forward(tokens, cotangent, pack, biases, parents, w_query, w_out, w_up, w_down):
    def kernel(tok, cot, pack, biases, parents, wq_in, wo_in, wu_in, wd_in,
               cot_out, h2, wu, wd, wq_out, wo_out, pack_out, h1_out, q_out, kv_out, o, log_sum, x1, best, vec, ub,
               tok_all, h1, packs, wq, wo, q, kv, scores, part, own, mine, got, local, *rest):
        *scratch, ss, rs = rest
        net = Net(ss, rs)
        z, yh, x, yl, c, y = net.z, net.yh, net.x, net.yl, net.c, net.y
        starts = [
            pltpu.make_async_copy(src, dst, local.at[i])
            for i, (src, dst) in enumerate(
                (
                    (tok, tok_all.at[y, c]),
                    (cot, cot_out.at[y, c]),
                    (pack.at[c], packs.at[z, yh, x, yl, c]),
                    (biases.at[yh], wq.at[z, yh, x, pl.ds(64, 16)]),
                )
            )
        ]
        for one in starts:
            one.start()
        net.barrier(PLANE + RING + ("yo",))

        def parameters():
            k = [net.slot() for _ in range(4)]
            pair = packs.at[z, yh, x, yl]
            net.send(pack.at[1 - c], packs.at[z, yh, x, yl, c], k[0], "c")
            yield
            starts[2].wait()
            net.got(packs.at[z, yh, x, yl, 1 - c], k[0])
            for i, name in enumerate(("yu", "yd", "yo")):
                net.send(pair, pair, k[1 + i], name)
            yield
            for i, d in enumerate((net.yd, net.yu, net.yo)):
                net.got(packs.at[z, d // 2, x, lax.rem(d, 2)], k[1 + i])

            def view(zz, half, xx, part):
                return packs.at[zz, part, xx, pl.ds(0, 2) if half == BOTH else half]

            yield from plane_gather(net, view)

        def bias():
            k = net.slot()
            there = wq.at[z, yh, x, pl.ds(64, 16)]
            net.send(biases.at[1 - yh], there, k, "yo")
            yield
            starts[3].wait()
            net.got(wq.at[z, 1 - yh, x, pl.ds(64, 16)], k)

        def query():
            steps = weight_gather(net, wq_in, wq, local.at[4])
            next(steps)
            yield from bias()
            yield from steps

        later = Ticks(
            weight_gather(net, wo_in, wo, local.at[5]),
            weight_gather(net, wu_in, wu, local.at[6]),
            weight_gather(net, wd_in, wd, local.at[7]),
        )

        def start_later():
            yield
            later.tick()

        run_all(group_gather(net, tok, tok_all), parameters(), query(), start_later())
        starts[0].wait()
        later.tick()

        lane = lax.broadcasted_iota(jnp.int32, (16, 128), 1)
        values = jnp.zeros((16, 128), F32)
        segs = jnp.zeros((16, 128), F32)
        for j in range(16):
            block = jnp.zeros((16, 128), F32)
            for k in range(8):
                dev = 8 * j + k
                dp, tp = dev // 4, dev % 4
                tile = packs[dp // 8, dp // 4 % 2, dp % 4, tp // 2, tp % 2, 16:32].astype(F32)
                block = jnp.where(lane // 16 == k, tile, block)
                values = jnp.where(lane == dev, tile, values)
                if tp == 0:
                    segs = jnp.where(lane == dp, tile, segs)
            vec[:, j * 128 : (j + 1) * 128] = block
        value_bias = values[6:7]
        segs = segs[7:8]
        vec[8:9, 0:128] = segs
        query_bias = jnp.zeros((16, 256), F32)
        lane = lax.broadcasted_iota(jnp.int32, (16, 256), 1) & 127
        for dp in range(32):
            tile = wq[dp // 8, dp // 4 % 2, dp % 4, 64:80].astype(F32)
            query_bias = jnp.where(lane // 4 == dp, tile, query_bias)
        ub[...] = query_bias[:8, 128:]
        query_bias = jnp.concatenate([query_bias[0:1, :128], query_bias[1:2, :128]], axis=1)

        gain1, shift1 = vec[0:1], vec[1:2]

        def norm_rows(i, carry):
            rows = tok_all[i // 2, i % 2].astype(F32)
            h1[pl.ds(pl.multiple_of(i * 64, 64), 64)] = (normed(rows)[0] * gain1 + shift1).astype(BF16)
            return carry

        lax.fori_loop(0, 8, norm_rows, 0)

        def project(i, carry):
            rows = pl.ds(pl.multiple_of(i * 256, 256), 256)
            h = h1[rows]
            weight = wq[:, :, :, :64].reshape(2048, 256)
            q[rows] = (jnp.dot(h, weight, preferred_element_type=F32) + query_bias).astype(BF16)
            weight = packs[:, :, :, :, :, :16].reshape(2048, 128)
            shift = value_bias * c.astype(F32)
            kv[c, z, i, x] = (jnp.dot(h, weight, preferred_element_type=F32) + shift).astype(BF16)
            return carry

        lax.fori_loop(0, 2, project, 0)

        def view(zz, half, xx, part):
            rows = pl.ds(0, 256) if half == BOTH else pl.ds(128 * half, 128)
            return kv.at[c, zz, part, xx, rows]

        keys = plane_gather(net, view)
        cots = group_gather(net, cot, cot_out)
        next(keys)
        later.tick()
        next(cots)
        next(keys)
        next(keys)
        next(cots)
        next(keys)
        later.tick()
        for _ in keys:
            pass
        k = net.slot()
        net.send(kv.at[c], kv.at[c], k, "c")
        next(cots)
        net.got(kv.at[1 - c], k)

        saves = [
            pltpu.make_async_copy(src, dst, local.at[8 + i])
            for i, (src, dst) in enumerate(
                ((wq, wq_out), (packs, pack_out), (h1, h1_out), (q, q_out), (kv, kv_out), (wo, wo_out))
            )
        ]
        for one in saves[:5]:
            one.start()
        parent = parents[0:1]
        top = attend(0, z, x, q, kv, segs, parent, scores, o, log_sum)
        next(later.steps[0], None)
        top = jnp.maximum(top, attend(1, z, x, q, kv, segs, parent, scores, o, log_sum))
        for h in range(2):
            mine[0, 8 * h : 8 * h + 8] = jnp.full((8, 128), jnp.max(top[:, h * 256 : (h + 1) * 256]), F32)
        for _ in later.steps[0]:
            pass
        saves[5].start()
        later.tick()

        def project_out(i, d):
            rows = o[pl.ds(pl.multiple_of(d * 128, 128), 128)]
            for j in range(4):
                weight = wo[j].reshape(512, 256)
                out = lax.dot_general(rows, weight, NT, preferred_element_type=F32).astype(BF16)
                part[d, 0, :, j * 512 : (j + 1) * 512] = out[:64]
                part[d, 1, :, j * 512 : (j + 1) * 512] = out[64:]

        def rows():
            def total(summed):
                value = tok[...].astype(F32) + (summed + vec[4:5])
                x1[...] = value
                own[...] = (normed(value)[0] * vec[2:3] + vec[3:4]).astype(BF16)

            yield from group_scatter(net, part, *scratch, total, project_out)
            me = pltpu.make_async_copy(own, h2.at[y, c], local.at[14])
            me.start()
            yield from group_gather(net, own, h2)
            me.wait()

        run_all(rows(), heads_max(net, mine, got, best))
        for _ in cots:
            pass
        later.tick()
        starts[1].wait()
        for one in saves:
            one.wait()
        net.finish()

    n, d = tokens.shape
    rows = jax.ShapeDtypeStruct((4, 2, n, d), BF16)

    def bf(*shape):
        return jax.ShapeDtypeStruct(shape, BF16)

    def f32(*shape):
        return jax.ShapeDtypeStruct(shape, F32)

    return pl.pallas_call(
        kernel,
        out_shape=(
            rows,
            rows,
            bf(4, 2, 4, n, 1024),
            bf(4, 2, 4, n, 1024),
            bf(4, 2, 4, 80, 256),
            bf(4, 2, 4, n, 256),
            bf(4, 2, 4, 2, 2, 32, 128),
            bf(512, d),
            bf(512, 256),
            bf(2, 4, 2, 4, 256, 128),
            bf(512, 256),
            f32(2, 8, 512),
            f32(n, d),
            f32(2, 16, 128),
            f32(16, d),
            f32(8, 128),
        ),
        in_specs=[INV, ANY, INV, INV, INV, ANY, ANY, ANY, ANY],
        out_specs=(ANY,) * 10 + (INV,) * 6,
        scratch_shapes=[
            VMEM((4, 2, n, d), BF16),
            VMEM((512, d), BF16),
            VMEM((4, 2, 4, 2, 2, 32, 128), BF16),
            VMEM((4, 2, 4, 80, 256), BF16),
            VMEM((4, 2, 4, n, 256), BF16),
            VMEM((512, 256), BF16),
            VMEM((2, 4, 2, 4, 256, 128), BF16),
            VMEM((10, 256, 512), F32),
            VMEM((4, 2, n, d), BF16),
            VMEM((n, d), BF16),
            VMEM((5, 16, 128), F32),
            VMEM((7, 16, 128), F32),
            pltpu.SemaphoreType.DMA((15,)),
        ]
        + scatter_scratch(n, d)
        + sems(160),
        compiler_params=params(1),
        name="forward",
    )(tokens, cotangent, pack, biases, parents, w_query, w_out, w_up, w_down)


def block_place(segs, parents, block):
    seg = segs[block]
    parent = parents[seg]
    trunk = parents[parent]
    parent_block = jnp.int32(16)
    for b in range(16, 32):
        parent_block = jnp.where(segs[b] == parent, b, parent_block)
    return trunk, parent_block, seg >= 10, seg >= 2


def attend_back(q, kv, o, go, log_sum, segs, parents):
    def kernel(segs, parents, q, kv, o, go, log_sum, dq, dkv):
        z, x = lax.axis_index("z"), lax.axis_index("x")
        lane = lax.broadcasted_iota(jnp.int32, (256, 512), 1) & 255
        row = lax.broadcasted_iota(jnp.int32, (256, 512), 0)
        for b in range(2):
            block = z * 8 + b * 4 + x
            trunk, parent_block, leaf, branch = block_place(segs, parents, block)

            def stacked(ref):
                return jnp.concatenate([ref[b, :, :128], ref[b, :, 128:]], axis=0)

            both, grad = stacked(q), stacked(go)
            logs = log_sum[b, 0:1]
            inner = jnp.sum((grad.astype(F32) * stacked(o).astype(F32)).T, axis=0, keepdims=True)

            def one(i, key_block, mask, acc):
                key, value = kv[key_block, :, :128], kv[key_block, :, 128:]
                nt = (((1,), (1,)), ((), ()))
                s = lax.dot_general(key, both, nt, preferred_element_type=F32) * 128**-0.5
                p = jnp.where(mask, jnp.exp(jnp.minimum(s - logs, 1.0)), 0.0)
                dp = lax.dot_general(value, grad, nt, preferred_element_type=F32)
                ds = (p * (dp - inner)).astype(BF16)
                dk = jnp.dot(ds, both, preferred_element_type=F32) * 128**-0.5
                dv = jnp.dot(p.astype(BF16), grad, preferred_element_type=F32)
                dkv[b, i, :, :128] = dk.astype(BF16)
                dkv[b, i, :, 128:] = dv.astype(BF16)
                return acc + lax.dot_general(key, ds, (((0,), (0,)), ((), ())), preferred_element_type=F32)

            def trunk_one(i, acc):
                gap = (block - trunk * 8 - i) * 256
                return one(i, trunk * 8 + i, row - lane <= gap, acc)

            acc = lax.fori_loop(0, 8, trunk_one, jnp.zeros((128, 512), F32))
            acc = one(8, parent_block, jnp.broadcast_to(leaf, (256, 512)), acc)
            acc = one(9, block, (row <= lane) & branch, acc)
            grad_q = (acc * 128**-0.5).T.astype(BF16)
            dq[b, :, :128] = grad_q[:256]
            dq[b, :, 128:] = grad_q[256:]

    return pl.pallas_call(
        kernel,
        out_shape=(
            jax.ShapeDtypeStruct((2, 256, 256), BF16),
            jax.ShapeDtypeStruct((2, 10, 256, 256), BF16),
        ),
        in_specs=[INS, INS, INV, INV, INV, INV, INV],
        out_specs=(INV, INV),
        compiler_params=pltpu.CompilerParams(vmem_limit_bytes=56 << 20),
        name="attend_back",
    )(segs, parents, q, kv, o, go, log_sum)


def normed(values):
    centred = values - jnp.mean(values, axis=-1, keepdims=True)
    inverse = lax.rsqrt(jnp.mean(centred * centred, axis=-1, keepdims=True) + EPS)
    return centred * inverse, inverse


def norm_back(grad, norm, inverse, gain):
    scaled = grad * gain
    return inverse * (
        scaled
        - jnp.mean(scaled, axis=-1, keepdims=True)
        - norm * jnp.mean(scaled * norm, axis=-1, keepdims=True)
    )


def heads_max(net, mine, got, best):
    for i, (up, down) in enumerate((("xu", "xd"), ("zu", "zd"))):
        k = [net.slot() for _ in range(3)]
        a, b, d = got.at[3 * i], got.at[3 * i + 1], got.at[3 * i + 2]
        net.send(mine.at[2 * i], a, k[0], up)
        net.send(mine.at[2 * i], b, k[1], down)
        yield
        net.got(a, k[0])
        net.got(b, k[1])
        mine[2 * i + 1] = jnp.maximum(mine[2 * i], jnp.maximum(a[...], b[...]))
        net.send(mine.at[2 * i + 1], d, k[2], up)
        yield
        net.got(d, k[2])
        mine[2 * i + 2] = jnp.maximum(mine[2 * i + 1], d[...])
    k = net.slot()
    net.send(mine.at[4], got.at[6], k, "yo")
    yield
    net.got(got.at[6], k)
    best[net.yh] = mine[4]
    best[1 - net.yh] = got[6]


def turn(mlp, back, x1, cotangent, gain, down_bias):
    def kernel(mlp, back, x1, cot, gain, bias, output, dx1, dz, sums, own, local, *rest):
        first, second, (ss, rs) = rest[:4], rest[4:8], rest[8:]
        net = Net(ss, rs)
        net.barrier(RING)

        def gradient():
            def total(summed):
                norm, inverse = normed(x1[...])
                grad = cot[...].astype(F32) + norm_back(summed, norm, inverse, gain[...])
                dx1[...] = grad
                rounded = grad.astype(BF16)
                own[...] = rounded
                parts = [
                    jnp.sum(v, axis=0, keepdims=True)
                    for v in (summed * norm, summed, rounded.astype(F32), cot[...].astype(F32))
                ]
                zero = jnp.zeros((2, parts[0].shape[1]), F32)
                sums[...] = jnp.concatenate([zero] + parts + [zero], axis=0)

            yield from group_scatter(net, back, *first, total)
            me = pltpu.make_async_copy(own, dz.at[net.y, net.c], local)
            me.start()
            yield from group_gather(net, own, dz)
            me.wait()

        def forward():
            def total(summed):
                output[...] = (x1[...] + (summed + bias[...])).astype(BF16)

            yield
            yield from group_scatter(net, mlp, *second, total)

        run_all(gradient(), forward())
        net.finish()

    n, d = cotangent.shape
    return pl.pallas_call(
        kernel,
        out_shape=(
            jax.ShapeDtypeStruct((n, d), BF16),
            jax.ShapeDtypeStruct((n, d), F32),
            jax.ShapeDtypeStruct((4, 2, n, d), BF16),
            jax.ShapeDtypeStruct((8, d), F32),
        ),
        in_specs=[INV] * 6,
        out_specs=(INV, INV, ANY, INV),
        scratch_shapes=[VMEM((n, d), BF16), pltpu.SemaphoreType.DMA]
        + scatter_scratch(n, d)
        + scatter_scratch(n, d)
        + sems(9 + 8 + 8),
        compiler_params=params(5),
        name="turn",
    )(mlp, back, x1, cotangent, gain, down_bias)


def weight_scatter(net, g, tmp, swap, out):
    z, yh, x = net.z, net.yh, net.x
    w = g.shape[-1]
    k = net.slot()
    yield from plane_scatter(net, column_view(g), tmp)
    net.send(g.at[z, 1 - yh, x], swap, k, "yo")
    out[:, pl.ds(pl.multiple_of(yh * w, 128), w)] = g[z, yh, x].astype(F32)
    yield
    net.got(swap, k)
    out[:, pl.ds(pl.multiple_of((1 - yh) * w, 128), w)] = swap[...].astype(F32)


def scatter_weights(grads, cid):
    count = len(grads)

    def kernel(*refs):
        g, outs = refs[:count], refs[count : 2 * count]
        scratch, (ss, rs) = refs[2 * count : -2], refs[-2:]
        net = Net(ss, rs)
        net.barrier(PLANE + ("yo",))
        run_all(
            *[
                weight_scatter(net, g[i], scratch[9 * i : 9 * i + 8], scratch[9 * i + 8], outs[i])
                for i in range(count)
            ]
        )
        net.finish()

    scratch = []
    for one in grads:
        n, w = one.shape[-2:]
        scratch += plane_scratch(n, w // 2) + [VMEM((n, w), BF16)]
    return pl.pallas_call(
        kernel,
        out_shape=tuple(jax.ShapeDtypeStruct((g.shape[-2], 2 * g.shape[-1]), F32) for g in grads),
        in_specs=[INV] * count,
        out_specs=(INV,) * count,
        scratch_shapes=scratch + sems(17 * count),
        compiler_params=params(cid),
        name="scatter_weights",
    )(*grads)


def scatter_kv(slots, segs, parents):
    def kernel(segs, parents, slots, out, full, from_core, held, ring, *rest):
        tmp, (ss, rs) = rest[:8], rest[8:]
        net = Net(ss, rs)
        z, x, c, y = net.z, net.x, net.c, net.y
        net.barrier(PLANE + RING + ("yo",))
        for b in range(2):
            block = z * 8 + b * 4 + x
            trunk, parent_block, leaf, branch = block_place(segs, parents, block)

            def place(kb, carry):
                slot = jnp.where(kb < 16, kb & 7, jnp.where(kb == block, 9, 8))
                valid = jnp.where(
                    kb < 16,
                    (kb >> 3) == trunk,
                    ((kb == block) & branch) | ((kb == parent_block) & leaf),
                )
                value = jnp.where(valid, slots[b, slot], jnp.zeros((256, 256), BF16))
                at = (kb >> 3, (kb >> 2) & 1, kb & 3)
                if b == 0:
                    full[at] = value
                else:
                    full[at] = full[at] + value
                return carry

            lax.fori_loop(0, 32, place, 0)
        k = [net.slot() for _ in range(8)]
        net.send(full.at[:, 1 - c], from_core, k[0], "c")
        net.got(from_core, k[0])
        for zz in range(4):
            for xx in range(4):
                held[zz, xx] = (full[zz, c, xx].astype(F32) + from_core[zz, xx].astype(F32)).astype(BF16)

        def view(zz, half, xx, part):
            rows = pl.ds(0, 256) if half == BOTH else pl.ds(128 * half, 128)
            return held.at[zz, xx, rows, pl.ds(part * 128, 128)]

        run_all(plane_scatter(net, view, tmp))
        mine = held.at[z, x]

        def rows(yy):
            return pl.ds(pl.multiple_of(yy * 64, 64), 64)

        for i, (name, d) in enumerate((("yu", net.yu), ("yd", net.yd), ("yo", net.yo))):
            net.send(mine.at[rows(d)], ring.at[i], k[1 + i], name)
        for i in range(3):
            net.got(ring.at[i], k[1 + i])
        own = held[z, x, rows(y)].astype(F32)
        for i in range(3):
            own = own + ring[i].astype(F32)
        out[c, rows(y)] = own.astype(BF16)
        view = out.at[c, rows(y)]
        for i, name in enumerate(("yu", "yd", "yo")):
            net.send(view, view, k[4 + i], name)
        for i, d in enumerate((net.yd, net.yu, net.yo)):
            net.got(out.at[c, rows(d)], k[4 + i])
        net.send(out.at[c], out.at[c], k[7], "c")
        net.got(out.at[1 - c], k[7])
        net.finish()

    return pl.pallas_call(
        kernel,
        out_shape=jax.ShapeDtypeStruct((2, 256, 256), BF16),
        in_specs=[INS, INS, INV],
        out_specs=INV,
        scratch_shapes=[
            VMEM((4, 2, 4, 256, 256), BF16),
            VMEM((4, 4, 256, 256), BF16),
            VMEM((4, 4, 256, 256), BF16),
            VMEM((3, 64, 256), BF16),
            VMEM((2, 4, 128, 128), BF16),
            VMEM((2, 4, 128, 128), BF16),
            VMEM((2, 4, 256, 128), BF16),
            VMEM((2, 4, 256, 128), BF16),
            VMEM((2, 128, 128), BF16),
            VMEM((2, 128, 128), BF16),
            VMEM((2, 256, 128), BF16),
            VMEM((2, 256, 128), BF16),
        ]
        + sems(16 + 8),
        compiler_params=params(6),
        name="scatter_kv",
    )(segs, parents, slots)


def closing(back, tokens, dx1, from_kv, gain, sums, grad_q, small):
    def kernel(back, tokens, dx1, from_kv, gain, sums, gq, small, grad_input, out_q, vec, small_out,
               vecs, vec_z, vec_x, lone, small_z, small_x, small_y, swap, *rest):
        first, tmp, (ss, rs) = rest[:4], rest[4:12], rest[12:]
        net = Net(ss, rs)
        z, yh, x, y, c = net.z, net.yh, net.x, net.y, net.c
        net.barrier(PLANE + RING + ("yo", "xo", "zo"))

        def rows():
            def total(summed):
                grad = summed + from_kv[...]
                norm, inverse = normed(tokens[...].astype(F32))
                grad_input[...] = dx1[...] + norm_back(grad, norm, inverse, gain[...])
                one = jnp.sum(grad * norm, axis=0, keepdims=True)
                two = jnp.sum(grad, axis=0, keepdims=True)
                vecs[y, c] = jnp.concatenate([one, two, sums[2:8]], axis=0)

            yield from group_scatter(net, back, *first, total)
            k = [net.slot() for _ in range(13)]
            at = vecs.at[y, c]
            for i, name in enumerate(("yu", "yd", "yo", "c")):
                net.send(at, at, k[i], name)
            yield
            for i, d in enumerate((net.yd, net.yu, net.yo)):
                net.got(vecs.at[d, c], k[i])
                net.send(vecs.at[d, c], vecs.at[d, c], k[4 + i], "c")
            yield
            for i, d in enumerate((y, net.yd, net.yu, net.yo)):
                net.got(vecs.at[d, 1 - c], k[3 + i])
            acc = vecs[0, 0]
            for i in range(1, 8):
                acc = acc + vecs[i // 2, i % 2]
            for i in range(4):
                vec_z[i] = acc[:, i * 512 : (i + 1) * 512]
            for i, (name, d) in enumerate((("zu", net.zu), ("zd", net.zd), ("zo", net.zo))):
                net.send(vec_z.at[d], vec_z.at[4 + i], k[7 + i], name)
            yield
            for i in range(3):
                net.got(vec_z.at[4 + i], k[7 + i])
            acc = vec_z[z] + vec_z[4] + vec_z[5] + vec_z[6]
            vec_x[0] = jnp.where(yh == 0, acc[:, :256], acc[:, 256:])
            for i, name in enumerate(("xu", "xd", "xo")):
                net.send(vec_x.at[0], vec_x.at[1 + i], k[10 + i], name)
            yield
            for i in range(3):
                net.got(vec_x.at[1 + i], k[10 + i])
            vec[...] = vec_x[0] + vec_x[1] + vec_x[2] + vec_x[3]

        def small_sums():
            k = [net.slot() for _ in range(7)]
            for i, (name, d) in enumerate((("zu", net.zu), ("zd", net.zd), ("zo", net.zo))):
                net.send(small.at[d], small_z.at[i], k[i], name)
            yield
            for i in range(3):
                net.got(small_z.at[i], k[i])
            for xx in range(4):
                small_x[xx] = small[z, xx] + small_z[0, xx] + small_z[1, xx] + small_z[2, xx]
            for i, (name, d) in enumerate((("xu", net.xu), ("xd", net.xd), ("xo", net.xo))):
                net.send(small_x.at[d], small_x.at[4 + i], k[3 + i], name)
            yield
            for i in range(3):
                net.got(small_x.at[4 + i], k[3 + i])
            lone[...] = small_x[x] + small_x[4] + small_x[5] + small_x[6]
            net.send(lone, small_y, k[6], "yo")
            yield
            net.got(small_y, k[6])
            small_out[0] = lone[...]
            small_out[1] = small_y[...]

        run_all(rows(), weight_scatter(net, gq, tmp, swap, out_q), small_sums())
        net.finish()

    n, d = tokens.shape
    w = grad_q.shape[-1]
    tile = small.shape[-2:]
    return pl.pallas_call(
        kernel,
        out_shape=(
            jax.ShapeDtypeStruct((n, d), F32),
            jax.ShapeDtypeStruct((n, 2 * w), F32),
            jax.ShapeDtypeStruct((8, 256), F32),
            jax.ShapeDtypeStruct((2,) + tile, F32),
        ),
        in_specs=[INV] * 8,
        out_specs=(INV,) * 4,
        scratch_shapes=[
            VMEM((4, 2, 8, d), F32),
            VMEM((7, 8, 512), F32),
            VMEM((4, 8, 256), F32),
            VMEM(tile, F32),
            VMEM((3, 4) + tile, F32),
            VMEM((7,) + tile, F32),
            VMEM(tile, F32),
            VMEM((n, w), BF16),
        ]
        + scatter_scratch(n, d)
        + plane_scratch(n, w // 2)
        + sems(8 + 13 + 7 + 17),
        compiler_params=params(7),
        name="closing",
    )(back, tokens, dx1, from_kv, gain, sums, grad_q, small)


def local(
    tokens,
    cotangent,
    seg_ids,
    parents,
    tau,
    w_query,
    w_up,
    w_out,
    w_down,
    query_bias,
    up_bias,
    w_keyval,
    value_bias,
    norm1_gain,
    norm1_bias,
    norm2_gain,
    norm2_bias,
    out_bias,
    down_bias,
):
    z, yh, x, yl, c = (lax.axis_index(a) for a in AXES)
    tp = yl * 2 + c
    d = tokens.shape[1]

    def dot(left, right, dims):
        return lax.dot_general(left, right, ((dims[:1], dims[1:]), ((), ())), preferred_element_type=F32)

    def row(values):
        return jnp.tile(values.astype(BF16).reshape(1, -1), (1, 128 // values.size))

    tile = [row(v) for v in (norm1_gain, norm1_bias, norm2_gain, norm2_bias, out_bias, down_bias, value_bias, seg_ids[:1])]
    tile = jnp.concatenate(tile + [jnp.zeros((8, 128), BF16)], axis=0)
    pack = jnp.stack([jnp.concatenate([w_keyval[:, :128], tile]), jnp.concatenate([w_keyval[:, 128:], tile])])
    qbt = jnp.pad(jnp.tile(query_bias.T, (1, 32)).reshape(2, 2, 128), ((0, 0), (0, 14), (0, 0)))
    ubt = jnp.pad(jnp.tile(up_bias.T, (1, 32)).reshape(2, 8, 128), ((0, 0), (0, 8), (0, 0)))
    biases = jnp.concatenate([qbt, ubt], axis=2)
    ancestors = jnp.pad(jnp.broadcast_to(parents.astype(F32)[None], (8, 18)), ((0, 0), (0, 110)))
    (cot_all, h2, wu, wd, wq, wo, packs, h1, q, kv6, o_rows, log_sum, x1, best, vec, ub) = forward(
        tokens, cotangent, pack, biases, ancestors, w_query, w_out, w_up, w_down
    )
    cot_all = cot_all.reshape(512, d)
    wq = wq[:, :, :, :64].reshape(d, -1)
    wo = wo.reshape(d, -1)
    wu = wu.reshape(d, -1)
    wd = wd.reshape(d, -1)
    h2 = h2.reshape(512, d)
    w_kv = lax.all_gather(packs[..., :16, :].reshape(d, 128), "c", axis=1, tiled=True)
    gain1, shift1, gain2, shift2, bias_out, bias_down = (vec[i : i + 1] for i in range(6))
    segs = vec[8, :32].astype(jnp.int32)
    ub = ub.reshape(1, 1024)
    q_blocks = q.reshape(2, 256, 256)
    o = o_rows.reshape(2, 256, 256)
    kv_all = kv6.reshape(2, 32, 256, 128).transpose(1, 2, 0, 3).reshape(32, 256, 256)
    limit = tau[0]
    head_max = best.reshape(4, 8, 128)[:, 0, 0]
    factor = limit / jnp.maximum(head_max, limit)
    clipped_query = (w_query.astype(F32) * jnp.repeat(factor, 128)[None, :]).astype(BF16)
    clipped_bias = (query_bias.astype(F32) * factor[None, :]).astype(BF16)

    def gate(values):
        return jax.nn.gelu(values, approximate=True)

    u = dot(h2, wu, (1, 0)) + ub
    a, gate_back = jax.vjp(gate, u)
    a = a.astype(BF16)
    mlp = dot(a, wd, (1, 1)).astype(BF16).reshape(4, 2, 64, d)
    du = gate_back(dot(cot_all, wd, (1, 0)))[0].astype(BF16)
    grad_ub = jnp.sum(du.astype(F32), axis=0)
    grad_down = dot(cot_all, a, (0, 0)).astype(BF16)
    grad_up = dot(h2, du, (0, 0)).astype(BF16)
    back2 = dot(du, wu, (1, 1)).astype(BF16).reshape(4, 2, 64, d)
    output, dx1, dz, sums = turn(mlp, back2, x1, cotangent, gain2, bias_down)
    dz = dz.reshape(512, d)
    go = dot(dz, wo, (1, 0)).astype(BF16).reshape(2, 256, 256)
    grad_out = dot(dz, o_rows, (0, 0)).astype(BF16)
    up_sum, down_sum, out_sum = scatter_weights(
        [v.reshape(4, 2, 4, 64, -1) for v in (grad_up, grad_down, grad_out)], 8
    )
    dq, slots = attend_back(q_blocks, kv_all, o, go, log_sum, segs, parents)
    dq = dq.reshape(512, 256)
    dkv = scatter_kv(slots, segs, parents).reshape(512, 256)
    back1 = dot(dq, wq, (1, 1)).astype(BF16).reshape(4, 2, 64, d)
    grad_q = dot(h1, dq, (0, 0)).astype(BF16).reshape(4, 2, 4, 64, 256)
    grad_kv = dot(h1, dkv, (0, 0)).reshape(4, 2, 4, 4, 16, 256)
    grad_kv = lax.dynamic_index_in_dim(lax.dynamic_index_in_dim(grad_kv, yh, 1, False), tp, 2, False)
    dkv_own = lax.dynamic_slice_in_dim(dkv, yh * 256 + tp * 64, 64, 0)
    from_kv = dot(dkv_own, w_kv, (1, 1))
    gqb = jnp.sum(dq.astype(F32), axis=0).reshape(2, 128).T.reshape(4, 2, 4, 8)
    gub = grad_ub.reshape(8, 128).T.reshape(4, 2, 4, 32)
    gvb = jnp.sum(dkv[:, 128:].astype(F32), axis=0).reshape(4, 2, 4, 4)
    gvb = lax.dynamic_index_in_dim(lax.dynamic_index_in_dim(gvb, yh, 1, False), tp, 2, False)
    bias_rows = jnp.concatenate([gqb, gub], axis=3).transpose(0, 2, 1, 3)
    bias_rows = jnp.pad(bias_rows, ((0, 0), (0, 0), (0, 1), (0, 256 - 40)))
    bias_rows = bias_rows.at[:, :, 2, 0].set(gvb)
    bias_rows = jnp.pad(bias_rows, ((0, 0), (0, 0), (0, 5), (0, 0)))
    small_grads = jnp.concatenate([grad_kv, bias_rows], axis=2)
    grad_input, query_sum, vec, small_sum = closing(
        back1, tokens, dx1, from_kv, gain1, sums, grad_q, small_grads
    )
    keyval_sum = small_sum[0, :16]
    valueb_sum = small_sum[0, 18, :1]
    own_bias = lax.dynamic_index_in_dim(small_sum[0, 16:18, :40], yh, 0, False)
    oth_bias = lax.dynamic_index_in_dim(small_sum[1, 16:18, :40], yh, 0, False)
    first = jnp.where(yh == 0, own_bias, oth_bias)
    second = jnp.where(yh == 0, oth_bias, own_bias)
    qbias_sum = jnp.concatenate([first[:8].reshape(4, 2), second[:8].reshape(4, 2)], axis=1)
    ubias_sum = jnp.concatenate([first[8:].reshape(4, 8), second[8:].reshape(4, 8)], axis=1)
    vec = lax.dynamic_slice(vec, (jnp.int32(0), x * 64 + tp * 16), (6, 16))
    return (
        output,
        grad_input,
        query_sum,
        up_sum,
        out_sum,
        down_sum,
        qbias_sum,
        ubias_sum,
        keyval_sum,
        valueb_sum,
        vec[0],
        vec[1],
        vec[2],
        vec[3],
        vec[4],
        vec[5],
        clipped_query,
        clipped_bias,
    )


def solution(mesh):
    fine = Mesh(mesh.devices.reshape(4, 2, 4, 2, 2), AXES)
    dp, tp = ("z", "yh", "x"), ("yl", "c")
    rows, flat, weight = P(AXES, None), P(AXES), P(dp, tp)
    in_specs = (rows, rows, P(dp), P(), P()) + (weight,) * 6 + (rows,) + (flat,) * 7
    out_specs = (rows, rows) + (weight,) * 6 + (rows,) + (flat,) * 7 + (weight, weight)
    return jax.shard_map(local, mesh=fine, in_specs=in_specs, out_specs=out_specs, check_vma=False)
```

```python
import itertools

import jax
import jax.numpy as jnp
from jax import lax
from jax.experimental import pallas as pl
from jax.experimental.pallas import tpu as pltpu
from jax.sharding import Mesh, PartitionSpec as P

EPS = 1e-05
AXES = ("z", "yh", "x", "yl", "c")
F32 = jnp.float32
BF16 = jnp.bfloat16
VMEM = pltpu.VMEM
NEG = -1e30


class Net:
    def __init__(self, send_sems, recv_sems):
        self.z, self.yh, self.x, self.yl, self.c = (lax.axis_index(a) for a in AXES)
        self.y = self.yh * 2 + self.yl
        self.yu, self.yo, self.yd = (lax.rem(self.y + s, 4) for s in (1, 2, 3))
        self.xu, self.xo, self.xd = (lax.rem(self.x + s, 4) for s in (1, 2, 3))
        self.zu, self.zo, self.zd = (lax.rem(self.z + s, 4) for s in (1, 2, 3))
        up, down = lax.rem(self.yh + self.yl, 2), lax.rem(self.yh + 1 - self.yl, 2)
        self.dev = {
            "yu": {"yh": up, "yl": 1 - self.yl},
            "yd": {"yh": down, "yl": 1 - self.yl},
            "yo": {"yh": 1 - self.yh},
            "c": {"c": 1 - self.c},
            "xu": {"x": self.xu},
            "xd": {"x": self.xd},
            "xo": {"x": self.xo},
            "zu": {"z": self.zu},
            "zd": {"z": self.zd},
            "zo": {"z": self.zo},
        }
        self.send_sems, self.recv_sems = send_sems, recv_sems
        self.count = 0
        self.sent = []

    def barrier(self, names):
        sem = pltpu.get_barrier_semaphore()
        for name in names:
            pl.semaphore_signal(
                sem, inc=1, device_id=self.dev[name], device_id_type=pl.DeviceIdType.MESH
            )
        pl.semaphore_wait(sem, len(names))

    def slot(self):
        self.count += 1
        return self.count - 1

    def copy(self, src, dst, k, name):
        return pltpu.make_async_remote_copy(
            src_ref=src,
            dst_ref=dst,
            send_sem=self.send_sems.at[k],
            recv_sem=self.recv_sems.at[k],
            device_id=self.dev[name],
            device_id_type=pl.DeviceIdType.MESH,
        )

    def send(self, src, dst, k, name):
        one = self.copy(src, dst, k, name)
        one.start()
        self.sent.append(one)

    def got(self, ref, k):
        self.copy(ref, ref, k, "c").wait_recv()

    def finish(self):
        for one in self.sent:
            one.wait_send()


def run_all(*steps):
    live = list(steps)
    while live:
        rest = []
        for one in live:
            try:
                next(one)
                rest.append(one)
            except StopIteration:
                pass
        live = rest


def group_gather(net, src, out):
    y, c, yu, yd, yo = net.y, net.c, net.yu, net.yd, net.yo
    k = [net.slot() for _ in range(9)]
    half = src.shape[0] // 2
    lo, hi = pl.ds(0, half), pl.ds(half, half)
    mine = out.at[y, c]
    net.send(src, mine, k[0], "yu")
    net.send(src, mine, k[1], "yd")
    net.send(src, mine, k[2], "c")
    yield
    net.got(out.at[yd, c], k[0])
    net.send(out.at[yd, c, lo], out.at[yd, c, lo], k[3], "yu")
    net.send(out.at[yd, c], out.at[yd, c], k[4], "c")
    net.got(out.at[yu, c], k[1])
    net.send(out.at[yu, c, hi], out.at[yu, c, hi], k[5], "yd")
    net.send(out.at[yu, c], out.at[yu, c], k[6], "c")
    yield
    net.got(out.at[yo, c, lo], k[3])
    net.send(out.at[yo, c, lo], out.at[yo, c, lo], k[7], "c")
    net.got(out.at[yo, c, hi], k[5])
    net.send(out.at[yo, c, hi], out.at[yo, c, hi], k[8], "c")
    yield
    net.got(out.at[y, 1 - c], k[2])
    net.got(out.at[yd, 1 - c], k[4])
    net.got(out.at[yu, 1 - c], k[6])
    net.got(out.at[yo, 1 - c, lo], k[7])
    net.got(out.at[yo, 1 - c, hi], k[8])


def group_scatter(net, part, acc, from_half, from_full, total, make=None):
    y, c, yu, yd, yo = net.y, net.c, net.yu, net.yd, net.yo
    k = [net.slot() for _ in range(8)]
    n = part.shape[2]
    half = n // 2
    lo, hi = pl.ds(0, half), pl.ds(half, half)

    sent = []

    def send(src, dst, i, name):
        sent.append(net.copy(src, dst, i, name))
        sent[-1].start()

    def start(i, d):
        if make is not None:
            make(i, d)
        send(part.at[d, 1 - c], acc.at[d], k[i], "c")

    def core_sum(i, d):
        net.got(acc.at[d], k[i])
        acc[d] = acc[d] + part[d, c]

    for i, d in enumerate((yo, yu, yd)):
        start(i, d)
    yield
    core_sum(0, yo)
    send(acc.at[yo, lo], from_half.at[0], k[4], "yu")
    send(acc.at[yo, hi], from_half.at[1], k[5], "yd")
    core_sum(1, yu)
    core_sum(2, yd)
    yield
    net.got(from_half.at[0], k[4])
    acc[yu, lo] = acc[yu, lo] + from_half[0]
    send(acc.at[yu], from_full.at[0], k[6], "yu")
    net.got(from_half.at[1], k[5])
    acc[yd, hi] = acc[yd, hi] + from_half[1]
    send(acc.at[yd], from_full.at[1], k[7], "yd")
    yield
    start(3, y)
    yield
    net.got(acc.at[y], k[3])
    mine = part[y, c].astype(F32) + acc[y].astype(F32)
    net.got(from_full.at[0], k[6])
    net.got(from_full.at[1], k[7])
    for one in sent:
        one.wait_send()
    total(mine + from_full[0].astype(F32) + from_full[1].astype(F32))


def scatter_scratch(n, w):
    return [VMEM((4, n, w), BF16), VMEM((2, n // 2, w), BF16), VMEM((2, n, w), BF16)]


BOTH = slice(None)


def plane_gather(net, o):
    z, x, xu, xd, xo, zu, zd, zo = net.z, net.x, net.xu, net.xd, net.xo, net.zu, net.zd, net.zo
    k = [net.slot() for _ in range(16)]
    every = slice(None)

    def send(view, i, name):
        net.send(view, view, k[i], name)

    def got(view, i):
        net.got(view, k[i])

    send(o(z, BOTH, x, 0), 0, "xu")
    send(o(z, BOTH, x, 0), 1, "xd")
    send(o(z, BOTH, x, 1), 2, "zu")
    send(o(z, BOTH, x, 1), 3, "zd")
    yield
    got(o(z, BOTH, xd, 0), 0)
    send(o(z, 0, xd, 0), 4, "xu")
    got(o(zd, BOTH, x, 1), 2)
    send(o(zd, 0, x, 1), 6, "zu")
    got(o(z, BOTH, xu, 0), 1)
    send(o(z, 1, xu, 0), 5, "xd")
    got(o(zu, BOTH, x, 1), 3)
    send(o(zu, 1, x, 1), 7, "zd")
    yield
    got(o(z, 0, xo, 0), 4)
    got(o(z, 1, xo, 0), 5)
    send(o(z, BOTH, every, 0), 8, "zu")
    send(o(z, BOTH, every, 0), 9, "zd")
    got(o(zo, 0, x, 1), 6)
    got(o(zo, 1, x, 1), 7)
    send(o(every, BOTH, x, 1), 10, "xu")
    send(o(every, BOTH, x, 1), 11, "xd")
    yield
    got(o(zd, BOTH, every, 0), 8)
    send(o(zd, 0, every, 0), 12, "zu")
    got(o(every, BOTH, xd, 1), 10)
    send(o(every, 0, xd, 1), 14, "xu")
    got(o(zu, BOTH, every, 0), 9)
    send(o(zu, 1, every, 0), 13, "zd")
    got(o(every, BOTH, xu, 1), 11)
    send(o(every, 1, xu, 1), 15, "xd")
    yield
    got(o(zo, 0, every, 0), 12)
    got(o(zo, 1, every, 0), 13)
    got(o(every, 0, xo, 1), 14)
    got(o(every, 1, xo, 1), 15)


def add_into(dst, *others):
    for index in itertools.product(*[range(n) for n in dst.shape[:-2]]):
        at = index + (slice(None), slice(None))
        total = dst[at]
        for other in others:
            total = total + other[at]
        dst[at] = total


def plane_scatter(net, g, tmp):
    z, x, xu, xd, xo, zu, zd, zo = net.z, net.x, net.xu, net.xd, net.xo, net.zu, net.zd, net.zo
    t1, t2, u1, u2, t3, t4, u3, u4 = tmp
    k = [net.slot() for _ in range(16)]
    every = slice(None)

    def send(src, dst, i, name):
        net.send(src, dst, k[i], name)

    def got(ref, i):
        net.got(ref, k[i])

    send(g(zo, 0, every, 0), t1.at[0], 0, "zu")
    send(g(zo, 1, every, 0), t1.at[1], 1, "zd")
    send(g(every, 0, xo, 1), t2.at[0], 2, "xu")
    send(g(every, 1, xo, 1), t2.at[1], 3, "xd")
    yield
    got(t1.at[0], 0)
    add_into(g(zu, 0, every, 0), t1.at[0])
    send(g(zu, BOTH, every, 0), u1.at[0], 4, "zu")
    got(t2.at[0], 2)
    add_into(g(every, 0, xu, 1), t2.at[0])
    send(g(every, BOTH, xu, 1), u2.at[0], 6, "xu")
    got(t1.at[1], 1)
    add_into(g(zd, 1, every, 0), t1.at[1])
    send(g(zd, BOTH, every, 0), u1.at[1], 5, "zd")
    got(t2.at[1], 3)
    add_into(g(every, 1, xd, 1), t2.at[1])
    send(g(every, BOTH, xd, 1), u2.at[1], 7, "xd")
    yield
    got(u1.at[0], 4)
    got(u1.at[1], 5)
    add_into(g(z, BOTH, every, 0), u1.at[0], u1.at[1])
    send(g(z, 0, xo, 0), t3.at[0], 8, "xu")
    send(g(z, 1, xo, 0), t3.at[1], 9, "xd")
    got(u2.at[0], 6)
    got(u2.at[1], 7)
    add_into(g(every, BOTH, x, 1), u2.at[0], u2.at[1])
    send(g(zo, 0, x, 1), t4.at[0], 10, "zu")
    send(g(zo, 1, x, 1), t4.at[1], 11, "zd")
    yield
    got(t3.at[0], 8)
    add_into(g(z, 0, xu, 0), t3.at[0])
    send(g(z, BOTH, xu, 0), u3.at[0], 12, "xu")
    got(t4.at[0], 10)
    add_into(g(zu, 0, x, 1), t4.at[0])
    send(g(zu, BOTH, x, 1), u4.at[0], 14, "zu")
    got(t3.at[1], 9)
    add_into(g(z, 1, xd, 0), t3.at[1])
    send(g(z, BOTH, xd, 0), u3.at[1], 13, "xd")
    got(t4.at[1], 11)
    add_into(g(zd, 1, x, 1), t4.at[1])
    send(g(zd, BOTH, x, 1), u4.at[1], 15, "zd")
    yield
    got(u3.at[0], 12)
    got(u3.at[1], 13)
    add_into(g(z, BOTH, x, 0), u3.at[0], u3.at[1])
    got(u4.at[0], 14)
    got(u4.at[1], 15)
    add_into(g(z, BOTH, x, 1), u4.at[0], u4.at[1])


def plane_scratch(n, w):
    return [
        VMEM((2, 4, n, w), BF16),
        VMEM((2, 4, n, w), BF16),
        VMEM((2, 2, 4, n, w), BF16),
        VMEM((2, 4, 2, n, w), BF16),
        VMEM((2, n, w), BF16),
        VMEM((2, n, w), BF16),
        VMEM((2, 2, n, w), BF16),
        VMEM((2, 2, n, w), BF16),
    ]


def column_view(ref):
    w = ref.shape[-1] // 2

    def view(zz, half, xx, part):
        return ref.at[zz, half, xx, :, pl.ds(part * w, w)]

    return view


def sems(n):
    return [pltpu.SemaphoreType.DMA((n,)), pltpu.SemaphoreType.DMA((n,))]


def params(cid, limit=56 << 20):
    return pltpu.CompilerParams(collective_id=cid, has_side_effects=True, vmem_limit_bytes=limit)


ANY = pl.BlockSpec(memory_space=pl.ANY)
INV = pl.BlockSpec(memory_space=pltpu.VMEM)
INS = pl.BlockSpec(memory_space=pltpu.SMEM)
PLANE = ("xu", "xd", "zu", "zd")
RING = ("yu", "yd", "c")


class Ticks:
    def __init__(self, *steps):
        self.steps = list(steps)

    def tick(self, count=1):
        for _ in range(count):
            for one in self.steps:
                next(one, None)


def weight_gather(net, weight, out, local):
    z, yh, x = net.z, net.yh, net.x
    n, w = weight.shape[0], weight.shape[1] // 2
    k = net.slot()

    def half(which):
        return weight.at[:, pl.ds(pl.multiple_of(which * w, 128), w)]

    mine = pltpu.make_async_copy(half(yh), out.at[z, yh, x, pl.ds(0, n)], local)
    mine.start()
    net.send(half(1 - yh), out.at[z, yh, x, pl.ds(0, n)], k, "yo")
    yield
    mine.wait()
    net.got(out.at[z, 1 - yh, x, pl.ds(0, n)], k)
    yield from plane_gather(net, column_view(out))


def splat(row, lane, at):
    return jnp.sum(jnp.where(lane == at, row, 0.0), axis=1, keepdims=True)


def place_of(segs, parents, block):
    lane = lax.broadcasted_iota(jnp.int32, (1, 128), 1)
    seg = splat(segs, lane, block)
    lanes = lane.astype(F32)
    parent = splat(parents, lanes, seg)
    trunk = splat(parents, lanes, parent)
    leaf = (seg >= 10.0).astype(F32)
    branch = (seg >= 2.0).astype(F32)
    above = [(splat(segs, lane, b) == parent).astype(F32) * leaf for b in range(16, 32)]
    return trunk, leaf, branch, above


def wide(value):
    return jnp.broadcast_to(value, (1, 128)).astype(BF16)


def trunk_block(kv, which, i, trunk):
    one = wide(trunk)
    return kv[which, 0, i // 4, i % 4] * (1 - one) + kv[which, 1, i // 4, i % 4] * one


def parent_block(kv, which, above):
    total = kv[which, 2, 0, 0] * wide(above[0])
    for j in range(1, 16):
        total = total + kv[which, 2 + j // 8, j // 4 % 2, j % 4] * wide(above[j])
    return total


NT = (((1,), (1,)), ((), ()))
TN = (((0,), (0,)), ((), ()))
SCALE = 128**-0.5


def attend(b, z, x, q, kv, segs, parents, scores, o, log_sum):
    lane = (lax.broadcasted_iota(jnp.int32, (256, 512), 1) & 255).astype(F32)
    row = lax.broadcasted_iota(jnp.int32, (256, 512), 0).astype(F32)
    block = z * 8 + b * 4 + x
    trunk, leaf, branch, above = place_of(segs, parents, block)
    rows = pl.ds(b * 256, 256)
    both = jnp.concatenate([q[rows, :128], q[rows, 128:]], axis=0)
    start = block.astype(F32) - 8.0 * trunk

    def score(key):
        return lax.dot_general(key, both, NT, preferred_element_type=F32) * SCALE

    def trunk_score(i, top):
        gap = (start - i.astype(F32)) * 256.0
        s = jnp.where(row - lane <= gap, score(trunk_block(kv, 0, i, trunk)), NEG)
        scores[i] = s
        return jnp.maximum(top, jnp.max(s, axis=0, keepdims=True))

    top = lax.fori_loop(0, 8, trunk_score, jnp.full((1, 512), NEG, F32))
    s = score(parent_block(kv, 0, above)) + (leaf - 1.0) * 1e30
    scores[8] = s
    top = jnp.maximum(top, jnp.max(s, axis=0, keepdims=True))
    s = jnp.where(row <= lane, score(kv[0, z, b, x]), NEG) + (branch - 1.0) * 1e30
    scores[9] = s
    top = jnp.maximum(top, jnp.max(s, axis=0, keepdims=True))

    def weigh(i, value, carry):
        acc, total = carry
        w = jnp.exp(scores[i] - top)
        acc = acc + lax.dot_general(value, w.astype(BF16), TN, preferred_element_type=F32)
        return acc, total + jnp.sum(w, axis=0, keepdims=True)

    carry = (jnp.zeros((128, 512), F32), jnp.zeros((1, 512), F32))
    carry = lax.fori_loop(0, 8, lambda i, c: weigh(i, trunk_block(kv, 1, i, trunk), c), carry)
    carry = weigh(8, parent_block(kv, 1, above), carry)
    acc, total = weigh(9, kv[1, z, b, x], carry)
    heads = (acc / total).T.astype(BF16)
    o[rows, :128] = heads[:256]
    o[rows, 128:] = heads[256:]
    log_sum[b] = jnp.broadcast_to(top + jnp.log(total), (8, 512))
    return top


def forward(tokens, cotangent, pack, biases, parents, w_query, w_out, w_up, w_down):
    def kernel(tok, cot, pack, biases, parents, wq_in, wo_in, wu_in, wd_in,
               cot_out, h2, wu, wd, wq_out, wo_out, pack_out, h1_out, q_out, kv_out, o, log_sum, x1, best, vec, ub,
               tok_all, h1, packs, wq, wo, q, kv, scores, part, own, mine, got, local, *rest):
        *scratch, ss, rs = rest
        net = Net(ss, rs)
        z, yh, x, yl, c, y = net.z, net.yh, net.x, net.yl, net.c, net.y
        starts = [
            pltpu.make_async_copy(src, dst, local.at[i])
            for i, (src, dst) in enumerate(
                (
                    (tok, tok_all.at[y, c]),
                    (cot, cot_out.at[y, c]),
                    (pack.at[c], packs.at[z, yh, x, yl, c]),
                    (biases.at[yh], wq.at[z, yh, x, pl.ds(64, 16)]),
                )
            )
        ]
        for one in starts:
            one.start()
        net.barrier(PLANE + RING + ("yo",))

        def parameters():
            k = [net.slot() for _ in range(4)]
            pair = packs.at[z, yh, x, yl]
            net.send(pack.at[1 - c], packs.at[z, yh, x, yl, c], k[0], "c")
            yield
            starts[2].wait()
            net.got(packs.at[z, yh, x, yl, 1 - c], k[0])
            for i, name in enumerate(("yu", "yd", "yo")):
                net.send(pair, pair, k[1 + i], name)
            yield
            for i, d in enumerate((net.yd, net.yu, net.yo)):
                net.got(packs.at[z, d // 2, x, lax.rem(d, 2)], k[1 + i])

            def view(zz, half, xx, part):
                return packs.at[zz, part, xx, pl.ds(0, 2) if half == BOTH else half]

            yield from plane_gather(net, view)

        def bias():
            k = net.slot()
            there = wq.at[z, yh, x, pl.ds(64, 16)]
            net.send(biases.at[1 - yh], there, k, "yo")
            yield
            starts[3].wait()
            net.got(wq.at[z, 1 - yh, x, pl.ds(64, 16)], k)

        def query():
            steps = weight_gather(net, wq_in, wq, local.at[4])
            next(steps)
            yield from bias()
            yield from steps

        later = Ticks(
            weight_gather(net, wo_in, wo, local.at[5]),
            weight_gather(net, wu_in, wu, local.at[6]),
            weight_gather(net, wd_in, wd, local.at[7]),
        )

        def start_later():
            yield
            later.tick()

        run_all(group_gather(net, tok, tok_all), parameters(), query(), start_later())
        starts[0].wait()
        later.tick()

        lane = lax.broadcasted_iota(jnp.int32, (16, 128), 1)
        values = jnp.zeros((16, 128), F32)
        segs = jnp.zeros((16, 128), F32)
        for j in range(16):
            block = jnp.zeros((16, 128), F32)
            for k in range(8):
                dev = 8 * j + k
                dp, tp = dev // 4, dev % 4
                tile = packs[dp // 8, dp // 4 % 2, dp % 4, tp // 2, tp % 2, 16:32].astype(F32)
                block = jnp.where(lane // 16 == k, tile, block)
                values = jnp.where(lane == dev, tile, values)
                if tp == 0:
                    segs = jnp.where(lane == dp, tile, segs)
            vec[:, j * 128 : (j + 1) * 128] = block
        value_bias = values[6:7]
        segs = segs[7:8]
        vec[8:9, 0:128] = segs
        query_bias = jnp.zeros((16, 256), F32)
        lane = lax.broadcasted_iota(jnp.int32, (16, 256), 1) & 127
        for dp in range(32):
            tile = wq[dp // 8, dp // 4 % 2, dp % 4, 64:80].astype(F32)
            query_bias = jnp.where(lane // 4 == dp, tile, query_bias)
        ub[...] = query_bias[:8, 128:]
        query_bias = jnp.concatenate([query_bias[0:1, :128], query_bias[1:2, :128]], axis=1)

        gain1, shift1 = vec[0:1], vec[1:2]

        def norm_rows(i, carry):
            rows = tok_all[i // 2, i % 2].astype(F32)
            h1[pl.ds(pl.multiple_of(i * 64, 64), 64)] = (normed(rows)[0] * gain1 + shift1).astype(BF16)
            return carry

        lax.fori_loop(0, 8, norm_rows, 0)

        def project(i, carry):
            rows = pl.ds(pl.multiple_of(i * 256, 256), 256)
            h = h1[rows]
            weight = wq[:, :, :, :64].reshape(2048, 256)
            q[rows] = (jnp.dot(h, weight, preferred_element_type=F32) + query_bias).astype(BF16)
            weight = packs[:, :, :, :, :, :16].reshape(2048, 128)
            shift = value_bias * c.astype(F32)
            kv[c, z, i, x] = (jnp.dot(h, weight, preferred_element_type=F32) + shift).astype(BF16)
            return carry

        lax.fori_loop(0, 2, project, 0)

        def view(zz, half, xx, part):
            rows = pl.ds(0, 256) if half == BOTH else pl.ds(128 * half, 128)
            return kv.at[c, zz, part, xx, rows]

        keys = plane_gather(net, view)
        cots = group_gather(net, cot, cot_out)
        next(keys)
        later.tick()
        next(cots)
        next(keys)
        next(keys)
        next(cots)
        next(keys)
        later.tick()
        for _ in keys:
            pass
        k = net.slot()
        net.send(kv.at[c], kv.at[c], k, "c")
        next(cots)
        net.got(kv.at[1 - c], k)

        saves = [
            pltpu.make_async_copy(src, dst, local.at[8 + i])
            for i, (src, dst) in enumerate(
                ((wq, wq_out), (packs, pack_out), (h1, h1_out), (q, q_out), (kv, kv_out), (wo, wo_out))
            )
        ]
        for one in saves[:5]:
            one.start()
        parent = parents[0:1]
        top = attend(0, z, x, q, kv, segs, parent, scores, o, log_sum)
        next(later.steps[0], None)
        top = jnp.maximum(top, attend(1, z, x, q, kv, segs, parent, scores, o, log_sum))
        for h in range(2):
            mine[0, 8 * h : 8 * h + 8] = jnp.full((8, 128), jnp.max(top[:, h * 256 : (h + 1) * 256]), F32)
        for _ in later.steps[0]:
            pass
        saves[5].start()
        later.tick()

        def project_out(i, d):
            rows = o[pl.ds(pl.multiple_of(d * 128, 128), 128)]
            for j in range(4):
                weight = wo[j].reshape(512, 256)
                out = lax.dot_general(rows, weight, NT, preferred_element_type=F32).astype(BF16)
                part[d, 0, :, j * 512 : (j + 1) * 512] = out[:64]
                part[d, 1, :, j * 512 : (j + 1) * 512] = out[64:]

        def rows():
            def total(summed):
                value = tok[...].astype(F32) + (summed + vec[4:5])
                x1[...] = value
                own[...] = (normed(value)[0] * vec[2:3] + vec[3:4]).astype(BF16)

            yield from group_scatter(net, part, *scratch, total, project_out)
            me = pltpu.make_async_copy(own, h2.at[y, c], local.at[14])
            me.start()
            yield from group_gather(net, own, h2)
            me.wait()

        run_all(rows(), heads_max(net, mine, got, best))
        for _ in cots:
            pass
        later.tick()
        starts[1].wait()
        for one in saves:
            one.wait()
        net.finish()

    n, d = tokens.shape
    rows = jax.ShapeDtypeStruct((4, 2, n, d), BF16)

    def bf(*shape):
        return jax.ShapeDtypeStruct(shape, BF16)

    def f32(*shape):
        return jax.ShapeDtypeStruct(shape, F32)

    return pl.pallas_call(
        kernel,
        out_shape=(
            rows,
            rows,
            bf(4, 2, 4, n, 1024),
            bf(4, 2, 4, n, 1024),
            bf(4, 2, 4, 80, 256),
            bf(4, 2, 4, n, 256),
            bf(4, 2, 4, 2, 2, 32, 128),
            bf(512, d),
            bf(512, 256),
            bf(2, 4, 2, 4, 256, 128),
            bf(512, 256),
            f32(2, 8, 512),
            f32(n, d),
            f32(2, 16, 128),
            f32(16, d),
            f32(8, 128),
        ),
        in_specs=[INV, ANY, INV, INV, INV, ANY, ANY, ANY, ANY],
        out_specs=(ANY,) * 10 + (INV,) * 6,
        scratch_shapes=[
            VMEM((4, 2, n, d), BF16),
            VMEM((512, d), BF16),
            VMEM((4, 2, 4, 2, 2, 32, 128), BF16),
            VMEM((4, 2, 4, 80, 256), BF16),
            VMEM((4, 2, 4, n, 256), BF16),
            VMEM((512, 256), BF16),
            VMEM((2, 4, 2, 4, 256, 128), BF16),
            VMEM((10, 256, 512), F32),
            VMEM((4, 2, n, d), BF16),
            VMEM((n, d), BF16),
            VMEM((5, 16, 128), F32),
            VMEM((7, 16, 128), F32),
            pltpu.SemaphoreType.DMA((15,)),
        ]
        + scatter_scratch(n, d)
        + sems(160),
        compiler_params=params(1),
        name="forward",
    )(tokens, cotangent, pack, biases, parents, w_query, w_out, w_up, w_down)


def normed(values):
    centred = values - jnp.mean(values, axis=-1, keepdims=True)
    inverse = lax.rsqrt(jnp.mean(centred * centred, axis=-1, keepdims=True) + EPS)
    return centred * inverse, inverse


def norm_back(grad, norm, inverse, gain):
    scaled = grad * gain
    return inverse * (
        scaled
        - jnp.mean(scaled, axis=-1, keepdims=True)
        - norm * jnp.mean(scaled * norm, axis=-1, keepdims=True)
    )


def heads_max(net, mine, got, best):
    for i, (up, down) in enumerate((("xu", "xd"), ("zu", "zd"))):
        k = [net.slot() for _ in range(3)]
        a, b, d = got.at[3 * i], got.at[3 * i + 1], got.at[3 * i + 2]
        net.send(mine.at[2 * i], a, k[0], up)
        net.send(mine.at[2 * i], b, k[1], down)
        yield
        net.got(a, k[0])
        net.got(b, k[1])
        mine[2 * i + 1] = jnp.maximum(mine[2 * i], jnp.maximum(a[...], b[...]))
        net.send(mine.at[2 * i + 1], d, k[2], up)
        yield
        net.got(d, k[2])
        mine[2 * i + 2] = jnp.maximum(mine[2 * i + 1], d[...])
    k = net.slot()
    net.send(mine.at[4], got.at[6], k, "yo")
    yield
    net.got(got.at[6], k)
    best[net.yh] = mine[4]
    best[1 - net.yh] = got[6]


def weight_scatter(net, g, tmp, out):
    z, yh, x = net.z, net.yh, net.x
    w = g.shape[-1]
    k = net.slot()
    yield from plane_scatter(net, column_view(g), tmp)
    mine = out.at[:, pl.ds(pl.multiple_of(yh * w, 128), w)]
    net.send(g.at[z, 1 - yh, x], mine, k, "yo")
    out[:, pl.ds(pl.multiple_of(yh * w, 128), w)] = g[z, yh, x]
    yield
    net.got(out.at[:, pl.ds(pl.multiple_of((1 - yh) * w, 128), w)], k)


def smooth_gate(u):
    scale = 0.7978845608028654
    square = u * u
    t = jnp.tanh(scale * u * (1.0 + 0.044715 * square))
    half = 0.5 * (1.0 + t)
    slope = half + 0.5 * u * (1.0 - t * t) * scale * (1.0 + 0.134145 * square)
    return u * half, slope


def piece(ref, which, zz, yy, xx):
    return jnp.concatenate(
        [ref[zz, yy, xx, :, (which * 4 + r) * 128 : (which * 4 + r + 1) * 128] for r in range(4)], axis=0
    )


def put_piece(ref, which, zz, yy, xx, value):
    for r in range(4):
        ref[zz, yy, xx, :, (which * 4 + r) * 128 : (which * 4 + r + 1) * 128] = value[r * 64 : (r + 1) * 64]


def attend_back(z, x, q, kv, o, go, log_sum, segs, parents, grad, lone, dq_sum, dq):
    lane = (lax.broadcasted_iota(jnp.int32, (256, 512), 1) & 255).astype(F32)
    row = lax.broadcasted_iota(jnp.int32, (256, 512), 0).astype(F32)
    places = [place_of(segs, parents, z * 8 + b * 4 + x) for b in range(2)]

    def stacked(ref, b):
        return jnp.concatenate([ref[b * 256 : b * 256 + 256, :128], ref[b * 256 : b * 256 + 256, 128:]], axis=0)

    logs, inner = [], []
    for b in range(2):
        logs.append(log_sum[b, 0:1])
        inner.append(
            jnp.sum((stacked(go, b).astype(F32) * stacked(o, b).astype(F32)).T, axis=0, keepdims=True)
        )

    def one(b, key, value, masked, first):
        both, up = stacked(q, b), stacked(go, b)
        s = masked(lax.dot_general(key, both, NT, preferred_element_type=F32) * SCALE)
        p = jnp.exp(s - logs[b])
        dp = lax.dot_general(value, up, NT, preferred_element_type=F32)
        ds = (p * (dp - inner[b])).astype(BF16)
        more = lax.dot_general(key, ds, TN, preferred_element_type=F32)
        dq_sum[b] = more if first else dq_sum[b] + more
        dk = jnp.dot(ds, both, preferred_element_type=F32) * SCALE
        dv = jnp.dot(p.astype(BF16), up, preferred_element_type=F32)
        return dk.astype(BF16), dv.astype(BF16)

    for b in range(2):
        trunk, leaf, branch, above = places[b]
        lone[b, 0, 0], lone[b, 0, 1] = one(
            b,
            piece(kv, 0, z, b, x),
            piece(kv, 1, z, b, x),
            lambda s: jnp.where(row <= lane, s, NEG) + (branch - 1.0) * 1e30,
            True,
        )
        key, value = (
            sum(piece(kv, w, 2 + j // 8, j // 4 % 2, j % 4) * wide(above[j]) for j in range(16)) for w in range(2)
        )
        lone[b, 1, 0], lone[b, 1, 1] = one(b, key, value, lambda s: s + (leaf - 1.0) * 1e30, False)
    yield

    for j in range(16):
        own = [
            wide((z * 8 + b * 4 + x == 16 + j).astype(F32) * jnp.ones((1, 1), F32)) for b in range(2)
        ]
        for w in range(2):
            value = sum(lone[b, 0, w] * own[b] + lone[b, 1, w] * wide(places[b][3][j]) for b in range(2))
            put_piece(grad, w, 2 + j // 8, j // 4 % 2, j % 4, value)

    def trunk_one(i, carry):
        yy, xx = i // 4, i % 4
        totals = None
        for b in range(2):
            trunk = places[b][0]
            second = wide(trunk)
            first = 1 - second
            key, value = (piece(kv, w, 0, yy, xx) * first + piece(kv, w, 1, yy, xx) * second for w in range(2))
            start = (z * 8 + b * 4 + x).astype(F32) - 8.0 * trunk
            gap = (start - i.astype(F32)) * 256.0
            dk, dv = one(b, key, value, lambda s: jnp.where(row - lane <= gap, s, NEG), False)
            parts = [dk * first, dv * first, dk * second, dv * second]
            totals = parts if totals is None else [t + p for t, p in zip(totals, parts)]
        for t in range(2):
            for w in range(2):
                put_piece(grad, w, t, yy, xx, totals[2 * t + w])
        return carry

    lax.fori_loop(0, 4, trunk_one, 0)
    yield
    lax.fori_loop(4, 8, trunk_one, 0)
    for b in range(2):
        rows = (dq_sum[b] * SCALE).T.astype(BF16)
        dq[b * 256 : b * 256 + 256, :128] = rows[:256]
        dq[b * 256 : b * 256 + 256, 128:] = rows[256:]


def spread(net, names, src, dst, k):
    for i, name in enumerate(names):
        net.send(src, dst.at[i], k[i], name)


def all_sums(net, mine, near, far):
    k = [net.slot() for _ in range(6)]
    spread(net, ("xu", "xd", "xo"), mine.at[0], near, k)
    yield
    for i in range(3):
        net.got(near.at[i], k[i])
    mine[1] = mine[0] + near[0] + near[1] + near[2]
    spread(net, ("zu", "zd", "zo"), mine.at[1], far, k[3:])
    yield
    for i in range(3):
        net.got(far.at[i], k[3 + i])
    mine[2] = mine[1] + far[0] + far[1] + far[2]


def backward(tokens, cotangent, parents, cot_all, h2, wu, wd, wq, wo, packs, h1, q, kv, o, log_sum, x1, vec, ub):
    def kernel(tok, cot, parents, cot_in, h2_in, wu_in, wd_in, wq_in, wo_in, packs_in, h1_in, q, kv_in, o, log_sum,
               x1, vec, ub_in,
               output, grad_input, up_out, down_out, wo_out, wq_out, vec_out, bias_out, kv_out, vb_out,
               h2, cots, wu, wd, wq, wo, packs, adu, us, das, part, part_mlp, gu, gd, gwo, gq, own, dz, dx1, sums, go,
               lone, dq_sum, dq, dkv_from, dkv, gkv, gkv_z, gkv_x, bias, bias_x, bias_z, vecs, vec_z, vec_x,
               local, *rest):
        *scratch, ss, rs = rest
        first, second, tmp_u, tmp_d, tmp_o, tmp_q, tmp_k = (
            scratch[:3],
            scratch[3:6],
            scratch[6:14],
            scratch[14:22],
            scratch[22:30],
            scratch[30:38],
            scratch[38:46],
        )
        net = Net(ss, rs)
        z, yh, x, yl, c, y = net.z, net.yh, net.x, net.yl, net.c, net.y

        def columns(ref, j):
            return ref.at[:, :, :, :, pl.ds(j * 256, 256)]

        def load(src, dst, i):
            one = pltpu.make_async_copy(src, dst, local.at[i])
            one.start()
            return one

        load(h2_in, h2, 0)
        load(columns(wu_in, 0), columns(wu, 0), 2)
        load(cot_in, cots, 1)
        load(columns(wd_in, 0), columns(wd, 0), 6)
        for j in range(1, 4):
            load(columns(wu_in, j), columns(wu, j), 2 + j)
            load(columns(wd_in, j), columns(wd, j), 6 + j)
        loads = [load(wo_in, wo, 10), load(wq_in.at[:, :, :, pl.ds(0, 64)], wq, 11)]
        loads.append(load(packs_in.at[:, :, :, :, :, pl.ds(0, 16)], packs, 12))
        net.barrier(PLANE + RING + ("yo", "xo", "zo"))
        pltpu.make_async_copy(h2_in, h2, local.at[0]).wait()
        pltpu.make_async_copy(cot_in, cots, local.at[1]).wait()

        def hidden(j, carry):
            at = pl.ds(pl.multiple_of(j * 256, 256), 256)
            there = pl.ds(0, 4), pl.ds(0, 2), pl.ds(0, 4), pl.ds(0, 64), at
            pltpu.make_async_copy(wu_in.at[there], wu.at[there], local.at[2 + j]).wait()
            us[...] = jnp.dot(
                h2[...].reshape(512, 2048), wu[there].reshape(2048, 256), preferred_element_type=F32
            )
            pltpu.make_async_copy(wd_in.at[there], wd.at[there], local.at[6 + j]).wait()
            das[...] = jnp.dot(
                cots[...].reshape(512, 2048), wd[there].reshape(2048, 256), preferred_element_type=F32
            )
            bias_row = jnp.concatenate([ub_in[pl.ds(2 * j, 1)], ub_in[pl.ds(2 * j + 1, 1)]], axis=1)

            def gate(i, total):
                rows = pl.ds(pl.multiple_of(i * 64, 64), 64)
                value, slope = smooth_gate(us[rows] + bias_row)
                adu[0, rows, at] = value.astype(BF16)
                du = (das[rows] * slope).astype(BF16)
                adu[1, rows, at] = du
                return total + jnp.sum(du.astype(F32), axis=0, keepdims=True)

            total = lax.fori_loop(0, 8, gate, jnp.zeros((1, 256), F32))
            bias[0, pl.ds(2 * j, 1)] = total[:, :128]
            bias[0, pl.ds(2 * j + 1, 1)] = total[:, 128:]
            return carry

        lax.fori_loop(0, 4, hidden, 0)

        def projected(dst, d, rows, weight):
            def column(j, carry):
                out = lax.dot_general(rows, weight(j), NT, preferred_element_type=F32).astype(BF16)
                at = pl.ds(pl.multiple_of(j * 512, 512), 512)
                dst[d, 0, :, at] = out[:64]
                dst[d, 1, :, at] = out[64:]
                return carry

            lax.fori_loop(0, 4, column, 0)

        def ring_rows(d):
            return pl.ds(pl.multiple_of(d * 128, 128), 128)

        def make_two(i, d):
            projected(part, d, adu[1, ring_rows(d)], lambda j: wu[j].reshape(512, 1024))

        def total_two(summed):
            norm, inverse = normed(x1[...])
            grad = cot[...].astype(F32) + norm_back(summed, norm, inverse, vec[2:3])
            dx1[...] = grad
            rounded = grad.astype(BF16)
            own[...] = rounded
            values = (summed * norm, summed, rounded.astype(F32), cot[...].astype(F32))
            for i, v in enumerate(values):
                sums[2 + i : 3 + i] = jnp.sum(v, axis=0, keepdims=True)

        def outer(dst, left, right):
            def block(j, carry):
                out = lax.dot_general(left(j), right, TN, preferred_element_type=F32)
                dst[j] = out.astype(BF16).reshape(2, 4, 64, right.shape[1])
                return carry

            lax.fori_loop(0, 4, block, 0)

        def wide_outer(dst, left, which):
            def block(i, carry):
                j, w = i // 2, i % 2
                at = pl.ds(pl.multiple_of(w * 512, 512), 512)
                out = lax.dot_general(
                    left[:, :, :, pl.ds(pl.multiple_of(j * 512, 512), 512)].reshape(512, 512),
                    adu[which, :, at],
                    TN,
                    preferred_element_type=F32,
                )
                dst[j, :, :, :, at] = out.astype(BF16).reshape(2, 4, 64, 512)
                return carry

            lax.fori_loop(0, 8, block, 0)

        rows_two = group_scatter(net, part, *first, total_two, make_two)
        next(rows_two)
        wide_outer(gd, cots, 0)
        down = weight_scatter(net, gd, tmp_d, down_out)
        next(down)
        next(rows_two)
        wide_outer(gu, h2, 1)
        up = weight_scatter(net, gu, tmp_u, up_out)
        next(up)
        next(rows_two)
        for d in range(4):
            projected(part_mlp, d, adu[0, d * 128 : d * 128 + 128], lambda j: wd[j].reshape(512, 1024))
        keep = [
            load(kv_in.at[w, :, :, :, pl.ds(r * 64, 64)], wd.at[:, :, :, :, pl.ds((w * 4 + r) * 128, 128)], 13 + 4 * w + r)
            for w in range(2)
            for r in range(4)
        ]
        next(rows_two)
        next(rows_two, None)
        me = load(own, dz.at[y, c], 23)
        spreading = group_gather(net, own, dz)
        next(spreading)
        late = [load(h1_in.at[:, pl.ds(w * 1024, 1024)], adu.at[w], 21 + w) for w in range(2)]
        next(spreading)
        next(down)
        next(spreading)
        next(up)
        for _ in spreading:
            pass
        me.wait()
        loads[0].wait()
        go[...] = jnp.dot(
            dz[...].reshape(512, 2048), wo[...].reshape(2048, 256), preferred_element_type=F32
        ).astype(BF16)

        def total_out(summed):
            output[...] = (x1[...] + (summed + vec[5:6])).astype(BF16)

        rows_out = group_scatter(net, part_mlp, *second, total_out)
        next(rows_out)
        for one in keep:
            one.wait()
        steps = attend_back(z, x, q, wd, o, go, log_sum, vec[8:9, 0:128], parents[0:1], wu, lone, dq_sum, dq)
        next(steps)
        next(rows_out)
        next(steps)
        next(rows_out)
        next(down)
        next(up)
        next(steps, None)
        next(rows_out)
        next(rows_out, None)

        kc = [net.slot() for _ in range(4)]
        theirs = pl.ds(pl.multiple_of((1 - c) * 512, 512), 512)
        for i in range(4):
            net.send(wu.at[:, :, i, :, theirs], cots.at[:, :, :, pl.ds(i * 512, 512)], kc[i], "c")
        for one in loads[1:] + late:
            one.wait()

        def make_one(i, d):
            if i == 3:
                lower = lax.dot_general(
                    dkv[y], packs[...].reshape(2048, 128), NT, preferred_element_type=F32
                )
                upper = lax.dot_general(
                    dq[ring_rows(d)], wq[...].reshape(2048, 256), NT, preferred_element_type=F32
                )
                out = (lower + upper).astype(BF16)
                h2[d, 0] = out[:64]
                h2[d, 1] = out[64:]
            else:
                projected(h2, d, dq[ring_rows(d)], lambda j: wq[j].reshape(512, 256))

        def total_one(summed):
            norm, inverse = normed(tok[...].astype(F32))
            grad_input[...] = dx1[...] + norm_back(summed, norm, inverse, vec[0:1])
            sums[0:1] = jnp.sum(summed * norm, axis=0, keepdims=True)
            sums[1:2] = jnp.sum(summed, axis=0, keepdims=True)
            sums[6:8] = jnp.zeros((2, 2048), F32)
            vecs[y, c] = sums[...]

        rows_one = group_scatter(net, h2, *first, total_one, make_one)
        next(rows_one)
        ours = pl.ds(pl.multiple_of(c * 512, 512), 512)
        for i in range(4):
            net.got(cots.at[:, :, :, pl.ds(i * 512, 512)], kc[i])

            def core_sum(j, carry):
                zz, yy = j // 2, j % 2
                wu[zz, yy, i, :, ours] = wu[zz, yy, i, :, ours] + cots[zz, yy, :, i * 512 : i * 512 + 512]
                return carry

            lax.fori_loop(0, 8, core_sum, 0)

        def view(zz, half, xx, part):
            at = ours if half == BOTH else pl.ds(pl.multiple_of(c * 512 + 256 * half, 256), 256)
            return wu.at[zz, part, xx, :, at]

        keys = plane_scatter(net, view, tmp_k)
        next(keys)
        next(rows_one)
        outer(gq, lambda j: adu[j // 2, :, pl.ds(pl.multiple_of((j % 2) * 512, 512), 512)], dq[...])
        bias[0, 8:9] = jnp.sum(dq[:, :128].astype(F32), axis=0, keepdims=True)
        bias[0, 9:10] = jnp.sum(dq[:, 128:].astype(F32), axis=0, keepdims=True)
        bias[0, 10:16] = jnp.zeros((6, 128), F32)
        next(keys)
        query = weight_scatter(net, gq, tmp_q, wq_out)
        next(query)
        small = all_sums(net, bias, bias_x, bias_z)
        next(small)
        next(rows_one)
        outer(gwo, lambda j: dz[:, :, :, pl.ds(pl.multiple_of(j * 512, 512), 512)].reshape(512, 512), o[...])
        next(keys)
        project = weight_scatter(net, gwo, tmp_o, wo_out)
        next(project)
        next(down)
        next(up)
        next(query)
        next(small)
        next(keys)
        next(project)
        for _ in keys:
            pass

        def ring_piece(ref, d):
            at = pl.ds(pl.multiple_of(c * 512 + lax.rem(d, 2) * 256, 256), 256)
            return ref.at[z, d // 2, x, :, at]

        kr = [net.slot() for _ in range(7)]
        for i, (name, d) in enumerate((("yu", net.yu), ("yd", net.yd), ("yo", net.yo))):
            net.send(ring_piece(wu, d), dkv_from.at[i], kr[i], name)
        next(query)
        next(project)
        for i in range(3):
            net.got(dkv_from.at[i], kr[i])
        mine = ring_piece(wu, y)[...].astype(F32)
        for i in range(3):
            mine = mine + dkv_from[i].astype(F32)
        mine = mine.astype(BF16)
        dkv[y] = jnp.concatenate([mine[:, :128], mine[:, 128:]], axis=0)
        for i, name in enumerate(("yu", "yd", "yo")):
            net.send(dkv.at[y], dkv.at[y], kr[3 + i], name)
        next(rows_one)
        next(down)
        next(up)
        next(small, None)
        for i, d in enumerate((net.yd, net.yu, net.yo)):
            net.got(dkv.at[d], kr[3 + i])

        every = dkv[...].reshape(512, 128)
        value_sum = jnp.broadcast_to(jnp.sum(every.astype(F32), axis=0, keepdims=True), (8, 128))
        for j in range(4):
            at = pl.ds(pl.multiple_of((j % 2) * 512 + yh * 256, 256), 256)
            out = lax.dot_general(adu[j // 2, :, at], every, TN, preferred_element_type=F32).reshape(4, 2, 32, 128)
            for i in range(4):
                gkv[j, i, 0:32] = jnp.where(yl == 0, out[i, 0], out[i, 1])
                gkv[j, i, 32:40] = value_sum

        def key_value():
            k = [net.slot() for _ in range(7)]
            for i, (name, d) in enumerate((("zu", net.zu), ("zd", net.zd), ("zo", net.zo))):
                net.send(gkv.at[d], gkv_z.at[i], k[i], name)
            yield
            for i in range(3):
                net.got(gkv_z.at[i], k[i])
            for i in range(4):
                gkv_x[i] = gkv[z, i] + gkv_z[0, i] + gkv_z[1, i] + gkv_z[2, i]
            for i, (name, d) in enumerate((("xu", net.xu), ("xd", net.xd), ("xo", net.xo))):
                net.send(gkv_x.at[d], gkv_x.at[4 + i], k[3 + i], name)
            yield
            for i in range(3):
                net.got(gkv_x.at[4 + i], k[3 + i])
            total = gkv_x[x] + gkv_x[4] + gkv_x[5] + gkv_x[6]
            gkv_x[7, 0:16] = jnp.where(c == 0, total[0:16], total[16:32])
            gkv_x[7, 16:32] = jnp.where(c == 0, total[16:32], total[0:16])
            gkv_x[7, 32:40] = total[32:40]
            net.send(gkv_x.at[7, pl.ds(16, 24)], gkv_x.at[8, pl.ds(16, 24)], k[6], "c")
            yield
            net.got(gkv_x.at[8, pl.ds(16, 24)], k[6])
            here, there = gkv_x[7, 0:16], gkv_x[8, 16:32]
            kv_out[:, 0:128] = jnp.where(c == 0, here, there)
            kv_out[:, 128:256] = jnp.where(c == 0, there, here)
            vb_out[...] = jnp.where(c == 0, gkv_x[8, 32:40], gkv_x[7, 32:40])

        def vectors():
            k = [net.slot() for _ in range(13)]
            at = vecs.at[y, c]
            for i, name in enumerate(("yu", "yd", "yo", "c")):
                net.send(at, at, k[i], name)
            yield
            for i, d in enumerate((net.yd, net.yu, net.yo)):
                net.got(vecs.at[d, c], k[i])
                net.send(vecs.at[d, c], vecs.at[d, c], k[4 + i], "c")
            yield
            for i, d in enumerate((y, net.yd, net.yu, net.yo)):
                net.got(vecs.at[d, 1 - c], k[3 + i])
            acc = vecs[0, 0]
            for i in range(1, 8):
                acc = acc + vecs[i // 2, i % 2]
            for i in range(4):
                vec_z[i] = acc[:, i * 512 : (i + 1) * 512]
            for i, (name, d) in enumerate((("zu", net.zu), ("zd", net.zd), ("zo", net.zo))):
                net.send(vec_z.at[d], vec_z.at[4 + i], k[7 + i], name)
            yield
            for i in range(3):
                net.got(vec_z.at[4 + i], k[7 + i])
            acc = vec_z[z] + vec_z[4] + vec_z[5] + vec_z[6]
            vec_x[0] = jnp.where(yh == 0, acc[:, :256], acc[:, 256:])
            spread(net, ("xu", "xd", "xo"), vec_x.at[0], vec_x.at[pl.ds(1, 3)], k[10:])
            yield
            for i in range(3):
                net.got(vec_x.at[1 + i], k[10 + i])
            vec_out[...] = vec_x[0] + vec_x[1] + vec_x[2] + vec_x[3]

        def partner_bias():
            k = net.slot()
            net.send(bias.at[2], bias_out.at[1], k, "yo")
            bias_out[0] = bias[2]
            yield
            net.got(bias_out.at[1], k)

        last = key_value()
        next(last)
        next(rows_one, None)
        run_all(vectors(), last, partner_bias(), query, project, down, up)
        net.finish()

    n, d = tokens.shape

    def bf(*shape):
        return jax.ShapeDtypeStruct(shape, BF16)

    def f32(*shape):
        return jax.ShapeDtypeStruct(shape, F32)

    return pl.pallas_call(
        kernel,
        out_shape=(
            bf(n, d),
            f32(n, d),
            bf(n, d),
            bf(n, d),
            bf(n, 512),
            bf(n, 512),
            f32(8, 256),
            f32(2, 16, 128),
            f32(16, 256),
            f32(8, 128),
        ),
        in_specs=[INV, INV, INV] + [ANY] * 8 + [INV, ANY] + [INV] * 5,
        out_specs=(INV,) * 10,
        scratch_shapes=[
            VMEM((4, 2, n, d), BF16),
            VMEM((4, 2, n, d), BF16),
            VMEM((4, 2, 4, n, 1024), BF16),
            VMEM((4, 2, 4, n, 1024), BF16),
            VMEM((4, 2, 4, n, 256), BF16),
            VMEM((4, 2, 4, n, 256), BF16),
            VMEM((4, 2, 4, 2, 2, 16, 128), BF16),
            VMEM((2, 512, 1024), BF16),
            VMEM((512, 256), F32),
            VMEM((512, 256), F32),
            VMEM((4, 2, n, d), BF16),
            VMEM((4, 2, n, d), BF16),
            VMEM((4, 2, 4, n, 1024), BF16),
            VMEM((4, 2, 4, n, 1024), BF16),
            VMEM((4, 2, 4, n, 256), BF16),
            VMEM((4, 2, 4, n, 256), BF16),
            VMEM((n, d), BF16),
            VMEM((4, 2, n, d), BF16),
            VMEM((n, d), F32),
            VMEM((8, d), F32),
            VMEM((512, 256), BF16),
            VMEM((2, 2, 2, 256, 128), BF16),
            VMEM((2, 128, 512), F32),
            VMEM((512, 256), BF16),
            VMEM((3, 64, 256), BF16),
            VMEM((4, 128, 128), BF16),
            VMEM((4, 4, 40, 128), F32),
            VMEM((3, 4, 40, 128), F32),
            VMEM((9, 40, 128), F32),
            VMEM((3, 16, 128), F32),
            VMEM((3, 16, 128), F32),
            VMEM((3, 16, 128), F32),
            VMEM((4, 2, 8, d), F32),
            VMEM((7, 8, 512), F32),
            VMEM((4, 8, 256), F32),
            pltpu.SemaphoreType.DMA((24,)),
        ]
        + scatter_scratch(n, d)
        + scatter_scratch(n, d)
        + plane_scratch(n, 512)
        + plane_scratch(n, 512)
        + plane_scratch(n, 128)
        + plane_scratch(n, 128)
        + [VMEM(s, BF16) for s in ((2, 4, n, 256), (2, 4, n, 256), (2, 4, n, 512), (2, 4, n, 512))]
        + [VMEM(s, BF16) for s in ((2, n, 256), (2, n, 256), (2, n, 512), (2, n, 512))]
        + sems(200),
        compiler_params=params(2, 62 << 20),
        name="backward",
    )(tokens, cotangent, parents, cot_all, h2, wu, wd, wq, wo, packs, h1, q, kv, o, log_sum, x1, vec, ub)


def local(
    tokens,
    cotangent,
    seg_ids,
    parents,
    tau,
    w_query,
    w_up,
    w_out,
    w_down,
    query_bias,
    up_bias,
    w_keyval,
    value_bias,
    norm1_gain,
    norm1_bias,
    norm2_gain,
    norm2_bias,
    out_bias,
    down_bias,
):
    z, yh, x, yl, c = (lax.axis_index(a) for a in AXES)
    tp = yl * 2 + c
    dp = (z * 2 + yh) * 4 + x

    def row(values):
        return jnp.tile(values.astype(BF16).reshape(1, -1), (1, 128 // values.size))

    tile = [row(v) for v in (norm1_gain, norm1_bias, norm2_gain, norm2_bias, out_bias, down_bias, value_bias, seg_ids[:1])]
    tile = jnp.concatenate(tile + [jnp.zeros((8, 128), BF16)], axis=0)
    pack = jnp.stack([jnp.concatenate([w_keyval[:, :128], tile]), jnp.concatenate([w_keyval[:, 128:], tile])])
    qbt = jnp.pad(jnp.tile(query_bias.T, (1, 32)).reshape(2, 2, 128), ((0, 0), (0, 14), (0, 0)))
    ubt = jnp.pad(jnp.tile(up_bias.T, (1, 32)).reshape(2, 8, 128), ((0, 0), (0, 8), (0, 0)))
    biases = jnp.concatenate([qbt, ubt], axis=2)
    ancestors = jnp.pad(jnp.broadcast_to(parents.astype(F32)[None], (8, 18)), ((0, 0), (0, 110)))
    (cot_all, h2, wu, wd, wq, wo, packs, h1, q, kv, o, log_sum, x1, best, vec, ub) = forward(
        tokens, cotangent, pack, biases, ancestors, w_query, w_out, w_up, w_down
    )
    output, grad_input, up_sum, down_sum, out_sum, query_sum, vec_sum, bias_sum, keyval_sum, vb_sum = backward(
        tokens, cotangent, ancestors, cot_all, h2, wu, wd, wq, wo, packs, h1, q, kv, o, log_sum, x1, vec, ub
    )
    limit = tau[0]
    head_max = best.reshape(4, 8, 128)[:, 0, 0]
    factor = limit / jnp.maximum(head_max, limit)
    clipped_query = (w_query.astype(F32) * jnp.repeat(factor, 128)[None, :]).astype(BF16)
    clipped_bias = (query_bias.astype(F32) * factor[None, :]).astype(BF16)

    own = lax.dynamic_slice(bias_sum, (jnp.int32(0), jnp.int32(0), dp * 4), (2, 10, 4))
    low = jnp.where(yh == 0, own[0], own[1])
    high = jnp.where(yh == 0, own[1], own[0])
    qbias_sum = jnp.concatenate([low[8:10], high[8:10]], axis=0).T
    ubias_sum = jnp.concatenate([low[:8], high[:8]], axis=0).T
    valueb_sum = lax.dynamic_slice(vb_sum, (jnp.int32(0), dp * 4 + tp), (1, 1)).reshape(1)
    vec_sum = lax.dynamic_slice(vec_sum, (jnp.int32(0), x * 64 + tp * 16), (6, 16))
    return (
        output,
        grad_input,
        query_sum.astype(F32),
        up_sum.astype(F32),
        out_sum.astype(F32),
        down_sum.astype(F32),
        qbias_sum,
        ubias_sum,
        keyval_sum,
        valueb_sum,
        vec_sum[0],
        vec_sum[1],
        vec_sum[2],
        vec_sum[3],
        vec_sum[4],
        vec_sum[5],
        clipped_query,
        clipped_bias,
    )


def solution(mesh):
    fine = Mesh(mesh.devices.reshape(4, 2, 4, 2, 2), AXES)
    dp, tp = ("z", "yh", "x"), ("yl", "c")
    rows, flat, weight = P(AXES, None), P(AXES), P(dp, tp)
    in_specs = (rows, rows, P(dp), P(), P()) + (weight,) * 6 + (rows,) + (flat,) * 7
    out_specs = (rows, rows) + (weight,) * 6 + (rows,) + (flat,) * 7 + (weight, weight)
    return jax.shard_map(local, mesh=fine, in_specs=in_specs, out_specs=out_specs, check_vma=False)
```

```python
import itertools

import jax
import jax.numpy as jnp
from jax import lax
from jax.experimental import pallas as pl
from jax.experimental.pallas import tpu as pltpu
from jax.sharding import Mesh, PartitionSpec as P

EPS = 1e-05
AXES = ("z", "yh", "x", "yl", "c")
F32 = jnp.float32
BF16 = jnp.bfloat16
VMEM = pltpu.VMEM
NEG = -1e30


class Net:
    def __init__(self, send_sems, recv_sems):
        self.z, self.yh, self.x, self.yl, self.c = (lax.axis_index(a) for a in AXES)
        self.y = self.yh * 2 + self.yl
        self.yu, self.yo, self.yd = (lax.rem(self.y + s, 4) for s in (1, 2, 3))
        self.xu, self.xo, self.xd = (lax.rem(self.x + s, 4) for s in (1, 2, 3))
        self.zu, self.zo, self.zd = (lax.rem(self.z + s, 4) for s in (1, 2, 3))
        up, down = lax.rem(self.yh + self.yl, 2), lax.rem(self.yh + 1 - self.yl, 2)
        self.dev = {
            "yu": {"yh": up, "yl": 1 - self.yl},
            "yd": {"yh": down, "yl": 1 - self.yl},
            "yo": {"yh": 1 - self.yh},
            "c": {"c": 1 - self.c},
            "xu": {"x": self.xu},
            "xd": {"x": self.xd},
            "xo": {"x": self.xo},
            "zu": {"z": self.zu},
            "zd": {"z": self.zd},
            "zo": {"z": self.zo},
        }
        self.send_sems, self.recv_sems = send_sems, recv_sems
        self.count = 0
        self.sent = []

    def barrier(self, names):
        sem = pltpu.get_barrier_semaphore()
        for name in names:
            pl.semaphore_signal(
                sem, inc=1, device_id=self.dev[name], device_id_type=pl.DeviceIdType.MESH
            )
        pl.semaphore_wait(sem, len(names))

    def slot(self):
        self.count += 1
        assert self.count <= self.send_sems.shape[0]
        return self.count - 1

    def copy(self, src, dst, k, name):
        return pltpu.make_async_remote_copy(
            src_ref=src,
            dst_ref=dst,
            send_sem=self.send_sems.at[k],
            recv_sem=self.recv_sems.at[k],
            device_id=self.dev[name],
            device_id_type=pl.DeviceIdType.MESH,
        )

    def send(self, src, dst, k, name):
        one = self.copy(src, dst, k, name)
        one.start()
        self.sent.append(one)

    def got(self, ref, k):
        self.copy(ref, ref, k, "c").wait_recv()

    def finish(self):
        for one in self.sent:
            one.wait_send()


def run_all(*steps):
    live = list(steps)
    while live:
        rest = []
        for one in live:
            try:
                next(one)
                rest.append(one)
            except StopIteration:
                pass
        live = rest


def group_gather(net, src, out):
    y, c, yu, yd, yo = net.y, net.c, net.yu, net.yd, net.yo
    k = [net.slot() for _ in range(9)]
    half = src.shape[0] // 2
    lo, hi = pl.ds(0, half), pl.ds(half, half)
    mine = out.at[y, c]
    net.send(src, mine, k[0], "yu")
    net.send(src, mine, k[1], "yd")
    net.send(src, mine, k[2], "c")
    yield
    net.got(out.at[yd, c], k[0])
    net.send(out.at[yd, c, lo], out.at[yd, c, lo], k[3], "yu")
    net.send(out.at[yd, c], out.at[yd, c], k[4], "c")
    net.got(out.at[yu, c], k[1])
    net.send(out.at[yu, c, hi], out.at[yu, c, hi], k[5], "yd")
    net.send(out.at[yu, c], out.at[yu, c], k[6], "c")
    yield
    net.got(out.at[yo, c, lo], k[3])
    net.send(out.at[yo, c, lo], out.at[yo, c, lo], k[7], "c")
    net.got(out.at[yo, c, hi], k[5])
    net.send(out.at[yo, c, hi], out.at[yo, c, hi], k[8], "c")
    yield
    net.got(out.at[y, 1 - c], k[2])
    net.got(out.at[yd, 1 - c], k[4])
    net.got(out.at[yu, 1 - c], k[6])
    net.got(out.at[yo, 1 - c, lo], k[7])
    net.got(out.at[yo, 1 - c, hi], k[8])


def group_scatter(net, part, acc, from_half, from_full, total, make=None):
    y, c, yu, yd, yo = net.y, net.c, net.yu, net.yd, net.yo
    k = [net.slot() for _ in range(8)]
    n = part.shape[2]
    half = n // 2
    lo, hi = pl.ds(0, half), pl.ds(half, half)

    sent = []

    def send(src, dst, i, name):
        sent.append(net.copy(src, dst, i, name))
        sent[-1].start()

    def start(i, d):
        if make is not None:
            make(i, d)
        send(part.at[d, 1 - c], acc.at[d], k[i], "c")

    def core_sum(i, d):
        net.got(acc.at[d], k[i])
        acc[d] = acc[d] + part[d, c]

    for i, d in enumerate((yo, yu, yd)):
        start(i, d)
    yield
    core_sum(0, yo)
    send(acc.at[yo, lo], from_half.at[0], k[4], "yu")
    send(acc.at[yo, hi], from_half.at[1], k[5], "yd")
    core_sum(1, yu)
    core_sum(2, yd)
    yield
    net.got(from_half.at[0], k[4])
    acc[yu, lo] = acc[yu, lo] + from_half[0]
    send(acc.at[yu], from_full.at[0], k[6], "yu")
    net.got(from_half.at[1], k[5])
    acc[yd, hi] = acc[yd, hi] + from_half[1]
    send(acc.at[yd], from_full.at[1], k[7], "yd")
    yield
    start(3, y)
    yield
    net.got(acc.at[y], k[3])
    mine = part[y, c].astype(F32) + acc[y].astype(F32)
    net.got(from_full.at[0], k[6])
    net.got(from_full.at[1], k[7])
    for one in sent:
        one.wait_send()
    total(mine + from_full[0].astype(F32) + from_full[1].astype(F32))


def scatter_scratch(n, w):
    return [VMEM((4, n, w), BF16), VMEM((2, n // 2, w), BF16), VMEM((2, n, w), BF16)]


BOTH = slice(None)


def plane_gather(net, o, theirs=None):
    z, x, xu, xd, xo, zu, zd, zo = net.z, net.x, net.xu, net.xd, net.xo, net.zu, net.zd, net.zo
    k = [net.slot() for _ in range(16)]
    every = slice(None)
    relayed = []

    def send(at, i, name):
        net.send(o(*at), o(*at), k[i], name)

    def got(at, i):
        net.got(o(*at), k[i])

    def relay(*at):
        if theirs is not None:
            slot = net.slot()
            net.send(o(*at), o(*at), slot, "c")
            relayed.append((at, slot))

    send((z, BOTH, x, 0), 0, "xu")
    send((z, BOTH, x, 0), 1, "xd")
    send((z, BOTH, x, 1), 2, "zu")
    send((z, BOTH, x, 1), 3, "zd")
    relay(z, BOTH, x, 0)
    relay(z, BOTH, x, 1)
    yield
    got((z, BOTH, xd, 0), 0)
    send((z, 0, xd, 0), 4, "xu")
    got((zd, BOTH, x, 1), 2)
    send((zd, 0, x, 1), 6, "zu")
    got((z, BOTH, xu, 0), 1)
    send((z, 1, xu, 0), 5, "xd")
    got((zu, BOTH, x, 1), 3)
    send((zu, 1, x, 1), 7, "zd")
    for at in ((z, BOTH, xd, 0), (zd, BOTH, x, 1), (z, BOTH, xu, 0), (zu, BOTH, x, 1)):
        relay(*at)
    yield
    got((z, 0, xo, 0), 4)
    got((z, 1, xo, 0), 5)
    send((z, BOTH, every, 0), 8, "zu")
    send((z, BOTH, every, 0), 9, "zd")
    got((zo, 0, x, 1), 6)
    got((zo, 1, x, 1), 7)
    send((every, BOTH, x, 1), 10, "xu")
    send((every, BOTH, x, 1), 11, "xd")
    relay(z, BOTH, xo, 0)
    relay(zo, BOTH, x, 1)
    yield
    got((zd, BOTH, every, 0), 8)
    send((zd, 0, every, 0), 12, "zu")
    got((every, BOTH, xd, 1), 10)
    send((every, 0, xd, 1), 14, "xu")
    got((zu, BOTH, every, 0), 9)
    send((zu, 1, every, 0), 13, "zd")
    got((every, BOTH, xu, 1), 11)
    send((every, 1, xu, 1), 15, "xd")
    for at in ((zd, BOTH, every, 0), (every, BOTH, xd, 1), (zu, BOTH, every, 0), (every, BOTH, xu, 1)):
        relay(*at)
    yield
    got((zo, 0, every, 0), 12)
    got((zo, 1, every, 0), 13)
    relay(zo, BOTH, every, 0)
    got((every, 0, xo, 1), 14)
    got((every, 1, xo, 1), 15)
    relay(every, BOTH, xo, 1)
    for at, slot in relayed:
        net.got(theirs(*at), slot)


def add_into(dst, *others):
    for index in itertools.product(*[range(n) for n in dst.shape[:-2]]):
        at = index + (slice(None), slice(None))
        total = dst[at]
        for other in others:
            total = total + other[at]
        dst[at] = total


def plane_scatter(net, g, tmp):
    z, x, xu, xd, xo, zu, zd, zo = net.z, net.x, net.xu, net.xd, net.xo, net.zu, net.zd, net.zo
    t1, t2, u1, u2, t3, t4, u3, u4 = tmp
    k = [net.slot() for _ in range(16)]
    every = slice(None)

    def send(src, dst, i, name):
        net.send(src, dst, k[i], name)

    def got(ref, i):
        net.got(ref, k[i])

    send(g(zo, 0, every, 0), t1.at[0], 0, "zu")
    send(g(zo, 1, every, 0), t1.at[1], 1, "zd")
    send(g(every, 0, xo, 1), t2.at[0], 2, "xu")
    send(g(every, 1, xo, 1), t2.at[1], 3, "xd")
    yield
    got(t1.at[0], 0)
    add_into(g(zu, 0, every, 0), t1.at[0])
    send(g(zu, BOTH, every, 0), u1.at[0], 4, "zu")
    got(t2.at[0], 2)
    add_into(g(every, 0, xu, 1), t2.at[0])
    send(g(every, BOTH, xu, 1), u2.at[0], 6, "xu")
    got(t1.at[1], 1)
    add_into(g(zd, 1, every, 0), t1.at[1])
    send(g(zd, BOTH, every, 0), u1.at[1], 5, "zd")
    got(t2.at[1], 3)
    add_into(g(every, 1, xd, 1), t2.at[1])
    send(g(every, BOTH, xd, 1), u2.at[1], 7, "xd")
    yield
    got(u1.at[0], 4)
    got(u1.at[1], 5)
    add_into(g(z, BOTH, every, 0), u1.at[0], u1.at[1])
    send(g(z, 0, xo, 0), t3.at[0], 8, "xu")
    send(g(z, 1, xo, 0), t3.at[1], 9, "xd")
    got(u2.at[0], 6)
    got(u2.at[1], 7)
    add_into(g(every, BOTH, x, 1), u2.at[0], u2.at[1])
    send(g(zo, 0, x, 1), t4.at[0], 10, "zu")
    send(g(zo, 1, x, 1), t4.at[1], 11, "zd")
    yield
    got(t3.at[0], 8)
    add_into(g(z, 0, xu, 0), t3.at[0])
    send(g(z, BOTH, xu, 0), u3.at[0], 12, "xu")
    got(t4.at[0], 10)
    add_into(g(zu, 0, x, 1), t4.at[0])
    send(g(zu, BOTH, x, 1), u4.at[0], 14, "zu")
    got(t3.at[1], 9)
    add_into(g(z, 1, xd, 0), t3.at[1])
    send(g(z, BOTH, xd, 0), u3.at[1], 13, "xd")
    got(t4.at[1], 11)
    add_into(g(zd, 1, x, 1), t4.at[1])
    send(g(zd, BOTH, x, 1), u4.at[1], 15, "zd")
    yield
    got(u3.at[0], 12)
    got(u3.at[1], 13)
    add_into(g(z, BOTH, x, 0), u3.at[0], u3.at[1])
    got(u4.at[0], 14)
    got(u4.at[1], 15)
    add_into(g(z, BOTH, x, 1), u4.at[0], u4.at[1])


def plane_scratch(n, w):
    return [
        VMEM((2, 4, n, w), BF16),
        VMEM((2, 4, n, w), BF16),
        VMEM((2, 2, 4, n, w), BF16),
        VMEM((2, 4, 2, n, w), BF16),
        VMEM((2, n, w), BF16),
        VMEM((2, n, w), BF16),
        VMEM((2, 2, n, w), BF16),
        VMEM((2, 2, n, w), BF16),
    ]


def column_view(ref):
    w = ref.shape[-1] // 2

    def view(zz, half, xx, part):
        return ref.at[zz, half, xx, :, pl.ds(part * w, w)]

    return view


def sems(n):
    return [pltpu.SemaphoreType.DMA((n,)), pltpu.SemaphoreType.DMA((n,))]


def params(cid, limit=56 << 20):
    return pltpu.CompilerParams(collective_id=cid, has_side_effects=True, vmem_limit_bytes=limit)


ANY = pl.BlockSpec(memory_space=pl.ANY)
INV = pl.BlockSpec(memory_space=pltpu.VMEM)
INS = pl.BlockSpec(memory_space=pltpu.SMEM)
PLANE = ("xu", "xd", "zu", "zd")
RING = ("yu", "yd", "c")


class Ticks:
    def __init__(self, *steps):
        self.steps = list(steps)

    def tick(self, count=1):
        for _ in range(count):
            for one in self.steps:
                next(one, None)


def weight_gather(net, weight, out, local):
    z, yh, x = net.z, net.yh, net.x
    n, w = weight.shape[0], weight.shape[1] // 2
    k = net.slot()

    def half(which):
        return weight.at[:, pl.ds(pl.multiple_of(which * w, 128), w)]

    mine = pltpu.make_async_copy(half(yh), out.at[z, yh, x, pl.ds(0, n)], local)
    mine.start()
    net.send(half(1 - yh), out.at[z, yh, x, pl.ds(0, n)], k, "yo")
    yield
    mine.wait()
    net.got(out.at[z, 1 - yh, x, pl.ds(0, n)], k)
    yield from plane_gather(net, column_view(out))


def splat(row, lane, at):
    return jnp.sum(jnp.where(lane == at, row, 0.0), axis=1, keepdims=True)


def place_of(segs, parents, block):
    lane = lax.broadcasted_iota(jnp.int32, (1, 128), 1)
    seg = splat(segs, lane, block)
    lanes = lane.astype(F32)
    parent = splat(parents, lanes, seg)
    trunk = splat(parents, lanes, parent)
    leaf = (seg >= 10.0).astype(F32)
    branch = (seg >= 2.0).astype(F32)
    above = [(splat(segs, lane, b) == parent).astype(F32) * leaf for b in range(16, 32)]
    return trunk, leaf, branch, above


def wide(value):
    return jnp.broadcast_to(value, (1, 128)).astype(BF16)


def trunk_block(kv, which, i, trunk):
    one = wide(trunk)
    return kv[which, 0, i // 4, i % 4] * (1 - one) + kv[which, 1, i // 4, i % 4] * one


def parent_block(kv, which, above):
    total = kv[which, 2, 0, 0] * wide(above[0])
    for j in range(1, 16):
        total = total + kv[which, 2 + j // 8, j // 4 % 2, j % 4] * wide(above[j])
    return total


NT = (((1,), (1,)), ((), ()))
TN = (((0,), (0,)), ((), ()))
SCALE = 128**-0.5


def attend(b, z, x, q, kv, segs, parents, scores, o, log_sum):
    lane = (lax.broadcasted_iota(jnp.int32, (256, 512), 1) & 255).astype(F32)
    row = lax.broadcasted_iota(jnp.int32, (256, 512), 0).astype(F32)
    block = z * 8 + b * 4 + x
    trunk, leaf, branch, above = place_of(segs, parents, block)
    rows = pl.ds(b * 256, 256)
    both = jnp.concatenate([q[rows, :128], q[rows, 128:]], axis=0)
    start = block.astype(F32) - 8.0 * trunk

    def score(key):
        return lax.dot_general(key, both, NT, preferred_element_type=F32) * SCALE

    def trunk_score(i, top):
        gap = (start - i.astype(F32)) * 256.0
        s = jnp.where(row - lane <= gap, score(trunk_block(kv, 0, i, trunk)), NEG)
        scores[i] = s
        return jnp.maximum(top, jnp.max(s, axis=0, keepdims=True))

    top = lax.fori_loop(0, 8, trunk_score, jnp.full((1, 512), NEG, F32))
    s = score(parent_block(kv, 0, above)) + (leaf - 1.0) * 1e30
    scores[8] = s
    top = jnp.maximum(top, jnp.max(s, axis=0, keepdims=True))
    s = jnp.where(row <= lane, score(kv[0, z, b, x]), NEG) + (branch - 1.0) * 1e30
    scores[9] = s
    top = jnp.maximum(top, jnp.max(s, axis=0, keepdims=True))

    def weigh(i, value, carry):
        acc, total = carry
        w = jnp.exp(scores[i] - top)
        acc = acc + lax.dot_general(value, w.astype(BF16), TN, preferred_element_type=F32)
        return acc, total + jnp.sum(w, axis=0, keepdims=True)

    carry = (jnp.zeros((128, 512), F32), jnp.zeros((1, 512), F32))
    carry = lax.fori_loop(0, 8, lambda i, c: weigh(i, trunk_block(kv, 1, i, trunk), c), carry)
    carry = weigh(8, parent_block(kv, 1, above), carry)
    acc, total = weigh(9, kv[1, z, b, x], carry)
    heads = (acc / total).T.astype(BF16)
    o[rows, :128] = heads[:256]
    o[rows, 128:] = heads[256:]
    log_sum[b] = jnp.broadcast_to(top + jnp.log(total), (8, 512))
    return top


def one_hot(rows, lanes, hit):
    row = lax.broadcasted_iota(jnp.int32, (rows, lanes), 0)
    lane = lax.broadcasted_iota(jnp.int32, (rows, lanes), 1)
    return hit(row, lane).astype(F32).astype(BF16)


def forward(tokens, cotangent, seg_ids, parents, vectors, query_bias, up_bias, w_keyval, w_query, w_out, w_up, w_down):
    def kernel(tok, cot, seg_in, par_in, vec_in, qb_in, ub_in, wkv_in, wq_in, wo_in, wu_in, wd_in,
               cot_out, h2, wu, wd, wq_out, wo_out, wkv_out, h1_out, q_out, kv_out, o, log_sum, x1, best, vec, ub,
               tok_all, h1, wkv, wq, wo, q, kv, scores, part, own, mine, got, pack, pairs, halves, tiles, local,
               *rest):
        *scratch, ss, rs = rest
        net = Net(ss, rs)
        z, yh, x, yl, c, y = net.z, net.yh, net.x, net.yl, net.c, net.y
        starts = [
            pltpu.make_async_copy(src, dst, local.at[i])
            for i, (src, dst) in enumerate(((tok, tok_all.at[y, c]), (cot, cot_out.at[y, c])))
        ]
        for one in starts:
            one.start()
        row = lax.broadcasted_iota(jnp.int32, (16, 128), 0)
        lane = lax.broadcasted_iota(jnp.int32, (16, 128), 1)
        periodic = jnp.dot(vec_in[...], one_hot(16, 128, lambda r, l: l % 16 == r), preferred_element_type=F32)
        first = jnp.dot(vec_in[...], one_hot(16, 128, lambda r, l: r == 0), preferred_element_type=F32)
        tile = jnp.where(row < 6, periodic, first)
        tile = jnp.where(row == 7, seg_in[0].astype(F32), tile).astype(BF16)
        for i in range(2):
            pack[i, 0:16] = wkv_in[:, i * 128 : (i + 1) * 128]
            pack[i, 16:32] = tile
        four = one_hot(4, 128, lambda r, l: l % 4 == r)
        heads = lax.dot_general(qb_in[...], four, TN, preferred_element_type=F32)
        units = lax.dot_general(ub_in[...], four, TN, preferred_element_type=F32)
        blank = jnp.zeros((6, 128), F32)
        for i in range(2):
            halves[i] = jnp.concatenate([units[8 * i : 8 * i + 8], heads[2 * i : 2 * i + 2], blank], axis=0).astype(BF16)
        pairs[yh, yl, c] = jnp.where(c == 0, pack[0], pack[1])
        net.barrier(PLANE + RING + ("yo", "xo", "zo"))

        query = weight_gather(net, wq_in, wq, local.at[4])
        later = Ticks(weight_gather(net, wu_in, wu, local.at[6]), weight_gather(net, wd_in, wd, local.at[7]))
        project_weight = weight_gather(net, wo_in, wo, local.at[5])
        toks = group_gather(net, tok, tok_all)
        ks = [net.slot() for _ in range(11)]
        net.send(pack.at[1 - c], pairs.at[yh, yl, c], ks[0], "c")
        net.send(halves.at[1 - yh], halves.at[2], ks[4], "yo")
        next(query)
        net.got(pairs.at[yh, yl, 1 - c], ks[0])
        for i, name in enumerate(("yu", "yd", "yo")):
            net.send(pairs.at[yh, yl], pairs.at[yh, yl], ks[1 + i], name)
        next(toks)
        next(query)
        net.got(halves.at[2], ks[4])
        here, there = jnp.where(yh == 0, halves[0], halves[1]), halves[2]
        low, high = jnp.where(yh == 0, here, there), jnp.where(yh == 0, there, here)
        tiles[z, x, 1] = jnp.where((lane // 16) % 2 == 0, low.astype(F32), high.astype(F32)).astype(BF16)
        for i, d in enumerate((net.yd, net.yu, net.yo)):
            net.got(pairs.at[d // 2, lax.rem(d, 2)], ks[1 + i])
        merged = jnp.zeros((16, 128), F32)
        for i in range(8):
            high, tp = i // 4, i % 4
            one = pairs[high, tp // 2, tp % 2, 16:32].astype(F32)
            hit = (row < 6) & (lane // 16 == i)
            hit = hit | ((row == 6) & (lane // 16 % 2 == high) & (lane % 4 == tp))
            hit = hit | ((row == 7) & ((lane // 4) % 2 == high))
            merged = jnp.where(hit, one, merged)
            wkv[z, high, x, tp // 2, tp % 2] = pairs[high, tp // 2, tp % 2, 0:16]
        tiles[z, x, 0] = merged.astype(BF16)
        for i, name in enumerate(("xu", "xd", "xo")):
            net.send(tiles.at[z, x], tiles.at[z, x], ks[5 + i], name)

        def key_view(zz, half, xx, part):
            return wkv.at[zz, part, xx, pl.ds(0, 2) if half == BOTH else half]

        keyval = plane_gather(net, key_view)
        next(keyval)
        next(project_weight)
        later.tick()
        for i, d in enumerate((net.xd, net.xu, net.xo)):
            net.got(tiles.at[z, d], ks[5 + i])
        for i, name in enumerate(("zu", "zd", "zo")):
            net.send(tiles.at[z], tiles.at[z], ks[8 + i], name)
        next(keyval)
        next(query)
        next(toks)
        next(keyval)
        next(query)
        next(project_weight)
        later.tick()
        next(toks)
        next(keyval)
        next(query)
        next(project_weight)
        for i, d in enumerate((net.zd, net.zu, net.zo)):
            net.got(tiles.at[d], ks[8 + i])

        value_bias = jnp.zeros((16, 128), F32)
        biases = jnp.zeros((16, 128), F32)
        segs = jnp.zeros((16, 128), F32)
        for zz in range(4):
            come = [tiles[zz, xx, 0].astype(F32) for xx in range(4)]
            turned = [pltpu.roll(one, 64, 1) for one in come]
            for xx in range(4):
                at = (lane // 32 == zz) & ((lane // 4) % 4 == xx)
                value_bias = jnp.where(at, come[xx], value_bias)
                biases = jnp.where(at, tiles[zz, xx, 1].astype(F32), biases)
                segs = jnp.where((lane // 8 == zz) & (lane % 4 == xx), come[xx], segs)
            for high in range(2):
                for pair in range(2):
                    even = come[2 * pair] if high == 0 else turned[2 * pair]
                    odd = turned[2 * pair + 1] if high == 0 else come[2 * pair + 1]
                    j = (zz * 2 + high) * 2 + pair
                    vec[:, j * 128 : (j + 1) * 128] = jnp.where(lane < 64, even, odd)
        value_bias = value_bias[6:7]
        segs = segs[7:8]
        vec[8:9, 0:128] = segs
        ub[...] = biases[0:8]
        query_bias = jnp.concatenate([biases[8:9], biases[9:10]], axis=1)
        parent = jnp.zeros((1, 128), F32)
        for i in range(18):
            parent = jnp.where(lane[0:1] == i, par_in[i].astype(F32), parent)
        vec[9:10, 0:128] = parent
        for _ in toks:
            pass
        starts[0].wait()

        gain1, shift1 = vec[0:1], vec[1:2]

        def norm_rows(i, carry):
            rows = tok_all[i // 2, i % 2].astype(F32)
            h1[pl.ds(pl.multiple_of(i * 64, 64), 64)] = (normed(rows)[0] * gain1 + shift1).astype(BF16)
            return carry

        lax.fori_loop(0, 8, norm_rows, 0)
        next(project_weight)
        for _ in query:
            pass
        for _ in keyval:
            pass

        def project(i, carry):
            rows = pl.ds(pl.multiple_of(i * 256, 256), 256)
            h = h1[rows]
            weight = wq[...].reshape(2048, 256)
            q[rows] = (jnp.dot(h, weight, preferred_element_type=F32) + query_bias).astype(BF16)
            weight = wkv[...].reshape(2048, 128)
            shift = value_bias * c.astype(F32)
            kv[c, z, i, x] = (jnp.dot(h, weight, preferred_element_type=F32) + shift).astype(BF16)
            return carry

        lax.fori_loop(0, 2, project, 0)

        def view(zz, half, xx, part):
            rows = pl.ds(0, 256) if half == BOTH else pl.ds(128 * half, 128)
            return kv.at[c, zz, part, xx, rows]

        def their_view(zz, half, xx, part):
            rows = pl.ds(0, 256) if half == BOTH else pl.ds(128 * half, 128)
            return kv.at[1 - c, zz, part, xx, rows]

        keys = plane_gather(net, view, their_view)
        cots = group_gather(net, cot, cot_out)
        next(keys)
        later.tick()
        next(cots)
        next(keys)
        next(project_weight)
        next(keys)
        next(cots)
        next(keys)
        later.tick()
        next(cots)
        for _ in keys:
            pass

        saves = [
            pltpu.make_async_copy(src, dst, local.at[8 + i])
            for i, (src, dst) in enumerate(
                ((wq, wq_out), (wkv, wkv_out), (h1, h1_out), (q, q_out), (kv, kv_out), (wo, wo_out))
            )
        ]
        for one in saves[:5]:
            one.start()
        top = attend(0, z, x, q, kv, segs, parent, scores, o, log_sum)
        top = jnp.maximum(top, attend(1, z, x, q, kv, segs, parent, scores, o, log_sum))
        for h in range(2):
            mine[0, 8 * h : 8 * h + 8] = jnp.full((8, 128), jnp.max(top[:, h * 256 : (h + 1) * 256]), F32)
        for _ in project_weight:
            pass
        saves[5].start()

        def project_out(i, d):
            rows = o[pl.ds(pl.multiple_of(d * 128, 128), 128)]
            for j in range(4):
                weight = wo[j].reshape(512, 256)
                out = lax.dot_general(rows, weight, NT, preferred_element_type=F32).astype(BF16)
                part[d, 0, :, j * 512 : (j + 1) * 512] = out[:64]
                part[d, 1, :, j * 512 : (j + 1) * 512] = out[64:]

        def total(summed):
            value = tok[...].astype(F32) + (summed + vec[4:5])
            x1[...] = value
            own[...] = (normed(value)[0] * vec[2:3] + vec[3:4]).astype(BF16)

        rows = group_scatter(net, part, *scratch, total, project_out)
        largest = heads_max(net, mine, got, best)
        for _ in range(3):
            next(rows)
            next(largest)
        next(rows)
        later.tick()
        next(rows, None)
        me = pltpu.make_async_copy(own, h2.at[y, c], local.at[14])
        me.start()
        spreading = group_gather(net, own, h2)
        next(spreading)
        for _ in largest:
            pass
        for _ in spreading:
            pass
        me.wait()
        for _ in cots:
            pass
        later.tick()
        starts[1].wait()
        for one in saves:
            one.wait()
        net.finish()

    n, d = tokens.shape
    rows = jax.ShapeDtypeStruct((4, 2, n, d), BF16)

    def bf(*shape):
        return jax.ShapeDtypeStruct(shape, BF16)

    def f32(*shape):
        return jax.ShapeDtypeStruct(shape, F32)

    return pl.pallas_call(
        kernel,
        out_shape=(
            rows,
            rows,
            bf(4, 2, 4, n, 1024),
            bf(4, 2, 4, n, 1024),
            bf(4, 2, 4, n, 256),
            bf(4, 2, 4, n, 256),
            bf(4, 2, 4, 2, 2, 16, 128),
            bf(512, d),
            bf(512, 256),
            bf(2, 4, 2, 4, 256, 128),
            bf(512, 256),
            f32(2, 8, 512),
            f32(n, d),
            f32(2, 16, 128),
            f32(16, d),
            f32(8, 128),
        ),
        in_specs=[INV, INV, INS, INS] + [INV] * 8,
        out_specs=(ANY,) * 10 + (INV,) * 6,
        scratch_shapes=[
            VMEM((4, 2, n, d), BF16),
            VMEM((512, d), BF16),
            VMEM((4, 2, 4, 2, 2, 16, 128), BF16),
            VMEM((4, 2, 4, n, 256), BF16),
            VMEM((4, 2, 4, n, 256), BF16),
            VMEM((512, 256), BF16),
            VMEM((2, 4, 2, 4, 256, 128), BF16),
            VMEM((10, 256, 512), F32),
            VMEM((4, 2, n, d), BF16),
            VMEM((n, d), BF16),
            VMEM((5, 16, 128), F32),
            VMEM((7, 16, 128), F32),
            VMEM((2, 32, 128), BF16),
            VMEM((2, 2, 2, 32, 128), BF16),
            VMEM((3, 16, 128), BF16),
            VMEM((4, 4, 2, 16, 128), BF16),
            pltpu.SemaphoreType.DMA((15,)),
        ]
        + scatter_scratch(n, d)
        + sems(190),
        compiler_params=params(1),
        name="forward",
    )(tokens, cotangent, seg_ids, parents, vectors, query_bias, up_bias, w_keyval, w_query, w_out, w_up, w_down)


def normed(values):
    centred = values - jnp.mean(values, axis=-1, keepdims=True)
    inverse = lax.rsqrt(jnp.mean(centred * centred, axis=-1, keepdims=True) + EPS)
    return centred * inverse, inverse


def norm_back(grad, norm, inverse, gain):
    scaled = grad * gain
    return inverse * (
        scaled
        - jnp.mean(scaled, axis=-1, keepdims=True)
        - norm * jnp.mean(scaled * norm, axis=-1, keepdims=True)
    )


def heads_max(net, mine, got, best):
    for i, (up, down) in enumerate((("xu", "xd"), ("zu", "zd"))):
        k = [net.slot() for _ in range(3)]
        a, b, d = got.at[3 * i], got.at[3 * i + 1], got.at[3 * i + 2]
        net.send(mine.at[2 * i], a, k[0], up)
        net.send(mine.at[2 * i], b, k[1], down)
        yield
        net.got(a, k[0])
        net.got(b, k[1])
        mine[2 * i + 1] = jnp.maximum(mine[2 * i], jnp.maximum(a[...], b[...]))
        net.send(mine.at[2 * i + 1], d, k[2], up)
        yield
        net.got(d, k[2])
        mine[2 * i + 2] = jnp.maximum(mine[2 * i + 1], d[...])
    k = net.slot()
    net.send(mine.at[4], got.at[6], k, "yo")
    yield
    net.got(got.at[6], k)
    best[net.yh] = mine[4]
    best[1 - net.yh] = got[6]


def weight_scatter(net, g, tmp, out):
    z, yh, x = net.z, net.yh, net.x
    w = g.shape[-1]
    k = net.slot()
    yield from plane_scatter(net, column_view(g), tmp)
    mine = out.at[:, pl.ds(pl.multiple_of(yh * w, 128), w)]
    net.send(g.at[z, 1 - yh, x], mine, k, "yo")
    out[:, pl.ds(pl.multiple_of(yh * w, 128), w)] = g[z, yh, x]
    yield
    net.got(out.at[:, pl.ds(pl.multiple_of((1 - yh) * w, 128), w)], k)


def smooth_gate(u):
    scale = 0.7978845608028654
    square = u * u
    t = jnp.tanh(scale * u * (1.0 + 0.044715 * square))
    half = 0.5 * (1.0 + t)
    slope = half + 0.5 * u * (1.0 - t * t) * scale * (1.0 + 0.134145 * square)
    return u * half, slope


def piece(ref, which, zz, yy, xx):
    return jnp.concatenate(
        [ref[zz, yy, xx, :, (which * 4 + r) * 128 : (which * 4 + r + 1) * 128] for r in range(4)], axis=0
    )


def put_piece(ref, which, zz, yy, xx, value):
    for r in range(4):
        ref[zz, yy, xx, :, (which * 4 + r) * 128 : (which * 4 + r + 1) * 128] = value[r * 64 : (r + 1) * 64]


def attend_back(z, x, q, kv, o, go, log_sum, segs, parents, grad, lone, dq_sum, dq):
    lane = (lax.broadcasted_iota(jnp.int32, (256, 512), 1) & 255).astype(F32)
    row = lax.broadcasted_iota(jnp.int32, (256, 512), 0).astype(F32)
    places = [place_of(segs, parents, z * 8 + b * 4 + x) for b in range(2)]

    def stacked(ref, b):
        return jnp.concatenate([ref[b * 256 : b * 256 + 256, :128], ref[b * 256 : b * 256 + 256, 128:]], axis=0)

    logs, inner = [], []
    for b in range(2):
        logs.append(log_sum[b, 0:1])
        inner.append(
            jnp.sum((stacked(go, b).astype(F32) * stacked(o, b).astype(F32)).T, axis=0, keepdims=True)
        )

    def one(b, key, value, masked, first):
        both, up = stacked(q, b), stacked(go, b)
        s = masked(lax.dot_general(key, both, NT, preferred_element_type=F32) * SCALE)
        p = jnp.exp(s - logs[b])
        dp = lax.dot_general(value, up, NT, preferred_element_type=F32)
        ds = (p * (dp - inner[b])).astype(BF16)
        more = lax.dot_general(key, ds, TN, preferred_element_type=F32)
        dq_sum[b] = more if first else dq_sum[b] + more
        dk = jnp.dot(ds, both, preferred_element_type=F32) * SCALE
        dv = jnp.dot(p.astype(BF16), up, preferred_element_type=F32)
        return dk.astype(BF16), dv.astype(BF16)

    for b in range(2):
        trunk, leaf, branch, above = places[b]
        lone[b, 0, 0], lone[b, 0, 1] = one(
            b,
            piece(kv, 0, z, b, x),
            piece(kv, 1, z, b, x),
            lambda s: jnp.where(row <= lane, s, NEG) + (branch - 1.0) * 1e30,
            True,
        )
        key, value = (
            sum(piece(kv, w, 2 + j // 8, j // 4 % 2, j % 4) * wide(above[j]) for j in range(16)) for w in range(2)
        )
        lone[b, 1, 0], lone[b, 1, 1] = one(b, key, value, lambda s: s + (leaf - 1.0) * 1e30, False)
    yield

    for j in range(16):
        own = [
            wide((z * 8 + b * 4 + x == 16 + j).astype(F32) * jnp.ones((1, 1), F32)) for b in range(2)
        ]
        for w in range(2):
            value = sum(lone[b, 0, w] * own[b] + lone[b, 1, w] * wide(places[b][3][j]) for b in range(2))
            put_piece(grad, w, 2 + j // 8, j // 4 % 2, j % 4, value)

    def trunk_one(i, carry):
        yy, xx = i // 4, i % 4
        totals = None
        for b in range(2):
            trunk = places[b][0]
            second = wide(trunk)
            first = 1 - second
            key, value = (piece(kv, w, 0, yy, xx) * first + piece(kv, w, 1, yy, xx) * second for w in range(2))
            start = (z * 8 + b * 4 + x).astype(F32) - 8.0 * trunk
            gap = (start - i.astype(F32)) * 256.0
            dk, dv = one(b, key, value, lambda s: jnp.where(row - lane <= gap, s, NEG), False)
            parts = [dk * first, dv * first, dk * second, dv * second]
            totals = parts if totals is None else [t + p for t, p in zip(totals, parts)]
        for t in range(2):
            for w in range(2):
                put_piece(grad, w, t, yy, xx, totals[2 * t + w])
        return carry

    lax.fori_loop(0, 4, trunk_one, 0)
    yield
    lax.fori_loop(4, 8, trunk_one, 0)
    for b in range(2):
        rows = (dq_sum[b] * SCALE).T.astype(BF16)
        dq[b * 256 : b * 256 + 256, :128] = rows[:256]
        dq[b * 256 : b * 256 + 256, 128:] = rows[256:]


def spread(net, names, src, dst, k):
    for i, name in enumerate(names):
        net.send(src, dst.at[i], k[i], name)


def all_sums(net, mine, near, far):
    k = [net.slot() for _ in range(6)]
    spread(net, ("xu", "xd", "xo"), mine.at[0], near, k)
    yield
    for i in range(3):
        net.got(near.at[i], k[i])
    mine[1] = mine[0] + near[0] + near[1] + near[2]
    spread(net, ("zu", "zd", "zo"), mine.at[1], far, k[3:])
    yield
    for i in range(3):
        net.got(far.at[i], k[3 + i])
    mine[2] = mine[1] + far[0] + far[1] + far[2]


def backward(tokens, cotangent, cot_all, h2, wu, wd, wq, wo, packs, h1, q, kv, o, log_sum, x1, vec, ub):
    def kernel(tok, cot, cot_in, h2_in, wu_in, wd_in, wq_in, wo_in, packs_in, h1_in, q, kv_in, o, log_sum,
               x1, vec, ub_in,
               output, grad_input, up_out, down_out, wo_out, wq_out, vec_out, bias_out, kv_out, vb_out,
               h2, cots, wu, wd, wq, wo, packs, adu, us, das, part, part_mlp, gu, gd, gwo, gq, own, dz, dx1, sums, go,
               lone, dq_sum, dq, dkv_from, dkv, gkv, gkv_z, gkv_x, bias, bias_x, bias_z, vecs, vec_z, vec_x,
               local, *rest):
        *scratch, ss, rs = rest
        first, second, tmp_u, tmp_d, tmp_o, tmp_q, tmp_k = (
            scratch[:3],
            scratch[3:6],
            scratch[6:14],
            scratch[14:22],
            scratch[22:30],
            scratch[30:38],
            scratch[38:46],
        )
        net = Net(ss, rs)
        z, yh, x, yl, c, y = net.z, net.yh, net.x, net.yl, net.c, net.y

        def columns(ref, j):
            return ref.at[:, :, :, :, pl.ds(j * 256, 256)]

        def load(src, dst, i):
            one = pltpu.make_async_copy(src, dst, local.at[i])
            one.start()
            return one

        load(h2_in, h2, 0)
        load(columns(wu_in, 0), columns(wu, 0), 2)
        load(cot_in, cots, 1)
        load(columns(wd_in, 0), columns(wd, 0), 6)
        for j in range(1, 4):
            load(columns(wu_in, j), columns(wu, j), 2 + j)
            load(columns(wd_in, j), columns(wd, j), 6 + j)
        loads = [load(wo_in, wo, 10), load(wq_in, wq, 11)]
        loads.append(load(packs_in, packs, 12))
        net.barrier(PLANE + RING + ("yo", "xo", "zo"))
        pltpu.make_async_copy(h2_in, h2, local.at[0]).wait()
        pltpu.make_async_copy(cot_in, cots, local.at[1]).wait()

        def hidden(j, carry):
            at = pl.ds(pl.multiple_of(j * 256, 256), 256)
            there = pl.ds(0, 4), pl.ds(0, 2), pl.ds(0, 4), pl.ds(0, 64), at
            pltpu.make_async_copy(wu_in.at[there], wu.at[there], local.at[2 + j]).wait()
            us[...] = jnp.dot(
                h2[...].reshape(512, 2048), wu[there].reshape(2048, 256), preferred_element_type=F32
            )
            pltpu.make_async_copy(wd_in.at[there], wd.at[there], local.at[6 + j]).wait()
            das[...] = jnp.dot(
                cots[...].reshape(512, 2048), wd[there].reshape(2048, 256), preferred_element_type=F32
            )
            bias_row = jnp.concatenate([ub_in[pl.ds(2 * j, 1)], ub_in[pl.ds(2 * j + 1, 1)]], axis=1)

            def gate(i, total):
                rows = pl.ds(pl.multiple_of(i * 64, 64), 64)
                value, slope = smooth_gate(us[rows] + bias_row)
                adu[0, rows, at] = value.astype(BF16)
                du = (das[rows] * slope).astype(BF16)
                adu[1, rows, at] = du
                return total + jnp.sum(du.astype(F32), axis=0, keepdims=True)

            total = lax.fori_loop(0, 8, gate, jnp.zeros((1, 256), F32))
            bias[0, pl.ds(2 * j, 1)] = total[:, :128]
            bias[0, pl.ds(2 * j + 1, 1)] = total[:, 128:]
            return carry

        lax.fori_loop(0, 4, hidden, 0)

        def projected(dst, d, rows, weight):
            def column(j, carry):
                out = lax.dot_general(rows, weight(j), NT, preferred_element_type=F32).astype(BF16)
                at = pl.ds(pl.multiple_of(j * 512, 512), 512)
                dst[d, 0, :, at] = out[:64]
                dst[d, 1, :, at] = out[64:]
                return carry

            lax.fori_loop(0, 4, column, 0)

        def ring_rows(d):
            return pl.ds(pl.multiple_of(d * 128, 128), 128)

        def make_two(i, d):
            projected(part, d, adu[1, ring_rows(d)], lambda j: wu[j].reshape(512, 1024))

        def total_two(summed):
            norm, inverse = normed(x1[...])
            grad = cot[...].astype(F32) + norm_back(summed, norm, inverse, vec[2:3])
            dx1[...] = grad
            rounded = grad.astype(BF16)
            own[...] = rounded
            values = (summed * norm, summed, rounded.astype(F32), cot[...].astype(F32))
            for i, v in enumerate(values):
                sums[2 + i : 3 + i] = jnp.sum(v, axis=0, keepdims=True)

        def outer(dst, left, right):
            def block(j, carry):
                out = lax.dot_general(left(j), right, TN, preferred_element_type=F32)
                dst[j] = out.astype(BF16).reshape(2, 4, 64, right.shape[1])
                return carry

            lax.fori_loop(0, 4, block, 0)

        def wide_outer(dst, left, which):
            def block(i, carry):
                j, w = i // 2, i % 2
                at = pl.ds(pl.multiple_of(w * 512, 512), 512)
                out = lax.dot_general(
                    left[:, :, :, pl.ds(pl.multiple_of(j * 512, 512), 512)].reshape(512, 512),
                    adu[which, :, at],
                    TN,
                    preferred_element_type=F32,
                )
                dst[j, :, :, :, at] = out.astype(BF16).reshape(2, 4, 64, 512)
                return carry

            lax.fori_loop(0, 8, block, 0)

        rows_two = group_scatter(net, part, *first, total_two, make_two)
        next(rows_two)
        wide_outer(gd, cots, 0)
        down = weight_scatter(net, gd, tmp_d, down_out)
        next(down)
        next(rows_two)
        next(rows_two)
        next(rows_two)
        next(rows_two, None)
        me = load(own, dz.at[y, c], 23)
        spreading = group_gather(net, own, dz)
        next(spreading)
        wide_outer(gu, h2, 1)
        next(spreading)
        up = weight_scatter(net, gu, tmp_u, up_out)
        next(up)
        for d in range(4):
            projected(part_mlp, d, adu[0, d * 128 : d * 128 + 128], lambda j: wd[j].reshape(512, 1024))
        keep = [
            load(kv_in.at[w, :, :, :, pl.ds(r * 64, 64)], wd.at[:, :, :, :, pl.ds((w * 4 + r) * 128, 128)], 13 + 4 * w + r)
            for w in range(2)
            for r in range(4)
        ]
        late = [load(h1_in.at[:, pl.ds(w * 1024, 1024)], adu.at[w], 21 + w) for w in range(2)]
        next(spreading)
        next(down)
        for _ in spreading:
            pass
        me.wait()
        loads[0].wait()
        go[...] = jnp.dot(
            dz[...].reshape(512, 2048), wo[...].reshape(2048, 256), preferred_element_type=F32
        ).astype(BF16)

        def total_out(summed):
            output[...] = (x1[...] + (summed + vec[5:6])).astype(BF16)

        rows_out = group_scatter(net, part_mlp, *second, total_out)
        next(rows_out)
        for one in keep:
            one.wait()
        steps = attend_back(z, x, q, wd, o, go, log_sum, vec[8:9, 0:128], vec[9:10, 0:128], wu, lone, dq_sum, dq)
        next(steps)
        next(up)
        next(rows_out)
        next(steps)
        next(rows_out)
        next(down)
        next(up)
        next(steps, None)
        next(rows_out)
        next(rows_out, None)

        kc = [net.slot() for _ in range(4)]
        theirs = pl.ds(pl.multiple_of((1 - c) * 512, 512), 512)
        for i in range(4):
            net.send(wu.at[:, :, i, :, theirs], cots.at[:, :, :, pl.ds(i * 512, 512)], kc[i], "c")
        for one in loads[1:] + late:
            one.wait()

        def make_one(i, d):
            if i == 3:
                lower = lax.dot_general(
                    dkv[y], packs[...].reshape(2048, 128), NT, preferred_element_type=F32
                )
                upper = lax.dot_general(
                    dq[ring_rows(d)], wq[...].reshape(2048, 256), NT, preferred_element_type=F32
                )
                out = (lower + upper).astype(BF16)
                h2[d, 0] = out[:64]
                h2[d, 1] = out[64:]
            else:
                projected(h2, d, dq[ring_rows(d)], lambda j: wq[j].reshape(512, 256))

        def total_one(summed):
            norm, inverse = normed(tok[...].astype(F32))
            grad_input[...] = dx1[...] + norm_back(summed, norm, inverse, vec[0:1])
            sums[0:1] = jnp.sum(summed * norm, axis=0, keepdims=True)
            sums[1:2] = jnp.sum(summed, axis=0, keepdims=True)
            sums[6:8] = jnp.zeros((2, 2048), F32)
            vecs[y, c] = sums[...]

        rows_one = group_scatter(net, h2, *first, total_one, make_one)
        next(rows_one)
        ours = pl.ds(pl.multiple_of(c * 512, 512), 512)
        for i in range(4):
            net.got(cots.at[:, :, :, pl.ds(i * 512, 512)], kc[i])

            def core_sum(j, carry):
                zz, yy = j // 2, j % 2
                wu[zz, yy, i, :, ours] = wu[zz, yy, i, :, ours] + cots[zz, yy, :, i * 512 : i * 512 + 512]
                return carry

            lax.fori_loop(0, 8, core_sum, 0)

        def view(zz, half, xx, part):
            at = ours if half == BOTH else pl.ds(pl.multiple_of(c * 512 + 256 * half, 256), 256)
            return wu.at[zz, part, xx, :, at]

        keys = plane_scatter(net, view, tmp_k)
        next(keys)
        next(rows_one)
        outer(gq, lambda j: adu[j // 2, :, pl.ds(pl.multiple_of((j % 2) * 512, 512), 512)], dq[...])
        bias[0, 8:9] = jnp.sum(dq[:, :128].astype(F32), axis=0, keepdims=True)
        bias[0, 9:10] = jnp.sum(dq[:, 128:].astype(F32), axis=0, keepdims=True)
        bias[0, 10:16] = jnp.zeros((6, 128), F32)
        next(keys)
        query = weight_scatter(net, gq, tmp_q, wq_out)
        next(query)
        small = all_sums(net, bias, bias_x, bias_z)
        next(small)
        next(rows_one)
        outer(gwo, lambda j: dz[:, :, :, pl.ds(pl.multiple_of(j * 512, 512), 512)].reshape(512, 512), o[...])
        next(keys)
        project = weight_scatter(net, gwo, tmp_o, wo_out)
        next(project)
        next(down)
        next(up)
        next(query)
        next(small)
        next(keys)
        next(project)
        for _ in keys:
            pass

        def ring_piece(ref, d):
            at = pl.ds(pl.multiple_of(c * 512 + lax.rem(d, 2) * 256, 256), 256)
            return ref.at[z, d // 2, x, :, at]

        kr = [net.slot() for _ in range(7)]
        for i, (name, d) in enumerate((("yu", net.yu), ("yd", net.yd), ("yo", net.yo))):
            net.send(ring_piece(wu, d), dkv_from.at[i], kr[i], name)
        next(query)
        next(project)
        for i in range(3):
            net.got(dkv_from.at[i], kr[i])
        mine = ring_piece(wu, y)[...].astype(F32)
        for i in range(3):
            mine = mine + dkv_from[i].astype(F32)
        mine = mine.astype(BF16)
        dkv[y] = jnp.concatenate([mine[:, :128], mine[:, 128:]], axis=0)
        for i, name in enumerate(("yu", "yd", "yo")):
            net.send(dkv.at[y], dkv.at[y], kr[3 + i], name)
        next(rows_one)
        next(down)
        next(up)
        next(small, None)
        for i, d in enumerate((net.yd, net.yu, net.yo)):
            net.got(dkv.at[d], kr[3 + i])

        every = dkv[...].reshape(512, 128)
        value_sum = jnp.broadcast_to(jnp.sum(every.astype(F32), axis=0, keepdims=True), (8, 128))
        for j in range(4):
            at = pl.ds(pl.multiple_of((j % 2) * 512 + yh * 256, 256), 256)
            out = lax.dot_general(adu[j // 2, :, at], every, TN, preferred_element_type=F32).reshape(4, 2, 32, 128)
            for i in range(4):
                gkv[j, i, 0:32] = jnp.where(yl == 0, out[i, 0], out[i, 1])
                gkv[j, i, 32:40] = value_sum

        def key_value():
            k = [net.slot() for _ in range(7)]
            for i, (name, d) in enumerate((("zu", net.zu), ("zd", net.zd), ("zo", net.zo))):
                net.send(gkv.at[d], gkv_z.at[i], k[i], name)
            yield
            for i in range(3):
                net.got(gkv_z.at[i], k[i])
            for i in range(4):
                gkv_x[i] = gkv[z, i] + gkv_z[0, i] + gkv_z[1, i] + gkv_z[2, i]
            for i, (name, d) in enumerate((("xu", net.xu), ("xd", net.xd), ("xo", net.xo))):
                net.send(gkv_x.at[d], gkv_x.at[4 + i], k[3 + i], name)
            yield
            for i in range(3):
                net.got(gkv_x.at[4 + i], k[3 + i])
            total = gkv_x[x] + gkv_x[4] + gkv_x[5] + gkv_x[6]
            gkv_x[7, 0:16] = jnp.where(c == 0, total[0:16], total[16:32])
            gkv_x[7, 16:32] = jnp.where(c == 0, total[16:32], total[0:16])
            gkv_x[7, 32:40] = total[32:40]
            net.send(gkv_x.at[7, pl.ds(16, 24)], gkv_x.at[8, pl.ds(16, 24)], k[6], "c")
            yield
            net.got(gkv_x.at[8, pl.ds(16, 24)], k[6])
            here, there = gkv_x[7, 0:16], gkv_x[8, 16:32]
            kv_out[:, 0:128] = jnp.where(c == 0, here, there)
            kv_out[:, 128:256] = jnp.where(c == 0, there, here)
            vb_out[...] = jnp.where(c == 0, gkv_x[8, 32:40], gkv_x[7, 32:40])

        def vectors():
            k = [net.slot() for _ in range(13)]
            at = vecs.at[y, c]
            for i, name in enumerate(("yu", "yd", "yo", "c")):
                net.send(at, at, k[i], name)
            yield
            for i, d in enumerate((net.yd, net.yu, net.yo)):
                net.got(vecs.at[d, c], k[i])
                net.send(vecs.at[d, c], vecs.at[d, c], k[4 + i], "c")
            yield
            for i, d in enumerate((y, net.yd, net.yu, net.yo)):
                net.got(vecs.at[d, 1 - c], k[3 + i])
            acc = vecs[0, 0]
            for i in range(1, 8):
                acc = acc + vecs[i // 2, i % 2]
            for i in range(4):
                vec_z[i] = acc[:, i * 512 : (i + 1) * 512]
            for i, (name, d) in enumerate((("zu", net.zu), ("zd", net.zd), ("zo", net.zo))):
                net.send(vec_z.at[d], vec_z.at[4 + i], k[7 + i], name)
            yield
            for i in range(3):
                net.got(vec_z.at[4 + i], k[7 + i])
            acc = vec_z[z] + vec_z[4] + vec_z[5] + vec_z[6]
            vec_x[0] = jnp.where(yh == 0, acc[:, :256], acc[:, 256:])
            spread(net, ("xu", "xd", "xo"), vec_x.at[0], vec_x.at[pl.ds(1, 3)], k[10:])
            yield
            for i in range(3):
                net.got(vec_x.at[1 + i], k[10 + i])
            vec_out[...] = vec_x[0] + vec_x[1] + vec_x[2] + vec_x[3]

        def partner_bias():
            k = net.slot()
            net.send(bias.at[2], bias_out.at[1], k, "yo")
            bias_out[0] = bias[2]
            yield
            net.got(bias_out.at[1], k)

        last = key_value()
        next(last)
        next(rows_one, None)
        run_all(vectors(), last, partner_bias(), query, project, down, up)
        net.finish()

    n, d = tokens.shape

    def bf(*shape):
        return jax.ShapeDtypeStruct(shape, BF16)

    def f32(*shape):
        return jax.ShapeDtypeStruct(shape, F32)

    return pl.pallas_call(
        kernel,
        out_shape=(
            bf(n, d),
            f32(n, d),
            bf(n, d),
            bf(n, d),
            bf(n, 512),
            bf(n, 512),
            f32(8, 256),
            f32(2, 16, 128),
            f32(16, 256),
            f32(8, 128),
        ),
        in_specs=[INV, INV] + [ANY] * 8 + [INV, ANY] + [INV] * 5,
        out_specs=(INV,) * 10,
        scratch_shapes=[
            VMEM((4, 2, n, d), BF16),
            VMEM((4, 2, n, d), BF16),
            VMEM((4, 2, 4, n, 1024), BF16),
            VMEM((4, 2, 4, n, 1024), BF16),
            VMEM((4, 2, 4, n, 256), BF16),
            VMEM((4, 2, 4, n, 256), BF16),
            VMEM((4, 2, 4, 2, 2, 16, 128), BF16),
            VMEM((2, 512, 1024), BF16),
            VMEM((512, 256), F32),
            VMEM((512, 256), F32),
            VMEM((4, 2, n, d), BF16),
            VMEM((4, 2, n, d), BF16),
            VMEM((4, 2, 4, n, 1024), BF16),
            VMEM((4, 2, 4, n, 1024), BF16),
            VMEM((4, 2, 4, n, 256), BF16),
            VMEM((4, 2, 4, n, 256), BF16),
            VMEM((n, d), BF16),
            VMEM((4, 2, n, d), BF16),
            VMEM((n, d), F32),
            VMEM((8, d), F32),
            VMEM((512, 256), BF16),
            VMEM((2, 2, 2, 256, 128), BF16),
            VMEM((2, 128, 512), F32),
            VMEM((512, 256), BF16),
            VMEM((3, 64, 256), BF16),
            VMEM((4, 128, 128), BF16),
            VMEM((4, 4, 40, 128), F32),
            VMEM((3, 4, 40, 128), F32),
            VMEM((9, 40, 128), F32),
            VMEM((3, 16, 128), F32),
            VMEM((3, 16, 128), F32),
            VMEM((3, 16, 128), F32),
            VMEM((4, 2, 8, d), F32),
            VMEM((7, 8, 512), F32),
            VMEM((4, 8, 256), F32),
            pltpu.SemaphoreType.DMA((24,)),
        ]
        + scatter_scratch(n, d)
        + scatter_scratch(n, d)
        + plane_scratch(n, 512)
        + plane_scratch(n, 512)
        + plane_scratch(n, 128)
        + plane_scratch(n, 128)
        + [VMEM(s, BF16) for s in ((2, 4, n, 256), (2, 4, n, 256), (2, 4, n, 512), (2, 4, n, 512))]
        + [VMEM(s, BF16) for s in ((2, n, 256), (2, n, 256), (2, n, 512), (2, n, 512))]
        + sems(200),
        compiler_params=params(2, 62 << 20),
        name="backward",
    )(tokens, cotangent, cot_all, h2, wu, wd, wq, wo, packs, h1, q, kv, o, log_sum, x1, vec, ub)


def finish(up, down, out, query, grad_input, output, keyval, vec, bias, value_bias, best, w_query, query_bias, tau):
    def kernel(up, down, out, query, grad_input, output, keyval, vec, bias, vb, best, wq, qb, tau,
               output_o, grad_o, query_o, up_o, out_o, down_o, qb_o, ub_o, kv_o, vb_o, v0, v1, v2, v3, v4, v5, wq_o, cb_o):
        for src, dst in ((output, output_o), (grad_input, grad_o), (keyval, kv_o)):
            dst[...] = src[...]
        z, yh, x, yl, c = (lax.axis_index(a) for a in AXES)
        tp = yl * 2 + c
        dp = (z * 2 + yh) * 4 + x
        for src, dst in ((up, up_o), (down, down_o), (out, out_o), (query, query_o)):
            dst[...] = src[...].astype(F32)

        def pick(rows, count, start):
            lanes = rows.shape[1]
            hot = (
                lax.broadcasted_iota(jnp.int32, (lanes, count), 0)
                == lax.broadcasted_iota(jnp.int32, (lanes, count), 1) + start
            ).astype(F32)
            return hot, rows

        low, high = jnp.where(yh == 0, bias[0], bias[1]), jnp.where(yh == 0, bias[1], bias[0])
        exact = lax.Precision.HIGHEST
        hot, rows = pick(jnp.concatenate([low[0:8], high[0:8]], axis=0), 4, dp * 4)
        ub_o[...] = lax.dot_general(hot, rows, (((0,), (1,)), ((), ())), precision=exact, preferred_element_type=F32)
        hot, rows = pick(jnp.concatenate([low[8:10], high[8:10], low[10:14]], axis=0), 4, dp * 4)
        heads = lax.dot_general(hot, rows, (((0,), (1,)), ((), ())), precision=exact, preferred_element_type=F32)
        qb_o[...] = heads[:, 0:4]
        hot, rows = pick(vec[...], 16, x * 64 + tp * 16)
        own = jnp.dot(rows, hot, precision=exact, preferred_element_type=F32)
        for i, ref in enumerate((v0, v1, v2, v3, v4, v5)):
            ref[...] = own[i : i + 1]
        lane = lax.broadcasted_iota(jnp.int32, (1, 128), 1)
        vb_o[...] = splat(vb[0:1], lane, dp * 4 + tp)
        limit = tau[0]
        factors = jnp.zeros((1, 128), F32)
        for h in range(4):
            factor = limit / jnp.maximum(best[h // 2, 8 * (h % 2) : 8 * (h % 2) + 1], limit)
            at = slice(h * 128, (h + 1) * 128)
            wq_o[:, at] = (wq[:, at].astype(F32) * factor).astype(BF16)
            factors = jnp.where(lane == h, factor, factors)
        cb_o[...] = (qb[...].astype(F32) * factors[:, 0:4]).astype(BF16)

    n, d = output.shape

    def f32(*shape):
        return jax.ShapeDtypeStruct(shape, F32)

    shapes = (
        jax.ShapeDtypeStruct((n, d), BF16),
        f32(n, d),
        f32(n, 512),
        f32(n, d),
        f32(n, 512),
        f32(n, d),
        f32(4, 4),
        f32(4, 16),
        f32(16, 256),
        f32(1, 1),
    )
    shapes += (f32(1, 16),) * 6
    shapes += (jax.ShapeDtypeStruct((n, 512), BF16), jax.ShapeDtypeStruct((4, 4), BF16))
    return pl.pallas_call(
        kernel,
        out_shape=shapes,
        in_specs=[INV] * 13 + [INS],
        out_specs=(INV,) * 18,
        compiler_params=pltpu.CompilerParams(vmem_limit_bytes=60 << 20),
        name="finish",
    )(up, down, out, query, grad_input, output, keyval, vec, bias, value_bias, best, w_query, query_bias, tau)


def local(
    tokens,
    cotangent,
    seg_ids,
    parents,
    tau,
    w_query,
    w_up,
    w_out,
    w_down,
    query_bias,
    up_bias,
    w_keyval,
    value_bias,
    norm1_gain,
    norm1_bias,
    norm2_gain,
    norm2_bias,
    out_bias,
    down_bias,
):
    vectors = jnp.pad(value_bias.reshape(1, 1), ((6, 9), (0, 15)))
    for i, one in enumerate((norm1_gain, norm1_bias, norm2_gain, norm2_bias, out_bias, down_bias)):
        vectors = vectors + jnp.pad(one.reshape(1, 16), ((i, 15 - i), (0, 0)))
    (cot_all, h2, wu, wd, wq, wo, wkv, h1, q, kv, o, log_sum, x1, best, vec, ub) = forward(
        tokens, cotangent, seg_ids, parents, vectors, query_bias, up_bias, w_keyval, w_query, w_out, w_up, w_down
    )
    output, grad_input, up_sum, down_sum, out_sum, query_sum, vec_sum, bias_sum, keyval_sum, vb_sum = backward(
        tokens, cotangent, cot_all, h2, wu, wd, wq, wo, wkv, h1, q, kv, o, log_sum, x1, vec, ub
    )
    outs = finish(
        up_sum, down_sum, out_sum, query_sum, grad_input, output, keyval_sum, vec_sum, bias_sum, vb_sum, best,
        w_query, query_bias, tau,
    )
    return outs[:9] + tuple(v.reshape(-1) for v in outs[9:16]) + outs[16:]


def solution(mesh):
    fine = Mesh(mesh.devices.reshape(4, 2, 4, 2, 2), AXES)
    dp, tp = ("z", "yh", "x"), ("yl", "c")
    rows, flat, weight = P(AXES, None), P(AXES), P(dp, tp)
    in_specs = (rows, rows, P(dp), P(), P()) + (weight,) * 6 + (rows,) + (flat,) * 7
    out_specs = (rows, rows) + (weight,) * 6 + (rows,) + (flat,) * 7 + (weight, weight)
    return jax.shard_map(local, mesh=fine, in_specs=in_specs, out_specs=out_specs, check_vma=False)
```

```python
import itertools

import jax
import jax.numpy as jnp
from jax import lax
from jax.experimental import pallas as pl
from jax.experimental.pallas import tpu as pltpu
from jax.sharding import Mesh, PartitionSpec as P

EPS = 1e-05
AXES = ("z", "yh", "x", "yl", "c")
F32 = jnp.float32
BF16 = jnp.bfloat16
VMEM = pltpu.VMEM
NEG = -1e30


class Net:
    def __init__(self, send_sems, recv_sems):
        self.z, self.yh, self.x, self.yl, self.c = (lax.axis_index(a) for a in AXES)
        self.y = self.yh * 2 + self.yl
        self.yu, self.yo, self.yd = (lax.rem(self.y + s, 4) for s in (1, 2, 3))
        self.xu, self.xo, self.xd = (lax.rem(self.x + s, 4) for s in (1, 2, 3))
        self.zu, self.zo, self.zd = (lax.rem(self.z + s, 4) for s in (1, 2, 3))
        up, down = lax.rem(self.yh + self.yl, 2), lax.rem(self.yh + 1 - self.yl, 2)
        self.dev = {
            "yu": {"yh": up, "yl": 1 - self.yl},
            "yd": {"yh": down, "yl": 1 - self.yl},
            "yo": {"yh": 1 - self.yh},
            "c": {"c": 1 - self.c},
            "xu": {"x": self.xu},
            "xd": {"x": self.xd},
            "xo": {"x": self.xo},
            "zu": {"z": self.zu},
            "zd": {"z": self.zd},
            "zo": {"z": self.zo},
        }
        self.send_sems, self.recv_sems = send_sems, recv_sems
        self.count = 0
        self.sent = []

    def barrier(self, names):
        sem = pltpu.get_barrier_semaphore()
        for name in names:
            pl.semaphore_signal(
                sem, inc=1, device_id=self.dev[name], device_id_type=pl.DeviceIdType.MESH
            )
        pl.semaphore_wait(sem, len(names))

    def slot(self):
        self.count += 1
        assert self.count <= self.send_sems.shape[0]
        return self.count - 1

    def copy(self, src, dst, k, name):
        return pltpu.make_async_remote_copy(
            src_ref=src,
            dst_ref=dst,
            send_sem=self.send_sems.at[k],
            recv_sem=self.recv_sems.at[k],
            device_id=self.dev[name],
            device_id_type=pl.DeviceIdType.MESH,
        )

    def send(self, src, dst, k, name):
        one = self.copy(src, dst, k, name)
        one.start()
        self.sent.append(one)

    def got(self, ref, k):
        self.copy(ref, ref, k, "c").wait_recv()

    def finish(self):
        for one in self.sent:
            one.wait_send()


def run_all(*steps):
    live = list(steps)
    while live:
        rest = []
        for one in live:
            try:
                next(one)
                rest.append(one)
            except StopIteration:
                pass
        live = rest


def in_turn(*steps):
    live = list(steps)
    while live:
        live = [one for one in live if next(one, 1) is None]
        if live:
            yield


def columns_of(ref, h):
    w = ref.shape[-1] // 2
    return ref.at[(slice(None),) * (len(ref.shape) - 1) + (pl.ds(h * w, w),)]


def group_gather(net, src, out):
    return in_turn(*(group_gather_one(net, columns_of(src, h), columns_of(out, h)) for h in range(2)))


def group_scatter(net, part, acc, from_half, from_full, whole, total, make=None):
    def one(h):
        refs = [columns_of(ref, h) for ref in (part, acc, from_half, from_full)]
        place = columns_of(whole, h)

        def keep(summed):
            place[...] = summed

        produce = None if make is None else lambda i, d: make(i, d, h)
        return group_scatter_one(net, *refs, keep, produce)

    yield from in_turn(one(0), one(1))
    total(whole[...])


def group_gather_one(net, src, out):
    y, c, yu, yd, yo = net.y, net.c, net.yu, net.yd, net.yo
    k = [net.slot() for _ in range(9)]
    half = src.shape[0] // 2
    lo, hi = pl.ds(0, half), pl.ds(half, half)
    mine = out.at[y, c]
    net.send(src, mine, k[0], "yu")
    net.send(src, mine, k[1], "yd")
    net.send(src, mine, k[2], "c")
    yield
    net.got(out.at[yd, c], k[0])
    net.send(out.at[yd, c, lo], out.at[yd, c, lo], k[3], "yu")
    net.send(out.at[yd, c], out.at[yd, c], k[4], "c")
    net.got(out.at[yu, c], k[1])
    net.send(out.at[yu, c, hi], out.at[yu, c, hi], k[5], "yd")
    net.send(out.at[yu, c], out.at[yu, c], k[6], "c")
    yield
    net.got(out.at[yo, c, lo], k[3])
    net.send(out.at[yo, c, lo], out.at[yo, c, lo], k[7], "c")
    net.got(out.at[yo, c, hi], k[5])
    net.send(out.at[yo, c, hi], out.at[yo, c, hi], k[8], "c")
    yield
    net.got(out.at[y, 1 - c], k[2])
    net.got(out.at[yd, 1 - c], k[4])
    net.got(out.at[yu, 1 - c], k[6])
    net.got(out.at[yo, 1 - c, lo], k[7])
    net.got(out.at[yo, 1 - c, hi], k[8])


def group_scatter_one(net, part, acc, from_half, from_full, total, make=None):
    y, c, yu, yd, yo = net.y, net.c, net.yu, net.yd, net.yo
    k = [net.slot() for _ in range(8)]
    n = part.shape[2]
    half = n // 2
    lo, hi = pl.ds(0, half), pl.ds(half, half)

    sent = []

    def send(src, dst, i, name):
        sent.append(net.copy(src, dst, i, name))
        sent[-1].start()

    def start(i, d):
        if make is not None:
            make(i, d)
        send(part.at[d, 1 - c], acc.at[d], k[i], "c")

    def core_sum(i, d):
        net.got(acc.at[d], k[i])
        acc[d] = acc[d] + part[d, c]

    for i, d in enumerate((yo, yu, yd)):
        start(i, d)
    yield
    core_sum(0, yo)
    send(acc.at[yo, lo], from_half.at[0], k[4], "yu")
    send(acc.at[yo, hi], from_half.at[1], k[5], "yd")
    core_sum(1, yu)
    core_sum(2, yd)
    yield
    net.got(from_half.at[0], k[4])
    acc[yu, lo] = acc[yu, lo] + from_half[0]
    send(acc.at[yu], from_full.at[0], k[6], "yu")
    net.got(from_half.at[1], k[5])
    acc[yd, hi] = acc[yd, hi] + from_half[1]
    send(acc.at[yd], from_full.at[1], k[7], "yd")
    yield
    start(3, y)
    yield
    net.got(acc.at[y], k[3])
    mine = part[y, c].astype(F32) + acc[y].astype(F32)
    net.got(from_full.at[0], k[6])
    net.got(from_full.at[1], k[7])
    for one in sent:
        one.wait_send()
    total(mine + from_full[0].astype(F32) + from_full[1].astype(F32))


def scatter_scratch(n, w):
    return [VMEM((4, n, w), BF16), VMEM((2, n // 2, w), BF16), VMEM((2, n, w), BF16), VMEM((n, w), F32)]


BOTH = slice(None)


def plane_gather(net, o, theirs=None):
    z, x, xu, xd, xo, zu, zd, zo = net.z, net.x, net.xu, net.xd, net.xo, net.zu, net.zd, net.zo
    k = [net.slot() for _ in range(16)]
    every = slice(None)
    relayed = []

    def send(at, i, name):
        net.send(o(*at), o(*at), k[i], name)

    def got(at, i):
        net.got(o(*at), k[i])

    def relay(*at):
        if theirs is not None:
            slot = net.slot()
            net.send(o(*at), o(*at), slot, "c")
            relayed.append((at, slot))

    send((z, BOTH, x, 0), 0, "xu")
    send((z, BOTH, x, 0), 1, "xd")
    send((z, BOTH, x, 1), 2, "zu")
    send((z, BOTH, x, 1), 3, "zd")
    relay(z, BOTH, x, 0)
    relay(z, BOTH, x, 1)
    yield
    got((z, BOTH, xd, 0), 0)
    send((z, 0, xd, 0), 4, "xu")
    got((zd, BOTH, x, 1), 2)
    send((zd, 0, x, 1), 6, "zu")
    got((z, BOTH, xu, 0), 1)
    send((z, 1, xu, 0), 5, "xd")
    got((zu, BOTH, x, 1), 3)
    send((zu, 1, x, 1), 7, "zd")
    for at in ((z, BOTH, xd, 0), (zd, BOTH, x, 1), (z, BOTH, xu, 0), (zu, BOTH, x, 1)):
        relay(*at)
    yield
    got((z, 0, xo, 0), 4)
    got((z, 1, xo, 0), 5)
    send((z, BOTH, every, 0), 8, "zu")
    send((z, BOTH, every, 0), 9, "zd")
    got((zo, 0, x, 1), 6)
    got((zo, 1, x, 1), 7)
    send((every, BOTH, x, 1), 10, "xu")
    send((every, BOTH, x, 1), 11, "xd")
    relay(z, BOTH, xo, 0)
    relay(zo, BOTH, x, 1)
    yield
    got((zd, BOTH, every, 0), 8)
    send((zd, 0, every, 0), 12, "zu")
    got((every, BOTH, xd, 1), 10)
    send((every, 0, xd, 1), 14, "xu")
    got((zu, BOTH, every, 0), 9)
    send((zu, 1, every, 0), 13, "zd")
    got((every, BOTH, xu, 1), 11)
    send((every, 1, xu, 1), 15, "xd")
    for at in ((zd, BOTH, every, 0), (every, BOTH, xd, 1), (zu, BOTH, every, 0), (every, BOTH, xu, 1)):
        relay(*at)
    yield
    got((zo, 0, every, 0), 12)
    got((zo, 1, every, 0), 13)
    relay(zo, BOTH, every, 0)
    got((every, 0, xo, 1), 14)
    got((every, 1, xo, 1), 15)
    relay(every, BOTH, xo, 1)
    for at, slot in relayed:
        net.got(theirs(*at), slot)


def add_into(dst, *others):
    for index in itertools.product(*[range(n) for n in dst.shape[:-2]]):
        at = index + (slice(None), slice(None))
        total = dst[at]
        for other in others:
            total = total + other[at]
        dst[at] = total


def plane_scatter(net, g, tmp):
    z, x, xu, xd, xo, zu, zd, zo = net.z, net.x, net.xu, net.xd, net.xo, net.zu, net.zd, net.zo
    t1, t2, u1, u2, t3, t4, u3, u4 = tmp
    k = [net.slot() for _ in range(16)]
    every = slice(None)

    def send(src, dst, i, name):
        net.send(src, dst, k[i], name)

    def got(ref, i):
        net.got(ref, k[i])

    send(g(zo, 0, every, 0), t1.at[0], 0, "zu")
    send(g(zo, 1, every, 0), t1.at[1], 1, "zd")
    send(g(every, 0, xo, 1), t2.at[0], 2, "xu")
    send(g(every, 1, xo, 1), t2.at[1], 3, "xd")
    yield
    got(t1.at[0], 0)
    add_into(g(zu, 0, every, 0), t1.at[0])
    send(g(zu, BOTH, every, 0), u1.at[0], 4, "zu")
    got(t2.at[0], 2)
    add_into(g(every, 0, xu, 1), t2.at[0])
    send(g(every, BOTH, xu, 1), u2.at[0], 6, "xu")
    got(t1.at[1], 1)
    add_into(g(zd, 1, every, 0), t1.at[1])
    send(g(zd, BOTH, every, 0), u1.at[1], 5, "zd")
    got(t2.at[1], 3)
    add_into(g(every, 1, xd, 1), t2.at[1])
    send(g(every, BOTH, xd, 1), u2.at[1], 7, "xd")
    yield
    got(u1.at[0], 4)
    got(u1.at[1], 5)
    add_into(g(z, BOTH, every, 0), u1.at[0], u1.at[1])
    send(g(z, 0, xo, 0), t3.at[0], 8, "xu")
    send(g(z, 1, xo, 0), t3.at[1], 9, "xd")
    got(u2.at[0], 6)
    got(u2.at[1], 7)
    add_into(g(every, BOTH, x, 1), u2.at[0], u2.at[1])
    send(g(zo, 0, x, 1), t4.at[0], 10, "zu")
    send(g(zo, 1, x, 1), t4.at[1], 11, "zd")
    yield
    got(t3.at[0], 8)
    add_into(g(z, 0, xu, 0), t3.at[0])
    send(g(z, BOTH, xu, 0), u3.at[0], 12, "xu")
    got(t4.at[0], 10)
    add_into(g(zu, 0, x, 1), t4.at[0])
    send(g(zu, BOTH, x, 1), u4.at[0], 14, "zu")
    got(t3.at[1], 9)
    add_into(g(z, 1, xd, 0), t3.at[1])
    send(g(z, BOTH, xd, 0), u3.at[1], 13, "xd")
    got(t4.at[1], 11)
    add_into(g(zd, 1, x, 1), t4.at[1])
    send(g(zd, BOTH, x, 1), u4.at[1], 15, "zd")
    yield
    got(u3.at[0], 12)
    got(u3.at[1], 13)
    add_into(g(z, BOTH, x, 0), u3.at[0], u3.at[1])
    got(u4.at[0], 14)
    got(u4.at[1], 15)
    add_into(g(z, BOTH, x, 1), u4.at[0], u4.at[1])


def plane_scratch(n, w):
    return [
        VMEM((2, 4, n, w), BF16),
        VMEM((2, 4, n, w), BF16),
        VMEM((2, 2, 4, n, w), BF16),
        VMEM((2, 4, 2, n, w), BF16),
        VMEM((2, n, w), BF16),
        VMEM((2, n, w), BF16),
        VMEM((2, 2, n, w), BF16),
        VMEM((2, 2, n, w), BF16),
    ]


def column_view(ref):
    w = ref.shape[-1] // 2

    def view(zz, half, xx, part):
        return ref.at[zz, half, xx, :, pl.ds(part * w, w)]

    return view


def sems(n):
    return [pltpu.SemaphoreType.DMA((n,)), pltpu.SemaphoreType.DMA((n,))]


def params(cid, limit=56 << 20):
    return pltpu.CompilerParams(collective_id=cid, has_side_effects=True, vmem_limit_bytes=limit)


ANY = pl.BlockSpec(memory_space=pl.ANY)
INV = pl.BlockSpec(memory_space=pltpu.VMEM)
INS = pl.BlockSpec(memory_space=pltpu.SMEM)
PLANE = ("xu", "xd", "zu", "zd")
RING = ("yu", "yd", "c")


class Ticks:
    def __init__(self, *steps):
        self.steps = list(steps)

    def tick(self, count=1):
        for _ in range(count):
            for one in self.steps:
                next(one, None)


def weight_gather(net, weight, out, local):
    z, yh, x = net.z, net.yh, net.x
    n, w = weight.shape[0], weight.shape[1] // 2
    k = net.slot()

    def half(which):
        return weight.at[:, pl.ds(pl.multiple_of(which * w, 128), w)]

    mine = pltpu.make_async_copy(half(yh), out.at[z, yh, x, pl.ds(0, n)], local)
    mine.start()
    net.send(half(1 - yh), out.at[z, yh, x, pl.ds(0, n)], k, "yo")
    yield
    mine.wait()
    net.got(out.at[z, 1 - yh, x, pl.ds(0, n)], k)
    yield from plane_gather(net, column_view(out))


def splat(row, lane, at):
    return jnp.sum(jnp.where(lane == at, row, 0.0), axis=1, keepdims=True)


def place_of(segs, parents, block):
    lane = lax.broadcasted_iota(jnp.int32, (1, 128), 1)
    seg = splat(segs, lane, block)
    lanes = lane.astype(F32)
    parent = splat(parents, lanes, seg)
    trunk = splat(parents, lanes, parent)
    leaf = (seg >= 10.0).astype(F32)
    branch = (seg >= 2.0).astype(F32)
    above = [(splat(segs, lane, b) == parent).astype(F32) * leaf for b in range(16, 32)]
    return trunk, leaf, branch, above


def wide(value):
    return jnp.broadcast_to(value, (1, 128)).astype(BF16)


def trunk_block(kv, which, i, trunk):
    one = wide(trunk)
    return kv[which, 0, i // 4, i % 4] * (1 - one) + kv[which, 1, i // 4, i % 4] * one


def parent_block(kv, which, above):
    total = kv[which, 2, 0, 0] * wide(above[0])
    for j in range(1, 16):
        total = total + kv[which, 2 + j // 8, j // 4 % 2, j % 4] * wide(above[j])
    return total


NT = (((1,), (1,)), ((), ()))
TN = (((0,), (0,)), ((), ()))
SCALE = 128**-0.5
LOG2E = 1.4426950408889634


def attend(b, z, x, q, kv, segs, parents, scores, o, log_sum):
    lane = (lax.broadcasted_iota(jnp.int32, (256, 512), 1) & 255).astype(F32)
    ahead = lax.broadcasted_iota(jnp.int32, (256, 512), 0).astype(F32) - lane
    block = z * 8 + b * 4 + x
    trunk, leaf, branch, above = place_of(segs, parents, block)
    rows = pl.ds(b * 256, 256)
    both = jnp.concatenate([q[rows, :128], q[rows, 128:]], axis=0)
    start = block.astype(F32) - 8.0 * trunk

    def score(key):
        return lax.dot_general(key, both, NT, preferred_element_type=F32) * (SCALE * LOG2E)

    def trunk_score(i, top):
        gap = (start - i.astype(F32)) * 256.0
        s = jnp.where(ahead <= gap, score(trunk_block(kv, 0, i, trunk)), NEG)
        scores[i] = s
        return jnp.maximum(top, jnp.max(s, axis=0, keepdims=True))

    top = lax.fori_loop(0, 8, trunk_score, jnp.full((1, 512), NEG, F32))
    s = score(parent_block(kv, 0, above)) + (leaf - 1.0) * 1e30
    scores[8] = s
    top = jnp.maximum(top, jnp.max(s, axis=0, keepdims=True))
    s = jnp.where(ahead <= 0.0, score(kv[0, z, b, x]), NEG) + (branch - 1.0) * 1e30
    scores[9] = s
    top = jnp.maximum(top, jnp.max(s, axis=0, keepdims=True))

    def weigh(i, value, carry):
        acc, total = carry
        w = jnp.exp2(scores[i] - top)
        acc = acc + lax.dot_general(value, w.astype(BF16), TN, preferred_element_type=F32)
        return acc, total + jnp.sum(w, axis=0, keepdims=True)

    carry = (jnp.zeros((128, 512), F32), jnp.zeros((1, 512), F32))
    carry = lax.fori_loop(0, 8, lambda i, c: weigh(i, trunk_block(kv, 1, i, trunk), c), carry)
    carry = weigh(8, parent_block(kv, 1, above), carry)
    acc, total = weigh(9, kv[1, z, b, x], carry)
    heads = (acc / total).T.astype(BF16)
    o[rows, :128] = heads[:256]
    o[rows, 128:] = heads[256:]
    log_sum[b] = jnp.broadcast_to(top + jnp.log2(total), (8, 512))
    return top * (1.0 / LOG2E)


def one_hot(rows, lanes, hit):
    row = lax.broadcasted_iota(jnp.int32, (rows, lanes), 0)
    lane = lax.broadcasted_iota(jnp.int32, (rows, lanes), 1)
    return hit(row, lane).astype(F32).astype(BF16)


def forward(tokens, cotangent, seg_ids, parents, vectors, query_bias, up_bias, w_keyval, w_query, w_out, w_up, w_down):
    def kernel(tok, cot, seg_in, par_in, vec_in, qb_in, ub_in, wkv_in, wq_in, wo_in, wu_in, wd_in,
               cot_out, h2, wu, wd, wq_out, wo_out, wkv_out, h1_out, q_out, kv_out, o, log_sum, x1, best, vec, ub,
               tok_all, h1, wkv, wq, wo, q, kv, scores, part, own, mine, got, pack, pairs, halves, tiles, local,
               *rest):
        *scratch, ss, rs = rest
        net = Net(ss, rs)
        z, yh, x, yl, c, y = net.z, net.yh, net.x, net.yl, net.c, net.y
        starts = [
            pltpu.make_async_copy(src, dst, local.at[i])
            for i, (src, dst) in enumerate(((tok, tok_all.at[y, c]), (cot, cot_out.at[y, c])))
        ]
        for one in starts:
            one.start()
        row = lax.broadcasted_iota(jnp.int32, (16, 128), 0)
        lane = lax.broadcasted_iota(jnp.int32, (16, 128), 1)
        periodic = jnp.dot(vec_in[...], one_hot(16, 128, lambda r, l: l % 16 == r), preferred_element_type=F32)
        first = jnp.dot(vec_in[...], one_hot(16, 128, lambda r, l: r == 0), preferred_element_type=F32)
        tile = jnp.where(row < 6, periodic, first)
        tile = jnp.where(row == 7, seg_in[0].astype(F32), tile).astype(BF16)
        for i in range(2):
            pack[i, 0:16] = wkv_in[:, i * 128 : (i + 1) * 128]
            pack[i, 16:32] = tile
        four = one_hot(4, 128, lambda r, l: l % 4 == r)
        heads = lax.dot_general(qb_in[...], four, TN, preferred_element_type=F32)
        units = lax.dot_general(ub_in[...], four, TN, preferred_element_type=F32)
        blank = jnp.zeros((6, 128), F32)
        for i in range(2):
            halves[i] = jnp.concatenate([units[8 * i : 8 * i + 8], heads[2 * i : 2 * i + 2], blank], axis=0).astype(BF16)
        pairs[yh, yl, c] = jnp.where(c == 0, pack[0], pack[1])
        net.barrier(PLANE + RING + ("yo", "xo", "zo"))

        query = weight_gather(net, wq_in, wq, local.at[4])
        later = Ticks(weight_gather(net, wu_in, wu, local.at[6]), weight_gather(net, wd_in, wd, local.at[7]))
        project_weight = weight_gather(net, wo_in, wo, local.at[5])
        toks = group_gather(net, tok, tok_all)
        ks = [net.slot() for _ in range(11)]
        net.send(pack.at[1 - c], pairs.at[yh, yl, c], ks[0], "c")
        net.send(halves.at[1 - yh], halves.at[2], ks[4], "yo")
        next(query)
        net.got(pairs.at[yh, yl, 1 - c], ks[0])
        for i, name in enumerate(("yu", "yd", "yo")):
            net.send(pairs.at[yh, yl], pairs.at[yh, yl], ks[1 + i], name)
        next(toks)
        next(query)
        net.got(halves.at[2], ks[4])
        here, there = jnp.where(yh == 0, halves[0], halves[1]), halves[2]
        low, high = jnp.where(yh == 0, here, there), jnp.where(yh == 0, there, here)
        tiles[z, x, 1] = jnp.where((lane // 16) % 2 == 0, low.astype(F32), high.astype(F32)).astype(BF16)
        for i, d in enumerate((net.yd, net.yu, net.yo)):
            net.got(pairs.at[d // 2, lax.rem(d, 2)], ks[1 + i])
        merged = jnp.zeros((16, 128), F32)
        for i in range(8):
            high, tp = i // 4, i % 4
            one = pairs[high, tp // 2, tp % 2, 16:32].astype(F32)
            hit = (row < 6) & (lane // 16 == i)
            hit = hit | ((row == 6) & (lane // 16 % 2 == high) & (lane % 4 == tp))
            hit = hit | ((row == 7) & ((lane // 4) % 2 == high))
            merged = jnp.where(hit, one, merged)
            wkv[z, high, x, tp // 2, tp % 2] = pairs[high, tp // 2, tp % 2, 0:16]
        tiles[z, x, 0] = merged.astype(BF16)
        for i, name in enumerate(("xu", "xd", "xo")):
            net.send(tiles.at[z, x], tiles.at[z, x], ks[5 + i], name)

        def key_view(zz, half, xx, part):
            return wkv.at[zz, part, xx, pl.ds(0, 2) if half == BOTH else half]

        keyval = plane_gather(net, key_view)
        next(keyval)
        next(project_weight)
        later.tick()
        for i, d in enumerate((net.xd, net.xu, net.xo)):
            net.got(tiles.at[z, d], ks[5 + i])
        for i, name in enumerate(("zu", "zd", "zo")):
            net.send(tiles.at[z], tiles.at[z], ks[8 + i], name)
        next(keyval)
        next(query)
        next(toks)
        next(keyval)
        next(query)
        next(project_weight)
        later.tick()
        next(toks)
        next(keyval)
        next(query)
        next(project_weight)
        for i, d in enumerate((net.zd, net.zu, net.zo)):
            net.got(tiles.at[d], ks[8 + i])

        value_bias = jnp.zeros((16, 128), F32)
        biases = jnp.zeros((16, 128), F32)
        segs = jnp.zeros((16, 128), F32)
        for zz in range(4):
            come = [tiles[zz, xx, 0].astype(F32) for xx in range(4)]
            turned = [pltpu.roll(one, 64, 1) for one in come]
            for xx in range(4):
                at = (lane // 32 == zz) & ((lane // 4) % 4 == xx)
                value_bias = jnp.where(at, come[xx], value_bias)
                biases = jnp.where(at, tiles[zz, xx, 1].astype(F32), biases)
                segs = jnp.where((lane // 8 == zz) & (lane % 4 == xx), come[xx], segs)
            for high in range(2):
                for pair in range(2):
                    even = come[2 * pair] if high == 0 else turned[2 * pair]
                    odd = turned[2 * pair + 1] if high == 0 else come[2 * pair + 1]
                    j = (zz * 2 + high) * 2 + pair
                    vec[:, j * 128 : (j + 1) * 128] = jnp.where(lane < 64, even, odd)
        value_bias = value_bias[6:7]
        segs = segs[7:8]
        vec[8:9, 0:128] = segs
        ub[...] = biases[0:8]
        query_bias = jnp.concatenate([biases[8:9], biases[9:10]], axis=1)
        parent = jnp.zeros((1, 128), F32)
        for i in range(18):
            parent = jnp.where(lane[0:1] == i, par_in[i].astype(F32), parent)
        vec[9:10, 0:128] = parent
        for _ in toks:
            pass
        starts[0].wait()

        gain1, shift1 = vec[0:1], vec[1:2]

        def norm_rows(i, carry):
            rows = tok_all[i // 2, i % 2].astype(F32)
            h1[pl.ds(pl.multiple_of(i * 64, 64), 64)] = (normed(rows)[0] * gain1 + shift1).astype(BF16)
            return carry

        lax.fori_loop(0, 8, norm_rows, 0)
        next(project_weight)
        for _ in query:
            pass
        for _ in keyval:
            pass

        def project(i, carry):
            rows = pl.ds(pl.multiple_of(i * 256, 256), 256)
            h = h1[rows]
            weight = wq[...].reshape(2048, 256)
            q[rows] = (jnp.dot(h, weight, preferred_element_type=F32) + query_bias).astype(BF16)
            weight = wkv[...].reshape(2048, 128)
            shift = value_bias * c.astype(F32)
            kv[c, z, i, x] = (jnp.dot(h, weight, preferred_element_type=F32) + shift).astype(BF16)
            return carry

        lax.fori_loop(0, 2, project, 0)

        def keys_of(r):
            def rows(half):
                return pl.ds(r * 128, 128) if half == BOTH else pl.ds(r * 128 + 64 * half, 64)

            def view(zz, half, xx, part):
                return kv.at[c, zz, part, xx, rows(half)]

            def their_view(zz, half, xx, part):
                return kv.at[1 - c, zz, part, xx, rows(half)]

            return plane_gather(net, view, their_view)

        keys = in_turn(keys_of(0), keys_of(1))
        cots = group_gather(net, cot, cot_out)
        next(keys)
        later.tick()
        next(cots)
        next(keys)
        next(project_weight)
        next(keys)
        next(cots)
        next(keys)
        later.tick()
        next(cots)
        for _ in keys:
            pass

        saves = [
            pltpu.make_async_copy(src, dst, local.at[8 + i])
            for i, (src, dst) in enumerate(
                ((wq, wq_out), (wkv, wkv_out), (h1, h1_out), (q, q_out), (kv, kv_out), (wo, wo_out))
            )
        ]
        for one in saves[:5]:
            one.start()
        top = attend(0, z, x, q, kv, segs, parent, scores, o, log_sum)
        top = jnp.maximum(top, attend(1, z, x, q, kv, segs, parent, scores, o, log_sum))
        for h in range(2):
            mine[0, 8 * h : 8 * h + 8] = jnp.full((8, 128), jnp.max(top[:, h * 256 : (h + 1) * 256]), F32)
        for _ in project_weight:
            pass
        saves[5].start()

        def project_out(i, d, h):
            rows = o[pl.ds(pl.multiple_of(d * 128, 128), 128)]
            for j in (2 * h, 2 * h + 1):
                weight = wo[j].reshape(512, 256)
                out = lax.dot_general(rows, weight, NT, preferred_element_type=F32).astype(BF16)
                part[d, 0, :, j * 512 : (j + 1) * 512] = out[:64]
                part[d, 1, :, j * 512 : (j + 1) * 512] = out[64:]

        def total(summed):
            value = tok[...].astype(F32) + (summed + vec[4:5])
            x1[...] = value
            own[...] = (normed(value)[0] * vec[2:3] + vec[3:4]).astype(BF16)

        rows = group_scatter(net, part, *scratch, total, project_out)
        largest = heads_max(net, mine, got, best)
        for _ in range(3):
            next(rows)
            next(largest)
        next(rows)
        later.tick()
        next(rows, None)
        me = pltpu.make_async_copy(own, h2.at[y, c], local.at[14])
        me.start()
        spreading = group_gather(net, own, h2)
        next(spreading)
        for _ in largest:
            pass
        for _ in spreading:
            pass
        me.wait()
        for _ in cots:
            pass
        later.tick()
        starts[1].wait()
        for one in saves:
            one.wait()
        net.finish()

    n, d = tokens.shape
    rows = jax.ShapeDtypeStruct((4, 2, n, d), BF16)

    def bf(*shape):
        return jax.ShapeDtypeStruct(shape, BF16)

    def f32(*shape):
        return jax.ShapeDtypeStruct(shape, F32)

    return pl.pallas_call(
        kernel,
        out_shape=(
            rows,
            rows,
            bf(4, 2, 4, n, 1024),
            bf(4, 2, 4, n, 1024),
            bf(4, 2, 4, n, 256),
            bf(4, 2, 4, n, 256),
            bf(4, 2, 4, 2, 2, 16, 128),
            bf(512, d),
            bf(512, 256),
            bf(2, 4, 2, 4, 256, 128),
            bf(512, 256),
            f32(2, 8, 512),
            f32(n, d),
            f32(2, 16, 128),
            f32(16, d),
            f32(8, 128),
        ),
        in_specs=[INV, INV, INS, INS] + [INV] * 8,
        out_specs=(ANY,) * 10 + (INV,) * 6,
        scratch_shapes=[
            VMEM((4, 2, n, d), BF16),
            VMEM((512, d), BF16),
            VMEM((4, 2, 4, 2, 2, 16, 128), BF16),
            VMEM((4, 2, 4, n, 256), BF16),
            VMEM((4, 2, 4, n, 256), BF16),
            VMEM((512, 256), BF16),
            VMEM((2, 4, 2, 4, 256, 128), BF16),
            VMEM((10, 256, 512), F32),
            VMEM((4, 2, n, d), BF16),
            VMEM((n, d), BF16),
            VMEM((5, 16, 128), F32),
            VMEM((7, 16, 128), F32),
            VMEM((2, 32, 128), BF16),
            VMEM((2, 2, 2, 32, 128), BF16),
            VMEM((3, 16, 128), BF16),
            VMEM((4, 4, 2, 16, 128), BF16),
            pltpu.SemaphoreType.DMA((15,)),
        ]
        + scatter_scratch(n, d)
        + sems(280),
        compiler_params=params(1),
        name="forward",
    )(tokens, cotangent, seg_ids, parents, vectors, query_bias, up_bias, w_keyval, w_query, w_out, w_up, w_down)


def normed(values):
    centred = values - jnp.mean(values, axis=-1, keepdims=True)
    inverse = lax.rsqrt(jnp.mean(centred * centred, axis=-1, keepdims=True) + EPS)
    return centred * inverse, inverse


def norm_back(grad, norm, inverse, gain):
    scaled = grad * gain
    return inverse * (
        scaled
        - jnp.mean(scaled, axis=-1, keepdims=True)
        - norm * jnp.mean(scaled * norm, axis=-1, keepdims=True)
    )


def heads_max(net, mine, got, best):
    for i, (up, down) in enumerate((("xu", "xd"), ("zu", "zd"))):
        k = [net.slot() for _ in range(3)]
        a, b, d = got.at[3 * i], got.at[3 * i + 1], got.at[3 * i + 2]
        net.send(mine.at[2 * i], a, k[0], up)
        net.send(mine.at[2 * i], b, k[1], down)
        yield
        net.got(a, k[0])
        net.got(b, k[1])
        mine[2 * i + 1] = jnp.maximum(mine[2 * i], jnp.maximum(a[...], b[...]))
        net.send(mine.at[2 * i + 1], d, k[2], up)
        yield
        net.got(d, k[2])
        mine[2 * i + 2] = jnp.maximum(mine[2 * i + 1], d[...])
    k = net.slot()
    net.send(mine.at[4], got.at[6], k, "yo")
    yield
    net.got(got.at[6], k)
    best[net.yh] = mine[4]
    best[1 - net.yh] = got[6]


def weight_scatter(net, g, tmp, out):
    z, yh, x = net.z, net.yh, net.x
    w = g.shape[-1]
    k = net.slot()
    yield from plane_scatter(net, column_view(g), tmp)
    mine = out.at[:, pl.ds(pl.multiple_of(yh * w, 128), w)]
    net.send(g.at[z, 1 - yh, x], mine, k, "yo")
    out[:, pl.ds(pl.multiple_of(yh * w, 128), w)] = g[z, yh, x]
    yield
    net.got(out.at[:, pl.ds(pl.multiple_of((1 - yh) * w, 128), w)], k)


def smooth_gate(u):
    scale = 0.7978845608028654
    square = u * u
    t = jnp.tanh(scale * u * (1.0 + 0.044715 * square))
    half = 0.5 * (1.0 + t)
    slope = half + 0.5 * u * (1.0 - t * t) * scale * (1.0 + 0.134145 * square)
    return u * half, slope


def piece(ref, which, zz, yy, xx):
    return jnp.concatenate(
        [ref[zz, yy, xx, :, (which * 4 + r) * 128 : (which * 4 + r + 1) * 128] for r in range(4)], axis=0
    )


def put_piece(ref, which, zz, yy, xx, value):
    for r in range(4):
        ref[zz, yy, xx, :, (which * 4 + r) * 128 : (which * 4 + r + 1) * 128] = value[r * 64 : (r + 1) * 64]


def attend_back(z, x, q, kv, o, go, log_sum, segs, parents, grad, lone, dq_sum, dq):
    lane = (lax.broadcasted_iota(jnp.int32, (256, 512), 1) & 255).astype(F32)
    ahead = lax.broadcasted_iota(jnp.int32, (256, 512), 0).astype(F32) - lane
    places = [place_of(segs, parents, z * 8 + b * 4 + x) for b in range(2)]

    def stacked(ref, b):
        return jnp.concatenate([ref[b * 256 : b * 256 + 256, :128], ref[b * 256 : b * 256 + 256, 128:]], axis=0)

    logs, inner = [], []
    for b in range(2):
        logs.append(log_sum[b, 0:1])
        inner.append(
            jnp.sum((stacked(go, b).astype(F32) * stacked(o, b).astype(F32)).T, axis=0, keepdims=True)
        )

    def one(b, key, value, masked, first):
        both, up = stacked(q, b), stacked(go, b)
        s = masked(lax.dot_general(key, both, NT, preferred_element_type=F32) * (SCALE * LOG2E))
        p = jnp.exp2(s - logs[b])
        dp = lax.dot_general(value, up, NT, preferred_element_type=F32)
        ds = (p * (dp - inner[b])).astype(BF16)
        more = lax.dot_general(key, ds, TN, preferred_element_type=F32)
        dq_sum[b] = more if first else dq_sum[b] + more
        dk = jnp.dot(ds, both, preferred_element_type=F32) * SCALE
        dv = jnp.dot(p.astype(BF16), up, preferred_element_type=F32)
        return dk.astype(BF16), dv.astype(BF16)

    for b in range(2):
        trunk, leaf, branch, above = places[b]
        lone[b, 0, 0], lone[b, 0, 1] = one(
            b,
            piece(kv, 0, z, b, x),
            piece(kv, 1, z, b, x),
            lambda s: jnp.where(ahead <= 0.0, s, NEG) + (branch - 1.0) * 1e30,
            True,
        )
        key, value = (
            sum(piece(kv, w, 2 + j // 8, j // 4 % 2, j % 4) * wide(above[j]) for j in range(16)) for w in range(2)
        )
        lone[b, 1, 0], lone[b, 1, 1] = one(b, key, value, lambda s: s + (leaf - 1.0) * 1e30, False)
    yield

    for j in range(16):
        own = [
            wide((z * 8 + b * 4 + x == 16 + j).astype(F32) * jnp.ones((1, 1), F32)) for b in range(2)
        ]
        for w in range(2):
            value = sum(lone[b, 0, w] * own[b] + lone[b, 1, w] * wide(places[b][3][j]) for b in range(2))
            put_piece(grad, w, 2 + j // 8, j // 4 % 2, j % 4, value)

    def trunk_one(i, carry):
        yy, xx = i // 4, i % 4
        totals = None
        for b in range(2):
            trunk = places[b][0]
            second = wide(trunk)
            first = 1 - second
            key, value = (piece(kv, w, 0, yy, xx) * first + piece(kv, w, 1, yy, xx) * second for w in range(2))
            start = (z * 8 + b * 4 + x).astype(F32) - 8.0 * trunk
            gap = (start - i.astype(F32)) * 256.0
            dk, dv = one(b, key, value, lambda s: jnp.where(ahead <= gap, s, NEG), False)
            parts = [dk * first, dv * first, dk * second, dv * second]
            totals = parts if totals is None else [t + p for t, p in zip(totals, parts)]
        for t in range(2):
            for w in range(2):
                put_piece(grad, w, t, yy, xx, totals[2 * t + w])
        return carry

    for i in range(0, 8, 2):
        lax.fori_loop(i, i + 2, trunk_one, 0)
        yield
    for b in range(2):
        rows = (dq_sum[b] * SCALE).T.astype(BF16)
        dq[b * 256 : b * 256 + 256, :128] = rows[:256]
        dq[b * 256 : b * 256 + 256, 128:] = rows[256:]


def spread(net, names, src, dst, k):
    for i, name in enumerate(names):
        net.send(src, dst.at[i], k[i], name)


def all_sums(net, mine, near, far):
    k = [net.slot() for _ in range(6)]
    spread(net, ("xu", "xd", "xo"), mine.at[0], near, k)
    yield
    for i in range(3):
        net.got(near.at[i], k[i])
    mine[1] = mine[0] + near[0] + near[1] + near[2]
    spread(net, ("zu", "zd", "zo"), mine.at[1], far, k[3:])
    yield
    for i in range(3):
        net.got(far.at[i], k[3 + i])
    mine[2] = mine[1] + far[0] + far[1] + far[2]


def backward(tokens, cotangent, cot_all, h2, wu, wd, wq, wo, packs, h1, q, kv, o, log_sum, x1, vec, ub):
    def kernel(tok, cot, cot_in, h2_in, wu_in, wd_in, wq_in, wo_in, packs_in, h1_in, q, kv_in, o, log_sum,
               x1, vec, ub_in,
               output, grad_input, up_out, down_out, wo_out, wq_out, vec_out, bias_out, kv_out, vb_out,
               h2, cots, wu, wd, wq, wo, packs, adu, us, das, part, part_mlp, gu, gd, gwo, gq, own, dz, dx1, sums, go,
               lone, dq_sum, dq, dkv_from, dkv, gkv, gkv_z, gkv_x, bias, bias_x, bias_z, vecs, vec_z, vec_x,
               local, *rest):
        *scratch, ss, rs = rest
        first, second, tmp_u, tmp_d, tmp_o, tmp_q, tmp_k, tmp_v = (
            scratch[:4],
            scratch[4:8],
            scratch[8:16],
            scratch[16:24],
            scratch[24:32],
            scratch[32:40],
            scratch[40:48],
            scratch[48:56],
        )
        net = Net(ss, rs)
        z, yh, x, yl, c, y = net.z, net.yh, net.x, net.yl, net.c, net.y

        def columns(ref, j):
            return ref.at[:, :, :, :, pl.ds(j * 256, 256)]

        def load(src, dst, i):
            one = pltpu.make_async_copy(src, dst, local.at[i])
            one.start()
            return one

        load(h2_in, h2, 0)
        load(columns(wu_in, 0), columns(wu, 0), 2)
        load(cot_in, cots, 1)
        load(columns(wd_in, 0), columns(wd, 0), 6)
        for j in range(1, 4):
            load(columns(wu_in, j), columns(wu, j), 2 + j)
            load(columns(wd_in, j), columns(wd, j), 6 + j)
        loads = [load(wo_in, wo, 10), load(wq_in, wq, 11)]
        loads.append(load(packs_in, packs, 12))
        net.barrier(PLANE + RING + ("yo", "xo", "zo"))
        pltpu.make_async_copy(h2_in, h2, local.at[0]).wait()
        pltpu.make_async_copy(cot_in, cots, local.at[1]).wait()

        def hidden(j, carry):
            at = pl.ds(pl.multiple_of(j * 256, 256), 256)
            there = pl.ds(0, 4), pl.ds(0, 2), pl.ds(0, 4), pl.ds(0, 64), at
            pltpu.make_async_copy(wu_in.at[there], wu.at[there], local.at[2 + j]).wait()
            us[...] = jnp.dot(
                h2[...].reshape(512, 2048), wu[there].reshape(2048, 256), preferred_element_type=F32
            )
            pltpu.make_async_copy(wd_in.at[there], wd.at[there], local.at[6 + j]).wait()
            das[...] = jnp.dot(
                cots[...].reshape(512, 2048), wd[there].reshape(2048, 256), preferred_element_type=F32
            )
            bias_row = jnp.concatenate([ub_in[pl.ds(2 * j, 1)], ub_in[pl.ds(2 * j + 1, 1)]], axis=1)

            def gate(i, total):
                rows = pl.ds(pl.multiple_of(i * 64, 64), 64)
                value, slope = smooth_gate(us[rows] + bias_row)
                adu[0, rows, at] = value.astype(BF16)
                du = (das[rows] * slope).astype(BF16)
                adu[1, rows, at] = du
                return total + jnp.sum(du.astype(F32), axis=0, keepdims=True)

            total = lax.fori_loop(0, 8, gate, jnp.zeros((1, 256), F32))
            bias[0, pl.ds(2 * j, 1)] = total[:, :128]
            bias[0, pl.ds(2 * j + 1, 1)] = total[:, 128:]
            return carry

        lax.fori_loop(0, 4, hidden, 0)

        def projected(dst, d, rows, weight, h=None):
            def column(j, carry):
                out = lax.dot_general(rows, weight(j), NT, preferred_element_type=F32).astype(BF16)
                at = pl.ds(pl.multiple_of(j * 512, 512), 512)
                dst[d, 0, :, at] = out[:64]
                dst[d, 1, :, at] = out[64:]
                return carry

            lax.fori_loop(0 if h is None else 2 * h, 4 if h is None else 2 * h + 2, column, 0)

        def ring_rows(d):
            return pl.ds(pl.multiple_of(d * 128, 128), 128)

        def make_two(i, d, h):
            projected(part, d, adu[1, ring_rows(d)], lambda j: wu[j].reshape(512, 1024), h)

        def total_two(summed):
            norm, inverse = normed(x1[...])
            grad = cot[...].astype(F32) + norm_back(summed, norm, inverse, vec[2:3])
            dx1[...] = grad
            rounded = grad.astype(BF16)
            own[...] = rounded
            values = (summed * norm, summed, rounded.astype(F32), cot[...].astype(F32))
            for i, v in enumerate(values):
                sums[2 + i : 3 + i] = jnp.sum(v, axis=0, keepdims=True)

        def outer(dst, left, right):
            def block(j, carry):
                out = lax.dot_general(left(j), right, TN, preferred_element_type=F32)
                dst[j] = out.astype(BF16).reshape(2, 4, 64, right.shape[1])
                return carry

            lax.fori_loop(0, 4, block, 0)

        def wide_outer(dst, left, which):
            def block(i, carry):
                j, w = i // 2, i % 2
                at = pl.ds(pl.multiple_of(w * 512, 512), 512)
                out = lax.dot_general(
                    left[:, :, :, pl.ds(pl.multiple_of(j * 512, 512), 512)].reshape(512, 512),
                    adu[which, :, at],
                    TN,
                    preferred_element_type=F32,
                )
                dst[j, :, :, :, at] = out.astype(BF16).reshape(2, 4, 64, 512)
                return carry

            lax.fori_loop(0, 8, block, 0)

        rows_two = group_scatter(net, part, *first, total_two, make_two)
        next(rows_two)
        next(rows_two)
        wide_outer(gd, cots, 0)
        down = weight_scatter(net, gd, tmp_d, down_out)
        next(down)
        next(rows_two)
        wide_outer(gu, h2, 1)
        up = weight_scatter(net, gu, tmp_u, up_out)
        next(up)
        next(rows_two)
        next(rows_two, None)
        me = load(own, dz.at[y, c], 23)
        spreading = group_gather(net, own, dz)
        next(spreading)
        for d in range(2):
            projected(part_mlp, d, adu[0, d * 128 : d * 128 + 128], lambda j: wd[j].reshape(512, 1024))
        next(spreading)
        next(down)
        for d in range(2, 4):
            projected(part_mlp, d, adu[0, d * 128 : d * 128 + 128], lambda j: wd[j].reshape(512, 1024))
        keep = [
            load(kv_in.at[w, :, :, :, pl.ds(r * 64, 64)], wd.at[:, :, :, :, pl.ds((w * 4 + r) * 128, 128)], 13 + 4 * w + r)
            for w in range(2)
            for r in range(4)
        ]
        next(spreading)
        next(up)
        late = [load(h1_in.at[:, pl.ds(w * 1024, 1024)], adu.at[w], 21 + w) for w in range(2)]
        for _ in spreading:
            pass
        me.wait()
        loads[0].wait()
        go[...] = jnp.dot(
            dz[...].reshape(512, 2048), wo[...].reshape(2048, 256), preferred_element_type=F32
        ).astype(BF16)

        def total_out(summed):
            output[...] = (x1[...] + (summed + vec[5:6])).astype(BF16)

        rows_out = group_scatter(net, part_mlp, *second, total_out)
        next(rows_out)
        outer(gwo, lambda j: dz[:, :, :, pl.ds(pl.multiple_of(j * 512, 512), 512)].reshape(512, 512), o[...])
        project = weight_scatter(net, gwo, tmp_o, wo_out)
        next(project)
        for one in keep:
            one.wait()
        steps = attend_back(z, x, q, wd, o, go, log_sum, vec[8:9, 0:128], vec[9:10, 0:128], wu, lone, dq_sum, dq)

        theirs = pl.ds(pl.multiple_of((1 - c) * 512, 512), 512)
        ours = pl.ds(pl.multiple_of(c * 512, 512), 512)

        def swap(zs, ys):
            k = [net.slot() for _ in range(4)]
            zr, yr = pl.ds(zs, 2), pl.ds(ys[0], len(ys))
            for i in range(4):
                net.send(wu.at[zr, yr, i, :, theirs], cots.at[zr, yr, :, pl.ds(i * 512, 512)], k[i], "c")
            yield
            for i in range(4):
                net.got(cots.at[zr, yr, :, pl.ds(i * 512, 512)], k[i])
                for zz in (zs, zs + 1):
                    for yy in ys:
                        wu[zz, yy, i, :, ours] = wu[zz, yy, i, :, ours] + cots[zz, yy, :, i * 512 : i * 512 + 512]

        swaps = [swap(2, (0, 1)), swap(0, (0,)), swap(0, (1,))]
        next(steps)
        next(down)
        next(rows_out)
        next(steps)
        next(swaps[0])
        next(up)
        next(steps)
        next(swaps[1])
        next(down)
        next(rows_out)
        next(steps)
        next(swaps[0], None)
        next(up)
        next(steps)
        next(swaps[2])
        next(swaps[1], None)
        next(down)
        next(rows_out)
        next(project)
        next(steps, None)
        next(up)
        next(rows_out, None)
        for one in loads[1:] + late:
            one.wait()

        def make_one(i, d, h):
            projected(h2, d, dq[ring_rows(d)], lambda j: wq[j].reshape(512, 256), h)
            if i == 3:
                for j in (2 * h, 2 * h + 1):
                    more = lax.dot_general(
                        dkv[y], packs[j].reshape(512, 128), NT, preferred_element_type=F32
                    ).astype(BF16)
                    at = slice(j * 512, (j + 1) * 512)
                    h2[d, 0, :, at] = h2[d, 0, :, at] + more[:64]
                    h2[d, 1, :, at] = h2[d, 1, :, at] + more[64:]

        def total_one(summed):
            norm, inverse = normed(tok[...].astype(F32))
            grad_input[...] = dx1[...] + norm_back(summed, norm, inverse, vec[0:1])
            sums[0:1] = jnp.sum(summed * norm, axis=0, keepdims=True)
            sums[1:2] = jnp.sum(summed, axis=0, keepdims=True)
            sums[6:8] = jnp.zeros((2, 2048), F32)
            vecs[y, c] = sums[...]

        rows_one = group_scatter(net, h2, *first, total_one, make_one)
        next(rows_one)
        next(swaps[2], None)

        def keys_of(r, tmp):
            def view(zz, half, xx, part):
                start = c * 512 + r * 256
                if half == BOTH:
                    return wu.at[zz, part, xx, :, pl.ds(pl.multiple_of(start, 256), 256)]
                return wu.at[zz, part, xx, :, pl.ds(pl.multiple_of(start + half * 128, 128), 128)]

            return plane_scatter(net, view, tmp)

        keys = in_turn(keys_of(0, tmp_k), keys_of(1, tmp_v))
        next(keys)
        next(rows_one)
        outer(gq, lambda j: adu[j // 2, :, pl.ds(pl.multiple_of((j % 2) * 512, 512), 512)], dq[...])
        bias[0, 8:9] = jnp.sum(dq[:, :128].astype(F32), axis=0, keepdims=True)
        bias[0, 9:10] = jnp.sum(dq[:, 128:].astype(F32), axis=0, keepdims=True)
        bias[0, 10:16] = jnp.zeros((6, 128), F32)
        next(keys)
        query = weight_scatter(net, gq, tmp_q, wq_out)
        next(query)
        small = all_sums(net, bias, bias_x, bias_z)
        next(small)
        next(rows_one)
        next(keys)
        next(down, None)
        next(up, None)
        next(query)
        next(small)
        next(keys)
        next(project)
        for _ in keys:
            pass

        def ring_piece(ref, d):
            at = pl.ds(pl.multiple_of(c * 512 + lax.rem(d, 2) * 256, 256), 256)
            return ref.at[z, d // 2, x, :, at]

        kr = [net.slot() for _ in range(7)]
        for i, (name, d) in enumerate((("yu", net.yu), ("yd", net.yd), ("yo", net.yo))):
            net.send(ring_piece(wu, d), dkv_from.at[i], kr[i], name)
        next(query)
        next(project)
        for i in range(3):
            net.got(dkv_from.at[i], kr[i])
        mine = ring_piece(wu, y)[...].astype(F32)
        for i in range(3):
            mine = mine + dkv_from[i].astype(F32)
        mine = mine.astype(BF16)
        dkv[y] = jnp.concatenate([mine[:, :128], mine[:, 128:]], axis=0)
        for i, name in enumerate(("yu", "yd", "yo")):
            net.send(dkv.at[y], dkv.at[y], kr[3 + i], name)
        next(rows_one)
        next(down, None)
        next(up, None)
        next(small, None)
        for i, d in enumerate((net.yd, net.yu, net.yo)):
            net.got(dkv.at[d], kr[3 + i])

        every = dkv[...].reshape(512, 128)
        value_sum = jnp.broadcast_to(jnp.sum(every.astype(F32), axis=0, keepdims=True), (8, 128))
        for j in range(4):
            at = pl.ds(pl.multiple_of((j % 2) * 512 + yh * 256, 256), 256)
            out = lax.dot_general(adu[j // 2, :, at], every, TN, preferred_element_type=F32).reshape(4, 2, 32, 128)
            for i in range(4):
                gkv[j, i, 0:32] = jnp.where(yl == 0, out[i, 0], out[i, 1])
                gkv[j, i, 32:40] = value_sum

        def key_value():
            k = [net.slot() for _ in range(7)]
            for i, (name, d) in enumerate((("zu", net.zu), ("zd", net.zd), ("zo", net.zo))):
                net.send(gkv.at[d], gkv_z.at[i], k[i], name)
            yield
            for i in range(3):
                net.got(gkv_z.at[i], k[i])
            for i in range(4):
                gkv_x[i] = gkv[z, i] + gkv_z[0, i] + gkv_z[1, i] + gkv_z[2, i]
            for i, (name, d) in enumerate((("xu", net.xu), ("xd", net.xd), ("xo", net.xo))):
                net.send(gkv_x.at[d], gkv_x.at[4 + i], k[3 + i], name)
            yield
            for i in range(3):
                net.got(gkv_x.at[4 + i], k[3 + i])
            total = gkv_x[x] + gkv_x[4] + gkv_x[5] + gkv_x[6]
            gkv_x[7, 0:16] = jnp.where(c == 0, total[0:16], total[16:32])
            gkv_x[7, 16:32] = jnp.where(c == 0, total[16:32], total[0:16])
            gkv_x[7, 32:40] = total[32:40]
            net.send(gkv_x.at[7, pl.ds(16, 24)], gkv_x.at[8, pl.ds(16, 24)], k[6], "c")
            yield
            net.got(gkv_x.at[8, pl.ds(16, 24)], k[6])
            here, there = gkv_x[7, 0:16], gkv_x[8, 16:32]
            kv_out[:, 0:128] = jnp.where(c == 0, here, there)
            kv_out[:, 128:256] = jnp.where(c == 0, there, here)
            vb_out[...] = jnp.where(c == 0, gkv_x[8, 32:40], gkv_x[7, 32:40])

        def vectors():
            k = [net.slot() for _ in range(13)]
            at = vecs.at[y, c]
            for i, name in enumerate(("yu", "yd", "yo", "c")):
                net.send(at, at, k[i], name)
            yield
            for i, d in enumerate((net.yd, net.yu, net.yo)):
                net.got(vecs.at[d, c], k[i])
                net.send(vecs.at[d, c], vecs.at[d, c], k[4 + i], "c")
            yield
            for i, d in enumerate((y, net.yd, net.yu, net.yo)):
                net.got(vecs.at[d, 1 - c], k[3 + i])
            acc = vecs[0, 0]
            for i in range(1, 8):
                acc = acc + vecs[i // 2, i % 2]
            for i in range(4):
                vec_z[i] = acc[:, i * 512 : (i + 1) * 512]
            for i, (name, d) in enumerate((("zu", net.zu), ("zd", net.zd), ("zo", net.zo))):
                net.send(vec_z.at[d], vec_z.at[4 + i], k[7 + i], name)
            yield
            for i in range(3):
                net.got(vec_z.at[4 + i], k[7 + i])
            acc = vec_z[z] + vec_z[4] + vec_z[5] + vec_z[6]
            vec_x[0] = jnp.where(yh == 0, acc[:, :256], acc[:, 256:])
            spread(net, ("xu", "xd", "xo"), vec_x.at[0], vec_x.at[pl.ds(1, 3)], k[10:])
            yield
            for i in range(3):
                net.got(vec_x.at[1 + i], k[10 + i])
            vec_out[...] = vec_x[0] + vec_x[1] + vec_x[2] + vec_x[3]

        def partner_bias():
            k = net.slot()
            net.send(bias.at[2], bias_out.at[1], k, "yo")
            bias_out[0] = bias[2]
            yield
            net.got(bias_out.at[1], k)

        last = key_value()
        next(last)
        next(rows_one, None)
        run_all(vectors(), last, partner_bias(), query, project, down, up)
        net.finish()

    n, d = tokens.shape

    def bf(*shape):
        return jax.ShapeDtypeStruct(shape, BF16)

    def f32(*shape):
        return jax.ShapeDtypeStruct(shape, F32)

    return pl.pallas_call(
        kernel,
        out_shape=(
            bf(n, d),
            f32(n, d),
            bf(n, d),
            bf(n, d),
            bf(n, 512),
            bf(n, 512),
            f32(8, 256),
            f32(2, 16, 128),
            f32(16, 256),
            f32(8, 128),
        ),
        in_specs=[INV, INV] + [ANY] * 8 + [INV, ANY] + [INV] * 5,
        out_specs=(INV,) * 10,
        scratch_shapes=[
            VMEM((4, 2, n, d), BF16),
            VMEM((4, 2, n, d), BF16),
            VMEM((4, 2, 4, n, 1024), BF16),
            VMEM((4, 2, 4, n, 1024), BF16),
            VMEM((4, 2, 4, n, 256), BF16),
            VMEM((4, 2, 4, n, 256), BF16),
            VMEM((4, 2, 4, 2, 2, 16, 128), BF16),
            VMEM((2, 512, 1024), BF16),
            VMEM((512, 256), F32),
            VMEM((512, 256), F32),
            VMEM((4, 2, n, d), BF16),
            VMEM((4, 2, n, d), BF16),
            VMEM((4, 2, 4, n, 1024), BF16),
            VMEM((4, 2, 4, n, 1024), BF16),
            VMEM((4, 2, 4, n, 256), BF16),
            VMEM((4, 2, 4, n, 256), BF16),
            VMEM((n, d), BF16),
            VMEM((4, 2, n, d), BF16),
            VMEM((n, d), F32),
            VMEM((8, d), F32),
            VMEM((512, 256), BF16),
            VMEM((2, 2, 2, 256, 128), BF16),
            VMEM((2, 128, 512), F32),
            VMEM((512, 256), BF16),
            VMEM((3, 64, 256), BF16),
            VMEM((4, 128, 128), BF16),
            VMEM((4, 4, 40, 128), F32),
            VMEM((3, 4, 40, 128), F32),
            VMEM((9, 40, 128), F32),
            VMEM((3, 16, 128), F32),
            VMEM((3, 16, 128), F32),
            VMEM((3, 16, 128), F32),
            VMEM((4, 2, 8, d), F32),
            VMEM((7, 8, 512), F32),
            VMEM((4, 8, 256), F32),
            pltpu.SemaphoreType.DMA((24,)),
        ]
        + scatter_scratch(n, d)
        + scatter_scratch(n, d)
        + plane_scratch(n, 512)
        + plane_scratch(n, 512)
        + plane_scratch(n, 128)
        + plane_scratch(n, 128)
        + [VMEM(s, BF16) for s in ((2, 4, n, 128), (2, 4, n, 128), (2, 4, n, 256), (2, 4, n, 256))]
        + [VMEM(s, BF16) for s in ((2, n, 128), (2, n, 128), (2, n, 256), (2, n, 256))]
        + [VMEM(s, BF16) for s in ((2, 4, n, 128), (2, 4, n, 128), (2, 4, n, 256), (2, 4, n, 256))]
        + [VMEM(s, BF16) for s in ((2, n, 128), (2, n, 128), (2, n, 256), (2, n, 256))]
        + sems(280),
        compiler_params=params(2, 62 << 20),
        name="backward",
    )(tokens, cotangent, cot_all, h2, wu, wd, wq, wo, packs, h1, q, kv, o, log_sum, x1, vec, ub)


def finish(up, down, out, query, grad_input, output, keyval, vec, bias, value_bias, best, w_query, query_bias, tau):
    def kernel(up, down, out, query, grad_input, output, keyval, vec, bias, vb, best, wq, qb, tau,
               output_o, grad_o, query_o, up_o, out_o, down_o, qb_o, ub_o, kv_o, vb_o, v0, v1, v2, v3, v4, v5, wq_o, cb_o):
        for src, dst in ((output, output_o), (grad_input, grad_o), (keyval, kv_o)):
            dst[...] = src[...]
        z, yh, x, yl, c = (lax.axis_index(a) for a in AXES)
        tp = yl * 2 + c
        dp = (z * 2 + yh) * 4 + x
        for src, dst in ((up, up_o), (down, down_o), (out, out_o), (query, query_o)):
            dst[...] = src[...].astype(F32)

        def pick(rows, count, start):
            lanes = rows.shape[1]
            hot = (
                lax.broadcasted_iota(jnp.int32, (lanes, count), 0)
                == lax.broadcasted_iota(jnp.int32, (lanes, count), 1) + start
            ).astype(F32)
            return hot, rows

        low, high = jnp.where(yh == 0, bias[0], bias[1]), jnp.where(yh == 0, bias[1], bias[0])
        exact = lax.Precision.HIGHEST
        hot, rows = pick(jnp.concatenate([low[0:8], high[0:8]], axis=0), 4, dp * 4)
        ub_o[...] = lax.dot_general(hot, rows, (((0,), (1,)), ((), ())), precision=exact, preferred_element_type=F32)
        hot, rows = pick(jnp.concatenate([low[8:10], high[8:10], low[10:14]], axis=0), 4, dp * 4)
        heads = lax.dot_general(hot, rows, (((0,), (1,)), ((), ())), precision=exact, preferred_element_type=F32)
        qb_o[...] = heads[:, 0:4]
        hot, rows = pick(vec[...], 16, x * 64 + tp * 16)
        own = jnp.dot(rows, hot, precision=exact, preferred_element_type=F32)
        for i, ref in enumerate((v0, v1, v2, v3, v4, v5)):
            ref[...] = own[i : i + 1]
        lane = lax.broadcasted_iota(jnp.int32, (1, 128), 1)
        vb_o[...] = splat(vb[0:1], lane, dp * 4 + tp)
        limit = tau[0]
        factors = jnp.zeros((1, 128), F32)
        for h in range(4):
            factor = limit / jnp.maximum(best[h // 2, 8 * (h % 2) : 8 * (h % 2) + 1], limit)
            at = slice(h * 128, (h + 1) * 128)
            wq_o[:, at] = (wq[:, at].astype(F32) * factor).astype(BF16)
            factors = jnp.where(lane == h, factor, factors)
        cb_o[...] = (qb[...].astype(F32) * factors[:, 0:4]).astype(BF16)

    n, d = output.shape

    def f32(*shape):
        return jax.ShapeDtypeStruct(shape, F32)

    shapes = (
        jax.ShapeDtypeStruct((n, d), BF16),
        f32(n, d),
        f32(n, 512),
        f32(n, d),
        f32(n, 512),
        f32(n, d),
        f32(4, 4),
        f32(4, 16),
        f32(16, 256),
        f32(1, 1),
    )
    shapes += (f32(1, 16),) * 6
    shapes += (jax.ShapeDtypeStruct((n, 512), BF16), jax.ShapeDtypeStruct((4, 4), BF16))
    return pl.pallas_call(
        kernel,
        out_shape=shapes,
        in_specs=[INV] * 13 + [INS],
        out_specs=(INV,) * 18,
        compiler_params=pltpu.CompilerParams(vmem_limit_bytes=60 << 20),
        name="finish",
    )(up, down, out, query, grad_input, output, keyval, vec, bias, value_bias, best, w_query, query_bias, tau)


def local(
    tokens,
    cotangent,
    seg_ids,
    parents,
    tau,
    w_query,
    w_up,
    w_out,
    w_down,
    query_bias,
    up_bias,
    w_keyval,
    value_bias,
    norm1_gain,
    norm1_bias,
    norm2_gain,
    norm2_bias,
    out_bias,
    down_bias,
):
    vectors = jnp.pad(value_bias.reshape(1, 1), ((6, 9), (0, 15)))
    for i, one in enumerate((norm1_gain, norm1_bias, norm2_gain, norm2_bias, out_bias, down_bias)):
        vectors = vectors + jnp.pad(one.reshape(1, 16), ((i, 15 - i), (0, 0)))
    (cot_all, h2, wu, wd, wq, wo, wkv, h1, q, kv, o, log_sum, x1, best, vec, ub) = forward(
        tokens, cotangent, seg_ids, parents, vectors, query_bias, up_bias, w_keyval, w_query, w_out, w_up, w_down
    )
    output, grad_input, up_sum, down_sum, out_sum, query_sum, vec_sum, bias_sum, keyval_sum, vb_sum = backward(
        tokens, cotangent, cot_all, h2, wu, wd, wq, wo, wkv, h1, q, kv, o, log_sum, x1, vec, ub
    )
    outs = finish(
        up_sum, down_sum, out_sum, query_sum, grad_input, output, keyval_sum, vec_sum, bias_sum, vb_sum, best,
        w_query, query_bias, tau,
    )
    return outs[:9] + tuple(v.reshape(-1) for v in outs[9:16]) + outs[16:]


def solution(mesh):
    fine = Mesh(mesh.devices.reshape(4, 2, 4, 2, 2), AXES)
    dp, tp = ("z", "yh", "x"), ("yl", "c")
    rows, flat, weight = P(AXES, None), P(AXES), P(dp, tp)
    in_specs = (rows, rows, P(dp), P(), P()) + (weight,) * 6 + (rows,) + (flat,) * 7
    out_specs = (rows, rows) + (weight,) * 6 + (rows,) + (flat,) * 7 + (weight, weight)
    return jax.shard_map(local, mesh=fine, in_specs=in_specs, out_specs=out_specs, check_vma=False)
```

```python
import itertools

import jax
import jax.numpy as jnp
from jax import lax
from jax.experimental import pallas as pl
from jax.experimental.pallas import tpu as pltpu
from jax.sharding import Mesh, PartitionSpec as P

EPS = 1e-05
AXES = ("z", "yh", "x", "yl", "c")
F32 = jnp.float32
BF16 = jnp.bfloat16
VMEM = pltpu.VMEM
NEG = -1e30


class Net:
    def __init__(self, send_sems, recv_sems):
        self.z, self.yh, self.x, self.yl, self.c = (lax.axis_index(a) for a in AXES)
        self.y = self.yh * 2 + self.yl
        self.yu, self.yo, self.yd = (lax.rem(self.y + s, 4) for s in (1, 2, 3))
        self.xu, self.xo, self.xd = (lax.rem(self.x + s, 4) for s in (1, 2, 3))
        self.zu, self.zo, self.zd = (lax.rem(self.z + s, 4) for s in (1, 2, 3))
        up, down = lax.rem(self.yh + self.yl, 2), lax.rem(self.yh + 1 - self.yl, 2)
        self.dev = {
            "yu": {"yh": up, "yl": 1 - self.yl},
            "yd": {"yh": down, "yl": 1 - self.yl},
            "yo": {"yh": 1 - self.yh},
            "c": {"c": 1 - self.c},
            "xu": {"x": self.xu},
            "xd": {"x": self.xd},
            "xo": {"x": self.xo},
            "zu": {"z": self.zu},
            "zd": {"z": self.zd},
            "zo": {"z": self.zo},
        }
        self.send_sems, self.recv_sems = send_sems, recv_sems
        self.count = 0
        self.sent = []

    def barrier(self, names):
        sem = pltpu.get_barrier_semaphore()
        for name in names:
            pl.semaphore_signal(
                sem, inc=1, device_id=self.dev[name], device_id_type=pl.DeviceIdType.MESH
            )
        pl.semaphore_wait(sem, len(names))

    def slot(self):
        self.count += 1
        assert self.count <= self.send_sems.shape[0]
        return self.count - 1

    def copy(self, src, dst, k, name):
        return pltpu.make_async_remote_copy(
            src_ref=src,
            dst_ref=dst,
            send_sem=self.send_sems.at[k],
            recv_sem=self.recv_sems.at[k],
            device_id=self.dev[name],
            device_id_type=pl.DeviceIdType.MESH,
        )

    def send(self, src, dst, k, name):
        one = self.copy(src, dst, k, name)
        one.start()
        self.sent.append(one)

    def got(self, ref, k):
        self.copy(ref, ref, k, "c").wait_recv()

    def finish(self):
        for one in self.sent:
            one.wait_send()


def run_all(*steps):
    live = list(steps)
    while live:
        rest = []
        for one in live:
            try:
                next(one)
                rest.append(one)
            except StopIteration:
                pass
        live = rest


def in_turn(*steps):
    live = list(steps)
    while live:
        live = [one for one in live if next(one, 1) is None]
        if live:
            yield


def columns_of(ref, h):
    w = ref.shape[-1] // 2
    return ref.at[(slice(None),) * (len(ref.shape) - 1) + (pl.ds(h * w, w),)]


def group_gather(net, src, out):
    return in_turn(*(group_gather_one(net, columns_of(src, h), columns_of(out, h)) for h in range(2)))


def group_scatter(net, part, acc, from_half, from_full, whole, total, make=None):
    def one(h):
        refs = [columns_of(ref, h) for ref in (part, acc, from_half, from_full)]
        place = columns_of(whole, h)

        def keep(summed):
            place[...] = summed

        produce = None if make is None else lambda i, d: make(i, d, h)
        return group_scatter_one(net, *refs, keep, produce)

    yield from in_turn(one(0), one(1))
    total(whole[...])


def group_gather_one(net, src, out):
    y, c, yu, yd, yo = net.y, net.c, net.yu, net.yd, net.yo
    k = [net.slot() for _ in range(9)]
    half = src.shape[0] // 2
    lo, hi = pl.ds(0, half), pl.ds(half, half)
    mine = out.at[y, c]
    net.send(src, mine, k[0], "yu")
    net.send(src, mine, k[1], "yd")
    net.send(src, mine, k[2], "c")
    yield
    net.got(out.at[yd, c], k[0])
    net.send(out.at[yd, c, lo], out.at[yd, c, lo], k[3], "yu")
    net.send(out.at[yd, c], out.at[yd, c], k[4], "c")
    net.got(out.at[yu, c], k[1])
    net.send(out.at[yu, c, hi], out.at[yu, c, hi], k[5], "yd")
    net.send(out.at[yu, c], out.at[yu, c], k[6], "c")
    yield
    net.got(out.at[yo, c, lo], k[3])
    net.send(out.at[yo, c, lo], out.at[yo, c, lo], k[7], "c")
    net.got(out.at[yo, c, hi], k[5])
    net.send(out.at[yo, c, hi], out.at[yo, c, hi], k[8], "c")
    yield
    net.got(out.at[y, 1 - c], k[2])
    net.got(out.at[yd, 1 - c], k[4])
    net.got(out.at[yu, 1 - c], k[6])
    net.got(out.at[yo, 1 - c, lo], k[7])
    net.got(out.at[yo, 1 - c, hi], k[8])


def group_scatter_one(net, part, acc, from_half, from_full, total, make=None):
    y, c, yu, yd, yo = net.y, net.c, net.yu, net.yd, net.yo
    k = [net.slot() for _ in range(8)]
    n = part.shape[2]
    half = n // 2
    lo, hi = pl.ds(0, half), pl.ds(half, half)

    sent = []

    def send(src, dst, i, name):
        sent.append(net.copy(src, dst, i, name))
        sent[-1].start()

    def start(i, d):
        if make is not None:
            make(i, d)
        send(part.at[d, 1 - c], acc.at[d], k[i], "c")

    def core_sum(i, d):
        net.got(acc.at[d], k[i])
        acc[d] = acc[d] + part[d, c]

    for i, d in enumerate((yo, yu, yd)):
        start(i, d)
    yield
    core_sum(0, yo)
    send(acc.at[yo, lo], from_half.at[0], k[4], "yu")
    send(acc.at[yo, hi], from_half.at[1], k[5], "yd")
    core_sum(1, yu)
    core_sum(2, yd)
    yield
    net.got(from_half.at[0], k[4])
    acc[yu, lo] = acc[yu, lo] + from_half[0]
    send(acc.at[yu], from_full.at[0], k[6], "yu")
    net.got(from_half.at[1], k[5])
    acc[yd, hi] = acc[yd, hi] + from_half[1]
    send(acc.at[yd], from_full.at[1], k[7], "yd")
    yield
    start(3, y)
    yield
    net.got(acc.at[y], k[3])
    mine = part[y, c].astype(F32) + acc[y].astype(F32)
    net.got(from_full.at[0], k[6])
    net.got(from_full.at[1], k[7])
    for one in sent:
        one.wait_send()
    total(mine + from_full[0].astype(F32) + from_full[1].astype(F32))


def scatter_scratch(n, w):
    return [VMEM((4, n, w), BF16), VMEM((2, n // 2, w), BF16), VMEM((2, n, w), BF16), VMEM((n, w), F32)]


BOTH = slice(None)


def plane_gather(net, o, theirs=None, last=True):
    z, x, xu, xd, xo, zu, zd, zo = net.z, net.x, net.xu, net.xd, net.xo, net.zu, net.zd, net.zo
    k = [net.slot() for _ in range(16)]
    every = slice(None)
    relayed = []

    def send(at, i, name):
        net.send(o(*at), o(*at), k[i], name)

    def got(at, i):
        net.got(o(*at), k[i])

    def relay(*at):
        if theirs is not None:
            slot = net.slot()
            net.send(o(*at), o(*at), slot, "c")
            relayed.append((at, slot))

    send((z, BOTH, x, 0), 0, "xu")
    send((z, BOTH, x, 0), 1, "xd")
    send((z, BOTH, x, 1), 2, "zu")
    send((z, BOTH, x, 1), 3, "zd")
    relay(z, BOTH, x, 0)
    relay(z, BOTH, x, 1)
    yield
    got((z, BOTH, xd, 0), 0)
    send((z, 0, xd, 0), 4, "xu")
    got((zd, BOTH, x, 1), 2)
    send((zd, 0, x, 1), 6, "zu")
    got((z, BOTH, xu, 0), 1)
    send((z, 1, xu, 0), 5, "xd")
    got((zu, BOTH, x, 1), 3)
    send((zu, 1, x, 1), 7, "zd")
    for at in ((z, BOTH, xd, 0), (zd, BOTH, x, 1), (z, BOTH, xu, 0), (zu, BOTH, x, 1)):
        relay(*at)
    yield
    got((z, 0, xo, 0), 4)
    got((z, 1, xo, 0), 5)
    send((z, BOTH, every, 0), 8, "zu")
    send((z, BOTH, every, 0), 9, "zd")
    got((zo, 0, x, 1), 6)
    got((zo, 1, x, 1), 7)
    send((every, BOTH, x, 1), 10, "xu")
    send((every, BOTH, x, 1), 11, "xd")
    relay(z, BOTH, xo, 0)
    relay(zo, BOTH, x, 1)
    yield
    if not last:
        for at, i in (((zd, BOTH, every, 0), 8), ((every, BOTH, xd, 1), 10), ((zu, BOTH, every, 0), 9), ((every, BOTH, xu, 1), 11)):
            got(at, i)
        return
    got((zd, BOTH, every, 0), 8)
    send((zd, 0, every, 0), 12, "zu")
    got((every, BOTH, xd, 1), 10)
    send((every, 0, xd, 1), 14, "xu")
    got((zu, BOTH, every, 0), 9)
    send((zu, 1, every, 0), 13, "zd")
    got((every, BOTH, xu, 1), 11)
    send((every, 1, xu, 1), 15, "xd")
    for at in ((zd, BOTH, every, 0), (every, BOTH, xd, 1), (zu, BOTH, every, 0), (every, BOTH, xu, 1)):
        relay(*at)
    yield
    got((zo, 0, every, 0), 12)
    got((zo, 1, every, 0), 13)
    relay(zo, BOTH, every, 0)
    got((every, 0, xo, 1), 14)
    got((every, 1, xo, 1), 15)
    relay(every, BOTH, xo, 1)
    for at, slot in relayed:
        net.got(theirs(*at), slot)


def add_into(dst, *others):
    for index in itertools.product(*[range(n) for n in dst.shape[:-2]]):
        at = index + (slice(None), slice(None))
        total = dst[at]
        for other in others:
            total = total + other[at]
        dst[at] = total


def plane_scatter(net, g, tmp):
    z, x, xu, xd, xo, zu, zd, zo = net.z, net.x, net.xu, net.xd, net.xo, net.zu, net.zd, net.zo
    t1, t2, u1, u2, t3, t4, u3, u4 = tmp
    k = [net.slot() for _ in range(16)]
    every = slice(None)

    def send(src, dst, i, name):
        net.send(src, dst, k[i], name)

    def got(ref, i):
        net.got(ref, k[i])

    send(g(zo, 0, every, 0), t1.at[0], 0, "zu")
    send(g(zo, 1, every, 0), t1.at[1], 1, "zd")
    send(g(every, 0, xo, 1), t2.at[0], 2, "xu")
    send(g(every, 1, xo, 1), t2.at[1], 3, "xd")
    yield
    got(t1.at[0], 0)
    add_into(g(zu, 0, every, 0), t1.at[0])
    send(g(zu, BOTH, every, 0), u1.at[0], 4, "zu")
    got(t2.at[0], 2)
    add_into(g(every, 0, xu, 1), t2.at[0])
    send(g(every, BOTH, xu, 1), u2.at[0], 6, "xu")
    got(t1.at[1], 1)
    add_into(g(zd, 1, every, 0), t1.at[1])
    send(g(zd, BOTH, every, 0), u1.at[1], 5, "zd")
    got(t2.at[1], 3)
    add_into(g(every, 1, xd, 1), t2.at[1])
    send(g(every, BOTH, xd, 1), u2.at[1], 7, "xd")
    yield
    got(u1.at[0], 4)
    got(u1.at[1], 5)
    add_into(g(z, BOTH, every, 0), u1.at[0], u1.at[1])
    send(g(z, 0, xo, 0), t3.at[0], 8, "xu")
    send(g(z, 1, xo, 0), t3.at[1], 9, "xd")
    got(u2.at[0], 6)
    got(u2.at[1], 7)
    add_into(g(every, BOTH, x, 1), u2.at[0], u2.at[1])
    send(g(zo, 0, x, 1), t4.at[0], 10, "zu")
    send(g(zo, 1, x, 1), t4.at[1], 11, "zd")
    yield
    got(t3.at[0], 8)
    add_into(g(z, 0, xu, 0), t3.at[0])
    send(g(z, BOTH, xu, 0), u3.at[0], 12, "xu")
    got(t4.at[0], 10)
    add_into(g(zu, 0, x, 1), t4.at[0])
    send(g(zu, BOTH, x, 1), u4.at[0], 14, "zu")
    got(t3.at[1], 9)
    add_into(g(z, 1, xd, 0), t3.at[1])
    send(g(z, BOTH, xd, 0), u3.at[1], 13, "xd")
    got(t4.at[1], 11)
    add_into(g(zd, 1, x, 1), t4.at[1])
    send(g(zd, BOTH, x, 1), u4.at[1], 15, "zd")
    yield
    got(u3.at[0], 12)
    got(u3.at[1], 13)
    add_into(g(z, BOTH, x, 0), u3.at[0], u3.at[1])
    got(u4.at[0], 14)
    got(u4.at[1], 15)
    add_into(g(z, BOTH, x, 1), u4.at[0], u4.at[1])


def plane_scratch(n, w):
    return [
        VMEM((2, 4, n, w), BF16),
        VMEM((2, 4, n, w), BF16),
        VMEM((2, 2, 4, n, w), BF16),
        VMEM((2, 4, 2, n, w), BF16),
        VMEM((2, n, w), BF16),
        VMEM((2, n, w), BF16),
        VMEM((2, 2, n, w), BF16),
        VMEM((2, 2, n, w), BF16),
    ]


def column_view(ref):
    w = ref.shape[-1] // 2

    def view(zz, half, xx, part):
        return ref.at[zz, half, xx, :, pl.ds(part * w, w)]

    return view


def sems(n):
    return [pltpu.SemaphoreType.DMA((n,)), pltpu.SemaphoreType.DMA((n,))]


def params(cid, limit=56 << 20):
    return pltpu.CompilerParams(collective_id=cid, has_side_effects=True, vmem_limit_bytes=limit)


ANY = pl.BlockSpec(memory_space=pl.ANY)
INV = pl.BlockSpec(memory_space=pltpu.VMEM)
INS = pl.BlockSpec(memory_space=pltpu.SMEM)
PLANE = ("xu", "xd", "zu", "zd")
RING = ("yu", "yd", "c")


class Ticks:
    def __init__(self, *steps):
        self.steps = list(steps)

    def tick(self, count=1):
        for _ in range(count):
            for one in self.steps:
                next(one, None)


def weight_gather(net, weight, out, local, last=True):
    z, yh, x = net.z, net.yh, net.x
    n, w = weight.shape[0], weight.shape[1] // 2
    k = net.slot()

    def half(which):
        return weight.at[:, pl.ds(pl.multiple_of(which * w, 128), w)]

    mine = pltpu.make_async_copy(half(yh), out.at[z, yh, x, pl.ds(0, n)], local)
    mine.start()
    net.send(half(1 - yh), out.at[z, yh, x, pl.ds(0, n)], k, "yo")
    yield
    mine.wait()
    net.got(out.at[z, 1 - yh, x, pl.ds(0, n)], k)
    yield from plane_gather(net, column_view(out), last=last)


def splat(row, lane, at):
    return jnp.sum(jnp.where(lane == at, row, 0.0), axis=1, keepdims=True)


def place_of(segs, parents, block):
    lane = lax.broadcasted_iota(jnp.int32, (1, 128), 1)
    seg = splat(segs, lane, block)
    lanes = lane.astype(F32)
    parent = splat(parents, lanes, seg)
    trunk = splat(parents, lanes, parent)
    leaf = (seg >= 10.0).astype(F32)
    branch = (seg >= 2.0).astype(F32)
    above = [(splat(segs, lane, b) == parent).astype(F32) * leaf for b in range(16, 32)]
    return trunk, leaf, branch, above


def wide(value):
    return jnp.broadcast_to(value, (1, 128)).astype(BF16)


def trunk_block(kv, which, i, trunk):
    one = wide(trunk)
    return kv[which, 0, i // 4, i % 4] * (1 - one) + kv[which, 1, i // 4, i % 4] * one


def parent_block(kv, which, above):
    total = kv[which, 2, 0, 0] * wide(above[0])
    for j in range(1, 16):
        total = total + kv[which, 2 + j // 8, j // 4 % 2, j % 4] * wide(above[j])
    return total


NT = (((1,), (1,)), ((), ()))
TN = (((0,), (0,)), ((), ()))
SCALE = 128**-0.5
LOG2E = 1.4426950408889634


def attend(b, z, x, q, kv, segs, parents, scores, o, log_sum):
    lane = (lax.broadcasted_iota(jnp.int32, (256, 512), 1) & 255).astype(F32)
    ahead = lax.broadcasted_iota(jnp.int32, (256, 512), 0).astype(F32) - lane
    block = z * 8 + b * 4 + x
    trunk, leaf, branch, above = place_of(segs, parents, block)
    rows = pl.ds(b * 256, 256)
    both = jnp.concatenate([q[rows, :128], q[rows, 128:]], axis=0)
    start = block.astype(F32) - 8.0 * trunk

    def score(key):
        return lax.dot_general(key, both, NT, preferred_element_type=F32) * (SCALE * LOG2E)

    def trunk_score(i, top):
        gap = (start - i.astype(F32)) * 256.0
        s = jnp.where(ahead <= gap, score(trunk_block(kv, 0, i, trunk)), NEG)
        scores[i] = s
        return jnp.maximum(top, jnp.max(s, axis=0, keepdims=True))

    top = lax.fori_loop(0, 8, trunk_score, jnp.full((1, 512), NEG, F32))
    s = score(parent_block(kv, 0, above)) + (leaf - 1.0) * 1e30
    scores[8] = s
    top = jnp.maximum(top, jnp.max(s, axis=0, keepdims=True))
    s = jnp.where(ahead <= 0.0, score(kv[0, z, b, x]), NEG) + (branch - 1.0) * 1e30
    scores[9] = s
    top = jnp.maximum(top, jnp.max(s, axis=0, keepdims=True))

    def weigh(i, value, carry):
        acc, total = carry
        w = jnp.exp2(scores[i] - top)
        acc = acc + lax.dot_general(value, w.astype(BF16), TN, preferred_element_type=F32)
        return acc, total + jnp.sum(w, axis=0, keepdims=True)

    carry = (jnp.zeros((128, 512), F32), jnp.zeros((1, 512), F32))
    carry = lax.fori_loop(0, 8, lambda i, c: weigh(i, trunk_block(kv, 1, i, trunk), c), carry)
    carry = weigh(8, parent_block(kv, 1, above), carry)
    acc, total = weigh(9, kv[1, z, b, x], carry)
    heads = (acc / total).T.astype(BF16)
    o[rows, :128] = heads[:256]
    o[rows, 128:] = heads[256:]
    log_sum[b] = jnp.broadcast_to(top + jnp.log2(total), (8, 512))
    return top * (1.0 / LOG2E)


def one_hot(rows, lanes, hit):
    row = lax.broadcasted_iota(jnp.int32, (rows, lanes), 0)
    lane = lax.broadcasted_iota(jnp.int32, (rows, lanes), 1)
    return hit(row, lane).astype(F32).astype(BF16)


def forward(tokens, cotangent, seg_ids, parents, vectors, query_bias, up_bias, w_keyval, w_query, w_out, w_up, w_down):
    def kernel(tok, cot, seg_in, par_in, vec_in, qb_in, ub_in, wkv_in, wq_in, wo_in, wu_in, wd_in,
               cot_out, h2, wu, wd, wq_out, wo_out, wkv_out, h1_out, q_out, kv_out, o, log_sum, x1, best, vec, ub,
               tok_all, h1, wkv, wq, wo, q, kv, scores, part, own, mine, got, pack, pairs, halves, tiles, local,
               *rest):
        *scratch, ss, rs = rest
        net = Net(ss, rs)
        z, yh, x, yl, c, y = net.z, net.yh, net.x, net.yl, net.c, net.y
        starts = [
            pltpu.make_async_copy(src, dst, local.at[i])
            for i, (src, dst) in enumerate(((tok, tok_all.at[y, c]), (cot, cot_out.at[y, c])))
        ]
        for one in starts:
            one.start()
        row = lax.broadcasted_iota(jnp.int32, (16, 128), 0)
        lane = lax.broadcasted_iota(jnp.int32, (16, 128), 1)
        periodic = jnp.dot(vec_in[...], one_hot(16, 128, lambda r, l: l % 16 == r), preferred_element_type=F32)
        first = jnp.dot(vec_in[...], one_hot(16, 128, lambda r, l: r == 0), preferred_element_type=F32)
        tile = jnp.where(row < 6, periodic, first)
        tile = jnp.where(row == 7, seg_in[0].astype(F32), tile).astype(BF16)
        for i in range(2):
            pack[i, 0:16] = wkv_in[:, i * 128 : (i + 1) * 128]
            pack[i, 16:32] = tile
        four = one_hot(4, 128, lambda r, l: l % 4 == r)
        heads = lax.dot_general(qb_in[...], four, TN, preferred_element_type=F32)
        units = lax.dot_general(ub_in[...], four, TN, preferred_element_type=F32)
        blank = jnp.zeros((6, 128), F32)
        for i in range(2):
            halves[i] = jnp.concatenate([units[8 * i : 8 * i + 8], heads[2 * i : 2 * i + 2], blank], axis=0).astype(BF16)
        pairs[yh, yl, c] = jnp.where(c == 0, pack[0], pack[1])
        net.barrier(PLANE + RING + ("yo", "xo", "zo"))

        query = weight_gather(net, wq_in, wq, local.at[4])
        later = Ticks(weight_gather(net, wu_in, wu, local.at[6]), weight_gather(net, wd_in, wd, local.at[7], False))
        project_weight = weight_gather(net, wo_in, wo, local.at[5])
        toks = group_gather(net, tok, tok_all)
        ks = [net.slot() for _ in range(11)]
        net.send(pack.at[1 - c], pairs.at[yh, yl, c], ks[0], "c")
        net.send(halves.at[1 - yh], halves.at[2], ks[4], "yo")
        next(query)
        net.got(pairs.at[yh, yl, 1 - c], ks[0])
        for i, name in enumerate(("yu", "yd", "yo")):
            net.send(pairs.at[yh, yl], pairs.at[yh, yl], ks[1 + i], name)
        next(toks)
        next(query)
        net.got(halves.at[2], ks[4])
        here, there = jnp.where(yh == 0, halves[0], halves[1]), halves[2]
        low, high = jnp.where(yh == 0, here, there), jnp.where(yh == 0, there, here)
        tiles[z, x, 1] = jnp.where((lane // 16) % 2 == 0, low.astype(F32), high.astype(F32)).astype(BF16)
        for i, d in enumerate((net.yd, net.yu, net.yo)):
            net.got(pairs.at[d // 2, lax.rem(d, 2)], ks[1 + i])
        merged = jnp.zeros((16, 128), F32)
        for i in range(8):
            high, tp = i // 4, i % 4
            one = pairs[high, tp // 2, tp % 2, 16:32].astype(F32)
            hit = (row < 6) & (lane // 16 == i)
            hit = hit | ((row == 6) & (lane // 16 % 2 == high) & (lane % 4 == tp))
            hit = hit | ((row == 7) & ((lane // 4) % 2 == high))
            merged = jnp.where(hit, one, merged)
            wkv[z, high, x, tp // 2, tp % 2] = pairs[high, tp // 2, tp % 2, 0:16]
        tiles[z, x, 0] = merged.astype(BF16)
        for i, name in enumerate(("xu", "xd", "xo")):
            net.send(tiles.at[z, x], tiles.at[z, x], ks[5 + i], name)

        def key_view(zz, half, xx, part):
            return wkv.at[zz, part, xx, pl.ds(0, 2) if half == BOTH else half]

        keyval = plane_gather(net, key_view)
        next(keyval)
        next(project_weight)
        later.tick()
        for i, d in enumerate((net.xd, net.xu, net.xo)):
            net.got(tiles.at[z, d], ks[5 + i])
        for i, name in enumerate(("zu", "zd", "zo")):
            net.send(tiles.at[z], tiles.at[z], ks[8 + i], name)
        next(keyval)
        next(query)
        next(toks)
        next(keyval)
        next(query)
        next(project_weight)
        later.tick()
        next(toks)
        next(keyval)
        next(query)
        next(project_weight)
        for i, d in enumerate((net.zd, net.zu, net.zo)):
            net.got(tiles.at[d], ks[8 + i])

        value_bias = jnp.zeros((16, 128), F32)
        biases = jnp.zeros((16, 128), F32)
        segs = jnp.zeros((16, 128), F32)
        for zz in range(4):
            come = [tiles[zz, xx, 0].astype(F32) for xx in range(4)]
            turned = [pltpu.roll(one, 64, 1) for one in come]
            for xx in range(4):
                at = (lane // 32 == zz) & ((lane // 4) % 4 == xx)
                value_bias = jnp.where(at, come[xx], value_bias)
                biases = jnp.where(at, tiles[zz, xx, 1].astype(F32), biases)
                segs = jnp.where((lane // 8 == zz) & (lane % 4 == xx), come[xx], segs)
            for high in range(2):
                for pair in range(2):
                    even = come[2 * pair] if high == 0 else turned[2 * pair]
                    odd = turned[2 * pair + 1] if high == 0 else come[2 * pair + 1]
                    j = (zz * 2 + high) * 2 + pair
                    vec[:, j * 128 : (j + 1) * 128] = jnp.where(lane < 64, even, odd)
        value_bias = value_bias[6:7]
        segs = segs[7:8]
        vec[8:9, 0:128] = segs
        ub[...] = biases[0:8]
        query_bias = jnp.concatenate([biases[8:9], biases[9:10]], axis=1)
        parent = jnp.zeros((1, 128), F32)
        for i in range(18):
            parent = jnp.where(lane[0:1] == i, par_in[i].astype(F32), parent)
        vec[9:10, 0:128] = parent
        for _ in toks:
            pass
        starts[0].wait()

        gain1, shift1 = vec[0:1], vec[1:2]

        def norm_rows(i, carry):
            rows = tok_all[i // 2, i % 2].astype(F32)
            h1[pl.ds(pl.multiple_of(i * 64, 64), 64)] = (normed(rows)[0] * gain1 + shift1).astype(BF16)
            return carry

        lax.fori_loop(0, 8, norm_rows, 0)
        next(project_weight)
        for _ in query:
            pass
        for _ in keyval:
            pass

        def project(i, carry):
            rows = pl.ds(pl.multiple_of(i * 256, 256), 256)
            h = h1[rows]
            weight = wq[...].reshape(2048, 256)
            q[rows] = (jnp.dot(h, weight, preferred_element_type=F32) + query_bias).astype(BF16)
            weight = wkv[...].reshape(2048, 128)
            shift = value_bias * c.astype(F32)
            kv[c, z, i, x] = (jnp.dot(h, weight, preferred_element_type=F32) + shift).astype(BF16)
            return carry

        lax.fori_loop(0, 2, project, 0)

        def keys_of(r):
            def rows(half):
                return pl.ds(r * 128, 128) if half == BOTH else pl.ds(r * 128 + 64 * half, 64)

            def view(zz, half, xx, part):
                return kv.at[c, zz, part, xx, rows(half)]

            def their_view(zz, half, xx, part):
                return kv.at[1 - c, zz, part, xx, rows(half)]

            return plane_gather(net, view, their_view)

        keys = in_turn(keys_of(0), keys_of(1))
        cots = group_gather(net, cot, cot_out)
        next(keys)
        later.tick()
        next(cots)
        next(keys)
        next(project_weight)
        next(keys)
        next(cots)
        next(keys)
        later.tick()
        next(cots)
        for _ in keys:
            pass

        saves = [
            pltpu.make_async_copy(src, dst, local.at[8 + i])
            for i, (src, dst) in enumerate(
                ((wq, wq_out), (wkv, wkv_out), (h1, h1_out), (q, q_out), (kv, kv_out), (wo, wo_out))
            )
        ]
        for one in saves[:5]:
            one.start()
        top = attend(0, z, x, q, kv, segs, parent, scores, o, log_sum)
        top = jnp.maximum(top, attend(1, z, x, q, kv, segs, parent, scores, o, log_sum))
        for h in range(2):
            mine[0, 8 * h : 8 * h + 8] = jnp.full((8, 128), jnp.max(top[:, h * 256 : (h + 1) * 256]), F32)
        for _ in project_weight:
            pass
        saves[5].start()

        def project_out(i, d, h):
            rows = o[pl.ds(pl.multiple_of(d * 128, 128), 128)]
            for j in (2 * h, 2 * h + 1):
                weight = wo[j].reshape(512, 256)
                out = lax.dot_general(rows, weight, NT, preferred_element_type=F32).astype(BF16)
                part[d, 0, :, j * 512 : (j + 1) * 512] = out[:64]
                part[d, 1, :, j * 512 : (j + 1) * 512] = out[64:]

        def total(summed):
            value = tok[...].astype(F32) + (summed + vec[4:5])
            x1[...] = value
            own[...] = (normed(value)[0] * vec[2:3] + vec[3:4]).astype(BF16)

        rows = group_scatter(net, part, *scratch, total, project_out)
        largest = heads_max(net, mine, got, best)
        for _ in range(3):
            next(rows)
            next(largest)
        next(rows)
        later.tick()
        next(rows, None)
        me = pltpu.make_async_copy(own, h2.at[y, c], local.at[14])
        me.start()
        spreading = group_gather(net, own, h2)
        next(spreading)
        for _ in largest:
            pass
        for _ in spreading:
            pass
        me.wait()
        for _ in cots:
            pass
        later.tick()
        starts[1].wait()
        for one in saves:
            one.wait()
        net.finish()

    n, d = tokens.shape
    rows = jax.ShapeDtypeStruct((4, 2, n, d), BF16)

    def bf(*shape):
        return jax.ShapeDtypeStruct(shape, BF16)

    def f32(*shape):
        return jax.ShapeDtypeStruct(shape, F32)

    return pl.pallas_call(
        kernel,
        out_shape=(
            rows,
            rows,
            bf(4, 2, 4, n, 1024),
            bf(4, 2, 4, n, 1024),
            bf(4, 2, 4, n, 256),
            bf(4, 2, 4, n, 256),
            bf(4, 2, 4, 2, 2, 16, 128),
            bf(512, d),
            bf(512, 256),
            bf(2, 4, 2, 4, 256, 128),
            bf(512, 256),
            f32(2, 8, 512),
            f32(n, d),
            f32(2, 16, 128),
            f32(16, d),
            f32(8, 128),
        ),
        in_specs=[INV, INV, INS, INS] + [INV] * 8,
        out_specs=(ANY,) * 10 + (INV,) * 6,
        scratch_shapes=[
            VMEM((4, 2, n, d), BF16),
            VMEM((512, d), BF16),
            VMEM((4, 2, 4, 2, 2, 16, 128), BF16),
            VMEM((4, 2, 4, n, 256), BF16),
            VMEM((4, 2, 4, n, 256), BF16),
            VMEM((512, 256), BF16),
            VMEM((2, 4, 2, 4, 256, 128), BF16),
            VMEM((10, 256, 512), F32),
            VMEM((4, 2, n, d), BF16),
            VMEM((n, d), BF16),
            VMEM((5, 16, 128), F32),
            VMEM((7, 16, 128), F32),
            VMEM((2, 32, 128), BF16),
            VMEM((2, 2, 2, 32, 128), BF16),
            VMEM((3, 16, 128), BF16),
            VMEM((4, 4, 2, 16, 128), BF16),
            pltpu.SemaphoreType.DMA((15,)),
        ]
        + scatter_scratch(n, d)
        + sems(280),
        compiler_params=params(1),
        name="forward",
    )(tokens, cotangent, seg_ids, parents, vectors, query_bias, up_bias, w_keyval, w_query, w_out, w_up, w_down)


def normed(values):
    centred = values - jnp.mean(values, axis=-1, keepdims=True)
    inverse = lax.rsqrt(jnp.mean(centred * centred, axis=-1, keepdims=True) + EPS)
    return centred * inverse, inverse


def norm_back(grad, norm, inverse, gain):
    scaled = grad * gain
    return inverse * (
        scaled
        - jnp.mean(scaled, axis=-1, keepdims=True)
        - norm * jnp.mean(scaled * norm, axis=-1, keepdims=True)
    )


def heads_max(net, mine, got, best):
    for i, (up, down) in enumerate((("xu", "xd"), ("zu", "zd"))):
        k = [net.slot() for _ in range(3)]
        a, b, d = got.at[3 * i], got.at[3 * i + 1], got.at[3 * i + 2]
        net.send(mine.at[2 * i], a, k[0], up)
        net.send(mine.at[2 * i], b, k[1], down)
        yield
        net.got(a, k[0])
        net.got(b, k[1])
        mine[2 * i + 1] = jnp.maximum(mine[2 * i], jnp.maximum(a[...], b[...]))
        net.send(mine.at[2 * i + 1], d, k[2], up)
        yield
        net.got(d, k[2])
        mine[2 * i + 2] = jnp.maximum(mine[2 * i + 1], d[...])
    k = net.slot()
    net.send(mine.at[4], got.at[6], k, "yo")
    yield
    net.got(got.at[6], k)
    best[net.yh] = mine[4]
    best[1 - net.yh] = got[6]


def weight_scatter(net, g, tmp, out):
    z, yh, x = net.z, net.yh, net.x
    w = g.shape[-1]
    k = net.slot()
    yield from plane_scatter(net, column_view(g), tmp)
    mine = out.at[:, pl.ds(pl.multiple_of(yh * w, 128), w)]
    net.send(g.at[z, 1 - yh, x], mine, k, "yo")
    out[:, pl.ds(pl.multiple_of(yh * w, 128), w)] = g[z, yh, x]
    yield
    net.got(out.at[:, pl.ds(pl.multiple_of((1 - yh) * w, 128), w)], k)


def smooth_gate(u):
    scale = 0.7978845608028654
    square = u * u
    t = jnp.tanh(scale * u * (1.0 + 0.044715 * square))
    half = 0.5 * (1.0 + t)
    slope = half + 0.5 * u * (1.0 - t * t) * scale * (1.0 + 0.134145 * square)
    return u * half, slope


def piece(ref, which, zz, yy, xx):
    return jnp.concatenate(
        [ref[zz, yy, xx, :, (which * 4 + r) * 128 : (which * 4 + r + 1) * 128] for r in range(4)], axis=0
    )


def put_piece(ref, which, zz, yy, xx, value):
    for r in range(4):
        ref[zz, yy, xx, :, (which * 4 + r) * 128 : (which * 4 + r + 1) * 128] = value[r * 64 : (r + 1) * 64]


def attend_back(z, x, q, kv, o, go, log_sum, segs, parents, grad, lone, dq_sum, dq):
    lane = (lax.broadcasted_iota(jnp.int32, (256, 512), 1) & 255).astype(F32)
    ahead = lax.broadcasted_iota(jnp.int32, (256, 512), 0).astype(F32) - lane
    places = [place_of(segs, parents, z * 8 + b * 4 + x) for b in range(2)]

    def stacked(ref, b):
        return jnp.concatenate([ref[b * 256 : b * 256 + 256, :128], ref[b * 256 : b * 256 + 256, 128:]], axis=0)

    logs, inner = [], []
    for b in range(2):
        logs.append(log_sum[b, 0:1])
        inner.append(
            jnp.sum((stacked(go, b).astype(F32) * stacked(o, b).astype(F32)).T, axis=0, keepdims=True)
        )

    def one(b, key, value, masked, first):
        both, up = stacked(q, b), stacked(go, b)
        s = masked(lax.dot_general(key, both, NT, preferred_element_type=F32) * (SCALE * LOG2E))
        p = jnp.exp2(s - logs[b])
        dp = lax.dot_general(value, up, NT, preferred_element_type=F32)
        ds = (p * (dp - inner[b])).astype(BF16)
        more = lax.dot_general(key, ds, TN, preferred_element_type=F32)
        dq_sum[b] = more if first else dq_sum[b] + more
        dk = jnp.dot(ds, both, preferred_element_type=F32) * SCALE
        dv = jnp.dot(p.astype(BF16), up, preferred_element_type=F32)
        return dk.astype(BF16), dv.astype(BF16)

    for b in range(2):
        trunk, leaf, branch, above = places[b]
        lone[b, 0, 0], lone[b, 0, 1] = one(
            b,
            piece(kv, 0, z, b, x),
            piece(kv, 1, z, b, x),
            lambda s: jnp.where(ahead <= 0.0, s, NEG) + (branch - 1.0) * 1e30,
            True,
        )
        key, value = (
            sum(piece(kv, w, 2 + j // 8, j // 4 % 2, j % 4) * wide(above[j]) for j in range(16)) for w in range(2)
        )
        lone[b, 1, 0], lone[b, 1, 1] = one(b, key, value, lambda s: s + (leaf - 1.0) * 1e30, False)
    yield

    for j in range(16):
        own = [
            wide((z * 8 + b * 4 + x == 16 + j).astype(F32) * jnp.ones((1, 1), F32)) for b in range(2)
        ]
        for w in range(2):
            value = sum(lone[b, 0, w] * own[b] + lone[b, 1, w] * wide(places[b][3][j]) for b in range(2))
            put_piece(grad, w, 2 + j // 8, j // 4 % 2, j % 4, value)

    def trunk_one(i, carry):
        yy, xx = i // 4, i % 4
        totals = None
        for b in range(2):
            trunk = places[b][0]
            second = wide(trunk)
            first = 1 - second
            key, value = (piece(kv, w, 0, yy, xx) * first + piece(kv, w, 1, yy, xx) * second for w in range(2))
            start = (z * 8 + b * 4 + x).astype(F32) - 8.0 * trunk
            gap = (start - i.astype(F32)) * 256.0
            dk, dv = one(b, key, value, lambda s: jnp.where(ahead <= gap, s, NEG), False)
            parts = [dk * first, dv * first, dk * second, dv * second]
            totals = parts if totals is None else [t + p for t, p in zip(totals, parts)]
        for t in range(2):
            for w in range(2):
                put_piece(grad, w, t, yy, xx, totals[2 * t + w])
        return carry

    for i in range(0, 8, 2):
        lax.fori_loop(i, i + 2, trunk_one, 0)
        yield
    for b in range(2):
        rows = (dq_sum[b] * SCALE).T.astype(BF16)
        dq[b * 256 : b * 256 + 256, :128] = rows[:256]
        dq[b * 256 : b * 256 + 256, 128:] = rows[256:]


def spread(net, names, src, dst, k):
    for i, name in enumerate(names):
        net.send(src, dst.at[i], k[i], name)


def all_sums(net, mine, near, far):
    k = [net.slot() for _ in range(6)]
    spread(net, ("xu", "xd", "xo"), mine.at[0], near, k)
    yield
    for i in range(3):
        net.got(near.at[i], k[i])
    mine[1] = mine[0] + near[0] + near[1] + near[2]
    spread(net, ("zu", "zd", "zo"), mine.at[1], far, k[3:])
    yield
    for i in range(3):
        net.got(far.at[i], k[3 + i])
    mine[2] = mine[1] + far[0] + far[1] + far[2]


def backward(tokens, cotangent, cot_all, h2, wu, wd, wq, wo, packs, h1, q, kv, o, log_sum, x1, vec, ub):
    def kernel(tok, cot, cot_in, h2_in, wu_in, wd_in, wq_in, wo_in, packs_in, h1_in, q, kv_in, o, log_sum,
               x1, vec, ub_in,
               output, grad_input, up_out, down_out, wo_out, wq_out, vec_out, bias_out, kv_out, vb_out,
               h2, cots, wu, wd, wq, wo, packs, adu, us, das, part, part_mlp, gu, gd, gwo, gq, own, dz, dx1, sums, go,
               lone, dq_sum, dq, dkv_from, dkv, gkv, gkv_z, gkv_x, bias, bias_x, bias_z, vecs, vec_z, vec_x,
               local, *rest):
        *scratch, ss, rs = rest
        first, second, tmp_u, tmp_d, tmp_o, tmp_q, tmp_k, tmp_v = (
            scratch[:4],
            scratch[4:8],
            scratch[8:16],
            scratch[16:24],
            scratch[24:32],
            scratch[32:40],
            scratch[40:48],
            scratch[48:56],
        )
        net = Net(ss, rs)
        z, yh, x, yl, c, y = net.z, net.yh, net.x, net.yl, net.c, net.y

        def columns(ref, j):
            return ref.at[:, :, :, :, pl.ds(j * 256, 256)]

        def load(src, dst, i):
            one = pltpu.make_async_copy(src, dst, local.at[i])
            one.start()
            return one

        load(h2_in, h2, 0)
        load(columns(wu_in, 0), columns(wu, 0), 2)
        load(cot_in, cots, 1)
        for j in range(1, 4):
            load(columns(wu_in, j), columns(wu, j), 2 + j)
        there_d, here_d, every = column_view(wd_in), column_view(wd), slice(None)
        parts_d = [(zz, BOTH, every, 0) for zz in (z, net.zu, net.zd)]
        parts_d += [(every, BOTH, xx, 1) for xx in (x, net.xu, net.xd)]
        loads_d = [load(there_d(*at), here_d(*at), i) for at, i in zip(parts_d, (6, 7, 8, 9, 24, 25))]
        loads = [load(wo_in, wo, 10), load(wq_in, wq, 11)]
        loads.append(load(packs_in, packs, 12))
        net.barrier(PLANE + RING + ("yo", "xo", "zo"))
        kd = [net.slot() for _ in range(4)]
        last_parts = (
            ((net.zd, 0, every, 0), "zu"),
            ((net.zu, 1, every, 0), "zd"),
            ((every, 0, net.xd, 1), "xu"),
            ((every, 1, net.xu, 1), "xd"),
        )
        for k, (at, name) in zip(kd, last_parts):
            net.send(there_d(*at), here_d(*at), k, name)
        pltpu.make_async_copy(h2_in, h2, local.at[0]).wait()

        def hidden(j, carry):
            at = pl.ds(pl.multiple_of(j * 256, 256), 256)
            there = pl.ds(0, 4), pl.ds(0, 2), pl.ds(0, 4), pl.ds(0, 64), at
            pltpu.make_async_copy(wu_in.at[there], wu.at[there], local.at[2 + j]).wait()
            us[:, at] = jnp.dot(
                h2[...].reshape(512, 2048), wu[there].reshape(2048, 256), preferred_element_type=F32
            )
            return carry

        def hidden_back(j, carry):
            at = pl.ds(pl.multiple_of(j * 256, 256), 256)
            there = pl.ds(0, 4), pl.ds(0, 2), pl.ds(0, 4), pl.ds(0, 64), at
            das[...] = jnp.dot(
                cots[...].reshape(512, 2048), wd[there].reshape(2048, 256), preferred_element_type=F32
            )
            bias_row = jnp.concatenate([ub_in[pl.ds(2 * j, 1)], ub_in[pl.ds(2 * j + 1, 1)]], axis=1)

            def gate(i, total):
                rows = pl.ds(pl.multiple_of(i * 64, 64), 64)
                value, slope = smooth_gate(us[rows, at] + bias_row)
                adu[0, rows, at] = value.astype(BF16)
                du = (das[rows] * slope).astype(BF16)
                adu[1, rows, at] = du
                return total + jnp.sum(du.astype(F32), axis=0, keepdims=True)

            total = lax.fori_loop(0, 8, gate, jnp.zeros((1, 256), F32))
            bias[0, pl.ds(2 * j, 1)] = total[:, :128]
            bias[0, pl.ds(2 * j + 1, 1)] = total[:, 128:]
            return carry

        lax.fori_loop(0, 4, hidden, 0)
        pltpu.make_async_copy(cot_in, cots, local.at[1]).wait()
        for one in loads_d:
            one.wait()
        for k, at in zip(kd, ((net.zo, 0, every, 0), (net.zo, 1, every, 0), (every, 0, net.xo, 1), (every, 1, net.xo, 1))):
            net.got(here_d(*at), k)
        lax.fori_loop(0, 4, hidden_back, 0)

        def projected(dst, d, rows, weight, h=None):
            def column(j, carry):
                out = lax.dot_general(rows, weight(j), NT, preferred_element_type=F32).astype(BF16)
                at = pl.ds(pl.multiple_of(j * 512, 512), 512)
                dst[d, 0, :, at] = out[:64]
                dst[d, 1, :, at] = out[64:]
                return carry

            lax.fori_loop(0 if h is None else 2 * h, 4 if h is None else 2 * h + 2, column, 0)

        def ring_rows(d):
            return pl.ds(pl.multiple_of(d * 128, 128), 128)

        def make_two(i, d, h):
            projected(part, d, adu[1, ring_rows(d)], lambda j: wu[j].reshape(512, 1024), h)

        def total_two(summed):
            norm, inverse = normed(x1[...])
            grad = cot[...].astype(F32) + norm_back(summed, norm, inverse, vec[2:3])
            dx1[...] = grad
            rounded = grad.astype(BF16)
            own[...] = rounded
            values = (summed * norm, summed, rounded.astype(F32), cot[...].astype(F32))
            for i, v in enumerate(values):
                sums[2 + i : 3 + i] = jnp.sum(v, axis=0, keepdims=True)

        def outer(dst, left, right):
            def block(j, carry):
                out = lax.dot_general(left(j), right, TN, preferred_element_type=F32)
                dst[j] = out.astype(BF16).reshape(2, 4, 64, right.shape[1])
                return carry

            lax.fori_loop(0, 4, block, 0)

        def wide_outer(dst, left, which):
            def block(i, carry):
                j, w = i // 2, i % 2
                at = pl.ds(pl.multiple_of(w * 512, 512), 512)
                out = lax.dot_general(
                    left[:, :, :, pl.ds(pl.multiple_of(j * 512, 512), 512)].reshape(512, 512),
                    adu[which, :, at],
                    TN,
                    preferred_element_type=F32,
                )
                dst[j, :, :, :, at] = out.astype(BF16).reshape(2, 4, 64, 512)
                return carry

            lax.fori_loop(0, 8, block, 0)

        rows_two = group_scatter(net, part, *first, total_two, make_two)
        next(rows_two)
        next(rows_two)
        wide_outer(gd, cots, 0)
        down = weight_scatter(net, gd, tmp_d, down_out)
        next(down)
        next(rows_two)
        wide_outer(gu, h2, 1)
        up = weight_scatter(net, gu, tmp_u, up_out)
        next(up)
        next(rows_two)
        next(rows_two, None)
        me = load(own, dz.at[y, c], 23)
        spreading = group_gather(net, own, dz)
        next(spreading)
        for d in range(2):
            projected(part_mlp, d, adu[0, d * 128 : d * 128 + 128], lambda j: wd[j].reshape(512, 1024))
        next(spreading)
        next(down)
        for d in range(2, 4):
            projected(part_mlp, d, adu[0, d * 128 : d * 128 + 128], lambda j: wd[j].reshape(512, 1024))
        keep = [
            load(kv_in.at[w, :, :, :, pl.ds(r * 64, 64)], wd.at[:, :, :, :, pl.ds((w * 4 + r) * 128, 128)], 13 + 4 * w + r)
            for w in range(2)
            for r in range(4)
        ]
        next(spreading)
        next(up)
        late = [load(h1_in.at[:, pl.ds(w * 1024, 1024)], adu.at[w], 21 + w) for w in range(2)]
        for _ in spreading:
            pass
        me.wait()
        loads[0].wait()
        go[...] = jnp.dot(
            dz[...].reshape(512, 2048), wo[...].reshape(2048, 256), preferred_element_type=F32
        ).astype(BF16)

        def total_out(summed):
            output[...] = (x1[...] + (summed + vec[5:6])).astype(BF16)

        rows_out = group_scatter(net, part_mlp, *second, total_out)
        next(rows_out)
        outer(gwo, lambda j: dz[:, :, :, pl.ds(pl.multiple_of(j * 512, 512), 512)].reshape(512, 512), o[...])
        project = weight_scatter(net, gwo, tmp_o, wo_out)
        next(project)
        for one in keep:
            one.wait()
        steps = attend_back(z, x, q, wd, o, go, log_sum, vec[8:9, 0:128], vec[9:10, 0:128], wu, lone, dq_sum, dq)

        theirs = pl.ds(pl.multiple_of((1 - c) * 512, 512), 512)
        ours = pl.ds(pl.multiple_of(c * 512, 512), 512)

        def swap(zs, ys):
            k = [net.slot() for _ in range(4)]
            zr, yr = pl.ds(zs, 2), pl.ds(ys[0], len(ys))
            for i in range(4):
                net.send(wu.at[zr, yr, i, :, theirs], cots.at[zr, yr, :, pl.ds(i * 512, 512)], k[i], "c")
            yield
            for i in range(4):
                net.got(cots.at[zr, yr, :, pl.ds(i * 512, 512)], k[i])
                for zz in (zs, zs + 1):
                    for yy in ys:
                        wu[zz, yy, i, :, ours] = wu[zz, yy, i, :, ours] + cots[zz, yy, :, i * 512 : i * 512 + 512]

        swaps = [swap(2, (0, 1)), swap(0, (0,)), swap(0, (1,))]
        next(steps)
        next(down)
        next(rows_out)
        next(steps)
        next(swaps[0])
        next(up)
        next(steps)
        next(swaps[1])
        next(down)
        next(rows_out)
        next(steps)
        next(swaps[0], None)
        next(up)
        next(steps)
        next(swaps[2])
        next(swaps[1], None)
        next(down)
        next(rows_out)
        next(project)
        next(steps, None)
        next(up)
        next(rows_out, None)
        for one in loads[1:] + late:
            one.wait()

        def make_one(i, d, h):
            projected(h2, d, dq[ring_rows(d)], lambda j: wq[j].reshape(512, 256), h)
            if i == 3:
                for j in (2 * h, 2 * h + 1):
                    more = lax.dot_general(
                        dkv[y], packs[j].reshape(512, 128), NT, preferred_element_type=F32
                    ).astype(BF16)
                    at = slice(j * 512, (j + 1) * 512)
                    h2[d, 0, :, at] = h2[d, 0, :, at] + more[:64]
                    h2[d, 1, :, at] = h2[d, 1, :, at] + more[64:]

        def total_one(summed):
            norm, inverse = normed(tok[...].astype(F32))
            grad_input[...] = dx1[...] + norm_back(summed, norm, inverse, vec[0:1])
            sums[0:1] = jnp.sum(summed * norm, axis=0, keepdims=True)
            sums[1:2] = jnp.sum(summed, axis=0, keepdims=True)
            sums[6:8] = jnp.zeros((2, 2048), F32)
            vecs[y, c] = sums[...]

        rows_one = group_scatter(net, h2, *first, total_one, make_one)
        next(rows_one)
        next(swaps[2], None)

        def keys_of(r, tmp):
            def view(zz, half, xx, part):
                start = c * 512 + r * 256
                if half == BOTH:
                    return wu.at[zz, part, xx, :, pl.ds(pl.multiple_of(start, 256), 256)]
                return wu.at[zz, part, xx, :, pl.ds(pl.multiple_of(start + half * 128, 128), 128)]

            return plane_scatter(net, view, tmp)

        keys = in_turn(keys_of(0, tmp_k), keys_of(1, tmp_v))
        next(keys)
        next(rows_one)
        outer(gq, lambda j: adu[j // 2, :, pl.ds(pl.multiple_of((j % 2) * 512, 512), 512)], dq[...])
        bias[0, 8:9] = jnp.sum(dq[:, :128].astype(F32), axis=0, keepdims=True)
        bias[0, 9:10] = jnp.sum(dq[:, 128:].astype(F32), axis=0, keepdims=True)
        bias[0, 10:16] = jnp.zeros((6, 128), F32)
        next(keys)
        query = weight_scatter(net, gq, tmp_q, wq_out)
        next(query)
        small = all_sums(net, bias, bias_x, bias_z)
        next(small)
        next(rows_one)
        next(keys)
        next(down, None)
        next(up, None)
        next(query)
        next(small)
        next(keys)
        next(project)
        for _ in keys:
            pass

        def ring_piece(ref, d):
            at = pl.ds(pl.multiple_of(c * 512 + lax.rem(d, 2) * 256, 256), 256)
            return ref.at[z, d // 2, x, :, at]

        kr = [net.slot() for _ in range(7)]
        for i, (name, d) in enumerate((("yu", net.yu), ("yd", net.yd), ("yo", net.yo))):
            net.send(ring_piece(wu, d), dkv_from.at[i], kr[i], name)
        for i in range(3):
            net.got(dkv_from.at[i], kr[i])
        mine = ring_piece(wu, y)[...].astype(F32)
        for i in range(3):
            mine = mine + dkv_from[i].astype(F32)
        mine = mine.astype(BF16)
        dkv[y] = jnp.concatenate([mine[:, :128], mine[:, 128:]], axis=0)
        for i, name in enumerate(("yu", "yd", "yo")):
            net.send(dkv.at[y], dkv.at[y], kr[3 + i], name)
        next(rows_one)
        next(query)
        next(rows_one, None)

        def vectors():
            k = [net.slot() for _ in range(13)]
            at = vecs.at[y, c]
            for i, name in enumerate(("yu", "yd", "yo", "c")):
                net.send(at, at, k[i], name)
            yield
            for i, d in enumerate((net.yd, net.yu, net.yo)):
                net.got(vecs.at[d, c], k[i])
                net.send(vecs.at[d, c], vecs.at[d, c], k[4 + i], "c")
            yield
            for i, d in enumerate((y, net.yd, net.yu, net.yo)):
                net.got(vecs.at[d, 1 - c], k[3 + i])
            acc = vecs[0, 0]
            for i in range(1, 8):
                acc = acc + vecs[i // 2, i % 2]
            for i in range(4):
                vec_z[i] = acc[:, i * 512 : (i + 1) * 512]
            for i, (name, d) in enumerate((("zu", net.zu), ("zd", net.zd), ("zo", net.zo))):
                net.send(vec_z.at[d], vec_z.at[4 + i], k[7 + i], name)
            yield
            for i in range(3):
                net.got(vec_z.at[4 + i], k[7 + i])
            acc = vec_z[z] + vec_z[4] + vec_z[5] + vec_z[6]
            vec_x[0] = jnp.where(yh == 0, acc[:, :256], acc[:, 256:])
            spread(net, ("xu", "xd", "xo"), vec_x.at[0], vec_x.at[pl.ds(1, 3)], k[10:])
            yield
            for i in range(3):
                net.got(vec_x.at[1 + i], k[10 + i])
            vec_out[...] = vec_x[0] + vec_x[1] + vec_x[2] + vec_x[3]

        vector = vectors()
        next(vector)
        next(small, None)
        for i, d in enumerate((net.yd, net.yu, net.yo)):
            net.got(dkv.at[d], kr[3 + i])

        every = dkv[...].reshape(512, 128)
        value_sum = jnp.broadcast_to(jnp.sum(every.astype(F32), axis=0, keepdims=True), (8, 128))
        for j in range(4):
            at = pl.ds(pl.multiple_of((j % 2) * 512 + yh * 256, 256), 256)
            out = lax.dot_general(adu[j // 2, :, at], every, TN, preferred_element_type=F32).reshape(4, 2, 32, 128)
            for i in range(4):
                gkv[j, i, 0:32] = jnp.where(yl == 0, out[i, 0], out[i, 1])
                gkv[j, i, 32:40] = value_sum

        def key_value():
            k = [net.slot() for _ in range(7)]
            for i, (name, d) in enumerate((("zu", net.zu), ("zd", net.zd), ("zo", net.zo))):
                net.send(gkv.at[d], gkv_z.at[i], k[i], name)
            yield
            for i in range(3):
                net.got(gkv_z.at[i], k[i])
            for i in range(4):
                gkv_x[i] = gkv[z, i] + gkv_z[0, i] + gkv_z[1, i] + gkv_z[2, i]
            for i, (name, d) in enumerate((("xu", net.xu), ("xd", net.xd), ("xo", net.xo))):
                net.send(gkv_x.at[d], gkv_x.at[4 + i], k[3 + i], name)
            yield
            for i in range(3):
                net.got(gkv_x.at[4 + i], k[3 + i])
            total = gkv_x[x] + gkv_x[4] + gkv_x[5] + gkv_x[6]
            gkv_x[7, 0:16] = jnp.where(c == 0, total[0:16], total[16:32])
            gkv_x[7, 16:32] = jnp.where(c == 0, total[16:32], total[0:16])
            gkv_x[7, 32:40] = total[32:40]
            net.send(gkv_x.at[7, pl.ds(16, 24)], gkv_x.at[8, pl.ds(16, 24)], k[6], "c")
            yield
            net.got(gkv_x.at[8, pl.ds(16, 24)], k[6])
            here, there = gkv_x[7, 0:16], gkv_x[8, 16:32]
            kv_out[:, 0:128] = jnp.where(c == 0, here, there)
            kv_out[:, 128:256] = jnp.where(c == 0, there, here)
            vb_out[...] = jnp.where(c == 0, gkv_x[8, 32:40], gkv_x[7, 32:40])

        def partner_bias():
            k = net.slot()
            net.send(bias.at[2], bias_out.at[1], k, "yo")
            bias_out[0] = bias[2]
            yield
            net.got(bias_out.at[1], k)

        last = key_value()
        next(last)
        run_all(vector, last, partner_bias(), query, project, down, up)
        net.finish()

    n, d = tokens.shape

    def bf(*shape):
        return jax.ShapeDtypeStruct(shape, BF16)

    def f32(*shape):
        return jax.ShapeDtypeStruct(shape, F32)

    return pl.pallas_call(
        kernel,
        out_shape=(
            bf(n, d),
            f32(n, d),
            bf(n, d),
            bf(n, d),
            bf(n, 512),
            bf(n, 512),
            f32(8, 256),
            f32(2, 16, 128),
            f32(16, 256),
            f32(8, 128),
        ),
        in_specs=[INV, INV] + [ANY] * 8 + [INV, ANY] + [INV] * 5,
        out_specs=(INV,) * 10,
        scratch_shapes=[
            VMEM((4, 2, n, d), BF16),
            VMEM((4, 2, n, d), BF16),
            VMEM((4, 2, 4, n, 1024), BF16),
            VMEM((4, 2, 4, n, 1024), BF16),
            VMEM((4, 2, 4, n, 256), BF16),
            VMEM((4, 2, 4, n, 256), BF16),
            VMEM((4, 2, 4, 2, 2, 16, 128), BF16),
            VMEM((2, 512, 1024), BF16),
            VMEM((512, 1024), F32),
            VMEM((512, 256), F32),
            VMEM((4, 2, n, d), BF16),
            VMEM((4, 2, n, d), BF16),
            VMEM((4, 2, 4, n, 1024), BF16),
            VMEM((4, 2, 4, n, 1024), BF16),
            VMEM((4, 2, 4, n, 256), BF16),
            VMEM((4, 2, 4, n, 256), BF16),
            VMEM((n, d), BF16),
            VMEM((4, 2, n, d), BF16),
            VMEM((n, d), F32),
            VMEM((8, d), F32),
            VMEM((512, 256), BF16),
            VMEM((2, 2, 2, 256, 128), BF16),
            VMEM((2, 128, 512), F32),
            VMEM((512, 256), BF16),
            VMEM((3, 64, 256), BF16),
            VMEM((4, 128, 128), BF16),
            VMEM((4, 4, 40, 128), F32),
            VMEM((3, 4, 40, 128), F32),
            VMEM((9, 40, 128), F32),
            VMEM((3, 16, 128), F32),
            VMEM((3, 16, 128), F32),
            VMEM((3, 16, 128), F32),
            VMEM((4, 2, 8, d), F32),
            VMEM((7, 8, 512), F32),
            VMEM((4, 8, 256), F32),
            pltpu.SemaphoreType.DMA((26,)),
        ]
        + scatter_scratch(n, d)
        + scatter_scratch(n, d)
        + plane_scratch(n, 512)
        + plane_scratch(n, 512)
        + plane_scratch(n, 128)
        + plane_scratch(n, 128)
        + [VMEM(s, BF16) for s in ((2, 4, n, 128), (2, 4, n, 128), (2, 4, n, 256), (2, 4, n, 256))]
        + [VMEM(s, BF16) for s in ((2, n, 128), (2, n, 128), (2, n, 256), (2, n, 256))]
        + [VMEM(s, BF16) for s in ((2, 4, n, 128), (2, 4, n, 128), (2, 4, n, 256), (2, 4, n, 256))]
        + [VMEM(s, BF16) for s in ((2, n, 128), (2, n, 128), (2, n, 256), (2, n, 256))]
        + sems(280),
        compiler_params=params(2, 62 << 20),
        name="backward",
    )(tokens, cotangent, cot_all, h2, wu, wd, wq, wo, packs, h1, q, kv, o, log_sum, x1, vec, ub)


def finish(up, down, out, query, grad_input, output, keyval, vec, bias, value_bias, best, w_query, query_bias, tau):
    def kernel(up, down, out, query, grad_input, output, keyval, vec, bias, vb, best, wq, qb, tau,
               output_o, grad_o, query_o, up_o, out_o, down_o, qb_o, ub_o, kv_o, vb_o, v0, v1, v2, v3, v4, v5, wq_o, cb_o):
        for src, dst in ((output, output_o), (grad_input, grad_o), (keyval, kv_o)):
            dst[...] = src[...]
        z, yh, x, yl, c = (lax.axis_index(a) for a in AXES)
        tp = yl * 2 + c
        dp = (z * 2 + yh) * 4 + x
        for src, dst in ((up, up_o), (down, down_o), (out, out_o), (query, query_o)):
            dst[...] = src[...].astype(F32)

        def pick(rows, count, start):
            lanes = rows.shape[1]
            hot = (
                lax.broadcasted_iota(jnp.int32, (lanes, count), 0)
                == lax.broadcasted_iota(jnp.int32, (lanes, count), 1) + start
            ).astype(F32)
            return hot, rows

        low, high = jnp.where(yh == 0, bias[0], bias[1]), jnp.where(yh == 0, bias[1], bias[0])
        exact = lax.Precision.HIGHEST
        hot, rows = pick(jnp.concatenate([low[0:8], high[0:8]], axis=0), 4, dp * 4)
        ub_o[...] = lax.dot_general(hot, rows, (((0,), (1,)), ((), ())), precision=exact, preferred_element_type=F32)
        hot, rows = pick(jnp.concatenate([low[8:10], high[8:10], low[10:14]], axis=0), 4, dp * 4)
        heads = lax.dot_general(hot, rows, (((0,), (1,)), ((), ())), precision=exact, preferred_element_type=F32)
        qb_o[...] = heads[:, 0:4]
        hot, rows = pick(vec[...], 16, x * 64 + tp * 16)
        own = jnp.dot(rows, hot, precision=exact, preferred_element_type=F32)
        for i, ref in enumerate((v0, v1, v2, v3, v4, v5)):
            ref[...] = own[i : i + 1]
        lane = lax.broadcasted_iota(jnp.int32, (1, 128), 1)
        vb_o[...] = splat(vb[0:1], lane, dp * 4 + tp)
        limit = tau[0]
        factors = jnp.zeros((1, 128), F32)
        for h in range(4):
            factor = limit / jnp.maximum(best[h // 2, 8 * (h % 2) : 8 * (h % 2) + 1], limit)
            at = slice(h * 128, (h + 1) * 128)
            wq_o[:, at] = (wq[:, at].astype(F32) * factor).astype(BF16)
            factors = jnp.where(lane == h, factor, factors)
        cb_o[...] = (qb[...].astype(F32) * factors[:, 0:4]).astype(BF16)

    n, d = output.shape

    def f32(*shape):
        return jax.ShapeDtypeStruct(shape, F32)

    shapes = (
        jax.ShapeDtypeStruct((n, d), BF16),
        f32(n, d),
        f32(n, 512),
        f32(n, d),
        f32(n, 512),
        f32(n, d),
        f32(4, 4),
        f32(4, 16),
        f32(16, 256),
        f32(1, 1),
    )
    shapes += (f32(1, 16),) * 6
    shapes += (jax.ShapeDtypeStruct((n, 512), BF16), jax.ShapeDtypeStruct((4, 4), BF16))
    return pl.pallas_call(
        kernel,
        out_shape=shapes,
        in_specs=[INV] * 13 + [INS],
        out_specs=(INV,) * 18,
        compiler_params=pltpu.CompilerParams(vmem_limit_bytes=60 << 20),
        name="finish",
    )(up, down, out, query, grad_input, output, keyval, vec, bias, value_bias, best, w_query, query_bias, tau)


def local(
    tokens,
    cotangent,
    seg_ids,
    parents,
    tau,
    w_query,
    w_up,
    w_out,
    w_down,
    query_bias,
    up_bias,
    w_keyval,
    value_bias,
    norm1_gain,
    norm1_bias,
    norm2_gain,
    norm2_bias,
    out_bias,
    down_bias,
):
    vectors = jnp.pad(value_bias.reshape(1, 1), ((6, 9), (0, 15)))
    for i, one in enumerate((norm1_gain, norm1_bias, norm2_gain, norm2_bias, out_bias, down_bias)):
        vectors = vectors + jnp.pad(one.reshape(1, 16), ((i, 15 - i), (0, 0)))
    (cot_all, h2, wu, wd, wq, wo, wkv, h1, q, kv, o, log_sum, x1, best, vec, ub) = forward(
        tokens, cotangent, seg_ids, parents, vectors, query_bias, up_bias, w_keyval, w_query, w_out, w_up, w_down
    )
    output, grad_input, up_sum, down_sum, out_sum, query_sum, vec_sum, bias_sum, keyval_sum, vb_sum = backward(
        tokens, cotangent, cot_all, h2, wu, wd, wq, wo, wkv, h1, q, kv, o, log_sum, x1, vec, ub
    )
    outs = finish(
        up_sum, down_sum, out_sum, query_sum, grad_input, output, keyval_sum, vec_sum, bias_sum, vb_sum, best,
        w_query, query_bias, tau,
    )
    return outs[:9] + tuple(v.reshape(-1) for v in outs[9:16]) + outs[16:]


def solution(mesh):
    fine = Mesh(mesh.devices.reshape(4, 2, 4, 2, 2), AXES)
    dp, tp = ("z", "yh", "x"), ("yl", "c")
    rows, flat, weight = P(AXES, None), P(AXES), P(dp, tp)
    in_specs = (rows, rows, P(dp), P(), P()) + (weight,) * 6 + (rows,) + (flat,) * 7
    out_specs = (rows, rows) + (weight,) * 6 + (rows,) + (flat,) * 7 + (weight, weight)
    return jax.shard_map(local, mesh=fine, in_specs=in_specs, out_specs=out_specs, check_vma=False)
```

```python
import itertools

import jax
import jax.numpy as jnp
from jax import lax
from jax.experimental import pallas as pl
from jax.experimental.pallas import tpu as pltpu
from jax.sharding import Mesh, PartitionSpec as P

EPS = 1e-05
AXES = ("z", "yh", "x", "yl", "c")
F32 = jnp.float32
BF16 = jnp.bfloat16
VMEM = pltpu.VMEM
NEG = -1e30


class Net:
    def __init__(self, send_sems, recv_sems):
        self.z, self.yh, self.x, self.yl, self.c = (lax.axis_index(a) for a in AXES)
        self.y = self.yh * 2 + self.yl
        self.yu, self.yo, self.yd = (lax.rem(self.y + s, 4) for s in (1, 2, 3))
        self.xu, self.xo, self.xd = (lax.rem(self.x + s, 4) for s in (1, 2, 3))
        self.zu, self.zo, self.zd = (lax.rem(self.z + s, 4) for s in (1, 2, 3))
        up, down = lax.rem(self.yh + self.yl, 2), lax.rem(self.yh + 1 - self.yl, 2)
        self.dev = {
            "yu": {"yh": up, "yl": 1 - self.yl},
            "yd": {"yh": down, "yl": 1 - self.yl},
            "yo": {"yh": 1 - self.yh},
            "c": {"c": 1 - self.c},
            "xu": {"x": self.xu},
            "xd": {"x": self.xd},
            "xo": {"x": self.xo},
            "zu": {"z": self.zu},
            "zd": {"z": self.zd},
            "zo": {"z": self.zo},
        }
        self.send_sems, self.recv_sems = send_sems, recv_sems
        self.count = 0
        self.sent = []

    def barrier(self, names):
        sem = pltpu.get_barrier_semaphore()
        for name in names:
            pl.semaphore_signal(
                sem, inc=1, device_id=self.dev[name], device_id_type=pl.DeviceIdType.MESH
            )
        pl.semaphore_wait(sem, len(names))

    def slot(self):
        self.count += 1
        assert self.count <= self.send_sems.shape[0]
        return self.count - 1

    def copy(self, src, dst, k, name):
        return pltpu.make_async_remote_copy(
            src_ref=src,
            dst_ref=dst,
            send_sem=self.send_sems.at[k],
            recv_sem=self.recv_sems.at[k],
            device_id=self.dev[name],
            device_id_type=pl.DeviceIdType.MESH,
        )

    def send(self, src, dst, k, name):
        one = self.copy(src, dst, k, name)
        one.start()
        self.sent.append(one)

    def got(self, ref, k):
        self.copy(ref, ref, k, "c").wait_recv()

    def finish(self):
        for one in self.sent:
            one.wait_send()


def run_all(*steps):
    live = list(steps)
    while live:
        rest = []
        for one in live:
            try:
                next(one)
                rest.append(one)
            except StopIteration:
                pass
        live = rest


def in_turn(*steps):
    live = list(steps)
    while live:
        live = [one for one in live if next(one, 1) is None]
        if live:
            yield


def columns_of(ref, h):
    w = ref.shape[-1] // 2
    return ref.at[(slice(None),) * (len(ref.shape) - 1) + (pl.ds(h * w, w),)]


def group_gather(net, src, out):
    return in_turn(*(group_gather_one(net, columns_of(src, h), columns_of(out, h)) for h in range(2)))


def group_scatter(net, part, acc, from_half, from_full, whole, total, make=None):
    def one(h):
        refs = [columns_of(ref, h) for ref in (part, acc, from_half, from_full)]
        place = columns_of(whole, h)

        def keep(summed):
            place[...] = summed

        produce = None if make is None else lambda i, d: make(i, d, h)
        return group_scatter_one(net, *refs, keep, produce)

    yield from in_turn(one(0), one(1))
    total(whole[...])


def group_gather_one(net, src, out):
    y, c, yu, yd, yo = net.y, net.c, net.yu, net.yd, net.yo
    k = [net.slot() for _ in range(9)]
    half = src.shape[0] // 2
    lo, hi = pl.ds(0, half), pl.ds(half, half)
    mine = out.at[y, c]
    net.send(src, mine, k[0], "yu")
    net.send(src, mine, k[1], "yd")
    net.send(src, mine, k[2], "c")
    yield
    net.got(out.at[yd, c], k[0])
    net.send(out.at[yd, c, lo], out.at[yd, c, lo], k[3], "yu")
    net.send(out.at[yd, c], out.at[yd, c], k[4], "c")
    net.got(out.at[yu, c], k[1])
    net.send(out.at[yu, c, hi], out.at[yu, c, hi], k[5], "yd")
    net.send(out.at[yu, c], out.at[yu, c], k[6], "c")
    yield
    net.got(out.at[yo, c, lo], k[3])
    net.send(out.at[yo, c, lo], out.at[yo, c, lo], k[7], "c")
    net.got(out.at[yo, c, hi], k[5])
    net.send(out.at[yo, c, hi], out.at[yo, c, hi], k[8], "c")
    yield
    net.got(out.at[y, 1 - c], k[2])
    net.got(out.at[yd, 1 - c], k[4])
    net.got(out.at[yu, 1 - c], k[6])
    net.got(out.at[yo, 1 - c, lo], k[7])
    net.got(out.at[yo, 1 - c, hi], k[8])


def group_scatter_one(net, part, acc, from_half, from_full, total, make=None):
    y, c, yu, yd, yo = net.y, net.c, net.yu, net.yd, net.yo
    k = [net.slot() for _ in range(8)]
    n = part.shape[2]
    half = n // 2
    lo, hi = pl.ds(0, half), pl.ds(half, half)

    sent = []

    def send(src, dst, i, name):
        sent.append(net.copy(src, dst, i, name))
        sent[-1].start()

    def start(i, d):
        if make is not None:
            make(i, d)
        send(part.at[d, 1 - c], acc.at[d], k[i], "c")

    def core_sum(i, d):
        net.got(acc.at[d], k[i])
        acc[d] = acc[d] + part[d, c]

    for i, d in enumerate((yo, yu, yd)):
        start(i, d)
    yield
    core_sum(0, yo)
    send(acc.at[yo, lo], from_half.at[0], k[4], "yu")
    send(acc.at[yo, hi], from_half.at[1], k[5], "yd")
    core_sum(1, yu)
    core_sum(2, yd)
    yield
    net.got(from_half.at[0], k[4])
    acc[yu, lo] = acc[yu, lo] + from_half[0]
    send(acc.at[yu], from_full.at[0], k[6], "yu")
    net.got(from_half.at[1], k[5])
    acc[yd, hi] = acc[yd, hi] + from_half[1]
    send(acc.at[yd], from_full.at[1], k[7], "yd")
    yield
    start(3, y)
    yield
    net.got(acc.at[y], k[3])
    mine = part[y, c].astype(F32) + acc[y].astype(F32)
    net.got(from_full.at[0], k[6])
    net.got(from_full.at[1], k[7])
    for one in sent:
        one.wait_send()
    total(mine + from_full[0].astype(F32) + from_full[1].astype(F32))


def scatter_scratch(n, w):
    return [VMEM((4, n, w), BF16), VMEM((2, n // 2, w), BF16), VMEM((2, n, w), BF16), VMEM((n, w), F32)]


BOTH = slice(None)


def plane_gather(net, o, theirs=None, last=True):
    z, x, xu, xd, xo, zu, zd, zo = net.z, net.x, net.xu, net.xd, net.xo, net.zu, net.zd, net.zo
    k = [net.slot() for _ in range(16)]
    every = slice(None)
    relayed = []

    def send(at, i, name):
        net.send(o(*at), o(*at), k[i], name)

    def got(at, i):
        net.got(o(*at), k[i])

    def relay(*at):
        if theirs is not None:
            slot = net.slot()
            net.send(o(*at), o(*at), slot, "c")
            relayed.append((at, slot))

    send((z, BOTH, x, 0), 0, "xu")
    send((z, BOTH, x, 0), 1, "xd")
    send((z, BOTH, x, 1), 2, "zu")
    send((z, BOTH, x, 1), 3, "zd")
    relay(z, BOTH, x, 0)
    relay(z, BOTH, x, 1)
    yield
    got((z, BOTH, xd, 0), 0)
    send((z, 0, xd, 0), 4, "xu")
    got((zd, BOTH, x, 1), 2)
    send((zd, 0, x, 1), 6, "zu")
    got((z, BOTH, xu, 0), 1)
    send((z, 1, xu, 0), 5, "xd")
    got((zu, BOTH, x, 1), 3)
    send((zu, 1, x, 1), 7, "zd")
    for at in ((z, BOTH, xd, 0), (zd, BOTH, x, 1), (z, BOTH, xu, 0), (zu, BOTH, x, 1)):
        relay(*at)
    yield
    got((z, 0, xo, 0), 4)
    got((z, 1, xo, 0), 5)
    send((z, BOTH, every, 0), 8, "zu")
    send((z, BOTH, every, 0), 9, "zd")
    got((zo, 0, x, 1), 6)
    got((zo, 1, x, 1), 7)
    send((every, BOTH, x, 1), 10, "xu")
    send((every, BOTH, x, 1), 11, "xd")
    relay(z, BOTH, xo, 0)
    relay(zo, BOTH, x, 1)
    yield
    if not last:
        for at, i in (((zd, BOTH, every, 0), 8), ((every, BOTH, xd, 1), 10), ((zu, BOTH, every, 0), 9), ((every, BOTH, xu, 1), 11)):
            got(at, i)
        return
    got((zd, BOTH, every, 0), 8)
    send((zd, 0, every, 0), 12, "zu")
    got((every, BOTH, xd, 1), 10)
    send((every, 0, xd, 1), 14, "xu")
    got((zu, BOTH, every, 0), 9)
    send((zu, 1, every, 0), 13, "zd")
    got((every, BOTH, xu, 1), 11)
    send((every, 1, xu, 1), 15, "xd")
    for at in ((zd, BOTH, every, 0), (every, BOTH, xd, 1), (zu, BOTH, every, 0), (every, BOTH, xu, 1)):
        relay(*at)
    yield
    got((zo, 0, every, 0), 12)
    got((zo, 1, every, 0), 13)
    relay(zo, BOTH, every, 0)
    got((every, 0, xo, 1), 14)
    got((every, 1, xo, 1), 15)
    relay(every, BOTH, xo, 1)
    for at, slot in relayed:
        net.got(theirs(*at), slot)


def add_into(dst, *others):
    for index in itertools.product(*[range(n) for n in dst.shape[:-2]]):
        at = index + (slice(None), slice(None))
        total = dst[at]
        for other in others:
            total = total + other[at]
        dst[at] = total


def plane_scatter(net, g, tmp):
    z, x, xu, xd, xo, zu, zd, zo = net.z, net.x, net.xu, net.xd, net.xo, net.zu, net.zd, net.zo
    t1, t2, u1, u2, t3, t4, u3, u4 = tmp
    k = [net.slot() for _ in range(16)]
    every = slice(None)

    def send(src, dst, i, name):
        net.send(src, dst, k[i], name)

    def got(ref, i):
        net.got(ref, k[i])

    send(g(zo, 0, every, 0), t1.at[0], 0, "zu")
    send(g(zo, 1, every, 0), t1.at[1], 1, "zd")
    send(g(every, 0, xo, 1), t2.at[0], 2, "xu")
    send(g(every, 1, xo, 1), t2.at[1], 3, "xd")
    yield
    got(t1.at[0], 0)
    add_into(g(zu, 0, every, 0), t1.at[0])
    send(g(zu, BOTH, every, 0), u1.at[0], 4, "zu")
    got(t2.at[0], 2)
    add_into(g(every, 0, xu, 1), t2.at[0])
    send(g(every, BOTH, xu, 1), u2.at[0], 6, "xu")
    got(t1.at[1], 1)
    add_into(g(zd, 1, every, 0), t1.at[1])
    send(g(zd, BOTH, every, 0), u1.at[1], 5, "zd")
    got(t2.at[1], 3)
    add_into(g(every, 1, xd, 1), t2.at[1])
    send(g(every, BOTH, xd, 1), u2.at[1], 7, "xd")
    yield
    got(u1.at[0], 4)
    got(u1.at[1], 5)
    add_into(g(z, BOTH, every, 0), u1.at[0], u1.at[1])
    send(g(z, 0, xo, 0), t3.at[0], 8, "xu")
    send(g(z, 1, xo, 0), t3.at[1], 9, "xd")
    got(u2.at[0], 6)
    got(u2.at[1], 7)
    add_into(g(every, BOTH, x, 1), u2.at[0], u2.at[1])
    send(g(zo, 0, x, 1), t4.at[0], 10, "zu")
    send(g(zo, 1, x, 1), t4.at[1], 11, "zd")
    yield
    got(t3.at[0], 8)
    add_into(g(z, 0, xu, 0), t3.at[0])
    send(g(z, BOTH, xu, 0), u3.at[0], 12, "xu")
    got(t4.at[0], 10)
    add_into(g(zu, 0, x, 1), t4.at[0])
    send(g(zu, BOTH, x, 1), u4.at[0], 14, "zu")
    got(t3.at[1], 9)
    add_into(g(z, 1, xd, 0), t3.at[1])
    send(g(z, BOTH, xd, 0), u3.at[1], 13, "xd")
    got(t4.at[1], 11)
    add_into(g(zd, 1, x, 1), t4.at[1])
    send(g(zd, BOTH, x, 1), u4.at[1], 15, "zd")
    yield
    got(u3.at[0], 12)
    got(u3.at[1], 13)
    add_into(g(z, BOTH, x, 0), u3.at[0], u3.at[1])
    got(u4.at[0], 14)
    got(u4.at[1], 15)
    add_into(g(z, BOTH, x, 1), u4.at[0], u4.at[1])


def plane_scratch(n, w):
    return [
        VMEM((2, 4, n, w), BF16),
        VMEM((2, 4, n, w), BF16),
        VMEM((2, 2, 4, n, w), BF16),
        VMEM((2, 4, 2, n, w), BF16),
        VMEM((2, n, w), BF16),
        VMEM((2, n, w), BF16),
        VMEM((2, 2, n, w), BF16),
        VMEM((2, 2, n, w), BF16),
    ]


def column_view(ref):
    w = ref.shape[-1] // 2

    def view(zz, half, xx, part):
        return ref.at[zz, half, xx, :, pl.ds(part * w, w)]

    return view


def sems(n):
    return [pltpu.SemaphoreType.DMA((n,)), pltpu.SemaphoreType.DMA((n,))]


def params(cid, limit=56 << 20):
    return pltpu.CompilerParams(collective_id=cid, has_side_effects=True, vmem_limit_bytes=limit)


ANY = pl.BlockSpec(memory_space=pl.ANY)
INV = pl.BlockSpec(memory_space=pltpu.VMEM)
INS = pl.BlockSpec(memory_space=pltpu.SMEM)
PLANE = ("xu", "xd", "zu", "zd")
RING = ("yu", "yd", "c")


class Ticks:
    def __init__(self, *steps):
        self.steps = list(steps)

    def tick(self, count=1):
        for _ in range(count):
            for one in self.steps:
                next(one, None)


def weight_gather(net, weight, out, local, last=True):
    z, yh, x = net.z, net.yh, net.x
    n, w = weight.shape[0], weight.shape[1] // 2
    k = net.slot()

    def half(which):
        return weight.at[:, pl.ds(pl.multiple_of(which * w, 128), w)]

    mine = pltpu.make_async_copy(half(yh), out.at[z, yh, x, pl.ds(0, n)], local)
    mine.start()
    net.send(half(1 - yh), out.at[z, yh, x, pl.ds(0, n)], k, "yo")
    yield
    mine.wait()
    net.got(out.at[z, 1 - yh, x, pl.ds(0, n)], k)
    yield from plane_gather(net, column_view(out), last=last)


def splat(row, lane, at):
    return jnp.sum(jnp.where(lane == at, row, 0.0), axis=1, keepdims=True)


def place_of(segs, parents, block):
    lane = lax.broadcasted_iota(jnp.int32, (1, 128), 1)
    seg = splat(segs, lane, block)
    lanes = lane.astype(F32)
    parent = splat(parents, lanes, seg)
    trunk = splat(parents, lanes, parent)
    leaf = (seg >= 10.0).astype(F32)
    branch = (seg >= 2.0).astype(F32)
    above = [(splat(segs, lane, b) == parent).astype(F32) * leaf for b in range(16, 32)]
    return trunk, leaf, branch, above


def wide(value):
    return jnp.broadcast_to(value, (1, 128)).astype(BF16)


def trunk_block(kv, which, i, trunk):
    one = wide(trunk)
    return kv[which, 0, i // 4, i % 4] * (1 - one) + kv[which, 1, i // 4, i % 4] * one


def parent_block(kv, which, above):
    total = kv[which, 2, 0, 0] * wide(above[0])
    for j in range(1, 16):
        total = total + kv[which, 2 + j // 8, j // 4 % 2, j % 4] * wide(above[j])
    return total


NT = (((1,), (1,)), ((), ()))
TN = (((0,), (0,)), ((), ()))
SCALE = 128**-0.5
LOG2E = 1.4426950408889634


def attend(b, z, x, q, kv, segs, parents, scores, o, log_sum):
    lane = (lax.broadcasted_iota(jnp.int32, (256, 512), 1) & 255).astype(F32)
    ahead = lax.broadcasted_iota(jnp.int32, (256, 512), 0).astype(F32) - lane
    block = z * 8 + b * 4 + x
    trunk, leaf, branch, above = place_of(segs, parents, block)
    rows = pl.ds(b * 256, 256)
    both = jnp.concatenate([q[rows, :128], q[rows, 128:]], axis=0)
    start = block.astype(F32) - 8.0 * trunk

    def score(key):
        return lax.dot_general(key, both, NT, preferred_element_type=F32) * (SCALE * LOG2E)

    def trunk_score(i, top):
        gap = (start - i.astype(F32)) * 256.0
        s = jnp.where(ahead <= gap, score(trunk_block(kv, 0, i, trunk)), NEG)
        scores[i] = s
        return jnp.maximum(top, jnp.max(s, axis=0, keepdims=True))

    top = lax.fori_loop(0, 8, trunk_score, jnp.full((1, 512), NEG, F32))
    s = score(parent_block(kv, 0, above)) + (leaf - 1.0) * 1e30
    scores[8] = s
    top = jnp.maximum(top, jnp.max(s, axis=0, keepdims=True))
    s = jnp.where(ahead <= 0.0, score(kv[0, z, b, x]), NEG) + (branch - 1.0) * 1e30
    scores[9] = s
    top = jnp.maximum(top, jnp.max(s, axis=0, keepdims=True))

    def weigh(i, value, carry):
        acc, total = carry
        w = jnp.exp2(scores[i] - top)
        acc = acc + lax.dot_general(value, w.astype(BF16), TN, preferred_element_type=F32)
        return acc, total + jnp.sum(w, axis=0, keepdims=True)

    carry = (jnp.zeros((128, 512), F32), jnp.zeros((1, 512), F32))
    carry = lax.fori_loop(0, 8, lambda i, c: weigh(i, trunk_block(kv, 1, i, trunk), c), carry)
    carry = weigh(8, parent_block(kv, 1, above), carry)
    acc, total = weigh(9, kv[1, z, b, x], carry)
    heads = (acc / total).T.astype(BF16)
    o[rows, :128] = heads[:256]
    o[rows, 128:] = heads[256:]
    log_sum[b] = jnp.broadcast_to(top + jnp.log2(total), (8, 512))
    return top * (1.0 / LOG2E)


def one_hot(rows, lanes, hit):
    row = lax.broadcasted_iota(jnp.int32, (rows, lanes), 0)
    lane = lax.broadcasted_iota(jnp.int32, (rows, lanes), 1)
    return hit(row, lane).astype(F32).astype(BF16)


def forward(tokens, cotangent, seg_ids, parents, vectors, query_bias, up_bias, w_keyval, w_query, w_out, w_up, w_down):
    def kernel(tok, cot, seg_in, par_in, vec_in, qb_in, ub_in, wkv_in, wq_in, wo_in, wu_in, wd_in,
               cot_out, h2, wu, wd, wq_out, wo_out, wkv_out, h1_out, q_out, kv_out, o, log_sum, x1, best, vec, ub,
               tok_all, h1, wkv, wq, wo, q, kv, scores, part, own, mine, got, pack, pairs, halves, tiles, local,
               *rest):
        *scratch, ss, rs = rest
        net = Net(ss, rs)
        z, yh, x, yl, c, y = net.z, net.yh, net.x, net.yl, net.c, net.y
        starts = [
            pltpu.make_async_copy(src, dst, local.at[i])
            for i, (src, dst) in enumerate(((tok, tok_all.at[y, c]), (cot, cot_out.at[y, c])))
        ]
        for one in starts:
            one.start()
        row = lax.broadcasted_iota(jnp.int32, (16, 128), 0)
        lane = lax.broadcasted_iota(jnp.int32, (16, 128), 1)
        periodic = jnp.dot(vec_in[...], one_hot(16, 128, lambda r, l: l % 16 == r), preferred_element_type=F32)
        first = jnp.dot(vec_in[...], one_hot(16, 128, lambda r, l: r == 0), preferred_element_type=F32)
        tile = jnp.where(row < 6, periodic, first)
        tile = jnp.where(row == 7, seg_in[0].astype(F32), tile).astype(BF16)
        for i in range(2):
            pack[i, 0:16] = wkv_in[:, i * 128 : (i + 1) * 128]
            pack[i, 16:32] = tile
        four = one_hot(4, 128, lambda r, l: l % 4 == r)
        heads = lax.dot_general(qb_in[...], four, TN, preferred_element_type=F32)
        units = lax.dot_general(ub_in[...], four, TN, preferred_element_type=F32)
        blank = jnp.zeros((6, 128), F32)
        for i in range(2):
            halves[i] = jnp.concatenate([units[8 * i : 8 * i + 8], heads[2 * i : 2 * i + 2], blank], axis=0).astype(BF16)
        pairs[yh, yl, c] = jnp.where(c == 0, pack[0], pack[1])
        net.barrier(PLANE + RING + ("yo", "xo", "zo"))

        query = weight_gather(net, wq_in, wq, local.at[4])
        later = Ticks(weight_gather(net, wu_in, wu, local.at[6]), weight_gather(net, wd_in, wd, local.at[7], False))
        project_weight = weight_gather(net, wo_in, wo, local.at[5])
        toks = group_gather(net, tok, tok_all)
        ks = [net.slot() for _ in range(11)]
        net.send(pack.at[1 - c], pairs.at[yh, yl, c], ks[0], "c")
        net.send(halves.at[1 - yh], halves.at[2], ks[4], "yo")
        next(query)
        net.got(pairs.at[yh, yl, 1 - c], ks[0])
        for i, name in enumerate(("yu", "yd", "yo")):
            net.send(pairs.at[yh, yl], pairs.at[yh, yl], ks[1 + i], name)
        next(toks)
        next(query)
        net.got(halves.at[2], ks[4])
        here, there = jnp.where(yh == 0, halves[0], halves[1]), halves[2]
        low, high = jnp.where(yh == 0, here, there), jnp.where(yh == 0, there, here)
        tiles[z, x, 1] = jnp.where((lane // 16) % 2 == 0, low.astype(F32), high.astype(F32)).astype(BF16)
        for i, d in enumerate((net.yd, net.yu, net.yo)):
            net.got(pairs.at[d // 2, lax.rem(d, 2)], ks[1 + i])
        merged = jnp.zeros((16, 128), F32)
        for i in range(8):
            high, tp = i // 4, i % 4
            one = pairs[high, tp // 2, tp % 2, 16:32].astype(F32)
            hit = (row < 6) & (lane // 16 == i)
            hit = hit | ((row == 6) & (lane // 16 % 2 == high) & (lane % 4 == tp))
            hit = hit | ((row == 7) & ((lane // 4) % 2 == high))
            merged = jnp.where(hit, one, merged)
            wkv[z, high, x, tp // 2, tp % 2] = pairs[high, tp // 2, tp % 2, 0:16]
        tiles[z, x, 0] = merged.astype(BF16)
        for i, name in enumerate(("xu", "xd", "xo")):
            net.send(tiles.at[z, x], tiles.at[z, x], ks[5 + i], name)

        def key_view(zz, half, xx, part):
            return wkv.at[zz, part, xx, pl.ds(0, 2) if half == BOTH else half]

        keyval = plane_gather(net, key_view)
        next(keyval)
        next(project_weight)
        later.tick()
        for i, d in enumerate((net.xd, net.xu, net.xo)):
            net.got(tiles.at[z, d], ks[5 + i])
        for i, name in enumerate(("zu", "zd", "zo")):
            net.send(tiles.at[z], tiles.at[z], ks[8 + i], name)
        next(keyval)
        next(query)
        next(toks)
        next(keyval)
        next(query)
        next(project_weight)
        later.tick()
        next(toks)
        next(keyval)
        next(query)
        next(project_weight)
        for i, d in enumerate((net.zd, net.zu, net.zo)):
            net.got(tiles.at[d], ks[8 + i])

        value_bias = jnp.zeros((16, 128), F32)
        biases = jnp.zeros((16, 128), F32)
        segs = jnp.zeros((16, 128), F32)
        for zz in range(4):
            come = [tiles[zz, xx, 0].astype(F32) for xx in range(4)]
            turned = [pltpu.roll(one, 64, 1) for one in come]
            for xx in range(4):
                at = (lane // 32 == zz) & ((lane // 4) % 4 == xx)
                value_bias = jnp.where(at, come[xx], value_bias)
                biases = jnp.where(at, tiles[zz, xx, 1].astype(F32), biases)
                segs = jnp.where((lane // 8 == zz) & (lane % 4 == xx), come[xx], segs)
            for high in range(2):
                for pair in range(2):
                    even = come[2 * pair] if high == 0 else turned[2 * pair]
                    odd = turned[2 * pair + 1] if high == 0 else come[2 * pair + 1]
                    j = (zz * 2 + high) * 2 + pair
                    vec[:, j * 128 : (j + 1) * 128] = jnp.where(lane < 64, even, odd)
        value_bias = value_bias[6:7]
        segs = segs[7:8]
        vec[8:9, 0:128] = segs
        ub[...] = biases[0:8]
        query_bias = jnp.concatenate([biases[8:9], biases[9:10]], axis=1)
        parent = jnp.zeros((1, 128), F32)
        for i in range(18):
            parent = jnp.where(lane[0:1] == i, par_in[i].astype(F32), parent)
        vec[9:10, 0:128] = parent
        for _ in toks:
            pass
        starts[0].wait()

        gain1, shift1 = vec[0:1], vec[1:2]

        def norm_rows(i, carry):
            rows = tok_all[i // 2, i % 2].astype(F32)
            h1[pl.ds(pl.multiple_of(i * 64, 64), 64)] = (normed(rows)[0] * gain1 + shift1).astype(BF16)
            return carry

        lax.fori_loop(0, 8, norm_rows, 0)
        next(project_weight)
        for _ in query:
            pass
        for _ in keyval:
            pass

        def project(i, carry):
            rows = pl.ds(pl.multiple_of(i * 256, 256), 256)
            h = h1[rows]
            weight = wq[...].reshape(2048, 256)
            q[rows] = (jnp.dot(h, weight, preferred_element_type=F32) + query_bias).astype(BF16)
            weight = wkv[...].reshape(2048, 128)
            shift = value_bias * c.astype(F32)
            kv[c, z, i, x] = (jnp.dot(h, weight, preferred_element_type=F32) + shift).astype(BF16)
            return carry

        lax.fori_loop(0, 2, project, 0)

        def keys_of(r):
            def rows(half):
                return pl.ds(r * 128, 128) if half == BOTH else pl.ds(r * 128 + 64 * half, 64)

            def view(zz, half, xx, part):
                return kv.at[c, zz, part, xx, rows(half)]

            def their_view(zz, half, xx, part):
                return kv.at[1 - c, zz, part, xx, rows(half)]

            return plane_gather(net, view, their_view)

        keys = in_turn(keys_of(0), keys_of(1))
        cots = group_gather(net, cot, cot_out)
        next(keys)
        later.tick()
        next(cots)
        next(keys)
        next(project_weight)
        next(keys)
        next(cots)
        later.tick()
        next(keys)
        next(cots)
        for _ in keys:
            pass

        saves = [
            pltpu.make_async_copy(src, dst, local.at[8 + i])
            for i, (src, dst) in enumerate(
                ((wq, wq_out), (wkv, wkv_out), (h1, h1_out), (q, q_out), (kv, kv_out), (wo, wo_out))
            )
        ]
        for one in saves[:5]:
            one.start()
        top = attend(0, z, x, q, kv, segs, parent, scores, o, log_sum)
        top = jnp.maximum(top, attend(1, z, x, q, kv, segs, parent, scores, o, log_sum))
        for h in range(2):
            mine[0, 8 * h : 8 * h + 8] = jnp.full((8, 128), jnp.max(top[:, h * 256 : (h + 1) * 256]), F32)
        for _ in project_weight:
            pass
        saves[5].start()

        def project_out(i, d, h):
            rows = o[pl.ds(pl.multiple_of(d * 128, 128), 128)]
            for j in (2 * h, 2 * h + 1):
                weight = wo[j].reshape(512, 256)
                out = lax.dot_general(rows, weight, NT, preferred_element_type=F32).astype(BF16)
                part[d, 0, :, j * 512 : (j + 1) * 512] = out[:64]
                part[d, 1, :, j * 512 : (j + 1) * 512] = out[64:]

        def total(summed):
            value = tok[...].astype(F32) + (summed + vec[4:5])
            x1[...] = value
            own[...] = (normed(value)[0] * vec[2:3] + vec[3:4]).astype(BF16)

        rows = group_scatter(net, part, *scratch, total, project_out)
        largest = heads_max(net, mine, got, best)
        for _ in range(3):
            next(rows)
            next(largest)
        next(rows)
        later.tick()
        next(rows, None)
        me = pltpu.make_async_copy(own, h2.at[y, c], local.at[14])
        me.start()
        spreading = group_gather(net, own, h2)
        next(spreading)
        for _ in largest:
            pass
        for _ in spreading:
            pass
        me.wait()
        for _ in cots:
            pass
        later.tick()
        starts[1].wait()
        for one in saves:
            one.wait()
        net.finish()

    n, d = tokens.shape
    rows = jax.ShapeDtypeStruct((4, 2, n, d), BF16)

    def bf(*shape):
        return jax.ShapeDtypeStruct(shape, BF16)

    def f32(*shape):
        return jax.ShapeDtypeStruct(shape, F32)

    return pl.pallas_call(
        kernel,
        out_shape=(
            rows,
            rows,
            bf(4, 2, 4, n, 1024),
            bf(4, 2, 4, n, 1024),
            bf(4, 2, 4, n, 256),
            bf(4, 2, 4, n, 256),
            bf(4, 2, 4, 2, 2, 16, 128),
            bf(512, d),
            bf(512, 256),
            bf(2, 4, 2, 4, 256, 128),
            bf(512, 256),
            f32(2, 8, 512),
            f32(n, d),
            f32(2, 16, 128),
            f32(16, d),
            f32(8, 128),
        ),
        in_specs=[INV, INV, INS, INS] + [INV] * 8,
        out_specs=(ANY,) * 10 + (INV,) * 6,
        scratch_shapes=[
            VMEM((4, 2, n, d), BF16),
            VMEM((512, d), BF16),
            VMEM((4, 2, 4, 2, 2, 16, 128), BF16),
            VMEM((4, 2, 4, n, 256), BF16),
            VMEM((4, 2, 4, n, 256), BF16),
            VMEM((512, 256), BF16),
            VMEM((2, 4, 2, 4, 256, 128), BF16),
            VMEM((10, 256, 512), F32),
            VMEM((4, 2, n, d), BF16),
            VMEM((n, d), BF16),
            VMEM((5, 16, 128), F32),
            VMEM((7, 16, 128), F32),
            VMEM((2, 32, 128), BF16),
            VMEM((2, 2, 2, 32, 128), BF16),
            VMEM((3, 16, 128), BF16),
            VMEM((4, 4, 2, 16, 128), BF16),
            pltpu.SemaphoreType.DMA((15,)),
        ]
        + scatter_scratch(n, d)
        + sems(280),
        compiler_params=params(1),
        name="forward",
    )(tokens, cotangent, seg_ids, parents, vectors, query_bias, up_bias, w_keyval, w_query, w_out, w_up, w_down)


def normed(values):
    centred = values - jnp.mean(values, axis=-1, keepdims=True)
    inverse = lax.rsqrt(jnp.mean(centred * centred, axis=-1, keepdims=True) + EPS)
    return centred * inverse, inverse


def norm_back(grad, norm, inverse, gain):
    scaled = grad * gain
    return inverse * (
        scaled
        - jnp.mean(scaled, axis=-1, keepdims=True)
        - norm * jnp.mean(scaled * norm, axis=-1, keepdims=True)
    )


def heads_max(net, mine, got, best):
    for i, (up, down) in enumerate((("xu", "xd"), ("zu", "zd"))):
        k = [net.slot() for _ in range(3)]
        a, b, d = got.at[3 * i], got.at[3 * i + 1], got.at[3 * i + 2]
        net.send(mine.at[2 * i], a, k[0], up)
        net.send(mine.at[2 * i], b, k[1], down)
        yield
        net.got(a, k[0])
        net.got(b, k[1])
        mine[2 * i + 1] = jnp.maximum(mine[2 * i], jnp.maximum(a[...], b[...]))
        net.send(mine.at[2 * i + 1], d, k[2], up)
        yield
        net.got(d, k[2])
        mine[2 * i + 2] = jnp.maximum(mine[2 * i + 1], d[...])
    k = net.slot()
    net.send(mine.at[4], got.at[6], k, "yo")
    yield
    net.got(got.at[6], k)
    best[net.yh] = mine[4]
    best[1 - net.yh] = got[6]


def weight_scatter(net, g, tmp, out):
    z, yh, x = net.z, net.yh, net.x
    w = g.shape[-1]
    k = net.slot()
    yield from plane_scatter(net, column_view(g), tmp)
    mine = out.at[:, pl.ds(pl.multiple_of(yh * w, 128), w)]
    net.send(g.at[z, 1 - yh, x], mine, k, "yo")
    out[:, pl.ds(pl.multiple_of(yh * w, 128), w)] = g[z, yh, x]
    yield
    net.got(out.at[:, pl.ds(pl.multiple_of((1 - yh) * w, 128), w)], k)


def smooth_gate(u):
    scale = 0.7978845608028654
    square = u * u
    t = jnp.tanh(scale * u * (1.0 + 0.044715 * square))
    half = 0.5 * (1.0 + t)
    slope = half + 0.5 * u * (1.0 - t * t) * scale * (1.0 + 0.134145 * square)
    return u * half, slope


def piece(ref, which, zz, yy, xx):
    return jnp.concatenate(
        [ref[zz, yy, xx, :, (which * 4 + r) * 128 : (which * 4 + r + 1) * 128] for r in range(4)], axis=0
    )


def put_piece(ref, which, zz, yy, xx, value):
    for r in range(4):
        ref[zz, yy, xx, :, (which * 4 + r) * 128 : (which * 4 + r + 1) * 128] = value[r * 64 : (r + 1) * 64]


def attend_back(z, x, q, kv, o, go, log_sum, segs, parents, grad, lone, dq_sum, dq):
    lane = (lax.broadcasted_iota(jnp.int32, (256, 512), 1) & 255).astype(F32)
    ahead = lax.broadcasted_iota(jnp.int32, (256, 512), 0).astype(F32) - lane
    places = [place_of(segs, parents, z * 8 + b * 4 + x) for b in range(2)]

    def stacked(ref, b):
        return jnp.concatenate([ref[b * 256 : b * 256 + 256, :128], ref[b * 256 : b * 256 + 256, 128:]], axis=0)

    logs, inner = [], []
    for b in range(2):
        logs.append(log_sum[b, 0:1])
        inner.append(
            jnp.sum((stacked(go, b).astype(F32) * stacked(o, b).astype(F32)).T, axis=0, keepdims=True)
        )

    def one(b, key, value, masked, first):
        both, up = stacked(q, b), stacked(go, b)
        s = masked(lax.dot_general(key, both, NT, preferred_element_type=F32) * (SCALE * LOG2E))
        p = jnp.exp2(s - logs[b])
        dp = lax.dot_general(value, up, NT, preferred_element_type=F32)
        ds = (p * (dp - inner[b])).astype(BF16)
        more = lax.dot_general(key, ds, TN, preferred_element_type=F32)
        dq_sum[b] = more if first else dq_sum[b] + more
        dk = jnp.dot(ds, both, preferred_element_type=F32) * SCALE
        dv = jnp.dot(p.astype(BF16), up, preferred_element_type=F32)
        return dk.astype(BF16), dv.astype(BF16)

    for b in range(2):
        trunk, leaf, branch, above = places[b]
        lone[b, 0, 0], lone[b, 0, 1] = one(
            b,
            piece(kv, 0, z, b, x),
            piece(kv, 1, z, b, x),
            lambda s: jnp.where(ahead <= 0.0, s, NEG) + (branch - 1.0) * 1e30,
            True,
        )
        key, value = (
            sum(piece(kv, w, 2 + j // 8, j // 4 % 2, j % 4) * wide(above[j]) for j in range(16)) for w in range(2)
        )
        lone[b, 1, 0], lone[b, 1, 1] = one(b, key, value, lambda s: s + (leaf - 1.0) * 1e30, False)
    yield

    for j in range(16):
        own = [
            wide((z * 8 + b * 4 + x == 16 + j).astype(F32) * jnp.ones((1, 1), F32)) for b in range(2)
        ]
        for w in range(2):
            value = sum(lone[b, 0, w] * own[b] + lone[b, 1, w] * wide(places[b][3][j]) for b in range(2))
            put_piece(grad, w, 2 + j // 8, j // 4 % 2, j % 4, value)

    def trunk_one(i, carry):
        yy, xx = i // 4, i % 4
        totals = None
        for b in range(2):
            trunk = places[b][0]
            second = wide(trunk)
            first = 1 - second
            key, value = (piece(kv, w, 0, yy, xx) * first + piece(kv, w, 1, yy, xx) * second for w in range(2))
            start = (z * 8 + b * 4 + x).astype(F32) - 8.0 * trunk
            gap = (start - i.astype(F32)) * 256.0
            dk, dv = one(b, key, value, lambda s: jnp.where(ahead <= gap, s, NEG), False)
            parts = [dk * first, dv * first, dk * second, dv * second]
            totals = parts if totals is None else [t + p for t, p in zip(totals, parts)]
        for t in range(2):
            for w in range(2):
                put_piece(grad, w, t, yy, xx, totals[2 * t + w])
        return carry

    for i in range(0, 8, 2):
        lax.fori_loop(i, i + 2, trunk_one, 0)
        yield
    for b in range(2):
        rows = (dq_sum[b] * SCALE).T.astype(BF16)
        dq[b * 256 : b * 256 + 256, :128] = rows[:256]
        dq[b * 256 : b * 256 + 256, 128:] = rows[256:]


def spread(net, names, src, dst, k):
    for i, name in enumerate(names):
        net.send(src, dst.at[i], k[i], name)


def all_sums(net, mine, near, far):
    k = [net.slot() for _ in range(6)]
    spread(net, ("xu", "xd", "xo"), mine.at[0], near, k)
    yield
    for i in range(3):
        net.got(near.at[i], k[i])
    mine[1] = mine[0] + near[0] + near[1] + near[2]
    spread(net, ("zu", "zd", "zo"), mine.at[1], far, k[3:])
    yield
    for i in range(3):
        net.got(far.at[i], k[3 + i])
    mine[2] = mine[1] + far[0] + far[1] + far[2]


def backward(tokens, cotangent, cot_all, h2, wu, wd, wq, wo, packs, h1, q, kv, o, log_sum, x1, vec, ub):
    def kernel(tok, cot, cot_in, h2_in, wu_in, wd_in, wq_in, wo_in, packs_in, h1_in, q, kv_in, o, log_sum,
               x1, vec, ub_in,
               output, grad_input, up_out, down_out, wo_out, wq_out, vec_out, bias_out, kv_out, vb_out,
               h2, cots, wu, wd, wq, wo, packs, adu, us, das, part, part_mlp, gu, gd, gwo, gq, own, dz, dx1, sums, go,
               lone, dq_sum, dq, dkv_from, dkv, gkv, gkv_z, gkv_x, bias, bias_x, bias_z, vecs, vec_z, vec_x,
               local, *rest):
        *scratch, ss, rs = rest
        first, second, tmp_u, tmp_d, tmp_o, tmp_q, tmp_k, tmp_v = (
            scratch[:4],
            scratch[4:8],
            scratch[8:16],
            scratch[16:24],
            scratch[24:32],
            scratch[32:40],
            scratch[40:48],
            scratch[48:56],
        )
        net = Net(ss, rs)
        z, yh, x, yl, c, y = net.z, net.yh, net.x, net.yl, net.c, net.y

        def columns(ref, j):
            return ref.at[:, :, :, :, pl.ds(j * 256, 256)]

        def load(src, dst, i):
            one = pltpu.make_async_copy(src, dst, local.at[i])
            one.start()
            return one

        load(h2_in, h2, 0)
        load(columns(wu_in, 0), columns(wu, 0), 2)
        load(cot_in, cots, 1)
        for j in range(1, 4):
            load(columns(wu_in, j), columns(wu, j), 2 + j)
        there_d, here_d, every = column_view(wd_in), column_view(wd), slice(None)
        parts_d = [(zz, BOTH, every, 0) for zz in (z, net.zu, net.zd)]
        parts_d += [(every, BOTH, xx, 1) for xx in (x, net.xu, net.xd)]
        loads_d = [load(there_d(*at), here_d(*at), i) for at, i in zip(parts_d, (6, 7, 8, 9, 24, 25))]
        loads = [load(wo_in, wo, 10), load(wq_in, wq, 11)]
        loads.append(load(packs_in, packs, 12))
        net.barrier(PLANE + RING + ("yo", "xo", "zo"))
        kd = [net.slot() for _ in range(4)]
        last_parts = (
            ((net.zd, 0, every, 0), "zu"),
            ((net.zu, 1, every, 0), "zd"),
            ((every, 0, net.xd, 1), "xu"),
            ((every, 1, net.xu, 1), "xd"),
        )
        for k, (at, name) in zip(kd, last_parts):
            net.send(there_d(*at), here_d(*at), k, name)
        pltpu.make_async_copy(h2_in, h2, local.at[0]).wait()

        def hidden(j, carry):
            at = pl.ds(pl.multiple_of(j * 256, 256), 256)
            there = pl.ds(0, 4), pl.ds(0, 2), pl.ds(0, 4), pl.ds(0, 64), at
            pltpu.make_async_copy(wu_in.at[there], wu.at[there], local.at[2 + j]).wait()
            us[:, at] = jnp.dot(
                h2[...].reshape(512, 2048), wu[there].reshape(2048, 256), preferred_element_type=F32
            )
            return carry

        def hidden_back(j, carry):
            at = pl.ds(pl.multiple_of(j * 256, 256), 256)
            there = pl.ds(0, 4), pl.ds(0, 2), pl.ds(0, 4), pl.ds(0, 64), at
            das[...] = jnp.dot(
                cots[...].reshape(512, 2048), wd[there].reshape(2048, 256), preferred_element_type=F32
            )
            bias_row = jnp.concatenate([ub_in[pl.ds(2 * j, 1)], ub_in[pl.ds(2 * j + 1, 1)]], axis=1)

            def gate(i, total):
                rows = pl.ds(pl.multiple_of(i * 64, 64), 64)
                value, slope = smooth_gate(us[rows, at] + bias_row)
                adu[0, rows, at] = value.astype(BF16)
                du = (das[rows] * slope).astype(BF16)
                adu[1, rows, at] = du
                return total + jnp.sum(du.astype(F32), axis=0, keepdims=True)

            total = lax.fori_loop(0, 8, gate, jnp.zeros((1, 256), F32))
            bias[0, pl.ds(2 * j, 1)] = total[:, :128]
            bias[0, pl.ds(2 * j + 1, 1)] = total[:, 128:]
            return carry

        lax.fori_loop(0, 4, hidden, 0)
        pltpu.make_async_copy(cot_in, cots, local.at[1]).wait()
        for one in loads_d:
            one.wait()
        for k, at in zip(kd, ((net.zo, 0, every, 0), (net.zo, 1, every, 0), (every, 0, net.xo, 1), (every, 1, net.xo, 1))):
            net.got(here_d(*at), k)
        lax.fori_loop(0, 4, hidden_back, 0)

        def projected(dst, d, rows, weight, h=None):
            def column(j, carry):
                out = lax.dot_general(rows, weight(j), NT, preferred_element_type=F32).astype(BF16)
                at = pl.ds(pl.multiple_of(j * 512, 512), 512)
                dst[d, 0, :, at] = out[:64]
                dst[d, 1, :, at] = out[64:]
                return carry

            lax.fori_loop(0 if h is None else 2 * h, 4 if h is None else 2 * h + 2, column, 0)

        def ring_rows(d):
            return pl.ds(pl.multiple_of(d * 128, 128), 128)

        def make_two(i, d, h):
            projected(part, d, adu[1, ring_rows(d)], lambda j: wu[j].reshape(512, 1024), h)

        def total_two(summed):
            norm, inverse = normed(x1[...])
            grad = cot[...].astype(F32) + norm_back(summed, norm, inverse, vec[2:3])
            dx1[...] = grad
            rounded = grad.astype(BF16)
            own[...] = rounded
            values = (summed * norm, summed, rounded.astype(F32), cot[...].astype(F32))
            for i, v in enumerate(values):
                sums[2 + i : 3 + i] = jnp.sum(v, axis=0, keepdims=True)

        def outer(dst, left, right):
            def block(j, carry):
                out = lax.dot_general(left(j), right, TN, preferred_element_type=F32)
                dst[j] = out.astype(BF16).reshape(2, 4, 64, right.shape[1])
                return carry

            lax.fori_loop(0, 4, block, 0)

        def wide_outer(dst, left, which):
            def block(i, carry):
                j, w = i // 2, i % 2
                at = pl.ds(pl.multiple_of(w * 512, 512), 512)
                out = lax.dot_general(
                    left[:, :, :, pl.ds(pl.multiple_of(j * 512, 512), 512)].reshape(512, 512),
                    adu[which, :, at],
                    TN,
                    preferred_element_type=F32,
                )
                dst[j, :, :, :, at] = out.astype(BF16).reshape(2, 4, 64, 512)
                return carry

            lax.fori_loop(0, 8, block, 0)

        rows_two = group_scatter(net, part, *first, total_two, make_two)
        next(rows_two)
        next(rows_two)
        wide_outer(gd, cots, 0)
        down = weight_scatter(net, gd, tmp_d, down_out)
        next(down)
        next(rows_two)
        wide_outer(gu, h2, 1)
        up = weight_scatter(net, gu, tmp_u, up_out)
        next(up)
        next(rows_two)
        next(rows_two, None)
        me = load(own, dz.at[y, c], 23)
        spreading = group_gather(net, own, dz)
        next(spreading)
        for d in range(2):
            projected(part_mlp, d, adu[0, d * 128 : d * 128 + 128], lambda j: wd[j].reshape(512, 1024))
        next(spreading)
        next(down)
        for d in range(2, 4):
            projected(part_mlp, d, adu[0, d * 128 : d * 128 + 128], lambda j: wd[j].reshape(512, 1024))
        keep = [
            load(kv_in.at[w, :, :, :, pl.ds(r * 64, 64)], wd.at[:, :, :, :, pl.ds((w * 4 + r) * 128, 128)], 13 + 4 * w + r)
            for w in range(2)
            for r in range(4)
        ]
        next(spreading)
        next(up)
        late = [load(h1_in.at[:, pl.ds(w * 1024, 1024)], adu.at[w], 21 + w) for w in range(2)]
        for _ in spreading:
            pass
        me.wait()
        loads[0].wait()
        go[...] = jnp.dot(
            dz[...].reshape(512, 2048), wo[...].reshape(2048, 256), preferred_element_type=F32
        ).astype(BF16)

        def total_out(summed):
            output[...] = (x1[...] + (summed + vec[5:6])).astype(BF16)

        rows_out = group_scatter(net, part_mlp, *second, total_out)
        next(rows_out)
        outer(gwo, lambda j: dz[:, :, :, pl.ds(pl.multiple_of(j * 512, 512), 512)].reshape(512, 512), o[...])
        project = weight_scatter(net, gwo, tmp_o, wo_out)
        next(project)
        for one in keep:
            one.wait()
        steps = attend_back(z, x, q, wd, o, go, log_sum, vec[8:9, 0:128], vec[9:10, 0:128], wu, lone, dq_sum, dq)

        theirs = pl.ds(pl.multiple_of((1 - c) * 512, 512), 512)
        ours = pl.ds(pl.multiple_of(c * 512, 512), 512)

        def swap(zs, ys):
            k = [net.slot() for _ in range(4)]
            zr, yr = pl.ds(zs, 2), pl.ds(ys[0], len(ys))
            for i in range(4):
                net.send(wu.at[zr, yr, i, :, theirs], cots.at[zr, yr, :, pl.ds(i * 512, 512)], k[i], "c")
            yield
            for i in range(4):
                net.got(cots.at[zr, yr, :, pl.ds(i * 512, 512)], k[i])
                for zz in (zs, zs + 1):
                    for yy in ys:
                        wu[zz, yy, i, :, ours] = wu[zz, yy, i, :, ours] + cots[zz, yy, :, i * 512 : i * 512 + 512]

        swaps = [swap(2, (0, 1)), swap(0, (0,)), swap(0, (1,))]
        next(steps)
        next(down)
        next(rows_out)
        next(steps)
        next(swaps[0])
        next(up)
        next(steps)
        next(swaps[1])
        next(down)
        next(rows_out)
        next(steps)
        next(swaps[0], None)
        next(up)
        next(steps)
        next(swaps[2])
        next(swaps[1], None)
        next(down)
        next(rows_out)
        next(project)
        next(steps, None)
        next(up)
        next(rows_out, None)
        for one in loads[1:] + late:
            one.wait()

        def make_one(i, d, h):
            projected(h2, d, dq[ring_rows(d)], lambda j: wq[j].reshape(512, 256), h)
            if i == 3:
                for j in (2 * h, 2 * h + 1):
                    more = lax.dot_general(
                        dkv[y], packs[j].reshape(512, 128), NT, preferred_element_type=F32
                    ).astype(BF16)
                    at = slice(j * 512, (j + 1) * 512)
                    h2[d, 0, :, at] = h2[d, 0, :, at] + more[:64]
                    h2[d, 1, :, at] = h2[d, 1, :, at] + more[64:]

        def total_one(summed):
            norm, inverse = normed(tok[...].astype(F32))
            grad_input[...] = dx1[...] + norm_back(summed, norm, inverse, vec[0:1])
            sums[0:1] = jnp.sum(summed * norm, axis=0, keepdims=True)
            sums[1:2] = jnp.sum(summed, axis=0, keepdims=True)
            sums[6:8] = jnp.zeros((2, 2048), F32)
            vecs[y, c] = sums[...]

        rows_one = group_scatter(net, h2, *first, total_one, make_one)
        next(rows_one)
        next(swaps[2], None)

        def keys_of(r, tmp):
            def view(zz, half, xx, part):
                start = c * 512 + r * 256
                if half == BOTH:
                    return wu.at[zz, part, xx, :, pl.ds(pl.multiple_of(start, 256), 256)]
                return wu.at[zz, part, xx, :, pl.ds(pl.multiple_of(start + half * 128, 128), 128)]

            return plane_scatter(net, view, tmp)

        keys = in_turn(keys_of(0, tmp_k), keys_of(1, tmp_v))
        next(keys)
        next(rows_one)
        outer(gq, lambda j: adu[j // 2, :, pl.ds(pl.multiple_of((j % 2) * 512, 512), 512)], dq[...])
        bias[0, 8:9] = jnp.sum(dq[:, :128].astype(F32), axis=0, keepdims=True)
        bias[0, 9:10] = jnp.sum(dq[:, 128:].astype(F32), axis=0, keepdims=True)
        bias[0, 10:16] = jnp.zeros((6, 128), F32)
        next(keys)
        query = weight_scatter(net, gq, tmp_q, wq_out)
        next(query)
        small = all_sums(net, bias, bias_x, bias_z)
        next(small)
        next(rows_one)
        next(keys)
        next(down, None)
        next(up, None)
        next(query)
        next(small)
        next(keys)
        next(project)
        for _ in keys:
            pass

        def ring_piece(ref, d):
            at = pl.ds(pl.multiple_of(c * 512 + lax.rem(d, 2) * 256, 256), 256)
            return ref.at[z, d // 2, x, :, at]

        kr = [net.slot() for _ in range(7)]
        for i, (name, d) in enumerate((("yu", net.yu), ("yd", net.yd), ("yo", net.yo))):
            net.send(ring_piece(wu, d), dkv_from.at[i], kr[i], name)
        for i in range(3):
            net.got(dkv_from.at[i], kr[i])
        mine = ring_piece(wu, y)[...].astype(F32)
        for i in range(3):
            mine = mine + dkv_from[i].astype(F32)
        mine = mine.astype(BF16)
        dkv[y] = jnp.concatenate([mine[:, :128], mine[:, 128:]], axis=0)
        for i, name in enumerate(("yu", "yd", "yo")):
            net.send(dkv.at[y], dkv.at[y], kr[3 + i], name)
        next(rows_one)
        next(query)
        next(rows_one, None)

        def vectors():
            k = [net.slot() for _ in range(13)]
            at = vecs.at[y, c]
            for i, name in enumerate(("yu", "yd", "yo", "c")):
                net.send(at, at, k[i], name)
            yield
            for i, d in enumerate((net.yd, net.yu, net.yo)):
                net.got(vecs.at[d, c], k[i])
                net.send(vecs.at[d, c], vecs.at[d, c], k[4 + i], "c")
            yield
            for i, d in enumerate((y, net.yd, net.yu, net.yo)):
                net.got(vecs.at[d, 1 - c], k[3 + i])
            acc = vecs[0, 0]
            for i in range(1, 8):
                acc = acc + vecs[i // 2, i % 2]
            for i in range(4):
                vec_z[i] = acc[:, i * 512 : (i + 1) * 512]
            for i, (name, d) in enumerate((("zu", net.zu), ("zd", net.zd), ("zo", net.zo))):
                net.send(vec_z.at[d], vec_z.at[4 + i], k[7 + i], name)
            yield
            for i in range(3):
                net.got(vec_z.at[4 + i], k[7 + i])
            acc = vec_z[z] + vec_z[4] + vec_z[5] + vec_z[6]
            vec_x[0] = jnp.where(yh == 0, acc[:, :256], acc[:, 256:])
            spread(net, ("xu", "xd", "xo"), vec_x.at[0], vec_x.at[pl.ds(1, 3)], k[10:])
            yield
            for i in range(3):
                net.got(vec_x.at[1 + i], k[10 + i])
            vec_out[...] = vec_x[0] + vec_x[1] + vec_x[2] + vec_x[3]

        vector = vectors()
        next(vector)
        next(small, None)
        for i, d in enumerate((net.yd, net.yu, net.yo)):
            net.got(dkv.at[d], kr[3 + i])

        every = dkv[...].reshape(512, 128)
        value_sum = jnp.broadcast_to(jnp.sum(every.astype(F32), axis=0, keepdims=True), (8, 128))
        for j in range(4):
            at = pl.ds(pl.multiple_of((j % 2) * 512 + yh * 256, 256), 256)
            out = lax.dot_general(adu[j // 2, :, at], every, TN, preferred_element_type=F32).reshape(4, 2, 32, 128)
            for i in range(4):
                gkv[j, i, 0:32] = jnp.where(yl == 0, out[i, 0], out[i, 1])
                gkv[j, i, 32:40] = value_sum

        def key_value():
            k = [net.slot() for _ in range(7)]
            for i, (name, d) in enumerate((("zu", net.zu), ("zd", net.zd), ("zo", net.zo))):
                net.send(gkv.at[d], gkv_z.at[i], k[i], name)
            yield
            for i in range(3):
                net.got(gkv_z.at[i], k[i])
            for i in range(4):
                gkv_x[i] = gkv[z, i] + gkv_z[0, i] + gkv_z[1, i] + gkv_z[2, i]
            for i, (name, d) in enumerate((("xu", net.xu), ("xd", net.xd), ("xo", net.xo))):
                net.send(gkv_x.at[d], gkv_x.at[4 + i], k[3 + i], name)
            yield
            for i in range(3):
                net.got(gkv_x.at[4 + i], k[3 + i])
            total = gkv_x[x] + gkv_x[4] + gkv_x[5] + gkv_x[6]
            gkv_x[7, 0:16] = jnp.where(c == 0, total[0:16], total[16:32])
            gkv_x[7, 16:32] = jnp.where(c == 0, total[16:32], total[0:16])
            gkv_x[7, 32:40] = total[32:40]
            net.send(gkv_x.at[7, pl.ds(16, 24)], gkv_x.at[8, pl.ds(16, 24)], k[6], "c")
            yield
            net.got(gkv_x.at[8, pl.ds(16, 24)], k[6])
            here, there = gkv_x[7, 0:16], gkv_x[8, 16:32]
            kv_out[:, 0:128] = jnp.where(c == 0, here, there)
            kv_out[:, 128:256] = jnp.where(c == 0, there, here)
            vb_out[...] = jnp.where(c == 0, gkv_x[8, 32:40], gkv_x[7, 32:40])

        def partner_bias():
            k = net.slot()
            net.send(bias.at[2], bias_out.at[1], k, "yo")
            bias_out[0] = bias[2]
            yield
            net.got(bias_out.at[1], k)

        last = key_value()
        next(last)
        run_all(vector, last, partner_bias(), query, project, down, up)
        net.finish()

    n, d = tokens.shape

    def bf(*shape):
        return jax.ShapeDtypeStruct(shape, BF16)

    def f32(*shape):
        return jax.ShapeDtypeStruct(shape, F32)

    return pl.pallas_call(
        kernel,
        out_shape=(
            bf(n, d),
            f32(n, d),
            bf(n, d),
            bf(n, d),
            bf(n, 512),
            bf(n, 512),
            f32(8, 256),
            f32(2, 16, 128),
            f32(16, 256),
            f32(8, 128),
        ),
        in_specs=[INV, INV] + [ANY] * 8 + [INV, ANY] + [INV] * 5,
        out_specs=(INV,) * 10,
        scratch_shapes=[
            VMEM((4, 2, n, d), BF16),
            VMEM((4, 2, n, d), BF16),
            VMEM((4, 2, 4, n, 1024), BF16),
            VMEM((4, 2, 4, n, 1024), BF16),
            VMEM((4, 2, 4, n, 256), BF16),
            VMEM((4, 2, 4, n, 256), BF16),
            VMEM((4, 2, 4, 2, 2, 16, 128), BF16),
            VMEM((2, 512, 1024), BF16),
            VMEM((512, 1024), F32),
            VMEM((512, 256), F32),
            VMEM((4, 2, n, d), BF16),
            VMEM((4, 2, n, d), BF16),
            VMEM((4, 2, 4, n, 1024), BF16),
            VMEM((4, 2, 4, n, 1024), BF16),
            VMEM((4, 2, 4, n, 256), BF16),
            VMEM((4, 2, 4, n, 256), BF16),
            VMEM((n, d), BF16),
            VMEM((4, 2, n, d), BF16),
            VMEM((n, d), F32),
            VMEM((8, d), F32),
            VMEM((512, 256), BF16),
            VMEM((2, 2, 2, 256, 128), BF16),
            VMEM((2, 128, 512), F32),
            VMEM((512, 256), BF16),
            VMEM((3, 64, 256), BF16),
            VMEM((4, 128, 128), BF16),
            VMEM((4, 4, 40, 128), F32),
            VMEM((3, 4, 40, 128), F32),
            VMEM((9, 40, 128), F32),
            VMEM((3, 16, 128), F32),
            VMEM((3, 16, 128), F32),
            VMEM((3, 16, 128), F32),
            VMEM((4, 2, 8, d), F32),
            VMEM((7, 8, 512), F32),
            VMEM((4, 8, 256), F32),
            pltpu.SemaphoreType.DMA((26,)),
        ]
        + scatter_scratch(n, d)
        + scatter_scratch(n, d)
        + plane_scratch(n, 512)
        + plane_scratch(n, 512)
        + plane_scratch(n, 128)
        + plane_scratch(n, 128)
        + [VMEM(s, BF16) for s in ((2, 4, n, 128), (2, 4, n, 128), (2, 4, n, 256), (2, 4, n, 256))]
        + [VMEM(s, BF16) for s in ((2, n, 128), (2, n, 128), (2, n, 256), (2, n, 256))]
        + [VMEM(s, BF16) for s in ((2, 4, n, 128), (2, 4, n, 128), (2, 4, n, 256), (2, 4, n, 256))]
        + [VMEM(s, BF16) for s in ((2, n, 128), (2, n, 128), (2, n, 256), (2, n, 256))]
        + sems(280),
        compiler_params=params(2, 62 << 20),
        name="backward",
    )(tokens, cotangent, cot_all, h2, wu, wd, wq, wo, packs, h1, q, kv, o, log_sum, x1, vec, ub)


def finish(up, down, out, query, grad_input, output, keyval, vec, bias, value_bias, best, w_query, query_bias, tau):
    def kernel(up, down, out, query, grad_input, output, keyval, vec, bias, vb, best, wq, qb, tau,
               output_o, grad_o, query_o, up_o, out_o, down_o, qb_o, ub_o, kv_o, vb_o, v0, v1, v2, v3, v4, v5, wq_o, cb_o):
        for src, dst in ((output, output_o), (grad_input, grad_o), (keyval, kv_o)):
            dst[...] = src[...]
        z, yh, x, yl, c = (lax.axis_index(a) for a in AXES)
        tp = yl * 2 + c
        dp = (z * 2 + yh) * 4 + x
        for src, dst in ((up, up_o), (down, down_o), (out, out_o), (query, query_o)):
            dst[...] = src[...].astype(F32)

        def pick(rows, count, start):
            lanes = rows.shape[1]
            hot = (
                lax.broadcasted_iota(jnp.int32, (lanes, count), 0)
                == lax.broadcasted_iota(jnp.int32, (lanes, count), 1) + start
            ).astype(F32)
            return hot, rows

        low, high = jnp.where(yh == 0, bias[0], bias[1]), jnp.where(yh == 0, bias[1], bias[0])
        exact = lax.Precision.HIGHEST
        hot, rows = pick(jnp.concatenate([low[0:8], high[0:8]], axis=0), 4, dp * 4)
        ub_o[...] = lax.dot_general(hot, rows, (((0,), (1,)), ((), ())), precision=exact, preferred_element_type=F32)
        hot, rows = pick(jnp.concatenate([low[8:10], high[8:10], low[10:14]], axis=0), 4, dp * 4)
        heads = lax.dot_general(hot, rows, (((0,), (1,)), ((), ())), precision=exact, preferred_element_type=F32)
        qb_o[...] = heads[:, 0:4]
        hot, rows = pick(vec[...], 16, x * 64 + tp * 16)
        own = jnp.dot(rows, hot, precision=exact, preferred_element_type=F32)
        for i, ref in enumerate((v0, v1, v2, v3, v4, v5)):
            ref[...] = own[i : i + 1]
        lane = lax.broadcasted_iota(jnp.int32, (1, 128), 1)
        vb_o[...] = splat(vb[0:1], lane, dp * 4 + tp)
        limit = tau[0]
        factors = jnp.zeros((1, 128), F32)
        for h in range(4):
            factor = limit / jnp.maximum(best[h // 2, 8 * (h % 2) : 8 * (h % 2) + 1], limit)
            at = slice(h * 128, (h + 1) * 128)
            wq_o[:, at] = (wq[:, at].astype(F32) * factor).astype(BF16)
            factors = jnp.where(lane == h, factor, factors)
        cb_o[...] = (qb[...].astype(F32) * factors[:, 0:4]).astype(BF16)

    n, d = output.shape

    def f32(*shape):
        return jax.ShapeDtypeStruct(shape, F32)

    shapes = (
        jax.ShapeDtypeStruct((n, d), BF16),
        f32(n, d),
        f32(n, 512),
        f32(n, d),
        f32(n, 512),
        f32(n, d),
        f32(4, 4),
        f32(4, 16),
        f32(16, 256),
        f32(1, 1),
    )
    shapes += (f32(1, 16),) * 6
    shapes += (jax.ShapeDtypeStruct((n, 512), BF16), jax.ShapeDtypeStruct((4, 4), BF16))
    return pl.pallas_call(
        kernel,
        out_shape=shapes,
        in_specs=[INV] * 13 + [INS],
        out_specs=(INV,) * 18,
        compiler_params=pltpu.CompilerParams(vmem_limit_bytes=60 << 20),
        name="finish",
    )(up, down, out, query, grad_input, output, keyval, vec, bias, value_bias, best, w_query, query_bias, tau)


def local(
    tokens,
    cotangent,
    seg_ids,
    parents,
    tau,
    w_query,
    w_up,
    w_out,
    w_down,
    query_bias,
    up_bias,
    w_keyval,
    value_bias,
    norm1_gain,
    norm1_bias,
    norm2_gain,
    norm2_bias,
    out_bias,
    down_bias,
):
    vectors = jnp.pad(value_bias.reshape(1, 1), ((6, 9), (0, 15)))
    for i, one in enumerate((norm1_gain, norm1_bias, norm2_gain, norm2_bias, out_bias, down_bias)):
        vectors = vectors + jnp.pad(one.reshape(1, 16), ((i, 15 - i), (0, 0)))
    (cot_all, h2, wu, wd, wq, wo, wkv, h1, q, kv, o, log_sum, x1, best, vec, ub) = forward(
        tokens, cotangent, seg_ids, parents, vectors, query_bias, up_bias, w_keyval, w_query, w_out, w_up, w_down
    )
    output, grad_input, up_sum, down_sum, out_sum, query_sum, vec_sum, bias_sum, keyval_sum, vb_sum = backward(
        tokens, cotangent, cot_all, h2, wu, wd, wq, wo, wkv, h1, q, kv, o, log_sum, x1, vec, ub
    )
    outs = finish(
        up_sum, down_sum, out_sum, query_sum, grad_input, output, keyval_sum, vec_sum, bias_sum, vb_sum, best,
        w_query, query_bias, tau,
    )
    return outs[:9] + tuple(v.reshape(-1) for v in outs[9:16]) + outs[16:]


def solution(mesh):
    fine = Mesh(mesh.devices.reshape(4, 2, 4, 2, 2), AXES)
    dp, tp = ("z", "yh", "x"), ("yl", "c")
    rows, flat, weight = P(AXES, None), P(AXES), P(dp, tp)
    in_specs = (rows, rows, P(dp), P(), P()) + (weight,) * 6 + (rows,) + (flat,) * 7
    out_specs = (rows, rows) + (weight,) * 6 + (rows,) + (flat,) * 7 + (weight, weight)
    return jax.shard_map(local, mesh=fine, in_specs=in_specs, out_specs=out_specs, check_vma=False)
```
